32 devices in a mesh: rep: 4 (over z), fsdp: 8 (over y, x, core).
Axes of the slice: x: 2, y: 2, z: 4, core: 2. Of those that a mesh axis runs over, the one named last changes fastest.
Arguments:
- latents: bfloat16 [32, 16, 16, 640], P(('rep', 'fsdp')), may hold values from -6 to 6
- cotangent: bfloat16 [32, 16, 16, 640], P(('rep', 'fsdp')), may hold values from -6 to 6
- conv_weight: bfloat16 [4, 5760, 640], P('rep', 'fsdp'), may hold values from -0.078125 to 0.078125
- norm_gain: float32 [4, 640], P('rep'), may hold values from 0.5 to 1.5
- norm_shift: float32 [4, 640], P('rep'), may hold values from -3 to 3
- partner_bit: int32 [8], replicated, may hold values from 0 to 1
Outputs:
- block_out: bfloat16 [32, 16, 16, 640], P(('rep', 'fsdp'))
- input_grad: bfloat16 [32, 16, 16, 640], P(('rep', 'fsdp'))
- weight_grad: float32 [4, 5760, 640], P('rep', 'fsdp')
- norm_grad: float32 [4, 2, 640], P('rep')
The draws below stay inside these ranges and needn't reach their ends.
Inputs may be any that keep to these rules, and one draw needn't show every extreme that they name: In row shard f, replica r is paired with replica r with bit partner_bit[f] of its index flipped.
All inputs are finite; a program needn't handle non-finite values.
Results may differ from the reference program's by a relative error of at most 0.0065.
Values may be sent and summed in bfloat16 or wider, within the bound.
No kernel may reach another device: no remote copies, remote signals or barrier semaphores. Data moves between devices by JAX's collectives and lax.ppermute only.
A program may use at most 128 MiB of HBM per device.

```python
import jax
import jax.numpy as jnp
from jax import lax

C = 640
GROUPS = 32
HW = 16
LAT = 1
KROWS = 5760
BATCH = 32
N_REP = 4
N_FSDP = 8


def place_ends(values, key, low, top_value):
    longest = values.shape.index(max(values.shape))
    spots = []
    for shift in (0, 1):
        where = [jax.random.randint(jax.random.fold_in(key, axis), (), 0, length) for axis, length in enumerate(values.shape)]
        where[longest] = (where[longest] + shift) % values.shape[longest]
        spots.append(tuple(where))
    return values.at[spots[0]].set(low).at[spots[1]].set(top_value)


def block_scale(stream_key, shape, cuts, low, top_value):
    factor_of = 1.0
    for position, blocks in cuts:
        draws = jax.random.uniform(jax.random.fold_in(jax.random.fold_in(stream_key, 6), position), (blocks,), jnp.float32, low / len(cuts), top_value / len(cuts))
        factor_of = factor_of * jnp.repeat(jnp.exp(draws), shape[position] // blocks).reshape((-1,) + (1,) * (len(shape) - 1 - position))
    return factor_of


def normal_values(own_key, shape, scale, reach, cuts=(), kind=jnp.bfloat16):
    values = scale * jax.random.normal(own_key, shape, jnp.float32)
    if cuts:
        values = values * block_scale(own_key, shape, cuts, -0.22, 0.18)
    return jnp.clip(values, -reach, reach).astype(kind)


def setup_inputs(seed: int = 0) -> dict:
    arg_keys = jax.random.split(jax.random.key(seed), 7)
    return {
        "latents": normal_values(arg_keys[0], (BATCH, HW, HW, C), 1.0, 6.0, ((0, 32),)),
        "cotangent": normal_values(arg_keys[1], (BATCH, HW, HW, C), 1.0, 6.0, ((0, 32),)),
        "conv_weight": normal_values(arg_keys[2], (N_REP, KROWS, C), KROWS ** -0.5, 0.078125, ((0, 4), (1, 8))),
        "norm_gain": jnp.clip(0.5 + 1.0 * jax.random.uniform(arg_keys[3], (N_REP, C), jnp.float32) ** block_scale(arg_keys[3], (N_REP, C), ((0, 4),), -0.2, 0.2), 0.5, 1.5),
        "norm_shift": normal_values(arg_keys[4], (N_REP, C), 0.5, 3.0, ((0, 4),), jnp.float32),
        "partner_bit": place_ends(jax.random.randint(arg_keys[5], (N_FSDP,), 0, 2), jax.random.fold_in(arg_keys[5], 1), 0, 1).astype(jnp.int32),
    }


def norm_forward(values_in, gain, shift, groups):
    count, side, chans = (values_in.shape[0], values_in.shape[1], values_in.shape[3])
    values = values_in.astype(jnp.float32).reshape(count, side * side, groups, chans // groups)
    center = lax.optimization_barrier(jnp.mean(values, axis=(1, 3), keepdims=True))
    spread = lax.optimization_barrier(jnp.mean(jnp.square(values - center), axis=(1, 3), keepdims=True))
    scale_inv = lax.rsqrt(spread + 1e-05)
    normed = (values - center) * scale_inv
    pre_act = normed * gain.reshape(groups, -1) + shift.reshape(groups, -1)
    return (normed, scale_inv, pre_act)

def make_patches(activation):
    count, side, chans = (activation.shape[0], activation.shape[1], activation.shape[3])
    padded = jnp.pad(activation, ((0, 0), (1, 1), (1, 1), (0, 0)))
    pieces = [padded[:, row_off:row_off + side, col_off:col_off + side, :] for row_off in range(3) for col_off in range(3)]
    return jnp.concatenate(pieces, axis=-1).reshape(count * side * side, 9 * chans)

def fold_patches(patch_grad, count, side, chans):
    grads = patch_grad.reshape(count, side, side, 9, chans)
    total = jnp.zeros((count, side + 2, side + 2, chans), jnp.float32)
    for row_off in range(3):
        for col_off in range(3):
            tap = grads[:, :, :, row_off * 3 + col_off, :]
            total = total + jnp.pad(tap, ((0, 0), (row_off, 2 - row_off), (col_off, 2 - col_off), (0, 0)))
    return total[:, 1:-1, 1:-1, :]

def backward_rest(act_grad, normed, scale_inv, pre_act, gain, groups, inv_batch):
    count, side, chans = (act_grad.shape[0], act_grad.shape[1], act_grad.shape[3])
    act_grad = act_grad.reshape(count, side * side, groups, chans // groups)
    sigma = jax.nn.sigmoid(pre_act)
    pre_grad = act_grad * sigma * (1.0 + pre_act * (1.0 - sigma))
    gain_grad = lax.optimization_barrier(jnp.sum(pre_grad * normed, axis=(0, 1))).reshape(-1) * inv_batch
    shift_grad = lax.optimization_barrier(jnp.sum(pre_grad, axis=(0, 1))).reshape(-1) * inv_batch
    normed_grad = pre_grad * gain.reshape(groups, -1)
    first = lax.optimization_barrier(jnp.mean(normed_grad, axis=(1, 3), keepdims=True))
    second = lax.optimization_barrier(jnp.mean(normed_grad * normed, axis=(1, 3), keepdims=True))
    input_grad = scale_inv * (normed_grad - first - normed * second)
    return (input_grad.reshape(count, side, side, chans).astype(jnp.bfloat16), jnp.stack([gain_grad, shift_grad]))

def local_block(block_in, block_cot, weights, gain, shift, inv_batch):
    count, side, chans = (block_in.shape[0], block_in.shape[1], block_in.shape[3])
    normed, scale_inv, pre_act = norm_forward(block_in, gain, shift, GROUPS)
    activation = jax.nn.silu(pre_act).astype(jnp.bfloat16).reshape(count, side, side, chans)
    patches = make_patches(activation)
    cot_rows = block_cot.reshape(count * side * side, chans)
    output = jnp.dot(patches, weights, preferred_element_type=jnp.float32).astype(jnp.bfloat16)
    patch_grad = lax.dot_general(cot_rows, weights, (((1,), (1,)), ((), ())), preferred_element_type=jnp.float32)
    act_grad = fold_patches(patch_grad, count, side, chans)
    input_grad, norm_term = backward_rest(act_grad, normed, scale_inv, pre_act, gain, GROUPS, inv_batch)
    weight_term = lax.dot_general(patches, cot_rows, (((0,), (0,)), ((), ())), preferred_element_type=jnp.float32) * inv_batch
    return (output.reshape(count, side, side, chans), input_grad, weight_term, norm_term)

def reference(latents, cotangent, conv_weight, norm_gain, norm_shift, partner_bit):
    inv_batch = 1.0 / (LAT * N_FSDP)
    shaped_in = latents.reshape(N_REP, N_FSDP, LAT, HW, HW, C)
    shaped_cot = cotangent.reshape(N_REP, N_FSDP, LAT, HW, HW, C)

    def replica(items):
        rep_in, rep_cot, weights, gain, shift = items

        def step(carry, block):
            weight_acc, norm_acc = carry
            output, input_grad, weight_term, norm_term = local_block(block[0], block[1], weights, gain, shift, inv_batch)
            return ((weight_acc + weight_term, norm_acc + norm_term), (output, input_grad))
        start = (jnp.zeros((KROWS, C), jnp.float32), jnp.zeros((2, C), jnp.float32))
        (weight_sum, norm_sum), (outputs, grads) = lax.scan(step, start, (rep_in, rep_cot))
        return (outputs, grads, weight_sum, norm_sum)
    outputs, grads, weight_sums, norm_sums = lax.map(replica, (shaped_in, shaped_cot, conv_weight, norm_gain, norm_shift))
    replica_ids = jnp.arange(N_REP, dtype=jnp.int32)
    shard_ids = jnp.arange(N_FSDP, dtype=jnp.int32)
    flips = jnp.left_shift(jnp.int32(1), partner_bit.astype(jnp.int32))
    partners = jnp.bitwise_xor(replica_ids[:, None], flips[None, :])
    shaped_weight = weight_sums.reshape(N_REP, N_FSDP, KROWS // N_FSDP, C)
    partner_weight = shaped_weight[partners, shard_ids[None, :]]
    weight_grad = (0.5 * (shaped_weight + partner_weight)).reshape(N_REP, KROWS, C)
    norm_partner = jnp.bitwise_xor(replica_ids, flips[0])
    norm_grad = 0.5 * (norm_sums + jnp.take(norm_sums, norm_partner, axis=0))
    block_out = outputs.reshape(BATCH, HW, HW, C)
    input_grad = grads.reshape(BATCH, HW, HW, C)
    return (block_out, input_grad, weight_grad, norm_grad)
```

```python
import functools

import jax
import jax.numpy as jnp
from jax import lax
from jax.experimental import pallas as pl
from jax.experimental.pallas import tpu as pltpu
from jax.sharding import PartitionSpec as P

GROUPS = 32


def partner(value, axis, stride):
    mask = 2**stride
    pairs = [(source, source ^ mask) for source in range(lax.axis_size(axis))]
    return lax.ppermute(value, axis, pairs)


def norm_forward(values_in, gain, shift, groups):
    count, side, chans = (values_in.shape[0], values_in.shape[1], values_in.shape[3])
    values = values_in.astype(jnp.float32).reshape(count, side * side, groups, chans // groups)
    center = jnp.mean(values, axis=(1, 3), keepdims=True)
    spread = jnp.mean(jnp.square(values - center), axis=(1, 3), keepdims=True)
    scale_inv = lax.rsqrt(spread + 1e-05)
    normed = (values - center) * scale_inv
    pre_act = normed * gain.reshape(groups, -1) + shift.reshape(groups, -1)
    return (normed, scale_inv, pre_act)


def make_patches(activation):
    count, side, chans = (activation.shape[0], activation.shape[1], activation.shape[3])
    padded = jnp.pad(activation, ((0, 0), (1, 1), (1, 1), (0, 0)))
    pieces = [
        padded[:, row_off : row_off + side, col_off : col_off + side, :]
        for row_off in range(3)
        for col_off in range(3)
    ]
    return jnp.concatenate(pieces, axis=-1).reshape(count * side * side, 9 * chans)


def fold_patches(patch_grad, count, side, chans):
    grads = patch_grad.reshape(count, side, side, 9, chans)
    total = jnp.zeros((count, side + 2, side + 2, chans), jnp.float32)
    for row_off in range(3):
        for col_off in range(3):
            tap = grads[:, :, :, row_off * 3 + col_off, :]
            total = total + jnp.pad(
                tap, ((0, 0), (row_off, 2 - row_off), (col_off, 2 - col_off), (0, 0))
            )
    return total[:, 1:-1, 1:-1, :]


def backward_rest(act_grad, normed, scale_inv, pre_act, gain, groups, inv_batch):
    count, side, chans = (act_grad.shape[0], act_grad.shape[1], act_grad.shape[3])
    act_grad = act_grad.reshape(count, side * side, groups, chans // groups)
    sigma = jax.nn.sigmoid(pre_act)
    pre_grad = act_grad * sigma * (1.0 + pre_act * (1.0 - sigma))
    gain_grad = jnp.sum(pre_grad * normed, axis=(0, 1)).reshape(-1) * inv_batch
    shift_grad = jnp.sum(pre_grad, axis=(0, 1)).reshape(-1) * inv_batch
    normed_grad = pre_grad * gain.reshape(groups, -1)
    first = jnp.mean(normed_grad, axis=(1, 3), keepdims=True)
    second = jnp.mean(normed_grad * normed, axis=(1, 3), keepdims=True)
    input_grad = scale_inv * (normed_grad - first - normed * second)
    return (
        input_grad.reshape(count, side, side, chans).astype(jnp.bfloat16),
        jnp.stack([gain_grad, shift_grad]),
    )


def shards_general(latents, cotangent, conv_weight, norm_gain, norm_shift, partner_bit):
    count, side, chans = (latents.shape[0], latents.shape[1], latents.shape[3])
    shard_total = lax.axis_size("fsdp")
    inv_batch = 1.0 / (count * shard_total)
    gain = norm_gain[0]
    normed, scale_inv, pre_act = norm_forward(latents, gain, norm_shift[0], GROUPS)
    activation = jax.nn.silu(pre_act).astype(jnp.bfloat16).reshape(count, side, side, chans)
    patches = make_patches(activation)
    cot_rows = cotangent.reshape(count * side * side, chans)
    weight_rows = conv_weight[0]
    output = jnp.dot(
        patches,
        lax.all_gather(weight_rows, "fsdp", axis=0, tiled=True),
        preferred_element_type=jnp.float32,
    )
    patch_grad = lax.dot_general(
        cot_rows,
        lax.all_gather(weight_rows, "fsdp", axis=0, tiled=True),
        (((1,), (1,)), ((), ())),
        preferred_element_type=jnp.float32,
    )
    block_out = output.astype(jnp.bfloat16).reshape(count, side, side, chans)
    act_grad = fold_patches(patch_grad, count, side, chans)
    input_grad, norm_term = backward_rest(
        act_grad, normed, scale_inv, pre_act, gain, GROUPS, inv_batch
    )
    weight_term = (
        lax.dot_general(
            patches, cot_rows, (((0,), (0,)), ((), ())), preferred_element_type=jnp.float32
        )
        * inv_batch
    )
    shard_rows = weight_rows.shape[0]
    term_pieces = weight_term.reshape(shard_total, shard_rows, chans)
    received = lax.all_to_all(
        term_pieces.astype(jnp.bfloat16), "fsdp", split_axis=0, concat_axis=0, tiled=True
    ).astype(term_pieces.dtype)
    weight_shard = jnp.sum(received, axis=0)
    bit_count = lax.axis_size("rep").bit_length() - 1
    shard_bit = lax.dynamic_index_in_dim(partner_bit, lax.axis_index("fsdp"), 0, keepdims=False)
    norm_bit = partner_bit[0]
    paired_norm = norm_term
    for bit_index in range(bit_count):
        other_norm = partner(norm_term, "rep", bit_index)
        paired_norm = jnp.where(norm_bit == bit_index, 0.5 * (norm_term + other_norm), paired_norm)
    norm_avg = lax.psum(paired_norm, "fsdp")
    weight_avg = weight_shard
    for bit_index in range(bit_count):
        other_weight = partner(weight_shard.astype(jnp.bfloat16), "rep", bit_index).astype(
            weight_shard.dtype
        )
        weight_avg = jnp.where(
            shard_bit == bit_index, 0.5 * (weight_shard + other_weight), weight_avg
        )
    return (block_out, input_grad, weight_avg[None], norm_avg[None])


CORE, ACROSS, ALONG = 1, 2, 4
VMEM_LIMIT = 48 * 1024 * 1024


def swap(value, axis, mask):
    pairs = [(source, source ^ mask) for source in range(lax.axis_size(axis))]
    return lax.ppermute(value, axis, pairs)


def call(kernel, outs, args, scratch=(), flops=0):
    vmem = pl.BlockSpec(memory_space=pltpu.VMEM)
    smem = pl.BlockSpec(memory_space=pltpu.SMEM)
    size = sum(a.size * a.dtype.itemsize for a in args)
    size += sum(o.size * o.dtype.itemsize for o in outs)
    return pl.pallas_call(
        kernel,
        out_shape=tuple(outs),
        in_specs=[smem if a.dtype == jnp.int32 else vmem for a in args],
        out_specs=tuple(vmem for _ in outs),
        scratch_shapes=list(scratch),
        compiler_params=pltpu.CompilerParams(vmem_limit_bytes=VMEM_LIMIT),
        cost_estimate=pl.CostEstimate(flops=flops, bytes_accessed=size, transcendentals=0),
    )(*args)


def shaped(shape, dtype):
    return jax.ShapeDtypeStruct(shape, dtype)


def group_matrix(chans, groups, transpose):
    width = chans // groups
    shape = (128, chans) if transpose else (chans, 128)
    chan = lax.broadcasted_iota(jnp.int32, shape, 1 if transpose else 0)
    low = lax.broadcasted_iota(jnp.int32, shape, 0 if transpose else 1) * width
    return ((chan >= low) & (chan < low + width)).astype(jnp.float32)


def group_mean(columns, total, groups):
    chans = columns.shape[1]
    exact = dict(precision=lax.Precision.HIGHEST, preferred_element_type=jnp.float32)
    sums = jnp.dot(columns, group_matrix(chans, groups, False), **exact)
    return jnp.dot(sums, group_matrix(chans, groups, True), **exact) * (1.0 / total)


def col_sums(*values):
    rows = [jnp.sum(value, axis=0, keepdims=True) for value in values]
    fill = jnp.zeros((8 - len(rows), rows[0].shape[1]), jnp.float32)
    return jnp.concatenate(rows + [fill], axis=0)


def norm_kernel(groups, latent, gain, shift, act, stats):
    values = latent[...].astype(jnp.float32)
    total = values.shape[0] * values.shape[1] // groups
    center = group_mean(col_sums(values), total, groups)[0:1]
    moved = values - center
    spread = group_mean(col_sums(moved * moved), total, groups)[0:1]
    scale_inv = lax.rsqrt(spread + 1e-05)
    pre = moved * scale_inv * gain[...] + shift[...]
    act[...] = (pre / (1.0 + jnp.exp(-pre))).astype(jnp.bfloat16)
    stats[0:1] = center
    stats[1:2] = scale_inv


def tap_matrix(tap, side, transpose):
    shape = (side * side, side * side)
    here = lax.broadcasted_iota(jnp.int32, shape, 1 if transpose else 0)
    there = lax.broadcasted_iota(jnp.int32, shape, 0 if transpose else 1)
    row_off = lax.div(tap, 3)
    col_off = tap - 3 * row_off
    bits = side.bit_length() - 1
    rows = lax.shift_right_logical(there, bits) - lax.shift_right_logical(here, bits)
    cols = (there & (side - 1)) - (here & (side - 1))
    hit = (rows == row_off - 1) & (cols == col_off - 1)
    return hit.astype(jnp.float32).astype(jnp.bfloat16)


def place_weights(info, own, other, wide):
    rows = own.shape[0]
    wide[...] = jnp.zeros_like(wide)
    wide[pl.ds(pl.multiple_of(info[1], 16), rows), :] = own[...]
    wide[pl.ds(pl.multiple_of(info[2], 16), rows), :] = other[...]


def make_cot_kernel(side, taps):
    def kernel(info, c0, c1, c2, c3, w_own, w_other, moved, g0, g1, g2, g3, cots, wide, tapm, grads):
        chans = w_own.shape[1]
        place_weights(info, w_own, w_other, wide)
        for index, ref in enumerate((c0, c1, c2, c3)):
            cots[index] = ref[...]
        for tap in range(taps):
            tapm[tap] = tap_matrix(info[0] + tap, side, True)

        @pl.loop(0, 4)
        def _(index):
            total = None
            for tap in range(taps):
                piece = jnp.dot(
                    tapm[tap], cots[index], preferred_element_type=jnp.float32
                ).astype(jnp.bfloat16)
                moved[tap, index] = piece
                term = lax.dot_general(
                    piece,
                    wide[tap * chans : (tap + 1) * chans, :],
                    (((1,), (1,)), ((), ())),
                    preferred_element_type=jnp.float32,
                )
                total = term if total is None else total + term
            grads[index] = total

        for index, ref in enumerate((g0, g1, g2, g3)):
            ref[...] = grads[index].astype(ref.dtype)

    return kernel


def make_out_kernel(side, taps):
    def kernel(info, a0, a1, a2, a3, w_own, w_other, y0, y1, y2, y3, acts, wide, tapm, outs):
        chans = w_own.shape[1]
        place_weights(info, w_own, w_other, wide)
        for index, ref in enumerate((a0, a1, a2, a3)):
            acts[index] = ref[...]
        for tap in range(taps):
            tapm[tap] = tap_matrix(info[0] + tap, side, False)

        @pl.loop(0, 4)
        def _(index):
            total = None
            for tap in range(taps):
                piece = jnp.dot(
                    tapm[tap], acts[index], preferred_element_type=jnp.float32
                ).astype(jnp.bfloat16)
                term = jnp.dot(
                    piece,
                    wide[tap * chans : (tap + 1) * chans, :],
                    preferred_element_type=jnp.float32,
                )
                total = term if total is None else total + term
            outs[index] = total

        for index, ref in enumerate((y0, y1, y2, y3)):
            ref[...] = outs[index].astype(ref.dtype)

    return kernel


def make_weight_kernel(taps, factor):
    def kernel(info, a0, a1, a2, a3, moved, keep, send, turned, wide):
        area, chans = a0.shape
        rows = keep.shape[0]
        for index, ref in enumerate((a0, a1, a2, a3)):
            turned[:, index * area : (index + 1) * area] = ref[...].T

        @pl.loop(0, taps)
        def _(tap):
            cots = moved[tap].reshape(4 * area, chans)
            wide[pl.ds(pl.multiple_of(tap * chans, 128), chans), :] = jnp.dot(
                turned[...], cots, preferred_element_type=jnp.float32
            )

        keep[...] = wide[pl.ds(pl.multiple_of(info[1], 16), rows), :] * factor
        send[...] = (wide[pl.ds(pl.multiple_of(info[2], 16), rows), :] * factor).astype(jnp.bfloat16)

    return kernel


def back_kernel(groups, factor, latent, stats, gain, shift, g0, g1, g2, grad, terms):
    values = latent[...].astype(jnp.float32)
    total = values.shape[0] * values.shape[1] // groups
    scale_inv = stats[1:2]
    normed = (values - stats[0:1]) * scale_inv
    pre = normed * gain[...] + shift[...]
    act_grad = g0[...] + g1[...].astype(jnp.float32) + g2[...].astype(jnp.float32)
    sigma = 1.0 / (1.0 + jnp.exp(-pre))
    pre_grad = act_grad * sigma * (1.0 + pre * (1.0 - sigma))
    sums = col_sums(pre_grad * normed, pre_grad)
    terms[...] = sums[0:2] * factor
    means = group_mean(sums * gain[...], total, groups)
    grad[...] = (scale_inv * (pre_grad * gain[...] - means[1:2] - normed * means[0:1])).astype(jnp.bfloat16)


def shards_plane(latents, cotangent, conv_weight, norm_gain, norm_shift, partner_bit):
    side, chans = latents.shape[1], latents.shape[3]
    area = side * side
    shard_total = lax.axis_size("fsdp")
    inv_batch = 1.0 / shard_total
    f32, bf16 = jnp.float32, jnp.bfloat16
    place = lax.axis_index("fsdp")
    weight = conv_weight[0]
    rows = weight.shape[0]
    starts = [2 * rows * chip for chip in range(shard_total // 2)]
    taps = max((start % chans + 2 * rows + chans - 1) // chans for start in starts)
    start = 2 * rows * (place // 2)
    first = jnp.minimum(start // chans, 9 - taps)
    offset = start - first * chans
    core = place % 2
    info = jnp.stack([first, offset + rows * core, offset + rows * (1 - core)]).astype(jnp.int32)

    latent = latents.reshape(area, chans)
    cot0 = cotangent.reshape(area, chans)
    cot1 = swap(cot0, "fsdp", ACROSS)
    cot2 = swap(cot0, "fsdp", ALONG)
    other_weight = swap(weight, "fsdp", CORE)
    act0, stats = call(
        functools.partial(norm_kernel, GROUPS),
        [shaped((area, chans), bf16), shaped((2, chans), f32)],
        [latent, norm_gain, norm_shift],
    )
    act1 = swap(act0, "fsdp", ACROSS)
    act2 = swap(act0, "fsdp", ALONG)
    cot3 = swap(cot1, "fsdp", ALONG)
    act3 = swap(act2, "fsdp", ACROSS)

    plane = shaped((area, chans), f32)
    plane_b = shaped((area, chans), bf16)
    scratch = [
        pltpu.VMEM((4, area, chans), bf16),
        pltpu.VMEM((taps * chans, chans), bf16),
        pltpu.VMEM((taps, area, area), bf16),
        pltpu.VMEM((4, area, chans), f32),
    ]
    conv_flops = 8 * area * taps * chans * (chans + area)
    moved, grad0, grad1, grad2, grad3 = call(
        make_cot_kernel(side, taps),
        [shaped((taps, 4, area, chans), bf16), plane, plane, plane_b, plane_b],
        [info, cot0, cot1, cot2, cot3, weight, other_weight],
        scratch,
        conv_flops,
    )
    keep, send = call(
        make_weight_kernel(taps, inv_batch),
        [shaped((rows, chans), f32), shaped((rows, chans), bf16)],
        [info, act0, act1, act2, act3, moved],
        [pltpu.VMEM((chans, 4 * area), bf16), pltpu.VMEM((taps * chans, chans), f32)],
        8 * area * taps * chans * chans,
    )
    weight_shard = keep + swap(send, "fsdp", CORE).astype(f32)
    weight_b = weight_shard.astype(bf16)
    pair1 = swap(weight_b, "rep", 1)
    pair2 = swap(weight_b, "rep", 2)

    grad_in = swap(grad3, "fsdp", ALONG)
    grad_y = swap(grad2, "fsdp", ALONG)
    grad_x = swap((grad1 + grad_in.astype(f32)).astype(bf16), "fsdp", ACROSS)
    out0, out1, out2, out3 = call(
        make_out_kernel(side, taps),
        [plane, plane_b, plane, plane_b],
        [info, act0, act1, act2, act3, weight, other_weight],
        scratch,
        conv_flops,
    )
    out_in = swap(out3, "fsdp", ACROSS)
    out_x = swap(out1, "fsdp", ACROSS)
    out_y = swap((out2 + out_in.astype(f32)).astype(bf16), "fsdp", ALONG)

    input_grad, terms = call(
        functools.partial(back_kernel, GROUPS, inv_batch),
        [plane_b, shaped((2, chans), f32)],
        [latent, stats, norm_gain, norm_shift, grad0, grad_x, grad_y],
    )
    for mask in (CORE, ACROSS, ALONG):
        terms = terms + swap(terms, "fsdp", mask)
    block_out = (out0 + out_x.astype(f32) + out_y.astype(f32)).astype(bf16)

    def paired(own, other1, other2, bit):
        other = jnp.where(bit == 0, other1, other2).astype(f32)
        return 0.5 * (own + other)

    norm_avg = paired(terms, swap(terms, "rep", 1), swap(terms, "rep", 2), partner_bit[0])
    shard_bit = lax.dynamic_index_in_dim(partner_bit, place, 0, keepdims=False)
    weight_avg = paired(weight_shard, pair1, pair2, shard_bit)
    shape = (1, side, side, chans)
    return (block_out.reshape(shape), input_grad.reshape(shape), weight_avg[None], norm_avg[None])


def solution(mesh):
    in_specs = (
        P(("rep", "fsdp"), None, None, None),
        P(("rep", "fsdp"), None, None, None),
        P("rep", "fsdp", None),
        P("rep", None),
        P("rep", None),
        P(),
    )
    out_specs = (
        P(("rep", "fsdp"), None, None, None),
        P(("rep", "fsdp"), None, None, None),
        P("rep", "fsdp", None),
        P("rep", None, None),
    )
    planes = mesh.shape["fsdp"] == 8 and mesh.shape["rep"] == 4
    shards = shards_plane if planes else shards_general
    return jax.shard_map(shards, mesh=mesh, in_specs=in_specs, out_specs=out_specs, check_vma=False)
```

```python
import functools

import jax
import jax.numpy as jnp
from jax import lax
from jax.experimental import pallas as pl
from jax.experimental.pallas import tpu as pltpu
from jax.sharding import PartitionSpec as P

GROUPS = 32


def partner(value, axis, stride):
    mask = 2**stride
    pairs = [(source, source ^ mask) for source in range(lax.axis_size(axis))]
    return lax.ppermute(value, axis, pairs)


def norm_forward(values_in, gain, shift, groups):
    count, side, chans = (values_in.shape[0], values_in.shape[1], values_in.shape[3])
    values = values_in.astype(jnp.float32).reshape(count, side * side, groups, chans // groups)
    center = jnp.mean(values, axis=(1, 3), keepdims=True)
    spread = jnp.mean(jnp.square(values - center), axis=(1, 3), keepdims=True)
    scale_inv = lax.rsqrt(spread + 1e-05)
    normed = (values - center) * scale_inv
    pre_act = normed * gain.reshape(groups, -1) + shift.reshape(groups, -1)
    return (normed, scale_inv, pre_act)


def make_patches(activation):
    count, side, chans = (activation.shape[0], activation.shape[1], activation.shape[3])
    padded = jnp.pad(activation, ((0, 0), (1, 1), (1, 1), (0, 0)))
    pieces = [
        padded[:, row_off : row_off + side, col_off : col_off + side, :]
        for row_off in range(3)
        for col_off in range(3)
    ]
    return jnp.concatenate(pieces, axis=-1).reshape(count * side * side, 9 * chans)


def fold_patches(patch_grad, count, side, chans):
    grads = patch_grad.reshape(count, side, side, 9, chans)
    total = jnp.zeros((count, side + 2, side + 2, chans), jnp.float32)
    for row_off in range(3):
        for col_off in range(3):
            tap = grads[:, :, :, row_off * 3 + col_off, :]
            total = total + jnp.pad(
                tap, ((0, 0), (row_off, 2 - row_off), (col_off, 2 - col_off), (0, 0))
            )
    return total[:, 1:-1, 1:-1, :]


def backward_rest(act_grad, normed, scale_inv, pre_act, gain, groups, inv_batch):
    count, side, chans = (act_grad.shape[0], act_grad.shape[1], act_grad.shape[3])
    act_grad = act_grad.reshape(count, side * side, groups, chans // groups)
    sigma = jax.nn.sigmoid(pre_act)
    pre_grad = act_grad * sigma * (1.0 + pre_act * (1.0 - sigma))
    gain_grad = jnp.sum(pre_grad * normed, axis=(0, 1)).reshape(-1) * inv_batch
    shift_grad = jnp.sum(pre_grad, axis=(0, 1)).reshape(-1) * inv_batch
    normed_grad = pre_grad * gain.reshape(groups, -1)
    first = jnp.mean(normed_grad, axis=(1, 3), keepdims=True)
    second = jnp.mean(normed_grad * normed, axis=(1, 3), keepdims=True)
    input_grad = scale_inv * (normed_grad - first - normed * second)
    return (
        input_grad.reshape(count, side, side, chans).astype(jnp.bfloat16),
        jnp.stack([gain_grad, shift_grad]),
    )


def shards_general(latents, cotangent, conv_weight, norm_gain, norm_shift, partner_bit):
    count, side, chans = (latents.shape[0], latents.shape[1], latents.shape[3])
    shard_total = lax.axis_size("fsdp")
    inv_batch = 1.0 / (count * shard_total)
    gain = norm_gain[0]
    normed, scale_inv, pre_act = norm_forward(latents, gain, norm_shift[0], GROUPS)
    activation = jax.nn.silu(pre_act).astype(jnp.bfloat16).reshape(count, side, side, chans)
    patches = make_patches(activation)
    cot_rows = cotangent.reshape(count * side * side, chans)
    weight_rows = conv_weight[0]
    output = jnp.dot(
        patches,
        lax.all_gather(weight_rows, "fsdp", axis=0, tiled=True),
        preferred_element_type=jnp.float32,
    )
    patch_grad = lax.dot_general(
        cot_rows,
        lax.all_gather(weight_rows, "fsdp", axis=0, tiled=True),
        (((1,), (1,)), ((), ())),
        preferred_element_type=jnp.float32,
    )
    block_out = output.astype(jnp.bfloat16).reshape(count, side, side, chans)
    act_grad = fold_patches(patch_grad, count, side, chans)
    input_grad, norm_term = backward_rest(
        act_grad, normed, scale_inv, pre_act, gain, GROUPS, inv_batch
    )
    weight_term = (
        lax.dot_general(
            patches, cot_rows, (((0,), (0,)), ((), ())), preferred_element_type=jnp.float32
        )
        * inv_batch
    )
    shard_rows = weight_rows.shape[0]
    term_pieces = weight_term.reshape(shard_total, shard_rows, chans)
    received = lax.all_to_all(
        term_pieces.astype(jnp.bfloat16), "fsdp", split_axis=0, concat_axis=0, tiled=True
    ).astype(term_pieces.dtype)
    weight_shard = jnp.sum(received, axis=0)
    bit_count = lax.axis_size("rep").bit_length() - 1
    shard_bit = lax.dynamic_index_in_dim(partner_bit, lax.axis_index("fsdp"), 0, keepdims=False)
    norm_bit = partner_bit[0]
    paired_norm = norm_term
    for bit_index in range(bit_count):
        other_norm = partner(norm_term, "rep", bit_index)
        paired_norm = jnp.where(norm_bit == bit_index, 0.5 * (norm_term + other_norm), paired_norm)
    norm_avg = lax.psum(paired_norm, "fsdp")
    weight_avg = weight_shard
    for bit_index in range(bit_count):
        other_weight = partner(weight_shard.astype(jnp.bfloat16), "rep", bit_index).astype(
            weight_shard.dtype
        )
        weight_avg = jnp.where(
            shard_bit == bit_index, 0.5 * (weight_shard + other_weight), weight_avg
        )
    return (block_out, input_grad, weight_avg[None], norm_avg[None])


CORE, ACROSS, ALONG = 1, 2, 4
EARLY = 256
VMEM_LIMIT = 32 * 1024 * 1024
F32, BF16 = jnp.float32, jnp.bfloat16


def swap(value, axis, mask):
    pairs = [(source, source ^ mask) for source in range(lax.axis_size(axis))]
    return lax.ppermute(value, axis, pairs)


def after(value, *others):
    return lax.optimization_barrier((value, *others))[0]


def call(kernel, outs, args, scratch=(), flops=0, spaces=None):
    vmem = pl.BlockSpec(memory_space=pltpu.VMEM)
    smem = pl.BlockSpec(memory_space=pltpu.SMEM)
    size = sum(a.size * a.dtype.itemsize for a in args)
    size += sum(o.size * o.dtype.itemsize for o in outs)
    specs = spaces or [smem if a.dtype == jnp.int32 else vmem for a in args]
    return pl.pallas_call(
        kernel,
        out_shape=tuple(outs),
        in_specs=specs,
        out_specs=tuple(vmem for _ in outs),
        scratch_shapes=list(scratch),
        compiler_params=pltpu.CompilerParams(vmem_limit_bytes=VMEM_LIMIT),
        cost_estimate=pl.CostEstimate(flops=flops, bytes_accessed=size, transcendentals=0),
    )(*args)


def shaped(shape, dtype):
    return jax.ShapeDtypeStruct(shape, dtype)


def matmul(left, right):
    return jnp.dot(left, right, preferred_element_type=F32)


def group_matrix(chans, groups, transpose):
    width = chans // groups
    shape = (128, chans) if transpose else (chans, 128)
    chan = lax.broadcasted_iota(jnp.int32, shape, 1 if transpose else 0)
    low = lax.broadcasted_iota(jnp.int32, shape, 0 if transpose else 1) * width
    return ((chan >= low) & (chan < low + width)).astype(F32)


def group_mean(columns, total, groups):
    chans = columns.shape[1]
    exact = dict(precision=lax.Precision.HIGHEST, preferred_element_type=F32)
    sums = jnp.dot(columns, group_matrix(chans, groups, False), **exact)
    return jnp.dot(sums, group_matrix(chans, groups, True), **exact) * (1.0 / total)


def col_sums(*values):
    rows = [jnp.sum(value, axis=0, keepdims=True) for value in values]
    fill = jnp.zeros((8 - len(rows), rows[0].shape[1]), F32)
    return jnp.concatenate(rows + [fill], axis=0)


def norm_kernel(groups, latent_hbm, gain_hbm, shift_hbm, act, stats, latent, gain, shift, sems):
    copies = [
        pltpu.make_async_copy(source, target, sems.at[index])
        for index, (source, target) in enumerate(
            ((latent_hbm, latent), (gain_hbm, gain), (shift_hbm, shift))
        )
    ]
    for copy in copies:
        copy.start()
    for copy in copies:
        copy.wait()
    values = latent[...].astype(F32)
    total = values.shape[0] * values.shape[1] // groups
    center = group_mean(col_sums(values), total, groups)[0:1]
    moved = values - center
    spread = group_mean(col_sums(moved * moved), total, groups)[0:1]
    scale_inv = lax.rsqrt(spread + 1e-05)
    pre = moved * scale_inv * gain[...] + shift[...]
    act[...] = (pre / (1.0 + jnp.exp(-pre))).astype(BF16)
    stats[0:1] = center
    stats[1:2] = scale_inv


def tap_matrix(tap, side, transpose):
    shape = (side * side, side * side)
    here = lax.broadcasted_iota(jnp.int32, shape, 1 if transpose else 0)
    there = lax.broadcasted_iota(jnp.int32, shape, 0 if transpose else 1)
    row_off = lax.div(tap, 3)
    col_off = tap - 3 * row_off
    bits = side.bit_length() - 1
    rows = lax.shift_right_logical(there, bits) - lax.shift_right_logical(here, bits)
    cols = (there & (side - 1)) - (here & (side - 1))
    hit = (rows == row_off - 1) & (cols == col_off - 1)
    return hit.astype(F32).astype(BF16)


def prepare_kernel(side, taps, info, own, other, wide, turned, gather, scatter):
    rows, chans = own.shape
    area = side * side
    wide[...] = jnp.zeros_like(wide)
    wide[pl.ds(pl.multiple_of(info[1], 16), rows), :] = own[...]
    wide[pl.ds(pl.multiple_of(info[2], 16), rows), :] = other[...]
    for tap in range(taps):
        part = slice(tap * chans, (tap + 1) * chans)
        turned[part, :] = wide[part, :].T
        gather[tap * area : (tap + 1) * area, :] = tap_matrix(info[0] + tap, side, False)
        scatter[tap * area : (tap + 1) * area, :] = tap_matrix(info[0] + tap, side, True)


def move_into(target, index, taps, matrices, value):
    area, width = value.shape
    moved = matmul(matrices, value).astype(BF16)
    for tap in range(taps):
        target[index * area : (index + 1) * area, tap * width : (tap + 1) * width] = moved[
            tap * area : (tap + 1) * area
        ]


def early_kernel(taps, scatter, c0, c1, c2, c3, a0, a1, a2, moved, part, turned):
    area = a0.shape[0]
    for index, ref in enumerate((c0, c1, c2, c3)):
        move_into(moved, index, taps, scatter[...], ref[...])
    for index, ref in enumerate((a0, a1, a2)):
        turned[:, index * area : (index + 1) * area] = ref[...].T
    part[...] = matmul(turned[...], moved[: 3 * area, :])


def put_terms(info, taps, factor, terms, keep, send, wide):
    rows, width = keep.shape
    chans = terms.shape[0]
    for tap in range(taps):
        wide[tap * chans : (tap + 1) * chans, :] = terms[:, tap * width : (tap + 1) * width] * factor
    keep[...] = wide[pl.ds(pl.multiple_of(info[1], 16), rows), :]
    send[...] = wide[pl.ds(pl.multiple_of(info[2], 16), rows), :].astype(BF16)


def finish_kernel(taps, factor, info, a3, moved, part, keep, send, wide):
    area = a3.shape[0]
    terms = part[...] + matmul(a3[...].T, moved[3 * area :, :])
    put_terms(info, taps, factor, terms, keep, send, wide)


def late_kernel(taps, factor, info, scatter, c0, c1, c2, c3, a0, a1, a2, a3, moved, keep, send, turned, wide):
    area = a0.shape[0]
    for index, ref in enumerate((c0, c1, c2, c3)):
        move_into(moved, index, taps, scatter[...], ref[...])
    for index, ref in enumerate((a0, a1, a2, a3)):
        turned[:, index * area : (index + 1) * area] = ref[...].T
    terms = matmul(turned[...], moved[...])
    put_terms(info, taps, factor, terms, keep, send, wide)


def split_latents(value, refs):
    area = refs[0].shape[0]
    for index, ref in enumerate(refs):
        ref[...] = value[index * area : (index + 1) * area].astype(ref.dtype)


def out_kernel(taps, gather, a0, a1, a2, a3, wide, y0, y1, y2, y3, moved):
    for index, ref in enumerate((a0, a1, a2, a3)):
        move_into(moved, index, taps, gather[...], ref[...])
    split_latents(matmul(moved[...], wide[...]), (y0, y1, y2, y3))


def grad_kernel(taps, early, late, turned, g0, g1, g2, g3, moved):
    first, second = early.shape[1] // taps, late.shape[1] // taps
    chans = first + second
    for tap in range(taps):
        moved[:, tap * chans : tap * chans + first] = early[:, tap * first : (tap + 1) * first]
        moved[:, tap * chans + first : (tap + 1) * chans] = late[:, tap * second : (tap + 1) * second]
    split_latents(matmul(moved[...], turned[...]), (g0, g1, g2, g3))


def back_kernel(groups, factor, latent, stats, gain, shift, g0, g1, g2, grad, terms):
    values = latent[...].astype(F32)
    total = values.shape[0] * values.shape[1] // groups
    scale_inv = stats[1:2]
    normed = (values - stats[0:1]) * scale_inv
    pre = normed * gain[...] + shift[...]
    act_grad = g0[...] + g1[...].astype(F32) + g2[...].astype(F32)
    sigma = 1.0 / (1.0 + jnp.exp(-pre))
    pre_grad = act_grad * sigma * (1.0 + pre * (1.0 - sigma))
    sums = col_sums(pre_grad * normed, pre_grad)
    terms[...] = sums[0:2] * factor
    means = group_mean(sums * gain[...], total, groups)
    grad[...] = (scale_inv * (pre_grad * gain[...] - means[1:2] - normed * means[0:1])).astype(BF16)


def shards_plane(latents, cotangent, conv_weight, norm_gain, norm_shift, partner_bit):
    side, chans = latents.shape[1], latents.shape[3]
    area = side * side
    shard_total = lax.axis_size("fsdp")
    inv_batch = 1.0 / shard_total
    place = lax.axis_index("fsdp")
    weight = conv_weight[0]
    rows = weight.shape[0]
    starts = [2 * rows * chip for chip in range(shard_total // 2)]
    taps = max((start % chans + 2 * rows + chans - 1) // chans for start in starts)
    start = 2 * rows * (place // 2)
    first = jnp.minimum(start // chans, 9 - taps)
    offset = start - first * chans
    core = place % 2
    info = jnp.stack([first, offset + rows * core, offset + rows * (1 - core)]).astype(jnp.int32)
    late = chans - EARLY

    latent = latents.reshape(area, chans)
    cot = cotangent.reshape(area, chans)
    cot0, rest0 = cot[:, :EARLY], cot[:, EARLY:]
    cot1 = swap(cot0, "fsdp", ACROSS)
    cot2 = swap(cot0, "fsdp", ALONG)
    other_weight = swap(weight, "fsdp", CORE)
    hbm = pl.BlockSpec(memory_space=pltpu.HBM)
    act0, stats = call(
        functools.partial(norm_kernel, GROUPS),
        [shaped((area, chans), BF16), shaped((2, chans), F32)],
        [latent, norm_gain, norm_shift],
        [
            pltpu.VMEM((area, chans), BF16),
            pltpu.VMEM((1, chans), F32),
            pltpu.VMEM((1, chans), F32),
            pltpu.SemaphoreType.DMA((3,)),
        ],
        spaces=[hbm] * 3,
    )
    act1 = swap(act0, "fsdp", ACROSS)
    act2 = swap(act0, "fsdp", ALONG)
    cot3 = swap(cot1, "fsdp", ALONG)
    act3 = swap(act2, "fsdp", ACROSS)
    wide_shape = (taps * chans, chans)
    wide, turned, gather, scatter = call(
        functools.partial(prepare_kernel, side, taps),
        [shaped(wide_shape, BF16)] * 2 + [shaped((taps * area, area), BF16)] * 2,
        [info, weight, other_weight],
    )
    moved, part = call(
        functools.partial(early_kernel, taps),
        [shaped((4 * area, taps * EARLY), BF16), shaped((chans, taps * EARLY), F32)],
        [scatter, cot0, cot1, cot2, cot3, act0, act1, act2],
        [pltpu.VMEM((chans, 3 * area), BF16)],
        6 * area * taps * EARLY * chans,
    )
    rest2 = swap(after(rest0, act2), "fsdp", ALONG)
    rest1 = swap(after(rest0, act3), "fsdp", ACROSS)
    rest3 = swap(rest1, "fsdp", ALONG)

    def shard_of(keep, send):
        own = keep + swap(send, "fsdp", CORE).astype(F32)
        narrow = own.astype(BF16)
        return own, swap(narrow, "rep", 1), swap(narrow, "rep", 2)

    keep, send = call(
        functools.partial(finish_kernel, taps, inv_batch),
        [shaped((rows, EARLY), F32), shaped((rows, EARLY), BF16)],
        [info, act3, moved, part],
        [pltpu.VMEM((taps * chans, EARLY), F32)],
        2 * area * taps * EARLY * chans,
    )
    early_shard = shard_of(keep, send)

    plane = shaped((area, chans), F32)
    plane_b = shaped((area, chans), BF16)
    conv_flops = 8 * area * taps * chans * chans
    out0, out1, out2, out3 = call(
        functools.partial(out_kernel, taps),
        [plane, plane_b, plane, plane_b],
        [gather, act0, act1, act2, act3, wide],
        [pltpu.VMEM((4 * area, taps * chans), BF16)],
        conv_flops,
    )
    out_in = swap(out3, "fsdp", ACROSS)
    out_x = swap(out1, "fsdp", ACROSS)
    out_y = swap((out2 + out_in.astype(F32)).astype(BF16), "fsdp", ALONG)

    moved_late, keep, send = call(
        functools.partial(late_kernel, taps, inv_batch),
        [shaped((4 * area, taps * late), BF16), shaped((rows, late), F32), shaped((rows, late), BF16)],
        [info, scatter, rest0, rest1, rest2, rest3, act0, act1, act2, act3],
        [pltpu.VMEM((chans, 4 * area), BF16), pltpu.VMEM((taps * chans, late), F32)],
        8 * area * taps * late * chans,
    )
    late_shard = shard_of(keep, send)

    grad0, grad1, grad2, grad3 = call(
        functools.partial(grad_kernel, taps),
        [plane, plane, plane_b, plane_b],
        [moved, moved_late, turned],
        [pltpu.VMEM((4 * area, taps * chans), BF16)],
        conv_flops,
    )
    grad_in = swap(grad3, "fsdp", ALONG)
    grad_y = swap(grad2, "fsdp", ALONG)
    grad_x = swap((grad1 + grad_in.astype(F32)).astype(BF16), "fsdp", ACROSS)

    input_grad, terms = call(
        functools.partial(back_kernel, GROUPS, inv_batch),
        [plane_b, shaped((2, chans), F32)],
        [latent, stats, norm_gain, norm_shift, grad0, grad_x, grad_y],
    )
    for mask in (CORE, ACROSS, ALONG):
        terms = terms + swap(terms, "fsdp", mask)
    block_out = (out0 + out_x.astype(F32) + out_y.astype(F32)).astype(BF16)

    def paired(own, other1, other2, bit):
        other = jnp.where(bit == 0, other1, other2).astype(F32)
        return 0.5 * (own + other)

    norm_avg = paired(terms, swap(terms, "rep", 1), swap(terms, "rep", 2), partner_bit[0])
    shard_bit = lax.dynamic_index_in_dim(partner_bit, place, 0, keepdims=False)
    weight_avg = jnp.concatenate(
        [paired(*early_shard, shard_bit), paired(*late_shard, shard_bit)], axis=1
    )
    shape = (1, side, side, chans)
    return (block_out.reshape(shape), input_grad.reshape(shape), weight_avg[None], norm_avg[None])


def solution(mesh):
    in_specs = (
        P(("rep", "fsdp"), None, None, None),
        P(("rep", "fsdp"), None, None, None),
        P("rep", "fsdp", None),
        P("rep", None),
        P("rep", None),
        P(),
    )
    out_specs = (
        P(("rep", "fsdp"), None, None, None),
        P(("rep", "fsdp"), None, None, None),
        P("rep", "fsdp", None),
        P("rep", None, None),
    )
    planes = mesh.shape["fsdp"] == 8 and mesh.shape["rep"] == 4
    shards = shards_plane if planes else shards_general
    return jax.shard_map(shards, mesh=mesh, in_specs=in_specs, out_specs=out_specs, check_vma=False)
```

```python
import functools

import jax
import jax.numpy as jnp
from jax import lax
from jax.experimental import pallas as pl
from jax.experimental.pallas import tpu as pltpu
from jax.sharding import PartitionSpec as P

GROUPS = 32


def partner(value, axis, stride):
    mask = 2**stride
    pairs = [(source, source ^ mask) for source in range(lax.axis_size(axis))]
    return lax.ppermute(value, axis, pairs)


def norm_forward(values_in, gain, shift, groups):
    count, side, chans = (values_in.shape[0], values_in.shape[1], values_in.shape[3])
    values = values_in.astype(jnp.float32).reshape(count, side * side, groups, chans // groups)
    center = jnp.mean(values, axis=(1, 3), keepdims=True)
    spread = jnp.mean(jnp.square(values - center), axis=(1, 3), keepdims=True)
    scale_inv = lax.rsqrt(spread + 1e-05)
    normed = (values - center) * scale_inv
    pre_act = normed * gain.reshape(groups, -1) + shift.reshape(groups, -1)
    return (normed, scale_inv, pre_act)


def make_patches(activation):
    count, side, chans = (activation.shape[0], activation.shape[1], activation.shape[3])
    padded = jnp.pad(activation, ((0, 0), (1, 1), (1, 1), (0, 0)))
    pieces = [
        padded[:, row_off : row_off + side, col_off : col_off + side, :]
        for row_off in range(3)
        for col_off in range(3)
    ]
    return jnp.concatenate(pieces, axis=-1).reshape(count * side * side, 9 * chans)


def fold_patches(patch_grad, count, side, chans):
    grads = patch_grad.reshape(count, side, side, 9, chans)
    total = jnp.zeros((count, side + 2, side + 2, chans), jnp.float32)
    for row_off in range(3):
        for col_off in range(3):
            tap = grads[:, :, :, row_off * 3 + col_off, :]
            total = total + jnp.pad(
                tap, ((0, 0), (row_off, 2 - row_off), (col_off, 2 - col_off), (0, 0))
            )
    return total[:, 1:-1, 1:-1, :]


def backward_rest(act_grad, normed, scale_inv, pre_act, gain, groups, inv_batch):
    count, side, chans = (act_grad.shape[0], act_grad.shape[1], act_grad.shape[3])
    act_grad = act_grad.reshape(count, side * side, groups, chans // groups)
    sigma = jax.nn.sigmoid(pre_act)
    pre_grad = act_grad * sigma * (1.0 + pre_act * (1.0 - sigma))
    gain_grad = jnp.sum(pre_grad * normed, axis=(0, 1)).reshape(-1) * inv_batch
    shift_grad = jnp.sum(pre_grad, axis=(0, 1)).reshape(-1) * inv_batch
    normed_grad = pre_grad * gain.reshape(groups, -1)
    first = jnp.mean(normed_grad, axis=(1, 3), keepdims=True)
    second = jnp.mean(normed_grad * normed, axis=(1, 3), keepdims=True)
    input_grad = scale_inv * (normed_grad - first - normed * second)
    return (
        input_grad.reshape(count, side, side, chans).astype(jnp.bfloat16),
        jnp.stack([gain_grad, shift_grad]),
    )


def shards_general(latents, cotangent, conv_weight, norm_gain, norm_shift, partner_bit):
    count, side, chans = (latents.shape[0], latents.shape[1], latents.shape[3])
    shard_total = lax.axis_size("fsdp")
    inv_batch = 1.0 / (count * shard_total)
    gain = norm_gain[0]
    normed, scale_inv, pre_act = norm_forward(latents, gain, norm_shift[0], GROUPS)
    activation = jax.nn.silu(pre_act).astype(jnp.bfloat16).reshape(count, side, side, chans)
    patches = make_patches(activation)
    cot_rows = cotangent.reshape(count * side * side, chans)
    weight_rows = conv_weight[0]
    output = jnp.dot(
        patches,
        lax.all_gather(weight_rows, "fsdp", axis=0, tiled=True),
        preferred_element_type=jnp.float32,
    )
    patch_grad = lax.dot_general(
        cot_rows,
        lax.all_gather(weight_rows, "fsdp", axis=0, tiled=True),
        (((1,), (1,)), ((), ())),
        preferred_element_type=jnp.float32,
    )
    block_out = output.astype(jnp.bfloat16).reshape(count, side, side, chans)
    act_grad = fold_patches(patch_grad, count, side, chans)
    input_grad, norm_term = backward_rest(
        act_grad, normed, scale_inv, pre_act, gain, GROUPS, inv_batch
    )
    weight_term = (
        lax.dot_general(
            patches, cot_rows, (((0,), (0,)), ((), ())), preferred_element_type=jnp.float32
        )
        * inv_batch
    )
    shard_rows = weight_rows.shape[0]
    term_pieces = weight_term.reshape(shard_total, shard_rows, chans)
    received = lax.all_to_all(
        term_pieces.astype(jnp.bfloat16), "fsdp", split_axis=0, concat_axis=0, tiled=True
    ).astype(term_pieces.dtype)
    weight_shard = jnp.sum(received, axis=0)
    bit_count = lax.axis_size("rep").bit_length() - 1
    shard_bit = lax.dynamic_index_in_dim(partner_bit, lax.axis_index("fsdp"), 0, keepdims=False)
    norm_bit = partner_bit[0]
    paired_norm = norm_term
    for bit_index in range(bit_count):
        other_norm = partner(norm_term, "rep", bit_index)
        paired_norm = jnp.where(norm_bit == bit_index, 0.5 * (norm_term + other_norm), paired_norm)
    norm_avg = lax.psum(paired_norm, "fsdp")
    weight_avg = weight_shard
    for bit_index in range(bit_count):
        other_weight = partner(weight_shard.astype(jnp.bfloat16), "rep", bit_index).astype(
            weight_shard.dtype
        )
        weight_avg = jnp.where(
            shard_bit == bit_index, 0.5 * (weight_shard + other_weight), weight_avg
        )
    return (block_out, input_grad, weight_avg[None], norm_avg[None])


CORE, ACROSS, ALONG = 1, 2, 4
VMEM_LIMIT = 24 * 1024 * 1024
F32, BF16 = jnp.float32, jnp.bfloat16


def swap(value, axis, mask):
    pairs = [(source, source ^ mask) for source in range(lax.axis_size(axis))]
    return lax.ppermute(value, axis, pairs)


def call(kernel, outs, args, scratch=(), order=()):
    vmem = pl.BlockSpec(memory_space=pltpu.VMEM)
    smem = pl.BlockSpec(memory_space=pltpu.SMEM)
    untouched = pl.BlockSpec(memory_space=pl.ANY)

    def body(*refs):
        kernel(*refs[: len(args)], *refs[len(args) + len(order) :])

    return pl.pallas_call(
        body,
        out_shape=tuple(outs),
        in_specs=[smem if a.dtype == jnp.int32 else vmem for a in args] + [untouched] * len(order),
        out_specs=tuple(vmem for _ in outs),
        scratch_shapes=list(scratch),
        compiler_params=pltpu.CompilerParams(vmem_limit_bytes=VMEM_LIMIT),
    )(*args, *order)


def hold(values, order):
    untouched = pl.BlockSpec(memory_space=pl.ANY)
    return pl.pallas_call(
        lambda *refs: None,
        out_shape=tuple(shaped(value.shape, value.dtype) for value in values),
        in_specs=[untouched] * (len(values) + len(order)),
        out_specs=tuple(untouched for _ in values),
        input_output_aliases={index: index for index in range(len(values))},
    )(*values, *order)


def shaped(shape, dtype):
    return jax.ShapeDtypeStruct(shape, dtype)


def matmul(left, right):
    return jnp.dot(left, right, preferred_element_type=F32)


def group_matrix(chans, groups, transpose):
    width = chans // groups
    shape = (128, chans) if transpose else (chans, 128)
    chan = lax.broadcasted_iota(jnp.int32, shape, 1 if transpose else 0)
    low = lax.broadcasted_iota(jnp.int32, shape, 0 if transpose else 1) * width
    return ((chan >= low) & (chan < low + width)).astype(F32)


def group_mean(columns, total, groups):
    chans = columns.shape[1]
    exact = dict(precision=lax.Precision.HIGHEST, preferred_element_type=F32)
    sums = jnp.dot(columns, group_matrix(chans, groups, False), **exact)
    return jnp.dot(sums, group_matrix(chans, groups, True), **exact) * (1.0 / total)


def col_sums(*values):
    rows = [jnp.sum(value, axis=0, keepdims=True) for value in values]
    fill = jnp.zeros((8 - len(rows), rows[0].shape[1]), F32)
    return jnp.concatenate(rows + [fill], axis=0)


def norm_kernel(groups, latent, gain, shift, act, stats):
    values = latent[...].astype(F32)
    total = values.shape[0] * values.shape[1] // groups
    center = group_mean(col_sums(values), total, groups)[0:1]
    moved = values - center
    spread = group_mean(col_sums(moved * moved), total, groups)[0:1]
    scale_inv = lax.rsqrt(spread + 1e-05)
    pre = moved * scale_inv * gain[...] + shift[...]
    act[...] = (pre / (1.0 + jnp.exp(-pre))).astype(BF16)
    stats[0:1] = center
    stats[1:2] = scale_inv


def tap_matrix(tap, side, transpose):
    shape = (side * side, side * side)
    here = lax.broadcasted_iota(jnp.int32, shape, 1 if transpose else 0)
    there = lax.broadcasted_iota(jnp.int32, shape, 0 if transpose else 1)
    row_off = lax.div(tap, 3)
    col_off = tap - 3 * row_off
    bits = side.bit_length() - 1
    rows = lax.shift_right_logical(there, bits) - lax.shift_right_logical(here, bits)
    cols = (there & (side - 1)) - (here & (side - 1))
    hit = (rows == row_off - 1) & (cols == col_off - 1)
    return hit.astype(F32).astype(BF16)


def prepare_kernel(side, taps, info, own, other, wide, turned, gather, scatter):
    rows, chans = own.shape
    area = side * side
    wide[...] = jnp.zeros_like(wide)
    wide[pl.ds(pl.multiple_of(info[1], 16), rows), :] = own[...]
    wide[pl.ds(pl.multiple_of(info[2], 16), rows), :] = other[...]
    for tap in range(taps):
        part = slice(tap * chans, (tap + 1) * chans)
        turned[part, :] = wide[part, :].T
        gather[tap * area : (tap + 1) * area, :] = tap_matrix(info[0] + tap, side, False)
        scatter[tap * area : (tap + 1) * area, :] = tap_matrix(info[0] + tap, side, True)


def move_into(target, index, taps, matrices, value):
    area, width = value.shape
    moved = matmul(matrices, value).astype(BF16)
    for tap in range(taps):
        target[index * area : (index + 1) * area, tap * width : (tap + 1) * width] = moved[
            tap * area : (tap + 1) * area
        ]


def split_latents(value, refs):
    area = refs[0].shape[0]
    for index, ref in enumerate(refs):
        ref[...] = value[index * area : (index + 1) * area].astype(ref.dtype)


def grad_kernel(taps, scatter, turned, c0, c1, c2, moved, g0, g1, g2):
    for index, ref in enumerate((c0, c1, c2)):
        move_into(moved, index, taps, scatter[...], ref[...])
    split_latents(matmul(moved[...], turned[...]), (g0, g1, g2))


def weight_kernel(taps, moved, a0, a1, a2, part, across):
    area, chans = a0.shape
    for index, ref in enumerate((a0, a1, a2)):
        across[:, index * area : (index + 1) * area] = ref[...].T
    for tap in range(taps):
        block = slice(tap * chans, (tap + 1) * chans)
        part[block, :] = matmul(across[...], moved[:, block])


def out_kernel(taps, gather, wide, a0, a1, a2, y0, y1, y2, moved):
    for index, ref in enumerate((a0, a1, a2)):
        move_into(moved, index, taps, gather[...], ref[...])
    split_latents(matmul(moved[...], wide[...]), (y0, y1, y2))


def finish_kernel(taps, factor, info, scatter, c3, a3, part, moved, keep, send, last):
    chans = a3.shape[1]
    rows = keep.shape[0]
    move_into(moved, 0, taps, scatter[...], c3[...])
    across = a3[...].T
    for tap in range(taps):
        block = slice(tap * chans, (tap + 1) * chans)
        last[block, :] = matmul(across, moved[:, block])
    own = pl.ds(pl.multiple_of(info[1], 16), rows)
    other = pl.ds(pl.multiple_of(info[2], 16), rows)
    send[...] = ((part[other, :] + last[other, :]) * factor).astype(BF16)
    keep[...] = (part[own, :] + last[own, :]) * factor


def last_kernel(taps, gather, wide, turned, a3, moved, y1, g2, y3, g3, y1_out, g2_out, placed):
    y1_out[...] = y1[...].astype(BF16)
    g2_out[...] = g2[...].astype(BF16)
    move_into(placed, 0, taps, gather[...], a3[...])
    y3[...] = matmul(placed[...], wide[...]).astype(BF16)
    g3[...] = matmul(moved[...], turned[...]).astype(BF16)


def back_kernel(groups, factor, latent, stats, gain, shift, g0, g1, g2, grad, terms):
    values = latent[...].astype(F32)
    total = values.shape[0] * values.shape[1] // groups
    scale_inv = stats[1:2]
    normed = (values - stats[0:1]) * scale_inv
    pre = normed * gain[...] + shift[...]
    act_grad = g0[...] + g1[...].astype(F32) + g2[...].astype(F32)
    sigma = 1.0 / (1.0 + jnp.exp(-pre))
    pre_grad = act_grad * sigma * (1.0 + pre * (1.0 - sigma))
    sums = col_sums(pre_grad * normed, pre_grad)
    terms[...] = sums[0:2] * factor
    means = group_mean(sums * gain[...], total, groups)
    grad[...] = (scale_inv * (pre_grad * gain[...] - means[1:2] - normed * means[0:1])).astype(BF16)


def shards_plane(latents, cotangent, conv_weight, norm_gain, norm_shift, partner_bit):
    side, chans = latents.shape[1], latents.shape[3]
    area = side * side
    shard_total = lax.axis_size("fsdp")
    inv_batch = 1.0 / shard_total
    place = lax.axis_index("fsdp")
    weight = conv_weight[0]
    rows = weight.shape[0]
    starts = [2 * rows * chip for chip in range(shard_total // 2)]
    taps = max((start % chans + 2 * rows + chans - 1) // chans for start in starts)
    start = 2 * rows * (place // 2)
    first = jnp.minimum(start // chans, 9 - taps)
    offset = start - first * chans
    core = place % 2
    info = jnp.stack([first, offset + rows * core, offset + rows * (1 - core)]).astype(jnp.int32)

    def columns(count, dtype=BF16):
        return shaped((count * area, taps * chans), dtype)

    plane, plane_b = shaped((area, chans), F32), shaped((area, chans), BF16)
    window = (taps * chans, chans)

    latent = latents.reshape(area, chans)
    cot0 = cotangent.reshape(area, chans)
    other_weight = swap(weight, "fsdp", CORE)
    cot1 = swap(cot0, "fsdp", ACROSS)
    cot2 = swap(cot0, "fsdp", ALONG)
    act0, stats = call(
        functools.partial(norm_kernel, GROUPS),
        [plane_b, shaped((2, chans), F32)],
        [latent, norm_gain, norm_shift],
    )
    act2 = swap(act0, "fsdp", ALONG)
    act1 = swap(act0, "fsdp", ACROSS)
    wide, turned, gather, scatter = call(
        functools.partial(prepare_kernel, side, taps),
        [shaped(window, BF16)] * 2 + [shaped((taps * area, area), BF16)] * 2,
        [info, weight, other_weight],
        order=[stats],
    )
    moved, grad0, grad1, grad2 = call(
        functools.partial(grad_kernel, taps),
        [columns(3), plane, plane, plane],
        [scatter, turned, cot0, cot1, cot2],
    )
    act2, cot1 = hold([act2, cot1], [grad0])
    act3 = swap(act2, "fsdp", ACROSS)
    cot3 = swap(cot1, "fsdp", ALONG)
    (part,) = call(
        functools.partial(weight_kernel, taps),
        [shaped(window, F32)],
        [moved, act0, act1, act2],
        [pltpu.VMEM((chans, 3 * area), BF16)],
    )
    out0, out1, out2 = call(
        functools.partial(out_kernel, taps),
        [plane, plane, plane],
        [gather, wide, act0, act1, act2],
        [pltpu.VMEM((3 * area, taps * chans), BF16)],
        order=[part],
    )
    moved3, keep, send = call(
        functools.partial(finish_kernel, taps, inv_batch),
        [columns(1), shaped((rows, chans), F32), shaped((rows, chans), BF16)],
        [info, scatter, cot3, act3, part],
        [pltpu.VMEM(window, F32)],
        order=[out0],
    )
    shard = keep + swap(send, "fsdp", CORE).astype(F32)
    narrow = shard.astype(BF16)
    pair1 = swap(narrow, "rep", 1)
    pair2 = swap(narrow, "rep", 2)

    out3, grad3, out1, grad2 = call(
        functools.partial(last_kernel, taps),
        [plane_b] * 4,
        [gather, wide, turned, act3, moved3, out1, grad2],
        [pltpu.VMEM((area, taps * chans), BF16)],
        order=[keep],
    )
    out1, grad2 = hold([out1, grad2], [narrow])
    grad_in = swap(grad3, "fsdp", ALONG)
    out_in = swap(out3, "fsdp", ACROSS)
    grad_y = swap(grad2, "fsdp", ALONG)
    grad_x = swap((grad1 + grad_in.astype(F32)).astype(BF16), "fsdp", ACROSS)
    out_x = swap(out1, "fsdp", ACROSS)
    out_y = swap((out2 + out_in.astype(F32)).astype(BF16), "fsdp", ALONG)

    input_grad, terms = call(
        functools.partial(back_kernel, GROUPS, inv_batch),
        [plane_b, shaped((2, chans), F32)],
        [latent, stats, norm_gain, norm_shift, grad0, grad_x, grad_y],
    )
    for mask in (CORE, ACROSS, ALONG):
        terms = terms + swap(terms, "fsdp", mask)
    block_out = (out0 + out_x.astype(F32) + out_y.astype(F32)).astype(BF16)

    def paired(own, other1, other2, bit):
        other = jnp.where(bit == 0, other1, other2).astype(F32)
        return 0.5 * (own + other)

    (terms,) = hold([terms], [pair1, pair2])
    norm_avg = paired(terms, swap(terms, "rep", 1), swap(terms, "rep", 2), partner_bit[0])
    shard_bit = lax.dynamic_index_in_dim(partner_bit, place, 0, keepdims=False)
    weight_avg = paired(shard, pair1, pair2, shard_bit)
    shape = (1, side, side, chans)
    return (block_out.reshape(shape), input_grad.reshape(shape), weight_avg[None], norm_avg[None])


def solution(mesh):
    in_specs = (
        P(("rep", "fsdp"), None, None, None),
        P(("rep", "fsdp"), None, None, None),
        P("rep", "fsdp", None),
        P("rep", None),
        P("rep", None),
        P(),
    )
    out_specs = (
        P(("rep", "fsdp"), None, None, None),
        P(("rep", "fsdp"), None, None, None),
        P("rep", "fsdp", None),
        P("rep", None, None),
    )
    planes = mesh.shape["fsdp"] == 8 and mesh.shape["rep"] == 4
    shards = shards_plane if planes else shards_general
    return jax.shard_map(shards, mesh=mesh, in_specs=in_specs, out_specs=out_specs, check_vma=False)
```

```python
import functools

import jax
import jax.numpy as jnp
from jax import lax
from jax.experimental import pallas as pl
from jax.experimental.pallas import tpu as pltpu
from jax.sharding import PartitionSpec as P

GROUPS = 32


def partner(value, axis, stride):
    mask = 2**stride
    pairs = [(source, source ^ mask) for source in range(lax.axis_size(axis))]
    return lax.ppermute(value, axis, pairs)


def norm_forward(values_in, gain, shift, groups):
    count, side, chans = (values_in.shape[0], values_in.shape[1], values_in.shape[3])
    values = values_in.astype(jnp.float32).reshape(count, side * side, groups, chans // groups)
    center = jnp.mean(values, axis=(1, 3), keepdims=True)
    spread = jnp.mean(jnp.square(values - center), axis=(1, 3), keepdims=True)
    scale_inv = lax.rsqrt(spread + 1e-05)
    normed = (values - center) * scale_inv
    pre_act = normed * gain.reshape(groups, -1) + shift.reshape(groups, -1)
    return (normed, scale_inv, pre_act)


def make_patches(activation):
    count, side, chans = (activation.shape[0], activation.shape[1], activation.shape[3])
    padded = jnp.pad(activation, ((0, 0), (1, 1), (1, 1), (0, 0)))
    pieces = [
        padded[:, row_off : row_off + side, col_off : col_off + side, :]
        for row_off in range(3)
        for col_off in range(3)
    ]
    return jnp.concatenate(pieces, axis=-1).reshape(count * side * side, 9 * chans)


def fold_patches(patch_grad, count, side, chans):
    grads = patch_grad.reshape(count, side, side, 9, chans)
    total = jnp.zeros((count, side + 2, side + 2, chans), jnp.float32)
    for row_off in range(3):
        for col_off in range(3):
            tap = grads[:, :, :, row_off * 3 + col_off, :]
            total = total + jnp.pad(
                tap, ((0, 0), (row_off, 2 - row_off), (col_off, 2 - col_off), (0, 0))
            )
    return total[:, 1:-1, 1:-1, :]


def backward_rest(act_grad, normed, scale_inv, pre_act, gain, groups, inv_batch):
    count, side, chans = (act_grad.shape[0], act_grad.shape[1], act_grad.shape[3])
    act_grad = act_grad.reshape(count, side * side, groups, chans // groups)
    sigma = jax.nn.sigmoid(pre_act)
    pre_grad = act_grad * sigma * (1.0 + pre_act * (1.0 - sigma))
    gain_grad = jnp.sum(pre_grad * normed, axis=(0, 1)).reshape(-1) * inv_batch
    shift_grad = jnp.sum(pre_grad, axis=(0, 1)).reshape(-1) * inv_batch
    normed_grad = pre_grad * gain.reshape(groups, -1)
    first = jnp.mean(normed_grad, axis=(1, 3), keepdims=True)
    second = jnp.mean(normed_grad * normed, axis=(1, 3), keepdims=True)
    input_grad = scale_inv * (normed_grad - first - normed * second)
    return (
        input_grad.reshape(count, side, side, chans).astype(jnp.bfloat16),
        jnp.stack([gain_grad, shift_grad]),
    )


def shards_general(latents, cotangent, conv_weight, norm_gain, norm_shift, partner_bit):
    count, side, chans = (latents.shape[0], latents.shape[1], latents.shape[3])
    shard_total = lax.axis_size("fsdp")
    inv_batch = 1.0 / (count * shard_total)
    gain = norm_gain[0]
    normed, scale_inv, pre_act = norm_forward(latents, gain, norm_shift[0], GROUPS)
    activation = jax.nn.silu(pre_act).astype(jnp.bfloat16).reshape(count, side, side, chans)
    patches = make_patches(activation)
    cot_rows = cotangent.reshape(count * side * side, chans)
    weight_rows = conv_weight[0]
    output = jnp.dot(
        patches,
        lax.all_gather(weight_rows, "fsdp", axis=0, tiled=True),
        preferred_element_type=jnp.float32,
    )
    patch_grad = lax.dot_general(
        cot_rows,
        lax.all_gather(weight_rows, "fsdp", axis=0, tiled=True),
        (((1,), (1,)), ((), ())),
        preferred_element_type=jnp.float32,
    )
    block_out = output.astype(jnp.bfloat16).reshape(count, side, side, chans)
    act_grad = fold_patches(patch_grad, count, side, chans)
    input_grad, norm_term = backward_rest(
        act_grad, normed, scale_inv, pre_act, gain, GROUPS, inv_batch
    )
    weight_term = (
        lax.dot_general(
            patches, cot_rows, (((0,), (0,)), ((), ())), preferred_element_type=jnp.float32
        )
        * inv_batch
    )
    shard_rows = weight_rows.shape[0]
    term_pieces = weight_term.reshape(shard_total, shard_rows, chans)
    received = lax.all_to_all(
        term_pieces.astype(jnp.bfloat16), "fsdp", split_axis=0, concat_axis=0, tiled=True
    ).astype(term_pieces.dtype)
    weight_shard = jnp.sum(received, axis=0)
    bit_count = lax.axis_size("rep").bit_length() - 1
    shard_bit = lax.dynamic_index_in_dim(partner_bit, lax.axis_index("fsdp"), 0, keepdims=False)
    norm_bit = partner_bit[0]
    paired_norm = norm_term
    for bit_index in range(bit_count):
        other_norm = partner(norm_term, "rep", bit_index)
        paired_norm = jnp.where(norm_bit == bit_index, 0.5 * (norm_term + other_norm), paired_norm)
    norm_avg = lax.psum(paired_norm, "fsdp")
    weight_avg = weight_shard
    for bit_index in range(bit_count):
        other_weight = partner(weight_shard.astype(jnp.bfloat16), "rep", bit_index).astype(
            weight_shard.dtype
        )
        weight_avg = jnp.where(
            shard_bit == bit_index, 0.5 * (weight_shard + other_weight), weight_avg
        )
    return (block_out, input_grad, weight_avg[None], norm_avg[None])


CORE, ACROSS, ALONG = 1, 2, 4
VMEM_LIMIT = 24 * 1024 * 1024
F32, BF16 = jnp.float32, jnp.bfloat16


def swap(value, axis, mask):
    pairs = [(source, source ^ mask) for source in range(lax.axis_size(axis))]
    return lax.ppermute(value, axis, pairs)


def call(kernel, outs, args, scratch=(), order=()):
    vmem = pl.BlockSpec(memory_space=pltpu.VMEM)
    smem = pl.BlockSpec(memory_space=pltpu.SMEM)
    untouched = pl.BlockSpec(memory_space=pl.ANY)

    def body(*refs):
        kernel(*refs[: len(args)], *refs[len(args) + len(order) :])

    return pl.pallas_call(
        body,
        out_shape=tuple(outs),
        in_specs=[smem if a.dtype == jnp.int32 else vmem for a in args] + [untouched] * len(order),
        out_specs=tuple(vmem for _ in outs),
        scratch_shapes=list(scratch),
        compiler_params=pltpu.CompilerParams(vmem_limit_bytes=VMEM_LIMIT),
    )(*args, *order)


def hold(values, order):
    untouched = pl.BlockSpec(memory_space=pl.ANY)
    return pl.pallas_call(
        lambda *refs: None,
        out_shape=tuple(shaped(value.shape, value.dtype) for value in values),
        in_specs=[untouched] * (len(values) + len(order)),
        out_specs=tuple(untouched for _ in values),
        input_output_aliases={index: index for index in range(len(values))},
        compiler_params=pltpu.CompilerParams(vmem_limit_bytes=1024 * 1024),
    )(*values, *order)


def shaped(shape, dtype):
    return jax.ShapeDtypeStruct(shape, dtype)


def matmul(left, right):
    return jnp.dot(left, right, preferred_element_type=F32)


def group_matrix(chans, groups, transpose):
    width = chans // groups
    shape = (128, chans) if transpose else (chans, 128)
    chan = lax.broadcasted_iota(jnp.int32, shape, 1 if transpose else 0)
    low = lax.broadcasted_iota(jnp.int32, shape, 0 if transpose else 1) * width
    return ((chan >= low) & (chan < low + width)).astype(F32)


def group_mean(columns, total, groups):
    chans = columns.shape[1]
    exact = dict(precision=lax.Precision.HIGHEST, preferred_element_type=F32)
    sums = jnp.dot(columns, group_matrix(chans, groups, False), **exact)
    return jnp.dot(sums, group_matrix(chans, groups, True), **exact) * (1.0 / total)


def col_sums(*values):
    rows = [jnp.sum(value, axis=0, keepdims=True) for value in values]
    fill = jnp.zeros((8 - len(rows), rows[0].shape[1]), F32)
    return jnp.concatenate(rows + [fill], axis=0)


def norm_kernel(groups, latent, gain, shift, act, stats):
    values = latent[...].astype(F32)
    total = values.shape[0] * values.shape[1] // groups
    center = group_mean(col_sums(values), total, groups)[0:1]
    moved = values - center
    spread = group_mean(col_sums(moved * moved), total, groups)[0:1]
    scale_inv = lax.rsqrt(spread + 1e-05)
    pre = moved * scale_inv * gain[...] + shift[...]
    act[...] = (pre / (1.0 + jnp.exp(-pre))).astype(BF16)
    stats[0:1] = center
    stats[1:2] = scale_inv


def tap_matrix(tap, side, transpose):
    shape = (side * side, side * side)
    here = lax.broadcasted_iota(jnp.int32, shape, 1 if transpose else 0)
    there = lax.broadcasted_iota(jnp.int32, shape, 0 if transpose else 1)
    row_off = lax.div(tap, 3)
    col_off = tap - 3 * row_off
    bits = side.bit_length() - 1
    rows = lax.shift_right_logical(there, bits) - lax.shift_right_logical(here, bits)
    cols = (there & (side - 1)) - (here & (side - 1))
    hit = (rows == row_off - 1) & (cols == col_off - 1)
    return hit.astype(F32).astype(BF16)


def prepare_kernel(side, taps, info, own, other, wide, turned, gather, scatter):
    rows, chans = own.shape
    area = side * side
    wide[...] = jnp.zeros_like(wide)
    wide[pl.ds(pl.multiple_of(info[1], 16), rows), :] = own[...]
    wide[pl.ds(pl.multiple_of(info[2], 16), rows), :] = other[...]
    for tap in range(taps):
        part = slice(tap * chans, (tap + 1) * chans)
        turned[part, :] = wide[part, :].T
        gather[tap * area : (tap + 1) * area, :] = tap_matrix(info[0] + tap, side, False)
        scatter[tap * area : (tap + 1) * area, :] = tap_matrix(info[0] + tap, side, True)


def move_into(target, index, taps, matrices, value):
    area, width = value.shape
    moved = matmul(matrices, value).astype(BF16)
    for tap in range(taps):
        target[index * area : (index + 1) * area, tap * width : (tap + 1) * width] = moved[
            tap * area : (tap + 1) * area
        ]


def split_latents(value, refs):
    area = refs[0].shape[0]
    for index, ref in enumerate(refs):
        ref[...] = value[index * area : (index + 1) * area].astype(ref.dtype)


def grad_kernel(taps, scatter, turned, c0, c1, c2, moved, g0, g1, g2):
    for index, ref in enumerate((c0, c1, c2)):
        move_into(moved, index, taps, scatter[...], ref[...])
    split_latents(matmul(moved[...], turned[...]), (g0, g1, g2))


def weight_kernel(taps, moved, a0, a1, a2, part, across):
    area, chans = a0.shape
    for index, ref in enumerate((a0, a1, a2)):
        across[:, index * area : (index + 1) * area] = ref[...].T
    for tap in range(taps):
        block = slice(tap * chans, (tap + 1) * chans)
        part[block, :] = matmul(across[...], moved[:, block])


def out_kernel(taps, gather, wide, a0, a1, a2, a3, y0, y1, y2, y3, moved):
    for index, ref in enumerate((a0, a1, a2, a3)):
        move_into(moved, index, taps, gather[...], ref[...])
    split_latents(matmul(moved[...], wide[...]), (y0, y1, y2, y3))


def finish_kernel(taps, factor, info, scatter, c3, a3, part, moved, keep, send, last):
    chans = a3.shape[1]
    rows = keep.shape[0]
    move_into(moved, 0, taps, scatter[...], c3[...])
    across = a3[...].T
    for tap in range(taps):
        block = slice(tap * chans, (tap + 1) * chans)
        last[block, :] = matmul(across, moved[:, block])
    own = pl.ds(pl.multiple_of(info[1], 16), rows)
    other = pl.ds(pl.multiple_of(info[2], 16), rows)
    send[...] = ((part[other, :] + last[other, :]) * factor).astype(BF16)
    keep[...] = (part[own, :] + last[own, :]) * factor


def last_kernel(turned, moved, g2, g3, g2_out):
    g2_out[...] = g2[...].astype(BF16)
    g3[...] = matmul(moved[...], turned[...]).astype(BF16)


def back_kernel(groups, factor, latent, stats, gain, shift, g0, g1, g2, grad, terms):
    values = latent[...].astype(F32)
    total = values.shape[0] * values.shape[1] // groups
    scale_inv = stats[1:2]
    normed = (values - stats[0:1]) * scale_inv
    pre = normed * gain[...] + shift[...]
    act_grad = g0[...] + g1[...].astype(F32) + g2[...].astype(F32)
    sigma = 1.0 / (1.0 + jnp.exp(-pre))
    pre_grad = act_grad * sigma * (1.0 + pre * (1.0 - sigma))
    sums = col_sums(pre_grad * normed, pre_grad)
    terms[...] = sums[0:2] * factor
    means = group_mean(sums * gain[...], total, groups)
    grad[...] = (scale_inv * (pre_grad * gain[...] - means[1:2] - normed * means[0:1])).astype(BF16)


def shards_plane(latents, cotangent, conv_weight, norm_gain, norm_shift, partner_bit):
    side, chans = latents.shape[1], latents.shape[3]
    area = side * side
    shard_total = lax.axis_size("fsdp")
    inv_batch = 1.0 / shard_total
    place = lax.axis_index("fsdp")
    weight = conv_weight[0]
    rows = weight.shape[0]
    starts = [2 * rows * chip for chip in range(shard_total // 2)]
    taps = max((start % chans + 2 * rows + chans - 1) // chans for start in starts)
    start = 2 * rows * (place // 2)
    first = jnp.minimum(start // chans, 9 - taps)
    offset = start - first * chans
    core = place % 2
    info = jnp.stack([first, offset + rows * core, offset + rows * (1 - core)]).astype(jnp.int32)

    def columns(count, dtype=BF16):
        return shaped((count * area, taps * chans), dtype)

    plane, plane_b = shaped((area, chans), F32), shaped((area, chans), BF16)
    window = (taps * chans, chans)

    latent = latents.reshape(area, chans)
    cot0 = cotangent.reshape(area, chans)
    other_weight = swap(weight, "fsdp", CORE)
    cot1 = swap(cot0, "fsdp", ACROSS)
    cot2 = swap(cot0, "fsdp", ALONG)
    act0, stats = call(
        functools.partial(norm_kernel, GROUPS),
        [plane_b, shaped((2, chans), F32)],
        [latent, norm_gain, norm_shift],
    )
    act2 = swap(act0, "fsdp", ALONG)
    act1 = swap(act0, "fsdp", ACROSS)
    wide, turned, gather, scatter = call(
        functools.partial(prepare_kernel, side, taps),
        [shaped(window, BF16)] * 2 + [shaped((taps * area, area), BF16)] * 2,
        [info, weight, other_weight],
        order=[stats],
    )
    moved, grad0, grad1, grad2 = call(
        functools.partial(grad_kernel, taps),
        [columns(3), plane, plane, plane],
        [scatter, turned, cot0, cot1, cot2],
    )
    act2, cot1 = hold([act2, cot1], [grad0])
    act3 = swap(act2, "fsdp", ACROSS)
    cot3 = swap(cot1, "fsdp", ALONG)
    (part,) = call(
        functools.partial(weight_kernel, taps),
        [shaped(window, F32)],
        [moved, act0, act1, act2],
        [pltpu.VMEM((chans, 3 * area), BF16)],
    )
    moved3, keep, send = call(
        functools.partial(finish_kernel, taps, inv_batch),
        [columns(1), shaped((rows, chans), F32), shaped((rows, chans), BF16)],
        [info, scatter, cot3, act3, part],
        [pltpu.VMEM(window, F32)],
    )
    shard = keep + swap(send, "fsdp", CORE).astype(F32)
    narrow = shard.astype(BF16)
    pair1 = swap(narrow, "rep", 1)
    pair2 = swap(narrow, "rep", 2)

    grad3, grad2 = call(
        last_kernel, [plane_b] * 2, [turned, moved3, grad2], order=[keep]
    )
    grad2, grad3 = hold([grad2, grad3], [narrow])
    grad_in = swap(grad3, "fsdp", ALONG)
    grad_y = swap(grad2, "fsdp", ALONG)
    grad1 = (grad1 + grad_in.astype(F32)).astype(BF16)
    grad_x = swap(grad1, "fsdp", ACROSS)
    out0, out1, out2, out3 = call(
        functools.partial(out_kernel, taps),
        [plane, plane_b, plane, plane_b],
        [gather, wide, act0, act1, act2, act3],
        [pltpu.VMEM((4 * area, taps * chans), BF16)],
        order=[grad1],
    )
    out_in = swap(out3, "fsdp", ACROSS)
    out_x = swap(out1, "fsdp", ACROSS)
    out2 = (out2 + out_in.astype(F32)).astype(BF16)
    out_y = swap(out2, "fsdp", ALONG)

    input_grad, terms = call(
        functools.partial(back_kernel, GROUPS, inv_batch),
        [plane_b, shaped((2, chans), F32)],
        [latent, stats, norm_gain, norm_shift, grad0, grad_x, grad_y],
        order=[out0],
    )
    for mask in (CORE, ACROSS, ALONG):
        terms = terms + swap(terms, "fsdp", mask)
    block_out = (out0 + out_x.astype(F32) + out_y.astype(F32)).astype(BF16)

    def paired(own, other1, other2, bit):
        other = jnp.where(bit == 0, other1, other2).astype(F32)
        return 0.5 * (own + other)

    (terms,) = hold([terms], [out_x, out_y])
    terms1, terms2 = swap(terms, "rep", 1), swap(terms, "rep", 2)
    norm_avg = paired(terms, terms1, terms2, partner_bit[0])
    shard_bit = lax.dynamic_index_in_dim(partner_bit, place, 0, keepdims=False)
    weight_avg = paired(shard, pair1, pair2, shard_bit)
    shape = (1, side, side, chans)
    return (block_out.reshape(shape), input_grad.reshape(shape), weight_avg[None], norm_avg[None])


def solution(mesh):
    in_specs = (
        P(("rep", "fsdp"), None, None, None),
        P(("rep", "fsdp"), None, None, None),
        P("rep", "fsdp", None),
        P("rep", None),
        P("rep", None),
        P(),
    )
    out_specs = (
        P(("rep", "fsdp"), None, None, None),
        P(("rep", "fsdp"), None, None, None),
        P("rep", "fsdp", None),
        P("rep", None, None),
    )
    planes = mesh.shape["fsdp"] == 8 and mesh.shape["rep"] == 4
    shards = shards_plane if planes else shards_general
    return jax.shard_map(shards, mesh=mesh, in_specs=in_specs, out_specs=out_specs, check_vma=False)
```

```python
import functools

import jax
import jax.numpy as jnp
from jax import lax
from jax.experimental import pallas as pl
from jax.experimental.pallas import tpu as pltpu
from jax.sharding import PartitionSpec as P

GROUPS = 32


def partner(value, axis, stride):
    mask = 2**stride
    pairs = [(source, source ^ mask) for source in range(lax.axis_size(axis))]
    return lax.ppermute(value, axis, pairs)


def norm_forward(values_in, gain, shift, groups):
    count, side, chans = (values_in.shape[0], values_in.shape[1], values_in.shape[3])
    values = values_in.astype(jnp.float32).reshape(count, side * side, groups, chans // groups)
    center = jnp.mean(values, axis=(1, 3), keepdims=True)
    spread = jnp.mean(jnp.square(values - center), axis=(1, 3), keepdims=True)
    scale_inv = lax.rsqrt(spread + 1e-05)
    normed = (values - center) * scale_inv
    pre_act = normed * gain.reshape(groups, -1) + shift.reshape(groups, -1)
    return (normed, scale_inv, pre_act)


def make_patches(activation):
    count, side, chans = (activation.shape[0], activation.shape[1], activation.shape[3])
    padded = jnp.pad(activation, ((0, 0), (1, 1), (1, 1), (0, 0)))
    pieces = [
        padded[:, row_off : row_off + side, col_off : col_off + side, :]
        for row_off in range(3)
        for col_off in range(3)
    ]
    return jnp.concatenate(pieces, axis=-1).reshape(count * side * side, 9 * chans)


def fold_patches(patch_grad, count, side, chans):
    grads = patch_grad.reshape(count, side, side, 9, chans)
    total = jnp.zeros((count, side + 2, side + 2, chans), jnp.float32)
    for row_off in range(3):
        for col_off in range(3):
            tap = grads[:, :, :, row_off * 3 + col_off, :]
            total = total + jnp.pad(
                tap, ((0, 0), (row_off, 2 - row_off), (col_off, 2 - col_off), (0, 0))
            )
    return total[:, 1:-1, 1:-1, :]


def backward_rest(act_grad, normed, scale_inv, pre_act, gain, groups, inv_batch):
    count, side, chans = (act_grad.shape[0], act_grad.shape[1], act_grad.shape[3])
    act_grad = act_grad.reshape(count, side * side, groups, chans // groups)
    sigma = jax.nn.sigmoid(pre_act)
    pre_grad = act_grad * sigma * (1.0 + pre_act * (1.0 - sigma))
    gain_grad = jnp.sum(pre_grad * normed, axis=(0, 1)).reshape(-1) * inv_batch
    shift_grad = jnp.sum(pre_grad, axis=(0, 1)).reshape(-1) * inv_batch
    normed_grad = pre_grad * gain.reshape(groups, -1)
    first = jnp.mean(normed_grad, axis=(1, 3), keepdims=True)
    second = jnp.mean(normed_grad * normed, axis=(1, 3), keepdims=True)
    input_grad = scale_inv * (normed_grad - first - normed * second)
    return (
        input_grad.reshape(count, side, side, chans).astype(jnp.bfloat16),
        jnp.stack([gain_grad, shift_grad]),
    )


def shards_general(latents, cotangent, conv_weight, norm_gain, norm_shift, partner_bit):
    count, side, chans = (latents.shape[0], latents.shape[1], latents.shape[3])
    shard_total = lax.axis_size("fsdp")
    inv_batch = 1.0 / (count * shard_total)
    gain = norm_gain[0]
    normed, scale_inv, pre_act = norm_forward(latents, gain, norm_shift[0], GROUPS)
    activation = jax.nn.silu(pre_act).astype(jnp.bfloat16).reshape(count, side, side, chans)
    patches = make_patches(activation)
    cot_rows = cotangent.reshape(count * side * side, chans)
    weight_rows = conv_weight[0]
    output = jnp.dot(
        patches,
        lax.all_gather(weight_rows, "fsdp", axis=0, tiled=True),
        preferred_element_type=jnp.float32,
    )
    patch_grad = lax.dot_general(
        cot_rows,
        lax.all_gather(weight_rows, "fsdp", axis=0, tiled=True),
        (((1,), (1,)), ((), ())),
        preferred_element_type=jnp.float32,
    )
    block_out = output.astype(jnp.bfloat16).reshape(count, side, side, chans)
    act_grad = fold_patches(patch_grad, count, side, chans)
    input_grad, norm_term = backward_rest(
        act_grad, normed, scale_inv, pre_act, gain, GROUPS, inv_batch
    )
    weight_term = (
        lax.dot_general(
            patches, cot_rows, (((0,), (0,)), ((), ())), preferred_element_type=jnp.float32
        )
        * inv_batch
    )
    shard_rows = weight_rows.shape[0]
    term_pieces = weight_term.reshape(shard_total, shard_rows, chans)
    received = lax.all_to_all(
        term_pieces.astype(jnp.bfloat16), "fsdp", split_axis=0, concat_axis=0, tiled=True
    ).astype(term_pieces.dtype)
    weight_shard = jnp.sum(received, axis=0)
    bit_count = lax.axis_size("rep").bit_length() - 1
    shard_bit = lax.dynamic_index_in_dim(partner_bit, lax.axis_index("fsdp"), 0, keepdims=False)
    norm_bit = partner_bit[0]
    paired_norm = norm_term
    for bit_index in range(bit_count):
        other_norm = partner(norm_term, "rep", bit_index)
        paired_norm = jnp.where(norm_bit == bit_index, 0.5 * (norm_term + other_norm), paired_norm)
    norm_avg = lax.psum(paired_norm, "fsdp")
    weight_avg = weight_shard
    for bit_index in range(bit_count):
        other_weight = partner(weight_shard.astype(jnp.bfloat16), "rep", bit_index).astype(
            weight_shard.dtype
        )
        weight_avg = jnp.where(
            shard_bit == bit_index, 0.5 * (weight_shard + other_weight), weight_avg
        )
    return (block_out, input_grad, weight_avg[None], norm_avg[None])


CORE, ACROSS, ALONG = 1, 2, 4
VMEM_LIMIT = 20 * 1024 * 1024
F32, BF16 = jnp.float32, jnp.bfloat16


def swap(value, axis, mask):
    pairs = [(source, source ^ mask) for source in range(lax.axis_size(axis))]
    return lax.ppermute(value, axis, pairs)


def call(kernel, outs, args, scratch=(), order=(), outside=()):
    vmem = pl.BlockSpec(memory_space=pltpu.VMEM)
    smem = pl.BlockSpec(memory_space=pltpu.SMEM)
    untouched = pl.BlockSpec(memory_space=pl.ANY)

    def body(*refs):
        kernel(*refs[: len(args)], *refs[len(args) + len(order) :])

    return pl.pallas_call(
        body,
        out_shape=tuple(outs),
        in_specs=[
            untouched if index in outside else smem if a.dtype == jnp.int32 else vmem
            for index, a in enumerate(args)
        ]
        + [untouched] * len(order),
        out_specs=tuple(untouched if outside else vmem for _ in outs),
        scratch_shapes=list(scratch),
        compiler_params=pltpu.CompilerParams(vmem_limit_bytes=VMEM_LIMIT),
    )(*args, *order)


def hold(values, order):
    untouched = pl.BlockSpec(memory_space=pl.ANY)
    return pl.pallas_call(
        lambda *refs: None,
        out_shape=tuple(shaped(value.shape, value.dtype) for value in values),
        in_specs=[untouched] * (len(values) + len(order)),
        out_specs=tuple(untouched for _ in values),
        input_output_aliases={index: index for index in range(len(values))},
        compiler_params=pltpu.CompilerParams(vmem_limit_bytes=1024 * 1024),
    )(*values, *order)


def shaped(shape, dtype):
    return jax.ShapeDtypeStruct(shape, dtype)


def matmul(left, right):
    return jnp.dot(left, right, preferred_element_type=F32)


def group_matrix(chans, groups, transpose):
    width = chans // groups
    shape = (128, chans) if transpose else (chans, 128)
    chan = lax.broadcasted_iota(jnp.int32, shape, 1 if transpose else 0)
    low = lax.broadcasted_iota(jnp.int32, shape, 0 if transpose else 1) * width
    return ((chan >= low) & (chan < low + width)).astype(F32)


def group_mean(columns, total, groups):
    chans = columns.shape[1]
    exact = dict(precision=lax.Precision.HIGHEST, preferred_element_type=F32)
    sums = jnp.dot(columns, group_matrix(chans, groups, False), **exact)
    return jnp.dot(sums, group_matrix(chans, groups, True), **exact) * (1.0 / total)


def col_sums(*values):
    rows = [jnp.sum(value, axis=0, keepdims=True) for value in values]
    fill = jnp.zeros((8 - len(rows), rows[0].shape[1]), F32)
    return jnp.concatenate(rows + [fill], axis=0)


def norm_kernel(groups, latent, params, act, stats):
    gain, shift = params[0:1], params[1:2]
    values = latent[...].astype(F32)
    total = values.shape[0] * values.shape[1] // groups
    center = group_mean(col_sums(values), total, groups)[0:1]
    moved = values - center
    spread = group_mean(col_sums(moved * moved), total, groups)[0:1]
    scale_inv = lax.rsqrt(spread + 1e-05)
    pre = moved * scale_inv * gain + shift
    act[...] = (pre / (1.0 + jnp.exp(-pre))).astype(BF16)
    stats[0:1] = center
    stats[1:2] = scale_inv


def tap_matrix(tap, side, transpose):
    shape = (side * side, side * side)
    here = lax.broadcasted_iota(jnp.int32, shape, 1 if transpose else 0)
    there = lax.broadcasted_iota(jnp.int32, shape, 0 if transpose else 1)
    row_off = lax.div(tap, 3)
    col_off = tap - 3 * row_off
    bits = side.bit_length() - 1
    rows = lax.shift_right_logical(there, bits) - lax.shift_right_logical(here, bits)
    cols = (there & (side - 1)) - (here & (side - 1))
    hit = (rows == row_off - 1) & (cols == col_off - 1)
    return hit.astype(F32).astype(BF16)


def prepare_kernel(side, taps, info, own, other, wide, turned, gather, scatter):
    rows, chans = own.shape
    area = side * side
    wide[...] = jnp.zeros_like(wide)
    wide[pl.ds(pl.multiple_of(info[1], 16), rows), :] = own[...]
    wide[pl.ds(pl.multiple_of(info[2], 16), rows), :] = other[...]
    for tap in range(taps):
        part = slice(tap * chans, (tap + 1) * chans)
        turned[part, :] = wide[part, :].T
        gather[tap * area : (tap + 1) * area, :] = tap_matrix(info[0] + tap, side, False)
        scatter[tap * area : (tap + 1) * area, :] = tap_matrix(info[0] + tap, side, True)


def move_into(target, index, taps, matrices, value):
    area, width = value.shape
    moved = matmul(matrices, value).astype(BF16)
    for tap in range(taps):
        target[index * area : (index + 1) * area, tap * width : (tap + 1) * width] = moved[
            tap * area : (tap + 1) * area
        ]


def split_latents(value, refs):
    area = refs[0].shape[0]
    for index, ref in enumerate(refs):
        ref[...] = value[index * area : (index + 1) * area].astype(ref.dtype)


def grad_kernel(taps, scatter, turned, c0, c1, c2, moved, g0, g1, g2):
    for index, ref in enumerate((c0, c1, c2)):
        move_into(moved, index, taps, scatter[...], ref[...])
    split_latents(matmul(moved[...], turned[...]), (g0, g1, g2))


def weight_kernel(taps, moved, a0, a1, a2, part, across):
    area, chans = a0.shape
    for index, ref in enumerate((a0, a1, a2)):
        across[:, index * area : (index + 1) * area] = ref[...].T
    for tap in range(taps):
        block = slice(tap * chans, (tap + 1) * chans)
        part[block, :] = matmul(across[...], moved[:, block])


def out_kernel(taps, gather, wide, a0, a1, a2, y0, y1, y2, moved):
    for index, ref in enumerate((a0, a1, a2)):
        move_into(moved, index, taps, gather[...], ref[...])
    split_latents(matmul(moved[...], wide[...]), (y0, y1, y2))


def finish_kernel(taps, factor, info, scatter, c3, a3, part, moved, keep, send, last):
    chans = a3.shape[1]
    rows = keep.shape[0]
    move_into(moved, 0, taps, scatter[...], c3[...])
    across = a3[...].T
    for tap in range(taps):
        block = slice(tap * chans, (tap + 1) * chans)
        last[block, :] = matmul(across, moved[:, block])
    own = pl.ds(pl.multiple_of(info[1], 16), rows)
    other = pl.ds(pl.multiple_of(info[2], 16), rows)
    send[...] = ((part[other, :] + last[other, :]) * factor).astype(BF16)
    keep[...] = (part[own, :] + last[own, :]) * factor


def last_kernel(taps, gather, wide, turned, a3, moved, g1, g2, y1, y2, p1, p2, p3, placed):
    area = a3.shape[0]
    for pack, grad, out in ((p1, g1, y1), (p2, g2, y2)):
        pack[:area] = grad[...]
        pack[area:] = out[...]
    p3[:area] = matmul(moved[...], turned[...]).astype(BF16)
    move_into(placed, 0, taps, gather[...], a3[...])
    p3[area:] = matmul(placed[...], wide[...]).astype(BF16)


def join_kernel(keep, got, half, narrow):
    total = keep[...] + got[...].astype(F32)
    half[...] = 0.5 * total
    narrow[...] = total.astype(BF16)


def pair_kernel(chunks, bit, half, pair1, pair2, mean, got, made, arrive, leave):
    size = half.shape[0] // chunks
    parts = [pl.ds(index * size, size) for index in range(chunks)]

    def fetch(source, index):
        return pltpu.make_async_copy(source.at[parts[index]], got.at[parts[index]], arrive.at[index])

    @pl.when(bit[0] == 0)
    def _():
        for index in range(chunks):
            fetch(pair1, index).start()

    @pl.when(bit[0] != 0)
    def _():
        for index in range(chunks):
            fetch(pair2, index).start()

    stores = []
    for index, rows in enumerate(parts):
        fetch(pair1, index).wait()
        made[rows, :] = half[rows, :] + 0.5 * got[rows, :].astype(F32)
        stores.append(pltpu.make_async_copy(made.at[rows], mean.at[rows], leave.at[index]))
        stores[-1].start()
    for store in stores:
        store.wait()


def back_kernel(groups, factor, latent, stats, params, g0, y0, p1, p2, p3, out, grad, terms):
    gain, shift = params[0:1], params[1:2]
    values = latent[...].astype(F32)
    total = values.shape[0] * values.shape[1] // groups
    scale_inv = stats[1:2]
    normed = (values - stats[0:1]) * scale_inv
    pre = normed * gain + shift
    area = latent.shape[0]
    packs = (p1, p2, p3)
    out[...] = (y0[...] + sum(pack[area:].astype(F32) for pack in packs)).astype(BF16)
    act_grad = g0[...] + sum(pack[:area].astype(F32) for pack in packs)
    sigma = 1.0 / (1.0 + jnp.exp(-pre))
    pre_grad = act_grad * sigma * (1.0 + pre * (1.0 - sigma))
    sums = col_sums(pre_grad * normed, pre_grad)
    terms[...] = sums[0:2] * factor
    means = group_mean(sums * gain, total, groups)
    grad[...] = (scale_inv * (pre_grad * gain - means[1:2] - normed * means[0:1])).astype(BF16)


def shards_plane(latents, cotangent, conv_weight, norm_gain, norm_shift, partner_bit):
    side, chans = latents.shape[1], latents.shape[3]
    area = side * side
    shard_total = lax.axis_size("fsdp")
    inv_batch = 1.0 / shard_total
    place = lax.axis_index("fsdp")
    weight = conv_weight[0]
    rows = weight.shape[0]
    starts = [2 * rows * chip for chip in range(shard_total // 2)]
    taps = max((start % chans + 2 * rows + chans - 1) // chans for start in starts)
    start = 2 * rows * (place // 2)
    first = jnp.minimum(start // chans, 9 - taps)
    offset = start - first * chans
    core = place % 2
    info = jnp.stack([first, offset + rows * core, offset + rows * (1 - core)]).astype(jnp.int32)

    def columns(count, dtype=BF16):
        return shaped((count * area, taps * chans), dtype)

    plane, plane_b = shaped((area, chans), F32), shaped((area, chans), BF16)
    window = (taps * chans, chans)

    latent = latents.reshape(area, chans)
    cot0 = cotangent.reshape(area, chans)
    params = jnp.concatenate([norm_gain, norm_shift])
    other_weight = swap(weight, "fsdp", CORE)
    cot1 = swap(cot0, "fsdp", ACROSS)
    cot2 = swap(cot0, "fsdp", ALONG)
    act0, stats = call(
        functools.partial(norm_kernel, GROUPS),
        [plane_b, shaped((2, chans), F32)],
        [latent, params],
    )
    act2 = swap(act0, "fsdp", ALONG)
    act1 = swap(act0, "fsdp", ACROSS)
    wide, turned, gather, scatter = call(
        functools.partial(prepare_kernel, side, taps),
        [shaped(window, BF16)] * 2 + [shaped((taps * area, area), BF16)] * 2,
        [info, weight, other_weight],
        order=[stats],
    )
    moved, grad0, grad1, grad2 = call(
        functools.partial(grad_kernel, taps),
        [columns(3), plane, plane_b, plane_b],
        [scatter, turned, cot0, cot1, cot2],
    )
    act2, cot1 = hold([act2, cot1], [grad0])
    act3 = swap(act2, "fsdp", ACROSS)
    cot3 = swap(cot1, "fsdp", ALONG)
    (part,) = call(
        functools.partial(weight_kernel, taps),
        [shaped(window, F32)],
        [moved, act0, act1, act2],
        [pltpu.VMEM((chans, 3 * area), BF16)],
    )
    out0, out1, out2 = call(
        functools.partial(out_kernel, taps),
        [plane, plane_b, plane_b],
        [gather, wide, act0, act1, act2],
        [pltpu.VMEM((3 * area, taps * chans), BF16)],
        order=[part],
    )
    moved3, keep, send = call(
        functools.partial(finish_kernel, taps, inv_batch),
        [columns(1), shaped((rows, chans), F32), shaped((rows, chans), BF16)],
        [info, scatter, cot3, act3, part],
        [pltpu.VMEM(window, F32)],
        order=[out0],
    )
    half, narrow = call(
        join_kernel,
        [shaped((rows, chans), F32), shaped((rows, chans), BF16)],
        [keep, swap(send, "fsdp", CORE)],
    )
    pair1 = swap(narrow, "rep", 1)
    pair2 = swap(narrow, "rep", 2)

    packs = call(
        functools.partial(last_kernel, taps),
        [shaped((2 * area, chans), BF16)] * 3,
        [gather, wide, turned, act3, moved3, grad1, grad2, out1, out2],
        [pltpu.VMEM((area, taps * chans), BF16)],
        order=[keep],
    )
    packs = hold(packs, [narrow])
    masks = (ACROSS, ALONG, ACROSS | ALONG)
    packs = [swap(pack, "fsdp", mask) for pack, mask in zip(packs, masks)]

    block_out, input_grad, terms = call(
        functools.partial(back_kernel, GROUPS, inv_batch),
        [plane_b, plane_b, shaped((2, chans), F32)],
        [latent, stats, params, grad0, out0, *packs],
    )
    across, along, both = [swap(terms, "fsdp", mask) for mask in masks]
    terms = (terms + across) + (along + both)
    terms = terms + swap(terms, "fsdp", CORE)
    other = jnp.where(partner_bit[0] == 0, swap(terms, "rep", 1), swap(terms, "rep", 2))
    norm_avg = 0.5 * (terms + other)
    shard_bit = lax.dynamic_slice_in_dim(partner_bit, place, 1)
    (weight_avg,) = call(
        functools.partial(pair_kernel, 3),
        [shaped((rows, chans), F32)],
        [shard_bit, half, pair1, pair2],
        [
            pltpu.VMEM((rows, chans), BF16),
            pltpu.VMEM((rows, chans), F32),
            pltpu.SemaphoreType.DMA((3,)),
            pltpu.SemaphoreType.DMA((3,)),
        ],
        outside=[2, 3],
    )
    shape = (1, side, side, chans)
    return (block_out.reshape(shape), input_grad.reshape(shape), weight_avg[None], norm_avg[None])


def solution(mesh):
    in_specs = (
        P(("rep", "fsdp"), None, None, None),
        P(("rep", "fsdp"), None, None, None),
        P("rep", "fsdp", None),
        P("rep", None),
        P("rep", None),
        P(),
    )
    out_specs = (
        P(("rep", "fsdp"), None, None, None),
        P(("rep", "fsdp"), None, None, None),
        P("rep", "fsdp", None),
        P("rep", None, None),
    )
    planes = mesh.shape["fsdp"] == 8 and mesh.shape["rep"] == 4
    shards = shards_plane if planes else shards_general
    return jax.shard_map(shards, mesh=mesh, in_specs=in_specs, out_specs=out_specs, check_vma=False)
```

```python
import functools

import jax
import jax.numpy as jnp
from jax import lax
from jax.experimental import pallas as pl
from jax.experimental.pallas import tpu as pltpu
from jax.sharding import PartitionSpec as P

GROUPS = 32


def partner(value, axis, stride):
    mask = 2**stride
    pairs = [(source, source ^ mask) for source in range(lax.axis_size(axis))]
    return lax.ppermute(value, axis, pairs)


def norm_forward(values_in, gain, shift, groups):
    count, side, chans = (values_in.shape[0], values_in.shape[1], values_in.shape[3])
    values = values_in.astype(jnp.float32).reshape(count, side * side, groups, chans // groups)
    center = jnp.mean(values, axis=(1, 3), keepdims=True)
    spread = jnp.mean(jnp.square(values - center), axis=(1, 3), keepdims=True)
    scale_inv = lax.rsqrt(spread + 1e-05)
    normed = (values - center) * scale_inv
    pre_act = normed * gain.reshape(groups, -1) + shift.reshape(groups, -1)
    return (normed, scale_inv, pre_act)


def make_patches(activation):
    count, side, chans = (activation.shape[0], activation.shape[1], activation.shape[3])
    padded = jnp.pad(activation, ((0, 0), (1, 1), (1, 1), (0, 0)))
    pieces = [
        padded[:, row_off : row_off + side, col_off : col_off + side, :]
        for row_off in range(3)
        for col_off in range(3)
    ]
    return jnp.concatenate(pieces, axis=-1).reshape(count * side * side, 9 * chans)


def fold_patches(patch_grad, count, side, chans):
    grads = patch_grad.reshape(count, side, side, 9, chans)
    total = jnp.zeros((count, side + 2, side + 2, chans), jnp.float32)
    for row_off in range(3):
        for col_off in range(3):
            tap = grads[:, :, :, row_off * 3 + col_off, :]
            total = total + jnp.pad(
                tap, ((0, 0), (row_off, 2 - row_off), (col_off, 2 - col_off), (0, 0))
            )
    return total[:, 1:-1, 1:-1, :]


def backward_rest(act_grad, normed, scale_inv, pre_act, gain, groups, inv_batch):
    count, side, chans = (act_grad.shape[0], act_grad.shape[1], act_grad.shape[3])
    act_grad = act_grad.reshape(count, side * side, groups, chans // groups)
    sigma = jax.nn.sigmoid(pre_act)
    pre_grad = act_grad * sigma * (1.0 + pre_act * (1.0 - sigma))
    gain_grad = jnp.sum(pre_grad * normed, axis=(0, 1)).reshape(-1) * inv_batch
    shift_grad = jnp.sum(pre_grad, axis=(0, 1)).reshape(-1) * inv_batch
    normed_grad = pre_grad * gain.reshape(groups, -1)
    first = jnp.mean(normed_grad, axis=(1, 3), keepdims=True)
    second = jnp.mean(normed_grad * normed, axis=(1, 3), keepdims=True)
    input_grad = scale_inv * (normed_grad - first - normed * second)
    return (
        input_grad.reshape(count, side, side, chans).astype(jnp.bfloat16),
        jnp.stack([gain_grad, shift_grad]),
    )


def shards_general(latents, cotangent, conv_weight, norm_gain, norm_shift, partner_bit):
    count, side, chans = (latents.shape[0], latents.shape[1], latents.shape[3])
    shard_total = lax.axis_size("fsdp")
    inv_batch = 1.0 / (count * shard_total)
    gain = norm_gain[0]
    normed, scale_inv, pre_act = norm_forward(latents, gain, norm_shift[0], GROUPS)
    activation = jax.nn.silu(pre_act).astype(jnp.bfloat16).reshape(count, side, side, chans)
    patches = make_patches(activation)
    cot_rows = cotangent.reshape(count * side * side, chans)
    weight_rows = conv_weight[0]
    output = jnp.dot(
        patches,
        lax.all_gather(weight_rows, "fsdp", axis=0, tiled=True),
        preferred_element_type=jnp.float32,
    )
    patch_grad = lax.dot_general(
        cot_rows,
        lax.all_gather(weight_rows, "fsdp", axis=0, tiled=True),
        (((1,), (1,)), ((), ())),
        preferred_element_type=jnp.float32,
    )
    block_out = output.astype(jnp.bfloat16).reshape(count, side, side, chans)
    act_grad = fold_patches(patch_grad, count, side, chans)
    input_grad, norm_term = backward_rest(
        act_grad, normed, scale_inv, pre_act, gain, GROUPS, inv_batch
    )
    weight_term = (
        lax.dot_general(
            patches, cot_rows, (((0,), (0,)), ((), ())), preferred_element_type=jnp.float32
        )
        * inv_batch
    )
    shard_rows = weight_rows.shape[0]
    term_pieces = weight_term.reshape(shard_total, shard_rows, chans)
    received = lax.all_to_all(
        term_pieces.astype(jnp.bfloat16), "fsdp", split_axis=0, concat_axis=0, tiled=True
    ).astype(term_pieces.dtype)
    weight_shard = jnp.sum(received, axis=0)
    bit_count = lax.axis_size("rep").bit_length() - 1
    shard_bit = lax.dynamic_index_in_dim(partner_bit, lax.axis_index("fsdp"), 0, keepdims=False)
    norm_bit = partner_bit[0]
    paired_norm = norm_term
    for bit_index in range(bit_count):
        other_norm = partner(norm_term, "rep", bit_index)
        paired_norm = jnp.where(norm_bit == bit_index, 0.5 * (norm_term + other_norm), paired_norm)
    norm_avg = lax.psum(paired_norm, "fsdp")
    weight_avg = weight_shard
    for bit_index in range(bit_count):
        other_weight = partner(weight_shard.astype(jnp.bfloat16), "rep", bit_index).astype(
            weight_shard.dtype
        )
        weight_avg = jnp.where(
            shard_bit == bit_index, 0.5 * (weight_shard + other_weight), weight_avg
        )
    return (block_out, input_grad, weight_avg[None], norm_avg[None])


CORE, ACROSS, ALONG = 1, 2, 4
VMEM_LIMIT = 20 * 1024 * 1024
F32, BF16 = jnp.float32, jnp.bfloat16


def swap(value, axis, mask):
    pairs = [(source, source ^ mask) for source in range(lax.axis_size(axis))]
    return lax.ppermute(value, axis, pairs)


def call(kernel, outs, args, scratch=(), order=(), outside=()):
    vmem = pl.BlockSpec(memory_space=pltpu.VMEM)
    smem = pl.BlockSpec(memory_space=pltpu.SMEM)
    untouched = pl.BlockSpec(memory_space=pl.ANY)

    def body(*refs):
        kernel(*refs[: len(args)], *refs[len(args) + len(order) :])

    return pl.pallas_call(
        body,
        out_shape=tuple(outs),
        in_specs=[
            untouched if index in outside else smem if a.dtype == jnp.int32 else vmem
            for index, a in enumerate(args)
        ]
        + [untouched] * len(order),
        out_specs=tuple(untouched if outside else vmem for _ in outs),
        scratch_shapes=list(scratch),
        compiler_params=pltpu.CompilerParams(vmem_limit_bytes=VMEM_LIMIT),
    )(*args, *order)


def hold(values, order):
    untouched = pl.BlockSpec(memory_space=pl.ANY)
    return pl.pallas_call(
        lambda *refs: None,
        out_shape=tuple(shaped(value.shape, value.dtype) for value in values),
        in_specs=[untouched] * (len(values) + len(order)),
        out_specs=tuple(untouched for _ in values),
        input_output_aliases={index: index for index in range(len(values))},
        compiler_params=pltpu.CompilerParams(vmem_limit_bytes=1024 * 1024),
    )(*values, *order)


def shaped(shape, dtype):
    return jax.ShapeDtypeStruct(shape, dtype)


def matmul(left, right):
    return jnp.dot(left, right, preferred_element_type=F32)


def group_matrix(chans, groups, transpose):
    width = chans // groups
    shape = (128, chans) if transpose else (chans, 128)
    chan = lax.broadcasted_iota(jnp.int32, shape, 1 if transpose else 0)
    low = lax.broadcasted_iota(jnp.int32, shape, 0 if transpose else 1) * width
    return ((chan >= low) & (chan < low + width)).astype(F32)


def group_mean(columns, total, groups):
    chans = columns.shape[1]
    exact = dict(precision=lax.Precision.HIGHEST, preferred_element_type=F32)
    sums = jnp.dot(columns, group_matrix(chans, groups, False), **exact)
    return jnp.dot(sums, group_matrix(chans, groups, True), **exact) * (1.0 / total)


def col_sums(*values):
    rows = [jnp.sum(value, axis=0, keepdims=True) for value in values]
    fill = jnp.zeros((8 - len(rows), rows[0].shape[1]), F32)
    return jnp.concatenate(rows + [fill], axis=0)


def norm_kernel(groups, latent, params, act, stats):
    gain, shift = params[0:1], params[1:2]
    values = latent[...].astype(F32)
    total = values.shape[0] * values.shape[1] // groups
    center = group_mean(col_sums(values), total, groups)[0:1]
    moved = values - center
    spread = group_mean(col_sums(moved * moved), total, groups)[0:1]
    scale_inv = lax.rsqrt(spread + 1e-05)
    pre = moved * scale_inv * gain + shift
    act[...] = (pre / (1.0 + jnp.exp(-pre))).astype(BF16)
    stats[0:1] = center
    stats[1:2] = scale_inv


def tap_matrix(tap, side, transpose):
    shape = (side * side, side * side)
    here = lax.broadcasted_iota(jnp.int32, shape, 1 if transpose else 0)
    there = lax.broadcasted_iota(jnp.int32, shape, 0 if transpose else 1)
    row_off = lax.div(tap, 3)
    col_off = tap - 3 * row_off
    bits = side.bit_length() - 1
    rows = lax.shift_right_logical(there, bits) - lax.shift_right_logical(here, bits)
    cols = (there & (side - 1)) - (here & (side - 1))
    hit = (rows == row_off - 1) & (cols == col_off - 1)
    return hit.astype(F32).astype(BF16)


def prepare_kernel(side, taps, info, own, other, wide, turned, gather, scatter):
    rows, chans = own.shape
    area = side * side
    wide[...] = jnp.zeros_like(wide)
    wide[pl.ds(pl.multiple_of(info[1], 16), rows), :] = own[...]
    wide[pl.ds(pl.multiple_of(info[2], 16), rows), :] = other[...]
    for tap in range(taps):
        part = slice(tap * chans, (tap + 1) * chans)
        turned[part, :] = wide[part, :].T
        gather[tap * area : (tap + 1) * area, :] = tap_matrix(info[0] + tap, side, False)
        scatter[tap * area : (tap + 1) * area, :] = tap_matrix(info[0] + tap, side, True)


def move_into(target, index, taps, matrices, value):
    area, width = value.shape
    moved = matmul(matrices, value).astype(BF16)
    for tap in range(taps):
        target[index * area : (index + 1) * area, tap * width : (tap + 1) * width] = moved[
            tap * area : (tap + 1) * area
        ]


def split_latents(value, refs):
    area = refs[0].shape[0]
    for index, ref in enumerate(refs):
        ref[...] = value[index * area : (index + 1) * area].astype(ref.dtype)


def grad_kernel(taps, scatter, turned, c0, c1, c2, moved, g0, g1, g2):
    for index, ref in enumerate((c0, c1, c2)):
        move_into(moved, index, taps, scatter[...], ref[...])
    split_latents(matmul(moved[...], turned[...]), (g0, g1, g2))


def weight_kernel(taps, moved, a0, a1, a2, part, across):
    area, chans = a0.shape
    for index, ref in enumerate((a0, a1, a2)):
        across[:, index * area : (index + 1) * area] = ref[...].T
    for tap in range(taps):
        block = slice(tap * chans, (tap + 1) * chans)
        part[block, :] = matmul(across[...], moved[:, block])


def out_kernel(taps, gather, wide, a0, a1, a2, g1, g2, y0, p1, p2, moved):
    area = a0.shape[0]
    for index, ref in enumerate((a0, a1, a2)):
        move_into(moved, index, taps, gather[...], ref[...])
    total = matmul(moved[...], wide[...])
    y0[...] = total[:area]
    for index, (grad, pack) in enumerate(((g1, p1), (g2, p2))):
        pack[:area] = grad[...]
        pack[area:] = total[(index + 1) * area : (index + 2) * area].astype(BF16)


def window_terms(start, rows, chans, across, moved, part):
    tap = lax.div(start, chans)
    offset = start - tap * chans
    picked = across[pl.ds(pl.multiple_of(offset, 16), rows), :]
    row = lax.broadcasted_iota(jnp.int32, picked.shape, 0)
    zero = jnp.zeros_like(picked)
    in_first = row < chans - offset
    left = jnp.concatenate(
        [jnp.where(in_first, picked, zero), jnp.where(in_first, zero, picked)], axis=1
    )
    right = jnp.concatenate(
        [moved[:, pl.ds(pl.multiple_of((tap + step) * chans, 128), chans)] for step in range(2)],
        axis=0,
    )
    return part[pl.ds(pl.multiple_of(start, 16), rows), :] + matmul(left, right)


def finish_kernel(taps, factor, info, scatter, c3, a3, part, moved, send, across):
    chans = a3.shape[1]
    move_into(moved, 0, taps, scatter[...], c3[...])
    turned = a3[...].T
    across[:chans] = turned
    across[chans:] = turned
    terms = window_terms(info[2], send.shape[0], chans, across, moved, part)
    send[...] = (terms * factor).astype(BF16)


def last_kernel(taps, factor, info, gather, wide, turned, a3, moved, part, keep, g3, y3, across, placed):
    chans = a3.shape[1]
    latent = a3[...].T
    across[:chans] = latent
    across[chans:] = latent
    keep[...] = window_terms(info[1], keep.shape[0], chans, across, moved, part) * factor
    g3[...] = matmul(moved[...], turned[...]).astype(BF16)
    move_into(placed, 0, taps, gather[...], a3[...])
    y3[...] = matmul(placed[...], wide[...]).astype(BF16)


def join_kernel(keep, got, narrow):
    narrow[...] = (keep[...] + got[...].astype(F32)).astype(BF16)


def half_kernel(keep, got, half):
    half[...] = 0.5 * (keep[...] + got[...].astype(F32))


def pair_kernel(chunks, bit, half, pair1, pair2, mean, got, made, arrive, leave):
    size = half.shape[0] // chunks
    parts = [pl.ds(index * size, size) for index in range(chunks)]

    def fetch(source, index):
        return pltpu.make_async_copy(source.at[parts[index]], got.at[parts[index]], arrive.at[index])

    @pl.when(bit[0] == 0)
    def _():
        for index in range(chunks):
            fetch(pair1, index).start()

    @pl.when(bit[0] != 0)
    def _():
        for index in range(chunks):
            fetch(pair2, index).start()

    stores = []
    for index, rows in enumerate(parts):
        fetch(pair1, index).wait()
        made[rows, :] = half[rows, :] + 0.5 * got[rows, :].astype(F32)
        stores.append(pltpu.make_async_copy(made.at[rows], mean.at[rows], leave.at[index]))
        stores[-1].start()
    for store in stores:
        store.wait()


def back_kernel(groups, factor, latent, stats, params, g0, y0, p1, p2, g3, grad, out_sum, terms):
    gain, shift = params[0:1], params[1:2]
    values = latent[...].astype(F32)
    total = values.shape[0] * values.shape[1] // groups
    scale_inv = stats[1:2]
    normed = (values - stats[0:1]) * scale_inv
    pre = normed * gain + shift
    area = latent.shape[0]
    act_grad = g0[...] + g3[...].astype(F32)
    act_grad = act_grad + p1[:area].astype(F32) + p2[:area].astype(F32)
    out_sum[...] = y0[...] + p1[area:].astype(F32) + p2[area:].astype(F32)
    sigma = 1.0 / (1.0 + jnp.exp(-pre))
    pre_grad = act_grad * sigma * (1.0 + pre * (1.0 - sigma))
    sums = col_sums(pre_grad * normed, pre_grad)
    terms[...] = sums[0:2] * factor
    means = group_mean(sums * gain, total, groups)
    grad[...] = (scale_inv * (pre_grad * gain - means[1:2] - normed * means[0:1])).astype(BF16)


def shards_plane(latents, cotangent, conv_weight, norm_gain, norm_shift, partner_bit):
    side, chans = latents.shape[1], latents.shape[3]
    area = side * side
    shard_total = lax.axis_size("fsdp")
    inv_batch = 1.0 / shard_total
    place = lax.axis_index("fsdp")
    weight = conv_weight[0]
    rows = weight.shape[0]
    starts = [2 * rows * chip for chip in range(shard_total // 2)]
    taps = max((start % chans + 2 * rows + chans - 1) // chans for start in starts)
    start = 2 * rows * (place // 2)
    first = jnp.minimum(start // chans, 9 - taps)
    offset = start - first * chans
    core = place % 2
    own_start, other_start = offset + rows * core, offset + rows * (1 - core)
    info = jnp.stack([first, own_start, other_start]).astype(jnp.int32)

    def columns(count, dtype=BF16):
        return shaped((count * area, taps * chans), dtype)

    plane, plane_b = shaped((area, chans), F32), shaped((area, chans), BF16)
    window = (taps * chans, chans)

    latent = latents.reshape(area, chans)
    cot0 = cotangent.reshape(area, chans)
    params = jnp.concatenate([norm_gain, norm_shift])
    other_weight = swap(weight, "fsdp", CORE)
    cot1 = swap(cot0, "fsdp", ACROSS)
    cot2 = swap(cot0, "fsdp", ALONG)
    act0, stats = call(
        functools.partial(norm_kernel, GROUPS),
        [plane_b, shaped((2, chans), F32)],
        [latent, params],
    )
    act2 = swap(act0, "fsdp", ALONG)
    act1 = swap(act0, "fsdp", ACROSS)
    wide, turned, gather, scatter = call(
        functools.partial(prepare_kernel, side, taps),
        [shaped(window, BF16)] * 2 + [shaped((taps * area, area), BF16)] * 2,
        [info, weight, other_weight],
        order=[stats],
    )
    moved, grad0, grad1, grad2 = call(
        functools.partial(grad_kernel, taps),
        [columns(3), plane, plane_b, plane_b],
        [scatter, turned, cot0, cot1, cot2],
    )
    act2, cot1 = hold([act2, cot1], [grad0])
    act3 = swap(act2, "fsdp", ACROSS)
    cot3 = swap(cot1, "fsdp", ALONG)
    (part,) = call(
        functools.partial(weight_kernel, taps),
        [shaped(window, F32)],
        [moved, act0, act1, act2],
        [pltpu.VMEM((chans, 3 * area), BF16)],
    )
    pair_shape = shaped((2 * area, chans), BF16)
    out0, pack1, pack2 = call(
        functools.partial(out_kernel, taps),
        [plane, pair_shape, pair_shape],
        [gather, wide, act0, act1, act2, grad1, grad2],
        [pltpu.VMEM((3 * area, taps * chans), BF16)],
        order=[part],
    )
    moved3, send = call(
        functools.partial(finish_kernel, taps, inv_batch),
        [columns(1), shaped((rows, chans), BF16)],
        [info, scatter, cot3, act3, part],
        [pltpu.VMEM((2 * chans, area), BF16)],
        order=[out0],
    )
    got = swap(send, "fsdp", CORE)
    keep, grad3, out3 = call(
        functools.partial(last_kernel, taps, inv_batch),
        [shaped((rows, chans), F32), plane_b, plane_b],
        [info, gather, wide, turned, act3, moved3, part],
        [pltpu.VMEM((2 * chans, area), BF16), pltpu.VMEM((area, taps * chans), BF16)],
    )
    (narrow,) = call(join_kernel, [shaped((rows, chans), BF16)], [keep, got])
    pair1 = swap(narrow, "rep", 1)
    pair2 = swap(narrow, "rep", 2)

    pack1, pack2, grad3 = hold([pack1, pack2, grad3], [narrow])
    pack1 = swap(pack1, "fsdp", ACROSS)
    pack2 = swap(pack2, "fsdp", ALONG)
    grad3 = swap(grad3, "fsdp", ACROSS | ALONG)
    (half,) = call(half_kernel, [shaped((rows, chans), F32)], [keep, got], order=[narrow])
    (out3,) = hold([out3], [pack1, pack2, grad3])
    out3 = swap(out3, "fsdp", ACROSS | ALONG)

    input_grad, out_sum, terms = call(
        functools.partial(back_kernel, GROUPS, inv_batch),
        [plane_b, plane, shaped((2, chans), F32)],
        [latent, stats, params, grad0, out0, pack1, pack2, grad3],
        order=[half],
    )
    for mask in (ACROSS, ALONG):
        terms = terms + swap(terms, "fsdp", mask)
    block_out = (out_sum + out3.astype(F32)).astype(BF16)
    other = jnp.where(partner_bit[0] == 0, swap(terms, "rep", 1), swap(terms, "rep", 2))
    (terms,) = hold([0.5 * (terms + other)], [pair1, pair2])
    norm_avg = terms + swap(terms, "fsdp", CORE)
    shard_bit = lax.dynamic_slice_in_dim(partner_bit, place, 1)
    (weight_avg,) = call(
        functools.partial(pair_kernel, 5),
        [shaped((rows, chans), F32)],
        [shard_bit, half, pair1, pair2],
        [
            pltpu.VMEM((rows, chans), BF16),
            pltpu.VMEM((rows, chans), F32),
            pltpu.SemaphoreType.DMA((5,)),
            pltpu.SemaphoreType.DMA((5,)),
        ],
        outside=[2, 3],
    )
    shape = (1, side, side, chans)
    return (block_out.reshape(shape), input_grad.reshape(shape), weight_avg[None], norm_avg[None])


def solution(mesh):
    in_specs = (
        P(("rep", "fsdp"), None, None, None),
        P(("rep", "fsdp"), None, None, None),
        P("rep", "fsdp", None),
        P("rep", None),
        P("rep", None),
        P(),
    )
    out_specs = (
        P(("rep", "fsdp"), None, None, None),
        P(("rep", "fsdp"), None, None, None),
        P("rep", "fsdp", None),
        P("rep", None, None),
    )
    planes = mesh.shape["fsdp"] == 8 and mesh.shape["rep"] == 4
    shards = shards_plane if planes else shards_general
    return jax.shard_map(shards, mesh=mesh, in_specs=in_specs, out_specs=out_specs, check_vma=False)
```

```python
import functools

import jax
import jax.numpy as jnp
from jax import lax
from jax.experimental import pallas as pl
from jax.experimental.pallas import tpu as pltpu
from jax.sharding import PartitionSpec as P

GROUPS = 32


def partner(value, axis, stride):
    mask = 2**stride
    pairs = [(source, source ^ mask) for source in range(lax.axis_size(axis))]
    return lax.ppermute(value, axis, pairs)


def norm_forward(values_in, gain, shift, groups):
    count, side, chans = (values_in.shape[0], values_in.shape[1], values_in.shape[3])
    values = values_in.astype(jnp.float32).reshape(count, side * side, groups, chans // groups)
    center = jnp.mean(values, axis=(1, 3), keepdims=True)
    spread = jnp.mean(jnp.square(values - center), axis=(1, 3), keepdims=True)
    scale_inv = lax.rsqrt(spread + 1e-05)
    normed = (values - center) * scale_inv
    pre_act = normed * gain.reshape(groups, -1) + shift.reshape(groups, -1)
    return (normed, scale_inv, pre_act)


def make_patches(activation):
    count, side, chans = (activation.shape[0], activation.shape[1], activation.shape[3])
    padded = jnp.pad(activation, ((0, 0), (1, 1), (1, 1), (0, 0)))
    pieces = [
        padded[:, row_off : row_off + side, col_off : col_off + side, :]
        for row_off in range(3)
        for col_off in range(3)
    ]
    return jnp.concatenate(pieces, axis=-1).reshape(count * side * side, 9 * chans)


def fold_patches(patch_grad, count, side, chans):
    grads = patch_grad.reshape(count, side, side, 9, chans)
    total = jnp.zeros((count, side + 2, side + 2, chans), jnp.float32)
    for row_off in range(3):
        for col_off in range(3):
            tap = grads[:, :, :, row_off * 3 + col_off, :]
            total = total + jnp.pad(
                tap, ((0, 0), (row_off, 2 - row_off), (col_off, 2 - col_off), (0, 0))
            )
    return total[:, 1:-1, 1:-1, :]


def backward_rest(act_grad, normed, scale_inv, pre_act, gain, groups, inv_batch):
    count, side, chans = (act_grad.shape[0], act_grad.shape[1], act_grad.shape[3])
    act_grad = act_grad.reshape(count, side * side, groups, chans // groups)
    sigma = jax.nn.sigmoid(pre_act)
    pre_grad = act_grad * sigma * (1.0 + pre_act * (1.0 - sigma))
    gain_grad = jnp.sum(pre_grad * normed, axis=(0, 1)).reshape(-1) * inv_batch
    shift_grad = jnp.sum(pre_grad, axis=(0, 1)).reshape(-1) * inv_batch
    normed_grad = pre_grad * gain.reshape(groups, -1)
    first = jnp.mean(normed_grad, axis=(1, 3), keepdims=True)
    second = jnp.mean(normed_grad * normed, axis=(1, 3), keepdims=True)
    input_grad = scale_inv * (normed_grad - first - normed * second)
    return (
        input_grad.reshape(count, side, side, chans).astype(jnp.bfloat16),
        jnp.stack([gain_grad, shift_grad]),
    )


def shards_general(latents, cotangent, conv_weight, norm_gain, norm_shift, partner_bit):
    count, side, chans = (latents.shape[0], latents.shape[1], latents.shape[3])
    shard_total = lax.axis_size("fsdp")
    inv_batch = 1.0 / (count * shard_total)
    gain = norm_gain[0]
    normed, scale_inv, pre_act = norm_forward(latents, gain, norm_shift[0], GROUPS)
    activation = jax.nn.silu(pre_act).astype(jnp.bfloat16).reshape(count, side, side, chans)
    patches = make_patches(activation)
    cot_rows = cotangent.reshape(count * side * side, chans)
    weight_rows = conv_weight[0]
    output = jnp.dot(
        patches,
        lax.all_gather(weight_rows, "fsdp", axis=0, tiled=True),
        preferred_element_type=jnp.float32,
    )
    patch_grad = lax.dot_general(
        cot_rows,
        lax.all_gather(weight_rows, "fsdp", axis=0, tiled=True),
        (((1,), (1,)), ((), ())),
        preferred_element_type=jnp.float32,
    )
    block_out = output.astype(jnp.bfloat16).reshape(count, side, side, chans)
    act_grad = fold_patches(patch_grad, count, side, chans)
    input_grad, norm_term = backward_rest(
        act_grad, normed, scale_inv, pre_act, gain, GROUPS, inv_batch
    )
    weight_term = (
        lax.dot_general(
            patches, cot_rows, (((0,), (0,)), ((), ())), preferred_element_type=jnp.float32
        )
        * inv_batch
    )
    shard_rows = weight_rows.shape[0]
    term_pieces = weight_term.reshape(shard_total, shard_rows, chans)
    received = lax.all_to_all(
        term_pieces.astype(jnp.bfloat16), "fsdp", split_axis=0, concat_axis=0, tiled=True
    ).astype(term_pieces.dtype)
    weight_shard = jnp.sum(received, axis=0)
    bit_count = lax.axis_size("rep").bit_length() - 1
    shard_bit = lax.dynamic_index_in_dim(partner_bit, lax.axis_index("fsdp"), 0, keepdims=False)
    norm_bit = partner_bit[0]
    paired_norm = norm_term
    for bit_index in range(bit_count):
        other_norm = partner(norm_term, "rep", bit_index)
        paired_norm = jnp.where(norm_bit == bit_index, 0.5 * (norm_term + other_norm), paired_norm)
    norm_avg = lax.psum(paired_norm, "fsdp")
    weight_avg = weight_shard
    for bit_index in range(bit_count):
        other_weight = partner(weight_shard.astype(jnp.bfloat16), "rep", bit_index).astype(
            weight_shard.dtype
        )
        weight_avg = jnp.where(
            shard_bit == bit_index, 0.5 * (weight_shard + other_weight), weight_avg
        )
    return (block_out, input_grad, weight_avg[None], norm_avg[None])


CORE, ACROSS, ALONG = 1, 2, 4
VMEM_LIMIT = 12 * 1024 * 1024
F32, BF16 = jnp.float32, jnp.bfloat16


def swap(value, axis, mask):
    pairs = [(source, source ^ mask) for source in range(lax.axis_size(axis))]
    return lax.ppermute(value, axis, pairs)


def call(kernel, outs, args, scratch=(), order=(), outside=()):
    vmem = pl.BlockSpec(memory_space=pltpu.VMEM)
    smem = pl.BlockSpec(memory_space=pltpu.SMEM)
    untouched = pl.BlockSpec(memory_space=pl.ANY)

    def body(*refs):
        kernel(*refs[: len(args)], *refs[len(args) + len(order) :])

    return pl.pallas_call(
        body,
        out_shape=tuple(outs),
        in_specs=[
            untouched if index in outside else smem if a.dtype == jnp.int32 else vmem
            for index, a in enumerate(args)
        ]
        + [untouched] * len(order),
        out_specs=tuple(untouched if outside else vmem for _ in outs),
        scratch_shapes=list(scratch),
        compiler_params=pltpu.CompilerParams(vmem_limit_bytes=VMEM_LIMIT),
    )(*args, *order)


def hold(values, order):
    untouched = pl.BlockSpec(memory_space=pl.ANY)
    return pl.pallas_call(
        lambda *refs: None,
        out_shape=tuple(shaped(value.shape, value.dtype) for value in values),
        in_specs=[untouched] * (len(values) + len(order)),
        out_specs=tuple(untouched for _ in values),
        input_output_aliases={index: index for index in range(len(values))},
        compiler_params=pltpu.CompilerParams(vmem_limit_bytes=1024 * 1024),
    )(*values, *order)


def shaped(shape, dtype):
    return jax.ShapeDtypeStruct(shape, dtype)


def matmul(left, right):
    return jnp.dot(left, right, preferred_element_type=F32)


def group_matrix(chans, groups, transpose):
    width = chans // groups
    shape = (128, chans) if transpose else (chans, 128)
    chan = lax.broadcasted_iota(jnp.int32, shape, 1 if transpose else 0)
    low = lax.broadcasted_iota(jnp.int32, shape, 0 if transpose else 1) * width
    return ((chan >= low) & (chan < low + width)).astype(F32)


def group_mean(columns, total, groups):
    chans = columns.shape[1]
    exact = dict(precision=lax.Precision.HIGHEST, preferred_element_type=F32)
    sums = jnp.dot(columns, group_matrix(chans, groups, False), **exact)
    return jnp.dot(sums, group_matrix(chans, groups, True), **exact) * (1.0 / total)


def col_sums(*values):
    rows = [jnp.sum(value, axis=0, keepdims=True) for value in values]
    fill = jnp.zeros((8 - len(rows), rows[0].shape[1]), F32)
    return jnp.concatenate(rows + [fill], axis=0)


def norm_kernel(groups, latent, params, act, stats):
    gain, shift = params[0:1], params[1:2]
    values = latent[...].astype(F32)
    total = values.shape[0] * values.shape[1] // groups
    center = group_mean(col_sums(values), total, groups)[0:1]
    moved = values - center
    spread = group_mean(col_sums(moved * moved), total, groups)[0:1]
    scale_inv = lax.rsqrt(spread + 1e-05)
    pre = moved * scale_inv * gain + shift
    act[...] = (pre / (1.0 + jnp.exp(-pre))).astype(BF16)
    stats[0:1] = center
    stats[1:2] = scale_inv


def tap_matrix(tap, side, transpose):
    shape = (side * side, side * side)
    here = lax.broadcasted_iota(jnp.int32, shape, 1 if transpose else 0)
    there = lax.broadcasted_iota(jnp.int32, shape, 0 if transpose else 1)
    row_off = lax.div(tap, 3)
    col_off = tap - 3 * row_off
    bits = side.bit_length() - 1
    rows = lax.shift_right_logical(there, bits) - lax.shift_right_logical(here, bits)
    cols = (there & (side - 1)) - (here & (side - 1))
    hit = (rows == row_off - 1) & (cols == col_off - 1)
    return hit.astype(F32).astype(BF16)


def prepare_kernel(side, taps, info, own, other, wide, turned, gather, scatter):
    rows, chans = own.shape
    area = side * side
    wide[...] = jnp.zeros_like(wide)
    wide[pl.ds(pl.multiple_of(info[1], 16), rows), :] = own[...]
    wide[pl.ds(pl.multiple_of(info[2], 16), rows), :] = other[...]
    for tap in range(taps):
        part = slice(tap * chans, (tap + 1) * chans)
        turned[part, :] = wide[part, :].T
        gather[tap * area : (tap + 1) * area, :] = tap_matrix(info[0] + tap, side, False)
        scatter[tap * area : (tap + 1) * area, :] = tap_matrix(info[0] + tap, side, True)


def move_into(target, index, taps, matrices, value):
    area, width = value.shape
    moved = matmul(matrices, value).astype(BF16)
    for tap in range(taps):
        target[index * area : (index + 1) * area, tap * width : (tap + 1) * width] = moved[
            tap * area : (tap + 1) * area
        ]


def split_latents(value, refs):
    area = refs[0].shape[0]
    for index, ref in enumerate(refs):
        ref[...] = value[index * area : (index + 1) * area].astype(ref.dtype)


def grad_kernel(taps, scatter, turned, c0, c1, c2, moved, g0, g1, g2):
    for index, ref in enumerate((c0, c1, c2)):
        move_into(moved, index, taps, scatter[...], ref[...])
    split_latents(matmul(moved[...], turned[...]), (g0, g1, g2))


def weight_kernel(taps, moved, a0, a1, a2, part, across):
    area, chans = a0.shape
    for index, ref in enumerate((a0, a1, a2)):
        across[:, index * area : (index + 1) * area] = ref[...].T
    for tap in range(taps):
        block = slice(tap * chans, (tap + 1) * chans)
        part[block, :] = matmul(across[...], moved[:, block])


def out_kernel(taps, gather, wide, a0, a1, a2, g1, g2, y0, p1, p2, moved):
    area = a0.shape[0]
    for index, ref in enumerate((a0, a1, a2)):
        move_into(moved, index, taps, gather[...], ref[...])
    total = matmul(moved[...], wide[...])
    y0[...] = total[:area]
    for index, (grad, pack) in enumerate(((g1, p1), (g2, p2))):
        pack[:area] = grad[...]
        pack[area:] = total[(index + 1) * area : (index + 2) * area].astype(BF16)


def window_terms(start, rows, chans, across, moved, part):
    tap = lax.div(start, chans)
    offset = start - tap * chans
    picked = across[pl.ds(pl.multiple_of(offset, 16), rows), :]
    row = lax.broadcasted_iota(jnp.int32, picked.shape, 0)
    zero = jnp.zeros_like(picked)
    in_first = row < chans - offset
    left = jnp.concatenate(
        [jnp.where(in_first, picked, zero), jnp.where(in_first, zero, picked)], axis=1
    )
    right = jnp.concatenate(
        [moved[:, pl.ds(pl.multiple_of((tap + step) * chans, 128), chans)] for step in range(2)],
        axis=0,
    )
    return part[pl.ds(pl.multiple_of(start, 16), rows), :] + matmul(left, right)


def finish_kernel(taps, factor, info, scatter, c3, a3, part, moved, send, across):
    chans = a3.shape[1]
    move_into(moved, 0, taps, scatter[...], c3[...])
    turned = a3[...].T
    across[:chans] = turned
    across[chans:] = turned
    terms = window_terms(info[2], send.shape[0], chans, across, moved, part)
    send[...] = (terms * factor).astype(BF16)


def keep_kernel(taps, factor, info, turned, a3, moved, part, keep, g3, across):
    chans = a3.shape[1]
    latent = a3[...].T
    across[:chans] = latent
    across[chans:] = latent
    keep[...] = window_terms(info[1], keep.shape[0], chans, across, moved, part) * factor
    g3[...] = matmul(moved[...], turned[...]).astype(BF16)


def last_kernel(taps, gather, wide, a3, y3, placed):
    move_into(placed, 0, taps, gather[...], a3[...])
    y3[...] = matmul(placed[...], wide[...]).astype(BF16)


def join_kernel(keep, got, narrow):
    narrow[...] = (keep[...] + got[...].astype(F32)).astype(BF16)


def half_kernel(keep, got, half):
    half[...] = 0.5 * (keep[...] + got[...].astype(F32))


def pair_kernel(chunks, bit, half, pair1, pair2, mean, got, made, arrive, leave):
    size = half.shape[0] // chunks
    parts = [pl.ds(index * size, size) for index in range(chunks)]

    def fetch(source, index):
        return pltpu.make_async_copy(source.at[parts[index]], got.at[parts[index]], arrive.at[index])

    @pl.when(bit[0] == 0)
    def _():
        for index in range(chunks):
            fetch(pair1, index).start()

    @pl.when(bit[0] != 0)
    def _():
        for index in range(chunks):
            fetch(pair2, index).start()

    stores = []
    for index, rows in enumerate(parts):
        fetch(pair1, index).wait()
        made[rows, :] = half[rows, :] + 0.5 * got[rows, :].astype(F32)
        stores.append(pltpu.make_async_copy(made.at[rows], mean.at[rows], leave.at[index]))
        stores[-1].start()
    for store in stores:
        store.wait()


def back_kernel(groups, factor, latent, stats, params, g0, y0, p1, p2, g3, grad, out_sum, terms):
    gain, shift = params[0:1], params[1:2]
    values = latent[...].astype(F32)
    total = values.shape[0] * values.shape[1] // groups
    scale_inv = stats[1:2]
    normed = (values - stats[0:1]) * scale_inv
    pre = normed * gain + shift
    area = latent.shape[0]
    act_grad = g0[...] + g3[...].astype(F32)
    act_grad = act_grad + p1[:area].astype(F32) + p2[:area].astype(F32)
    out_sum[...] = y0[...] + p1[area:].astype(F32) + p2[area:].astype(F32)
    sigma = 1.0 / (1.0 + jnp.exp(-pre))
    pre_grad = act_grad * sigma * (1.0 + pre * (1.0 - sigma))
    sums = col_sums(pre_grad * normed, pre_grad)
    terms[...] = sums[0:2] * factor
    means = group_mean(sums * gain, total, groups)
    grad[...] = (scale_inv * (pre_grad * gain - means[1:2] - normed * means[0:1])).astype(BF16)


def shards_plane(latents, cotangent, conv_weight, norm_gain, norm_shift, partner_bit):
    side, chans = latents.shape[1], latents.shape[3]
    area = side * side
    shard_total = lax.axis_size("fsdp")
    inv_batch = 1.0 / shard_total
    place = lax.axis_index("fsdp")
    weight = conv_weight[0]
    rows = weight.shape[0]
    starts = [2 * rows * chip for chip in range(shard_total // 2)]
    taps = max((start % chans + 2 * rows + chans - 1) // chans for start in starts)
    start = 2 * rows * (place // 2)
    first = jnp.minimum(start // chans, 9 - taps)
    offset = start - first * chans
    core = place % 2
    own_start, other_start = offset + rows * core, offset + rows * (1 - core)
    info = jnp.stack([first, own_start, other_start]).astype(jnp.int32)

    def columns(count, dtype=BF16):
        return shaped((count * area, taps * chans), dtype)

    plane, plane_b = shaped((area, chans), F32), shaped((area, chans), BF16)
    window = (taps * chans, chans)

    latent = latents.reshape(area, chans)
    cot0 = cotangent.reshape(area, chans)
    params = jnp.concatenate([norm_gain, norm_shift])
    other_weight = swap(weight, "fsdp", CORE)
    cot1 = swap(cot0, "fsdp", ACROSS)
    cot2 = swap(cot0, "fsdp", ALONG)
    act0, stats = call(
        functools.partial(norm_kernel, GROUPS),
        [plane_b, shaped((2, chans), F32)],
        [latent, params],
    )
    act2 = swap(act0, "fsdp", ALONG)
    act1 = swap(act0, "fsdp", ACROSS)
    wide, turned, gather, scatter = call(
        functools.partial(prepare_kernel, side, taps),
        [shaped(window, BF16)] * 2 + [shaped((taps * area, area), BF16)] * 2,
        [info, weight, other_weight],
        order=[stats],
    )
    moved, grad0, grad1, grad2 = call(
        functools.partial(grad_kernel, taps),
        [columns(3), plane, plane_b, plane_b],
        [scatter, turned, cot0, cot1, cot2],
    )
    act2, cot1 = hold([act2, cot1], [grad0])
    act3 = swap(act2, "fsdp", ACROSS)
    cot3 = swap(cot1, "fsdp", ALONG)
    (part,) = call(
        functools.partial(weight_kernel, taps),
        [shaped(window, F32)],
        [moved, act0, act1, act2],
        [pltpu.VMEM((chans, 3 * area), BF16)],
    )
    pair_shape = shaped((2 * area, chans), BF16)
    out0, pack1, pack2 = call(
        functools.partial(out_kernel, taps),
        [plane, pair_shape, pair_shape],
        [gather, wide, act0, act1, act2, grad1, grad2],
        [pltpu.VMEM((3 * area, taps * chans), BF16)],
        order=[part],
    )
    moved3, send = call(
        functools.partial(finish_kernel, taps, inv_batch),
        [columns(1), shaped((rows, chans), BF16)],
        [info, scatter, cot3, act3, part],
        [pltpu.VMEM((2 * chans, area), BF16)],
        order=[out0],
    )
    got = swap(send, "fsdp", CORE)
    keep, grad3 = call(
        functools.partial(keep_kernel, taps, inv_batch),
        [shaped((rows, chans), F32), plane_b],
        [info, turned, act3, moved3, part],
        [pltpu.VMEM((2 * chans, area), BF16)],
    )
    (narrow,) = call(join_kernel, [shaped((rows, chans), BF16)], [keep, got])
    pair1 = swap(narrow, "rep", 1)
    pair2 = swap(narrow, "rep", 2)

    pack1, pack2, grad3 = hold([pack1, pack2, grad3], [narrow])
    pack1 = swap(pack1, "fsdp", ACROSS)
    pack2 = swap(pack2, "fsdp", ALONG)
    grad3 = swap(grad3, "fsdp", ACROSS | ALONG)
    (out3,) = call(
        functools.partial(last_kernel, taps),
        [plane_b],
        [gather, wide, act3],
        [pltpu.VMEM((area, taps * chans), BF16)],
        order=[narrow],
    )
    (half,) = call(half_kernel, [shaped((rows, chans), F32)], [keep, got], order=[narrow])
    (last,) = hold([out3], [pack1, pack2, grad3])
    last = swap(last, "fsdp", ACROSS | ALONG)

    input_grad, out_sum, terms = call(
        functools.partial(back_kernel, GROUPS, inv_batch),
        [plane_b, plane, shaped((2, chans), F32)],
        [latent, stats, params, grad0, out0, pack1, pack2, grad3],
        order=[half, out3],
    )
    for mask in (ACROSS, ALONG):
        terms = terms + swap(terms, "fsdp", mask)
    block_out = (out_sum + last.astype(F32)).astype(BF16)
    other = jnp.where(partner_bit[0] == 0, swap(terms, "rep", 1), swap(terms, "rep", 2))
    (terms,) = hold([0.5 * (terms + other)], [pair1, pair2, last])
    norm_avg = terms + swap(terms, "fsdp", CORE)
    shard_bit = lax.dynamic_slice_in_dim(partner_bit, place, 1)
    (weight_avg,) = call(
        functools.partial(pair_kernel, 5),
        [shaped((rows, chans), F32)],
        [shard_bit, half, pair1, pair2],
        [
            pltpu.VMEM((rows, chans), BF16),
            pltpu.VMEM((rows, chans), F32),
            pltpu.SemaphoreType.DMA((5,)),
            pltpu.SemaphoreType.DMA((5,)),
        ],
        outside=[2, 3],
    )
    shape = (1, side, side, chans)
    return (block_out.reshape(shape), input_grad.reshape(shape), weight_avg[None], norm_avg[None])


def solution(mesh):
    in_specs = (
        P(("rep", "fsdp"), None, None, None),
        P(("rep", "fsdp"), None, None, None),
        P("rep", "fsdp", None),
        P("rep", None),
        P("rep", None),
        P(),
    )
    out_specs = (
        P(("rep", "fsdp"), None, None, None),
        P(("rep", "fsdp"), None, None, None),
        P("rep", "fsdp", None),
        P("rep", None, None),
    )
    planes = mesh.shape["fsdp"] == 8 and mesh.shape["rep"] == 4
    shards = shards_plane if planes else shards_general
    return jax.shard_map(shards, mesh=mesh, in_specs=in_specs, out_specs=out_specs, check_vma=False)
```

```python
import functools

import jax
import jax.numpy as jnp
from jax import lax
from jax.experimental import pallas as pl
from jax.experimental.pallas import tpu as pltpu
from jax.sharding import PartitionSpec as P

GROUPS = 32


def partner(value, axis, stride):
    mask = 2**stride
    pairs = [(source, source ^ mask) for source in range(lax.axis_size(axis))]
    return lax.ppermute(value, axis, pairs)


def norm_forward(values_in, gain, shift, groups):
    count, side, chans = (values_in.shape[0], values_in.shape[1], values_in.shape[3])
    values = values_in.astype(jnp.float32).reshape(count, side * side, groups, chans // groups)
    center = jnp.mean(values, axis=(1, 3), keepdims=True)
    spread = jnp.mean(jnp.square(values - center), axis=(1, 3), keepdims=True)
    scale_inv = lax.rsqrt(spread + 1e-05)
    normed = (values - center) * scale_inv
    pre_act = normed * gain.reshape(groups, -1) + shift.reshape(groups, -1)
    return (normed, scale_inv, pre_act)


def make_patches(activation):
    count, side, chans = (activation.shape[0], activation.shape[1], activation.shape[3])
    padded = jnp.pad(activation, ((0, 0), (1, 1), (1, 1), (0, 0)))
    pieces = [
        padded[:, row_off : row_off + side, col_off : col_off + side, :]
        for row_off in range(3)
        for col_off in range(3)
    ]
    return jnp.concatenate(pieces, axis=-1).reshape(count * side * side, 9 * chans)


def fold_patches(patch_grad, count, side, chans):
    grads = patch_grad.reshape(count, side, side, 9, chans)
    total = jnp.zeros((count, side + 2, side + 2, chans), jnp.float32)
    for row_off in range(3):
        for col_off in range(3):
            tap = grads[:, :, :, row_off * 3 + col_off, :]
            total = total + jnp.pad(
                tap, ((0, 0), (row_off, 2 - row_off), (col_off, 2 - col_off), (0, 0))
            )
    return total[:, 1:-1, 1:-1, :]


def backward_rest(act_grad, normed, scale_inv, pre_act, gain, groups, inv_batch):
    count, side, chans = (act_grad.shape[0], act_grad.shape[1], act_grad.shape[3])
    act_grad = act_grad.reshape(count, side * side, groups, chans // groups)
    sigma = jax.nn.sigmoid(pre_act)
    pre_grad = act_grad * sigma * (1.0 + pre_act * (1.0 - sigma))
    gain_grad = jnp.sum(pre_grad * normed, axis=(0, 1)).reshape(-1) * inv_batch
    shift_grad = jnp.sum(pre_grad, axis=(0, 1)).reshape(-1) * inv_batch
    normed_grad = pre_grad * gain.reshape(groups, -1)
    first = jnp.mean(normed_grad, axis=(1, 3), keepdims=True)
    second = jnp.mean(normed_grad * normed, axis=(1, 3), keepdims=True)
    input_grad = scale_inv * (normed_grad - first - normed * second)
    return (
        input_grad.reshape(count, side, side, chans).astype(jnp.bfloat16),
        jnp.stack([gain_grad, shift_grad]),
    )


def shards_general(latents, cotangent, conv_weight, norm_gain, norm_shift, partner_bit):
    count, side, chans = (latents.shape[0], latents.shape[1], latents.shape[3])
    shard_total = lax.axis_size("fsdp")
    inv_batch = 1.0 / (count * shard_total)
    gain = norm_gain[0]
    normed, scale_inv, pre_act = norm_forward(latents, gain, norm_shift[0], GROUPS)
    activation = jax.nn.silu(pre_act).astype(jnp.bfloat16).reshape(count, side, side, chans)
    patches = make_patches(activation)
    cot_rows = cotangent.reshape(count * side * side, chans)
    weight_rows = conv_weight[0]
    output = jnp.dot(
        patches,
        lax.all_gather(weight_rows, "fsdp", axis=0, tiled=True),
        preferred_element_type=jnp.float32,
    )
    patch_grad = lax.dot_general(
        cot_rows,
        lax.all_gather(weight_rows, "fsdp", axis=0, tiled=True),
        (((1,), (1,)), ((), ())),
        preferred_element_type=jnp.float32,
    )
    block_out = output.astype(jnp.bfloat16).reshape(count, side, side, chans)
    act_grad = fold_patches(patch_grad, count, side, chans)
    input_grad, norm_term = backward_rest(
        act_grad, normed, scale_inv, pre_act, gain, GROUPS, inv_batch
    )
    weight_term = (
        lax.dot_general(
            patches, cot_rows, (((0,), (0,)), ((), ())), preferred_element_type=jnp.float32
        )
        * inv_batch
    )
    shard_rows = weight_rows.shape[0]
    term_pieces = weight_term.reshape(shard_total, shard_rows, chans)
    received = lax.all_to_all(
        term_pieces.astype(jnp.bfloat16), "fsdp", split_axis=0, concat_axis=0, tiled=True
    ).astype(term_pieces.dtype)
    weight_shard = jnp.sum(received, axis=0)
    bit_count = lax.axis_size("rep").bit_length() - 1
    shard_bit = lax.dynamic_index_in_dim(partner_bit, lax.axis_index("fsdp"), 0, keepdims=False)
    norm_bit = partner_bit[0]
    paired_norm = norm_term
    for bit_index in range(bit_count):
        other_norm = partner(norm_term, "rep", bit_index)
        paired_norm = jnp.where(norm_bit == bit_index, 0.5 * (norm_term + other_norm), paired_norm)
    norm_avg = lax.psum(paired_norm, "fsdp")
    weight_avg = weight_shard
    for bit_index in range(bit_count):
        other_weight = partner(weight_shard.astype(jnp.bfloat16), "rep", bit_index).astype(
            weight_shard.dtype
        )
        weight_avg = jnp.where(
            shard_bit == bit_index, 0.5 * (weight_shard + other_weight), weight_avg
        )
    return (block_out, input_grad, weight_avg[None], norm_avg[None])


CORE, ACROSS, ALONG = 1, 2, 4
VMEM_LIMIT = 12 * 1024 * 1024
EARLY = 384
NORM_LIMIT = 60 * 1024 * 1024
F32, BF16 = jnp.float32, jnp.bfloat16


def swap(value, axis, mask):
    pairs = [(source, source ^ mask) for source in range(lax.axis_size(axis))]
    return lax.ppermute(value, axis, pairs)


def call(kernel, outs, args, scratch=(), order=(), outside=(), limit=VMEM_LIMIT, alias=None):
    vmem = pl.BlockSpec(memory_space=pltpu.VMEM)
    smem = pl.BlockSpec(memory_space=pltpu.SMEM)
    untouched = pl.BlockSpec(memory_space=pl.ANY)

    def body(*refs):
        kernel(*refs[: len(args)], *refs[len(args) + len(order) :])

    return pl.pallas_call(
        body,
        out_shape=tuple(outs),
        in_specs=[
            untouched if index in outside else smem if a.dtype == jnp.int32 else vmem
            for index, a in enumerate(args)
        ]
        + [untouched] * len(order),
        out_specs=tuple(untouched if outside else vmem for _ in outs),
        scratch_shapes=list(scratch),
        input_output_aliases=alias or {},
        compiler_params=pltpu.CompilerParams(vmem_limit_bytes=limit),
    )(*args, *order)


def hold(values, order):
    untouched = pl.BlockSpec(memory_space=pl.ANY)
    return pl.pallas_call(
        lambda *refs: None,
        out_shape=tuple(shaped(value.shape, value.dtype) for value in values),
        in_specs=[untouched] * (len(values) + len(order)),
        out_specs=tuple(untouched for _ in values),
        input_output_aliases={index: index for index in range(len(values))},
        compiler_params=pltpu.CompilerParams(vmem_limit_bytes=1024 * 1024),
    )(*values, *order)


def shaped(shape, dtype):
    return jax.ShapeDtypeStruct(shape, dtype)


def matmul(left, right):
    return jnp.dot(left, right, preferred_element_type=F32)


def group_matrix(chans, groups, transpose):
    width = chans // groups
    shape = (128, chans) if transpose else (chans, 128)
    chan = lax.broadcasted_iota(jnp.int32, shape, 1 if transpose else 0)
    low = lax.broadcasted_iota(jnp.int32, shape, 0 if transpose else 1) * width
    return ((chan >= low) & (chan < low + width)).astype(F32)


def group_mean(columns, total, groups):
    chans = columns.shape[1]
    exact = dict(precision=lax.Precision.HIGHEST, preferred_element_type=F32)
    sums = jnp.dot(columns, group_matrix(chans, groups, False), **exact)
    return jnp.dot(sums, group_matrix(chans, groups, True), **exact) * (1.0 / total)


def col_sums(*values):
    rows = [jnp.sum(value, axis=0, keepdims=True) for value in values]
    fill = jnp.zeros((8 - len(rows), rows[0].shape[1]), F32)
    return jnp.concatenate(rows + [fill], axis=0)


def norm_kernel(groups, latent, gain_in, shift_in, cot, act, stats, cot_early, cot_late):
    gain, shift = gain_in[...], shift_in[...]
    cot_early[...] = cot[:, :EARLY]
    cot_late[...] = cot[:, EARLY:]
    values = latent[...].astype(F32)
    total = values.shape[0] * values.shape[1] // groups
    center = group_mean(col_sums(values), total, groups)[0:1]
    moved = values - center
    spread = group_mean(col_sums(moved * moved), total, groups)[0:1]
    scale_inv = lax.rsqrt(spread + 1e-05)
    pre = moved * scale_inv * gain + shift
    act[...] = (pre / (1.0 + jnp.exp(-pre))).astype(BF16)
    stats[0:1] = center
    stats[1:2] = scale_inv


def tap_matrix(tap, side, transpose):
    shape = (side * side, side * side)
    here = lax.broadcasted_iota(jnp.int32, shape, 1 if transpose else 0)
    there = lax.broadcasted_iota(jnp.int32, shape, 0 if transpose else 1)
    row_off = lax.div(tap, 3)
    col_off = tap - 3 * row_off
    bits = side.bit_length() - 1
    rows = lax.shift_right_logical(there, bits) - lax.shift_right_logical(here, bits)
    cols = (there & (side - 1)) - (here & (side - 1))
    hit = (rows == row_off - 1) & (cols == col_off - 1)
    return hit.astype(F32).astype(BF16)


def prepare_kernel(side, taps, info, own, other, wide, turned, gather, scatter):
    rows, chans = own.shape
    area = side * side
    wide[...] = jnp.zeros_like(wide)
    wide[pl.ds(pl.multiple_of(info[1], 16), rows), :] = own[...]
    wide[pl.ds(pl.multiple_of(info[2], 16), rows), :] = other[...]
    for tap in range(taps):
        part = slice(tap * chans, (tap + 1) * chans)
        turned[part, :] = wide[part, :].T
        gather[tap * area : (tap + 1) * area, :] = tap_matrix(info[0] + tap, side, False)
        scatter[tap * area : (tap + 1) * area, :] = tap_matrix(info[0] + tap, side, True)


def move_into(target, index, taps, matrices, value):
    area, width = value.shape
    moved = matmul(matrices, value).astype(BF16)
    for tap in range(taps):
        target[index * area : (index + 1) * area, tap * width : (tap + 1) * width] = moved[
            tap * area : (tap + 1) * area
        ]


def split_latents(value, refs):
    area = refs[0].shape[0]
    for index, ref in enumerate(refs):
        ref[...] = value[index * area : (index + 1) * area].astype(ref.dtype)


def early_kernel(taps, scatter, c0, c1, c2, a0, a1, a2, moved, part, across):
    area, chans = a0.shape
    width = c0.shape[1]
    for index, ref in enumerate((c0, c1, c2)):
        move_into(moved, index, taps, scatter[...], ref[...])
    for index, ref in enumerate((a0, a1, a2)):
        across[:, index * area : (index + 1) * area] = ref[...].T
    for tap in range(taps):
        part[tap * chans : (tap + 1) * chans, :] = matmul(
            across[...], moved[:, tap * width : (tap + 1) * width]
        )


def out_kernel(taps, gather, wide, a0, a1, a2, y0, y1, y2, moved):
    for index, ref in enumerate((a0, a1, a2)):
        move_into(moved, index, taps, gather[...], ref[...])
    split_latents(matmul(moved[...], wide[...]), (y0, y1, y2))


def window_terms(start, rows, chans, across, moved, part):
    tap = lax.div(start, chans)
    offset = start - tap * chans
    picked = across[pl.ds(pl.multiple_of(offset, 16), rows), :]
    row = lax.broadcasted_iota(jnp.int32, picked.shape, 0)
    zero = jnp.zeros_like(picked)
    in_first = row < chans - offset
    left = jnp.concatenate(
        [jnp.where(in_first, picked, zero), jnp.where(in_first, zero, picked)], axis=1
    )
    width = part.shape[1]
    right = jnp.concatenate(
        [moved[:, pl.ds(pl.multiple_of((tap + step) * width, 128), width)] for step in range(2)],
        axis=0,
    )
    return part[pl.ds(pl.multiple_of(start, 16), rows), :] + matmul(left, right)


def finish_kernel(taps, factor, info, scatter, c3, a3, part, moved, send, across):
    chans = a3.shape[1]
    move_into(moved, 0, taps, scatter[...], c3[...])
    turned = a3[...].T
    across[:chans] = turned
    across[chans:] = turned
    terms = window_terms(info[2], send.shape[0], chans, across, moved, part)
    send[...] = (terms * factor).astype(BF16)


def keep_kernel(taps, factor, info, a3, moved, part, keep, across):
    chans = a3.shape[1]
    latent = a3[...].T
    across[:chans] = latent
    across[chans:] = latent
    keep[...] = window_terms(info[1], keep.shape[0], chans, across, moved, part) * factor


def late_kernel(taps, factor, info, a0, a1, a2, a3, moved, send, keep, across, terms):
    area, chans = a0.shape
    rows, width = keep.shape
    for index, ref in enumerate((a0, a1, a2, a3)):
        across[:, index * area : (index + 1) * area] = ref[...].T
    for tap in range(taps):
        terms[tap * chans : (tap + 1) * chans, :] = matmul(
            across[...], moved[:, tap * width : (tap + 1) * width]
        )
    send[...] = (terms[pl.ds(pl.multiple_of(info[2], 16), rows), :] * factor).astype(BF16)
    keep[...] = terms[pl.ds(pl.multiple_of(info[1], 16), rows), :] * factor


def grad_kernel(taps, scatter, c0, c1, c2, c3, early, early3, turned, y1, y2, late, g0, p1, p2, g3, moved):
    for index, ref in enumerate((c0, c1, c2, c3)):
        move_into(late, index, taps, scatter[...], ref[...])
    first, second = early.shape[1] // taps, late.shape[1] // taps
    chans = first + second
    three, area = early.shape[0], early3.shape[0]
    for tap in range(taps):
        low, mid, high = tap * chans, tap * chans + first, (tap + 1) * chans
        moved[:three, low:mid] = early[:, tap * first : (tap + 1) * first]
        moved[three:, low:mid] = early3[:, tap * first : (tap + 1) * first]
        moved[:, mid:high] = late[:, tap * second : (tap + 1) * second]
    total = matmul(moved[...], turned[...])
    g0[...] = total[:area]
    g3[...] = total[3 * area :].astype(BF16)
    for index, (out, pack) in enumerate(((y1, p1), (y2, p2))):
        pack[:area] = total[(index + 1) * area : (index + 2) * area].astype(BF16)
        pack[area:] = out[...]


def last_kernel(taps, gather, wide, a3, y3, placed):
    move_into(placed, 0, taps, gather[...], a3[...])
    y3[...] = matmul(placed[...], wide[...]).astype(BF16)


def join_kernel(keep, got, narrow):
    narrow[...] = (keep[...] + got[...].astype(F32)).astype(BF16)


def half_kernel(keep, got, half):
    half[...] = 0.5 * (keep[...] + got[...].astype(F32))


def pair_kernel(chunks, low, bit, half, pair1, pair2, *rest):
    mean, got, made, arrive, leave = rest[-5:]
    width = half.shape[1]
    size = half.shape[0] // chunks
    parts = [pl.ds(index * size, size) for index in range(chunks)]

    def fetch(source, index):
        return pltpu.make_async_copy(source.at[parts[index]], got.at[parts[index]], arrive.at[index])

    @pl.when(bit[0] == 0)
    def _():
        for index in range(chunks):
            fetch(pair1, index).start()

    @pl.when(bit[0] != 0)
    def _():
        for index in range(chunks):
            fetch(pair2, index).start()

    stores = []
    for index, rows in enumerate(parts):
        fetch(pair1, index).wait()
        made[rows, :] = half[rows, :] + 0.5 * got[rows, :].astype(F32)
        stores.append(
            pltpu.make_async_copy(made.at[rows], mean.at[rows, pl.ds(low, width)], leave.at[index])
        )
        stores[-1].start()
    for store in stores:
        store.wait()


def back_kernel(groups, factor, latent, stats, gain_in, shift_in, g0, y0, p1, p2, g3, out_sum, grad, terms):
    gain, shift = gain_in[...], shift_in[...]
    values = latent[...].astype(F32)
    total = values.shape[0] * values.shape[1] // groups
    scale_inv = stats[1:2]
    normed = (values - stats[0:1]) * scale_inv
    pre = normed * gain + shift
    area = latent.shape[0]
    act_grad = g0[...] + g3[...].astype(F32)
    act_grad = act_grad + p1[:area].astype(F32) + p2[:area].astype(F32)
    out_sum[...] = y0[...] + p1[area:].astype(F32) + p2[area:].astype(F32)
    sigma = 1.0 / (1.0 + jnp.exp(-pre))
    pre_grad = act_grad * sigma * (1.0 + pre * (1.0 - sigma))
    sums = col_sums(pre_grad * normed, pre_grad)
    terms[...] = sums[0:2] * factor
    means = group_mean(sums * gain, total, groups)
    grad[...] = (scale_inv * (pre_grad * gain - means[1:2] - normed * means[0:1])).astype(BF16)


def shards_plane(latents, cotangent, conv_weight, norm_gain, norm_shift, partner_bit):
    side, chans = latents.shape[1], latents.shape[3]
    area = side * side
    late = chans - EARLY
    shard_total = lax.axis_size("fsdp")
    inv_batch = 1.0 / shard_total
    place = lax.axis_index("fsdp")
    weight = conv_weight[0]
    rows = weight.shape[0]
    starts = [2 * rows * chip for chip in range(shard_total // 2)]
    taps = max((start % chans + 2 * rows + chans - 1) // chans for start in starts)
    start = 2 * rows * (place // 2)
    first = jnp.minimum(start // chans, 9 - taps)
    offset = start - first * chans
    core = place % 2
    own_start, other_start = offset + rows * core, offset + rows * (1 - core)
    info = jnp.stack([first, own_start, other_start]).astype(jnp.int32)
    masks = (ACROSS, ALONG, ACROSS | ALONG)

    def columns(count, width):
        return shaped((count * area, taps * width), BF16)

    plane, plane_b = shaped((area, chans), F32), shaped((area, chans), BF16)
    window = (taps * chans, chans)

    latent = latents.reshape(area, chans)
    cot = cotangent.reshape(area, chans)
    act0, stats, cot0, rest0 = call(
        functools.partial(norm_kernel, GROUPS),
        [plane_b, shaped((2, chans), F32), shaped((area, EARLY), BF16), shaped((area, late), BF16)],
        [latent, norm_gain, norm_shift, cot],
        limit=NORM_LIMIT,
    )
    act2 = swap(act0, "fsdp", ALONG)
    act1 = swap(act0, "fsdp", ACROSS)
    cot1 = swap(cot0, "fsdp", ACROSS)
    cot2 = swap(cot0, "fsdp", ALONG)
    other_weight = swap(weight, "fsdp", CORE)
    wide, turned, gather, scatter = call(
        functools.partial(prepare_kernel, side, taps),
        [shaped(window, BF16)] * 2 + [shaped((taps * area, area), BF16)] * 2,
        [info, weight, other_weight],
        order=[stats],
    )
    act2, cot1, cot2 = hold([act2, cot1, cot2], [scatter])
    act3 = swap(act2, "fsdp", ACROSS)
    cot3 = swap(cot1, "fsdp", ALONG)
    moved, part = call(
        functools.partial(early_kernel, taps),
        [columns(3, EARLY), shaped((taps * chans, EARLY), F32)],
        [scatter, cot0, cot1, cot2, act0, act1, act2],
        [pltpu.VMEM((chans, 3 * area), BF16)],
    )
    out0, out1, out2 = call(
        functools.partial(out_kernel, taps),
        [plane, plane_b, plane_b],
        [gather, wide, act0, act1, act2],
        [pltpu.VMEM((3 * area, taps * chans), BF16)],
        order=[part],
    )
    moved3, send = call(
        functools.partial(finish_kernel, taps, inv_batch),
        [columns(1, EARLY), shaped((rows, EARLY), BF16)],
        [info, scatter, cot3, act3, part],
        [pltpu.VMEM((2 * chans, area), BF16)],
        order=[out0],
    )
    got = swap(send, "fsdp", CORE)
    (keep,) = call(
        functools.partial(keep_kernel, taps, inv_batch),
        [shaped((rows, EARLY), F32)],
        [info, act3, moved3, part],
        [pltpu.VMEM((2 * chans, area), BF16)],
    )

    (rest,) = hold([rest0], [send])
    rests = [swap(rest, "fsdp", mask) for mask in masks]

    (narrow,) = call(join_kernel, [shaped((rows, EARLY), BF16)], [keep, got])
    early1, early2 = [swap(narrow, "rep", mask) for mask in (1, 2)]
    (half,) = call(half_kernel, [shaped((rows, EARLY), F32)], [keep, got], order=[narrow])
    moved_late, grad0, pack1, pack2, grad3 = call(
        functools.partial(grad_kernel, taps),
        [columns(4, late), plane] + [shaped((2 * area, chans), BF16)] * 2 + [plane_b],
        [scatter, rest0, *rests, moved, moved3, turned, out1, out2],
        [pltpu.VMEM((4 * area, taps * chans), BF16)],
        order=[half],
    )
    send, keep = call(
        functools.partial(late_kernel, taps, inv_batch),
        [shaped((rows, late), BF16), shaped((rows, late), F32)],
        [info, act0, act1, act2, act3, moved_late],
        [pltpu.VMEM((chans, 4 * area), BF16), pltpu.VMEM((taps * chans, late), F32)],
        order=[grad0],
    )
    (out3,) = call(
        functools.partial(last_kernel, taps),
        [plane_b],
        [gather, wide, act3],
        [pltpu.VMEM((area, taps * chans), BF16)],
        order=[send],
    )
    (send,) = hold([send], [early1, early2, out3])
    got = swap(send, "fsdp", CORE)
    (narrow,) = call(join_kernel, [shaped((rows, late), BF16)], [keep, got])
    (late_half,) = call(half_kernel, [shaped((rows, late), F32)], [keep, got], order=[narrow])
    late1, late2 = [swap(narrow, "rep", mask) for mask in (1, 2)]

    pack1 = swap(pack1, "fsdp", ACROSS)
    pack2 = swap(pack2, "fsdp", ALONG)
    grad3 = swap(grad3, "fsdp", ACROSS | ALONG)
    (out3,) = hold([out3], [pack1, pack2, grad3])
    out3 = swap(out3, "fsdp", ACROSS | ALONG)

    shard_bit = lax.dynamic_slice_in_dim(partner_bit, place, 1)

    def pair_mean(low, half, pair1, pair2, into=(), order=()):
        width = half.shape[1]
        (mean,) = call(
            functools.partial(pair_kernel, 5, low),
            [shaped((rows, chans), F32)],
            [shard_bit, half, pair1, pair2, *into],
            [
                pltpu.VMEM((rows, width), BF16),
                pltpu.VMEM((rows, width), F32),
                pltpu.SemaphoreType.DMA((5,)),
                pltpu.SemaphoreType.DMA((5,)),
            ],
            order=order,
            outside=[2, 3, 4],
            alias={4: 0} if into else None,
        )
        return mean

    weight_avg = pair_mean(0, half, early1, early2, order=[late_half])

    out_sum, input_grad, terms = call(
        functools.partial(back_kernel, GROUPS, inv_batch),
        [plane, plane_b, shaped((2, chans), F32)],
        [latent, stats, norm_gain, norm_shift, grad0, out0, pack1, pack2, grad3],
        order=[weight_avg],
    )
    for mask in (ACROSS, ALONG):
        terms = terms + swap(terms, "fsdp", mask)
    block_out = (out_sum + out3.astype(F32)).astype(BF16)
    other = jnp.where(partner_bit[0] == 0, swap(terms, "rep", 1), swap(terms, "rep", 2))
    (terms,) = hold([0.5 * (terms + other)], [late1, late2, out3])
    norm_avg = terms + swap(terms, "fsdp", CORE)
    weight_avg = pair_mean(EARLY, late_half, late1, late2, [weight_avg])
    shape = (1, side, side, chans)
    return (block_out.reshape(shape), input_grad.reshape(shape), weight_avg[None], norm_avg[None])


def solution(mesh):
    in_specs = (
        P(("rep", "fsdp"), None, None, None),
        P(("rep", "fsdp"), None, None, None),
        P("rep", "fsdp", None),
        P("rep", None),
        P("rep", None),
        P(),
    )
    out_specs = (
        P(("rep", "fsdp"), None, None, None),
        P(("rep", "fsdp"), None, None, None),
        P("rep", "fsdp", None),
        P("rep", None, None),
    )
    planes = mesh.shape["fsdp"] == 8 and mesh.shape["rep"] == 4
    shards = shards_plane if planes else shards_general
    return jax.shard_map(shards, mesh=mesh, in_specs=in_specs, out_specs=out_specs, check_vma=False)
```

```python
import functools

import jax
import jax.numpy as jnp
from jax import lax
from jax.experimental import pallas as pl
from jax.experimental.pallas import tpu as pltpu
from jax.sharding import PartitionSpec as P

GROUPS = 32


def partner(value, axis, stride):
    mask = 2**stride
    pairs = [(source, source ^ mask) for source in range(lax.axis_size(axis))]
    return lax.ppermute(value, axis, pairs)


def norm_forward(values_in, gain, shift, groups):
    count, side, chans = (values_in.shape[0], values_in.shape[1], values_in.shape[3])
    values = values_in.astype(jnp.float32).reshape(count, side * side, groups, chans // groups)
    center = jnp.mean(values, axis=(1, 3), keepdims=True)
    spread = jnp.mean(jnp.square(values - center), axis=(1, 3), keepdims=True)
    scale_inv = lax.rsqrt(spread + 1e-05)
    normed = (values - center) * scale_inv
    pre_act = normed * gain.reshape(groups, -1) + shift.reshape(groups, -1)
    return (normed, scale_inv, pre_act)


def make_patches(activation):
    count, side, chans = (activation.shape[0], activation.shape[1], activation.shape[3])
    padded = jnp.pad(activation, ((0, 0), (1, 1), (1, 1), (0, 0)))
    pieces = [
        padded[:, row_off : row_off + side, col_off : col_off + side, :]
        for row_off in range(3)
        for col_off in range(3)
    ]
    return jnp.concatenate(pieces, axis=-1).reshape(count * side * side, 9 * chans)


def fold_patches(patch_grad, count, side, chans):
    grads = patch_grad.reshape(count, side, side, 9, chans)
    total = jnp.zeros((count, side + 2, side + 2, chans), jnp.float32)
    for row_off in range(3):
        for col_off in range(3):
            tap = grads[:, :, :, row_off * 3 + col_off, :]
            total = total + jnp.pad(
                tap, ((0, 0), (row_off, 2 - row_off), (col_off, 2 - col_off), (0, 0))
            )
    return total[:, 1:-1, 1:-1, :]


def backward_rest(act_grad, normed, scale_inv, pre_act, gain, groups, inv_batch):
    count, side, chans = (act_grad.shape[0], act_grad.shape[1], act_grad.shape[3])
    act_grad = act_grad.reshape(count, side * side, groups, chans // groups)
    sigma = jax.nn.sigmoid(pre_act)
    pre_grad = act_grad * sigma * (1.0 + pre_act * (1.0 - sigma))
    gain_grad = jnp.sum(pre_grad * normed, axis=(0, 1)).reshape(-1) * inv_batch
    shift_grad = jnp.sum(pre_grad, axis=(0, 1)).reshape(-1) * inv_batch
    normed_grad = pre_grad * gain.reshape(groups, -1)
    first = jnp.mean(normed_grad, axis=(1, 3), keepdims=True)
    second = jnp.mean(normed_grad * normed, axis=(1, 3), keepdims=True)
    input_grad = scale_inv * (normed_grad - first - normed * second)
    return (
        input_grad.reshape(count, side, side, chans).astype(jnp.bfloat16),
        jnp.stack([gain_grad, shift_grad]),
    )


def shards_general(latents, cotangent, conv_weight, norm_gain, norm_shift, partner_bit):
    count, side, chans = (latents.shape[0], latents.shape[1], latents.shape[3])
    shard_total = lax.axis_size("fsdp")
    inv_batch = 1.0 / (count * shard_total)
    gain = norm_gain[0]
    normed, scale_inv, pre_act = norm_forward(latents, gain, norm_shift[0], GROUPS)
    activation = jax.nn.silu(pre_act).astype(jnp.bfloat16).reshape(count, side, side, chans)
    patches = make_patches(activation)
    cot_rows = cotangent.reshape(count * side * side, chans)
    weight_rows = conv_weight[0]
    output = jnp.dot(
        patches,
        lax.all_gather(weight_rows, "fsdp", axis=0, tiled=True),
        preferred_element_type=jnp.float32,
    )
    patch_grad = lax.dot_general(
        cot_rows,
        lax.all_gather(weight_rows, "fsdp", axis=0, tiled=True),
        (((1,), (1,)), ((), ())),
        preferred_element_type=jnp.float32,
    )
    block_out = output.astype(jnp.bfloat16).reshape(count, side, side, chans)
    act_grad = fold_patches(patch_grad, count, side, chans)
    input_grad, norm_term = backward_rest(
        act_grad, normed, scale_inv, pre_act, gain, GROUPS, inv_batch
    )
    weight_term = (
        lax.dot_general(
            patches, cot_rows, (((0,), (0,)), ((), ())), preferred_element_type=jnp.float32
        )
        * inv_batch
    )
    shard_rows = weight_rows.shape[0]
    term_pieces = weight_term.reshape(shard_total, shard_rows, chans)
    received = lax.all_to_all(
        term_pieces.astype(jnp.bfloat16), "fsdp", split_axis=0, concat_axis=0, tiled=True
    ).astype(term_pieces.dtype)
    weight_shard = jnp.sum(received, axis=0)
    bit_count = lax.axis_size("rep").bit_length() - 1
    shard_bit = lax.dynamic_index_in_dim(partner_bit, lax.axis_index("fsdp"), 0, keepdims=False)
    norm_bit = partner_bit[0]
    paired_norm = norm_term
    for bit_index in range(bit_count):
        other_norm = partner(norm_term, "rep", bit_index)
        paired_norm = jnp.where(norm_bit == bit_index, 0.5 * (norm_term + other_norm), paired_norm)
    norm_avg = lax.psum(paired_norm, "fsdp")
    weight_avg = weight_shard
    for bit_index in range(bit_count):
        other_weight = partner(weight_shard.astype(jnp.bfloat16), "rep", bit_index).astype(
            weight_shard.dtype
        )
        weight_avg = jnp.where(
            shard_bit == bit_index, 0.5 * (weight_shard + other_weight), weight_avg
        )
    return (block_out, input_grad, weight_avg[None], norm_avg[None])


CORE, ACROSS, ALONG = 1, 2, 4
VMEM_LIMIT = 12 * 1024 * 1024
F32, BF16 = jnp.float32, jnp.bfloat16


def swap(value, axis, mask):
    pairs = [(source, source ^ mask) for source in range(lax.axis_size(axis))]
    return lax.ppermute(value, axis, pairs)


def call(kernel, outs, args, scratch=(), order=(), outside=()):
    vmem = pl.BlockSpec(memory_space=pltpu.VMEM)
    smem = pl.BlockSpec(memory_space=pltpu.SMEM)
    untouched = pl.BlockSpec(memory_space=pl.ANY)

    def body(*refs):
        kernel(*refs[: len(args)], *refs[len(args) + len(order) :])

    return pl.pallas_call(
        body,
        out_shape=tuple(outs),
        in_specs=[
            untouched if index in outside else smem if a.dtype == jnp.int32 else vmem
            for index, a in enumerate(args)
        ]
        + [untouched] * len(order),
        out_specs=tuple(untouched if outside else vmem for _ in outs),
        scratch_shapes=list(scratch),
        compiler_params=pltpu.CompilerParams(vmem_limit_bytes=VMEM_LIMIT),
    )(*args, *order)


def hold(values, order):
    untouched = pl.BlockSpec(memory_space=pl.ANY)
    return pl.pallas_call(
        lambda *refs: None,
        out_shape=tuple(shaped(value.shape, value.dtype) for value in values),
        in_specs=[untouched] * (len(values) + len(order)),
        out_specs=tuple(untouched for _ in values),
        input_output_aliases={index: index for index in range(len(values))},
        compiler_params=pltpu.CompilerParams(vmem_limit_bytes=1024 * 1024),
    )(*values, *order)


def shaped(shape, dtype):
    return jax.ShapeDtypeStruct(shape, dtype)


def matmul(left, right):
    return jnp.dot(left, right, preferred_element_type=F32)


def group_matrix(chans, groups, transpose):
    width = chans // groups
    shape = (128, chans) if transpose else (chans, 128)
    chan = lax.broadcasted_iota(jnp.int32, shape, 1 if transpose else 0)
    low = lax.broadcasted_iota(jnp.int32, shape, 0 if transpose else 1) * width
    return ((chan >= low) & (chan < low + width)).astype(F32)


def group_mean(columns, total, groups):
    chans = columns.shape[1]
    exact = dict(precision=lax.Precision.HIGHEST, preferred_element_type=F32)
    sums = jnp.dot(columns, group_matrix(chans, groups, False), **exact)
    return jnp.dot(sums, group_matrix(chans, groups, True), **exact) * (1.0 / total)


def col_sums(*values):
    rows = [jnp.sum(value, axis=0, keepdims=True) for value in values]
    fill = jnp.zeros((8 - len(rows), rows[0].shape[1]), F32)
    return jnp.concatenate(rows + [fill], axis=0)


def norm_kernel(groups, latent, params, act, stats):
    gain, shift = params[0:1], params[1:2]
    values = latent[...].astype(F32)
    total = values.shape[0] * values.shape[1] // groups
    center = group_mean(col_sums(values), total, groups)[0:1]
    moved = values - center
    spread = group_mean(col_sums(moved * moved), total, groups)[0:1]
    scale_inv = lax.rsqrt(spread + 1e-05)
    pre = moved * scale_inv * gain + shift
    act[...] = (pre / (1.0 + jnp.exp(-pre))).astype(BF16)
    stats[0:1] = center
    stats[1:2] = scale_inv


def tap_matrix(tap, side, transpose):
    shape = (side * side, side * side)
    here = lax.broadcasted_iota(jnp.int32, shape, 1 if transpose else 0)
    there = lax.broadcasted_iota(jnp.int32, shape, 0 if transpose else 1)
    row_off = lax.div(tap, 3)
    col_off = tap - 3 * row_off
    bits = side.bit_length() - 1
    rows = lax.shift_right_logical(there, bits) - lax.shift_right_logical(here, bits)
    cols = (there & (side - 1)) - (here & (side - 1))
    hit = (rows == row_off - 1) & (cols == col_off - 1)
    return hit.astype(F32).astype(BF16)


def prepare_kernel(side, taps, info, own, other, wide, turned, gather, scatter):
    rows, chans = own.shape
    area = side * side
    wide[...] = jnp.zeros_like(wide)
    wide[pl.ds(pl.multiple_of(info[1], 16), rows), :] = own[...]
    wide[pl.ds(pl.multiple_of(info[2], 16), rows), :] = other[...]
    for tap in range(taps):
        part = slice(tap * chans, (tap + 1) * chans)
        turned[part, :] = wide[part, :].T
        gather[tap * area : (tap + 1) * area, :] = tap_matrix(info[0] + tap, side, False)
        scatter[tap * area : (tap + 1) * area, :] = tap_matrix(info[0] + tap, side, True)


def move_into(target, index, taps, matrices, value):
    area, width = value.shape
    moved = matmul(matrices, value).astype(BF16)
    for tap in range(taps):
        target[index * area : (index + 1) * area, tap * width : (tap + 1) * width] = moved[
            tap * area : (tap + 1) * area
        ]


def split_latents(value, refs):
    area = refs[0].shape[0]
    for index, ref in enumerate(refs):
        ref[...] = value[index * area : (index + 1) * area].astype(ref.dtype)


def grad_kernel(taps, scatter, turned, c0, c1, c2, moved, g0, g1, g2):
    for index, ref in enumerate((c0, c1, c2)):
        move_into(moved, index, taps, scatter[...], ref[...])
    split_latents(matmul(moved[...], turned[...]), (g0, g1, g2))


def weight_kernel(taps, moved, a0, a1, a2, part, across):
    area, chans = a0.shape
    for index, ref in enumerate((a0, a1, a2)):
        across[:, index * area : (index + 1) * area] = ref[...].T
    for tap in range(taps):
        block = slice(tap * chans, (tap + 1) * chans)
        part[block, :] = matmul(across[...], moved[:, block])


def out_kernel(taps, gather, wide, a0, a1, a2, g1, g2, y0, p1, p2, moved):
    area = a0.shape[0]
    for index, ref in enumerate((a0, a1, a2)):
        move_into(moved, index, taps, gather[...], ref[...])
    total = matmul(moved[...], wide[...])
    y0[...] = total[:area]
    for index, (grad, pack) in enumerate(((g1, p1), (g2, p2))):
        pack[:area] = grad[...]
        pack[area:] = total[(index + 1) * area : (index + 2) * area].astype(BF16)


def window_terms(start, rows, chans, across, moved, part):
    tap = lax.div(start, chans)
    offset = start - tap * chans
    picked = across[pl.ds(pl.multiple_of(offset, 16), rows), :]
    row = lax.broadcasted_iota(jnp.int32, picked.shape, 0)
    zero = jnp.zeros_like(picked)
    in_first = row < chans - offset
    left = jnp.concatenate(
        [jnp.where(in_first, picked, zero), jnp.where(in_first, zero, picked)], axis=1
    )
    right = jnp.concatenate(
        [moved[:, pl.ds(pl.multiple_of((tap + step) * chans, 128), chans)] for step in range(2)],
        axis=0,
    )
    return part[pl.ds(pl.multiple_of(start, 16), rows), :] + matmul(left, right)


def finish_kernel(taps, factor, info, scatter, c3, a3, part, moved, send, across):
    chans = a3.shape[1]
    move_into(moved, 0, taps, scatter[...], c3[...])
    turned = a3[...].T
    across[:chans] = turned
    across[chans:] = turned
    terms = window_terms(info[2], send.shape[0], chans, across, moved, part)
    send[...] = (terms * factor).astype(BF16)


def keep_kernel(taps, factor, info, turned, a3, moved, part, keep, g3, across):
    chans = a3.shape[1]
    latent = a3[...].T
    across[:chans] = latent
    across[chans:] = latent
    keep[...] = window_terms(info[1], keep.shape[0], chans, across, moved, part) * factor
    g3[...] = matmul(moved[...], turned[...]).astype(BF16)


def last_kernel(taps, gather, wide, a3, y3, placed):
    move_into(placed, 0, taps, gather[...], a3[...])
    y3[...] = matmul(placed[...], wide[...]).astype(BF16)


def join_kernel(keep, got, narrow):
    narrow[...] = (keep[...] + got[...].astype(F32)).astype(BF16)


def pair_kernel(chunks, bit, own, pair1, pair2, y0, y1, mean, out, got, made, done, arrive, leave):
    size = own.shape[0] // chunks
    parts = [pl.ds(index * size, size) for index in range(chunks)]

    def fetch(source, index):
        return pltpu.make_async_copy(source.at[parts[index]], got.at[parts[index]], arrive.at[index])

    @pl.when(bit[0] == 0)
    def _():
        for index in range(chunks):
            fetch(pair1, index).start()

    @pl.when(bit[0] != 0)
    def _():
        for index in range(chunks):
            fetch(pair2, index).start()

    done[...] = (y0[...] + y1[...].astype(F32)).astype(BF16)
    stores = [pltpu.make_async_copy(done, out, leave.at[chunks])]
    stores[0].start()
    for index, rows in enumerate(parts):
        fetch(pair1, index).wait()
        made[rows, :] = 0.5 * (own[rows, :].astype(F32) + got[rows, :].astype(F32))
        stores.append(pltpu.make_async_copy(made.at[rows], mean.at[rows], leave.at[index]))
        stores[-1].start()
    for store in stores:
        store.wait()


def back_kernel(groups, factor, latent, stats, params, g0, y0, p1, p2, g3, grad, out_sum, terms):
    gain, shift = params[0:1], params[1:2]
    values = latent[...].astype(F32)
    total = values.shape[0] * values.shape[1] // groups
    scale_inv = stats[1:2]
    normed = (values - stats[0:1]) * scale_inv
    pre = normed * gain + shift
    area = latent.shape[0]
    act_grad = g0[...] + g3[...].astype(F32)
    act_grad = act_grad + p1[:area].astype(F32) + p2[:area].astype(F32)
    out_sum[...] = y0[...] + p1[area:].astype(F32) + p2[area:].astype(F32)
    sigma = 1.0 / (1.0 + jnp.exp(-pre))
    pre_grad = act_grad * sigma * (1.0 + pre * (1.0 - sigma))
    sums = col_sums(pre_grad * normed, pre_grad)
    terms[...] = sums[0:2] * factor
    means = group_mean(sums * gain, total, groups)
    grad[...] = (scale_inv * (pre_grad * gain - means[1:2] - normed * means[0:1])).astype(BF16)


def shards_plane(latents, cotangent, conv_weight, norm_gain, norm_shift, partner_bit):
    side, chans = latents.shape[1], latents.shape[3]
    area = side * side
    shard_total = lax.axis_size("fsdp")
    inv_batch = 1.0 / shard_total
    place = lax.axis_index("fsdp")
    weight = conv_weight[0]
    rows = weight.shape[0]
    starts = [2 * rows * chip for chip in range(shard_total // 2)]
    taps = max((start % chans + 2 * rows + chans - 1) // chans for start in starts)
    start = 2 * rows * (place // 2)
    first = jnp.minimum(start // chans, 9 - taps)
    offset = start - first * chans
    core = place % 2
    own_start, other_start = offset + rows * core, offset + rows * (1 - core)
    info = jnp.stack([first, own_start, other_start]).astype(jnp.int32)

    def columns(count, dtype=BF16):
        return shaped((count * area, taps * chans), dtype)

    plane, plane_b = shaped((area, chans), F32), shaped((area, chans), BF16)
    window = (taps * chans, chans)

    latent = latents.reshape(area, chans)
    cot0 = cotangent.reshape(area, chans)
    params = jnp.concatenate([norm_gain, norm_shift])
    other_weight = swap(weight, "fsdp", CORE)
    cot1 = swap(cot0, "fsdp", ACROSS)
    cot2 = swap(cot0, "fsdp", ALONG)
    act0, stats = call(
        functools.partial(norm_kernel, GROUPS),
        [plane_b, shaped((2, chans), F32)],
        [latent, params],
    )
    act2 = swap(act0, "fsdp", ALONG)
    act1 = swap(act0, "fsdp", ACROSS)
    wide, turned, gather, scatter = call(
        functools.partial(prepare_kernel, side, taps),
        [shaped(window, BF16)] * 2 + [shaped((taps * area, area), BF16)] * 2,
        [info, weight, other_weight],
        order=[stats],
    )
    moved, grad0, grad1, grad2 = call(
        functools.partial(grad_kernel, taps),
        [columns(3), plane, plane_b, plane_b],
        [scatter, turned, cot0, cot1, cot2],
    )
    act2, cot1 = hold([act2, cot1], [grad0])
    act3 = swap(act2, "fsdp", ACROSS)
    cot3 = swap(cot1, "fsdp", ALONG)
    (part,) = call(
        functools.partial(weight_kernel, taps),
        [shaped(window, F32)],
        [moved, act0, act1, act2],
        [pltpu.VMEM((chans, 3 * area), BF16)],
    )
    pair_shape = shaped((2 * area, chans), BF16)
    out0, pack1, pack2 = call(
        functools.partial(out_kernel, taps),
        [plane, pair_shape, pair_shape],
        [gather, wide, act0, act1, act2, grad1, grad2],
        [pltpu.VMEM((3 * area, taps * chans), BF16)],
        order=[part],
    )
    moved3, send = call(
        functools.partial(finish_kernel, taps, inv_batch),
        [columns(1), shaped((rows, chans), BF16)],
        [info, scatter, cot3, act3, part],
        [pltpu.VMEM((2 * chans, area), BF16)],
        order=[out0],
    )
    got = swap(send, "fsdp", CORE)
    keep, grad3 = call(
        functools.partial(keep_kernel, taps, inv_batch),
        [shaped((rows, chans), F32), plane_b],
        [info, turned, act3, moved3, part],
        [pltpu.VMEM((2 * chans, area), BF16)],
    )
    (narrow,) = call(join_kernel, [shaped((rows, chans), BF16)], [keep, got])
    pair1 = swap(narrow, "rep", 1)
    pair2 = swap(narrow, "rep", 2)

    pack1, pack2, grad3 = hold([pack1, pack2, grad3], [narrow])
    pack1 = swap(pack1, "fsdp", ACROSS)
    pack2 = swap(pack2, "fsdp", ALONG)
    grad3 = swap(grad3, "fsdp", ACROSS | ALONG)
    (out3,) = call(
        functools.partial(last_kernel, taps),
        [plane_b],
        [gather, wide, act3],
        [pltpu.VMEM((area, taps * chans), BF16)],
        order=[narrow],
    )
    (last,) = hold([out3], [pack1, pack2, grad3])
    last = swap(last, "fsdp", ACROSS | ALONG)

    input_grad, out_sum, terms = call(
        functools.partial(back_kernel, GROUPS, inv_batch),
        [plane_b, plane, shaped((2, chans), F32)],
        [latent, stats, params, grad0, out0, pack1, pack2, grad3],
        order=[out3],
    )
    for mask in (ACROSS, ALONG):
        terms = terms + swap(terms, "fsdp", mask)
    other = jnp.where(partner_bit[0] == 0, swap(terms, "rep", 1), swap(terms, "rep", 2))
    (terms,) = hold([0.5 * (terms + other)], [pair1, pair2, last])
    norm_avg = terms + swap(terms, "fsdp", CORE)
    shard_bit = lax.dynamic_slice_in_dim(partner_bit, place, 1)
    weight_avg, block_out = call(
        functools.partial(pair_kernel, 5),
        [shaped((rows, chans), F32), plane_b],
        [shard_bit, narrow, pair1, pair2, out_sum, last],
        [
            pltpu.VMEM((rows, chans), BF16),
            pltpu.VMEM((rows, chans), F32),
            pltpu.VMEM((area, chans), BF16),
            pltpu.SemaphoreType.DMA((5,)),
            pltpu.SemaphoreType.DMA((6,)),
        ],
        outside=[2, 3],
    )
    shape = (1, side, side, chans)
    return (block_out.reshape(shape), input_grad.reshape(shape), weight_avg[None], norm_avg[None])


def solution(mesh):
    in_specs = (
        P(("rep", "fsdp"), None, None, None),
        P(("rep", "fsdp"), None, None, None),
        P("rep", "fsdp", None),
        P("rep", None),
        P("rep", None),
        P(),
    )
    out_specs = (
        P(("rep", "fsdp"), None, None, None),
        P(("rep", "fsdp"), None, None, None),
        P("rep", "fsdp", None),
        P("rep", None, None),
    )
    planes = mesh.shape["fsdp"] == 8 and mesh.shape["rep"] == 4
    shards = shards_plane if planes else shards_general
    return jax.shard_map(shards, mesh=mesh, in_specs=in_specs, out_specs=out_specs, check_vma=False)
```

```python
import functools

import jax
import jax.numpy as jnp
from jax import lax
from jax.experimental import pallas as pl
from jax.experimental.pallas import tpu as pltpu
from jax.sharding import PartitionSpec as P

GROUPS = 32


def partner(value, axis, stride):
    mask = 2**stride
    pairs = [(source, source ^ mask) for source in range(lax.axis_size(axis))]
    return lax.ppermute(value, axis, pairs)


def norm_forward(values_in, gain, shift, groups):
    count, side, chans = (values_in.shape[0], values_in.shape[1], values_in.shape[3])
    values = values_in.astype(jnp.float32).reshape(count, side * side, groups, chans // groups)
    center = jnp.mean(values, axis=(1, 3), keepdims=True)
    spread = jnp.mean(jnp.square(values - center), axis=(1, 3), keepdims=True)
    scale_inv = lax.rsqrt(spread + 1e-05)
    normed = (values - center) * scale_inv
    pre_act = normed * gain.reshape(groups, -1) + shift.reshape(groups, -1)
    return (normed, scale_inv, pre_act)


def make_patches(activation):
    count, side, chans = (activation.shape[0], activation.shape[1], activation.shape[3])
    padded = jnp.pad(activation, ((0, 0), (1, 1), (1, 1), (0, 0)))
    pieces = [
        padded[:, row_off : row_off + side, col_off : col_off + side, :]
        for row_off in range(3)
        for col_off in range(3)
    ]
    return jnp.concatenate(pieces, axis=-1).reshape(count * side * side, 9 * chans)


def fold_patches(patch_grad, count, side, chans):
    grads = patch_grad.reshape(count, side, side, 9, chans)
    total = jnp.zeros((count, side + 2, side + 2, chans), jnp.float32)
    for row_off in range(3):
        for col_off in range(3):
            tap = grads[:, :, :, row_off * 3 + col_off, :]
            total = total + jnp.pad(
                tap, ((0, 0), (row_off, 2 - row_off), (col_off, 2 - col_off), (0, 0))
            )
    return total[:, 1:-1, 1:-1, :]


def backward_rest(act_grad, normed, scale_inv, pre_act, gain, groups, inv_batch):
    count, side, chans = (act_grad.shape[0], act_grad.shape[1], act_grad.shape[3])
    act_grad = act_grad.reshape(count, side * side, groups, chans // groups)
    sigma = jax.nn.sigmoid(pre_act)
    pre_grad = act_grad * sigma * (1.0 + pre_act * (1.0 - sigma))
    gain_grad = jnp.sum(pre_grad * normed, axis=(0, 1)).reshape(-1) * inv_batch
    shift_grad = jnp.sum(pre_grad, axis=(0, 1)).reshape(-1) * inv_batch
    normed_grad = pre_grad * gain.reshape(groups, -1)
    first = jnp.mean(normed_grad, axis=(1, 3), keepdims=True)
    second = jnp.mean(normed_grad * normed, axis=(1, 3), keepdims=True)
    input_grad = scale_inv * (normed_grad - first - normed * second)
    return (
        input_grad.reshape(count, side, side, chans).astype(jnp.bfloat16),
        jnp.stack([gain_grad, shift_grad]),
    )


def shards_general(latents, cotangent, conv_weight, norm_gain, norm_shift, partner_bit):
    count, side, chans = (latents.shape[0], latents.shape[1], latents.shape[3])
    shard_total = lax.axis_size("fsdp")
    inv_batch = 1.0 / (count * shard_total)
    gain = norm_gain[0]
    normed, scale_inv, pre_act = norm_forward(latents, gain, norm_shift[0], GROUPS)
    activation = jax.nn.silu(pre_act).astype(jnp.bfloat16).reshape(count, side, side, chans)
    patches = make_patches(activation)
    cot_rows = cotangent.reshape(count * side * side, chans)
    weight_rows = conv_weight[0]
    output = jnp.dot(
        patches,
        lax.all_gather(weight_rows, "fsdp", axis=0, tiled=True),
        preferred_element_type=jnp.float32,
    )
    patch_grad = lax.dot_general(
        cot_rows,
        lax.all_gather(weight_rows, "fsdp", axis=0, tiled=True),
        (((1,), (1,)), ((), ())),
        preferred_element_type=jnp.float32,
    )
    block_out = output.astype(jnp.bfloat16).reshape(count, side, side, chans)
    act_grad = fold_patches(patch_grad, count, side, chans)
    input_grad, norm_term = backward_rest(
        act_grad, normed, scale_inv, pre_act, gain, GROUPS, inv_batch
    )
    weight_term = (
        lax.dot_general(
            patches, cot_rows, (((0,), (0,)), ((), ())), preferred_element_type=jnp.float32
        )
        * inv_batch
    )
    shard_rows = weight_rows.shape[0]
    term_pieces = weight_term.reshape(shard_total, shard_rows, chans)
    received = lax.all_to_all(
        term_pieces.astype(jnp.bfloat16), "fsdp", split_axis=0, concat_axis=0, tiled=True
    ).astype(term_pieces.dtype)
    weight_shard = jnp.sum(received, axis=0)
    bit_count = lax.axis_size("rep").bit_length() - 1
    shard_bit = lax.dynamic_index_in_dim(partner_bit, lax.axis_index("fsdp"), 0, keepdims=False)
    norm_bit = partner_bit[0]
    paired_norm = norm_term
    for bit_index in range(bit_count):
        other_norm = partner(norm_term, "rep", bit_index)
        paired_norm = jnp.where(norm_bit == bit_index, 0.5 * (norm_term + other_norm), paired_norm)
    norm_avg = lax.psum(paired_norm, "fsdp")
    weight_avg = weight_shard
    for bit_index in range(bit_count):
        other_weight = partner(weight_shard.astype(jnp.bfloat16), "rep", bit_index).astype(
            weight_shard.dtype
        )
        weight_avg = jnp.where(
            shard_bit == bit_index, 0.5 * (weight_shard + other_weight), weight_avg
        )
    return (block_out, input_grad, weight_avg[None], norm_avg[None])


CORE, ACROSS, ALONG = 1, 2, 4
VMEM_LIMIT = 12 * 1024 * 1024
F32, BF16 = jnp.float32, jnp.bfloat16


def swap(value, axis, mask):
    pairs = [(source, source ^ mask) for source in range(lax.axis_size(axis))]
    return lax.ppermute(value, axis, pairs)


def call(kernel, outs, args, scratch=(), order=(), copies_out=False):
    vmem = pl.BlockSpec(memory_space=pltpu.VMEM)
    smem = pl.BlockSpec(memory_space=pltpu.SMEM)
    untouched = pl.BlockSpec(memory_space=pl.ANY)

    def body(*refs):
        kernel(*refs[: len(args)], *refs[len(args) + len(order) :])

    return pl.pallas_call(
        body,
        out_shape=tuple(outs),
        in_specs=[
            smem if a.dtype == jnp.int32 else vmem
            for a in args
        ]
        + [untouched] * len(order),
        out_specs=tuple(untouched if copies_out else vmem for _ in outs),
        scratch_shapes=list(scratch),
        compiler_params=pltpu.CompilerParams(vmem_limit_bytes=VMEM_LIMIT),
    )(*args, *order)


def hold(values, order):
    untouched = pl.BlockSpec(memory_space=pl.ANY)
    return pl.pallas_call(
        lambda *refs: None,
        out_shape=tuple(shaped(value.shape, value.dtype) for value in values),
        in_specs=[untouched] * (len(values) + len(order)),
        out_specs=tuple(untouched for _ in values),
        input_output_aliases={index: index for index in range(len(values))},
        compiler_params=pltpu.CompilerParams(vmem_limit_bytes=1024 * 1024),
    )(*values, *order)


def shaped(shape, dtype):
    return jax.ShapeDtypeStruct(shape, dtype)


def matmul(left, right):
    return jnp.dot(left, right, preferred_element_type=F32)


def group_matrix(chans, groups, transpose):
    width = chans // groups
    shape = (128, chans) if transpose else (chans, 128)
    chan = lax.broadcasted_iota(jnp.int32, shape, 1 if transpose else 0)
    low = lax.broadcasted_iota(jnp.int32, shape, 0 if transpose else 1) * width
    return ((chan >= low) & (chan < low + width)).astype(F32)


def group_mean(columns, total, groups):
    chans = columns.shape[1]
    exact = dict(precision=lax.Precision.HIGHEST, preferred_element_type=F32)
    sums = jnp.dot(columns, group_matrix(chans, groups, False), **exact)
    return jnp.dot(sums, group_matrix(chans, groups, True), **exact) * (1.0 / total)


def col_sums(*values):
    rows = [jnp.sum(value, axis=0, keepdims=True) for value in values]
    fill = jnp.zeros((8 - len(rows), rows[0].shape[1]), F32)
    return jnp.concatenate(rows + [fill], axis=0)


def norm_kernel(groups, latent, params, act, stats):
    gain, shift = params[0:1], params[1:2]
    values = latent[...].astype(F32)
    total = values.shape[0] * values.shape[1] // groups
    center = group_mean(col_sums(values), total, groups)[0:1]
    moved = values - center
    spread = group_mean(col_sums(moved * moved), total, groups)[0:1]
    scale_inv = lax.rsqrt(spread + 1e-05)
    pre = moved * scale_inv * gain + shift
    act[...] = (pre / (1.0 + jnp.exp(-pre))).astype(BF16)
    stats[0:1] = center
    stats[1:2] = scale_inv


def tap_matrix(tap, side, transpose):
    shape = (side * side, side * side)
    here = lax.broadcasted_iota(jnp.int32, shape, 1 if transpose else 0)
    there = lax.broadcasted_iota(jnp.int32, shape, 0 if transpose else 1)
    row_off = lax.div(tap, 3)
    col_off = tap - 3 * row_off
    bits = side.bit_length() - 1
    rows = lax.shift_right_logical(there, bits) - lax.shift_right_logical(here, bits)
    cols = (there & (side - 1)) - (here & (side - 1))
    hit = (rows == row_off - 1) & (cols == col_off - 1)
    return hit.astype(F32).astype(BF16)


def prepare_kernel(side, taps, info, own, other, wide, turned, gather, scatter):
    rows, chans = own.shape
    area = side * side
    wide[...] = jnp.zeros_like(wide)
    wide[pl.ds(pl.multiple_of(info[1], 16), rows), :] = own[...]
    wide[pl.ds(pl.multiple_of(info[2], 16), rows), :] = other[...]
    for tap in range(taps):
        part = slice(tap * chans, (tap + 1) * chans)
        turned[part, :] = wide[part, :].T
        gather[tap * area : (tap + 1) * area, :] = tap_matrix(info[0] + tap, side, False)
        scatter[tap * area : (tap + 1) * area, :] = tap_matrix(info[0] + tap, side, True)


def move_into(target, index, taps, matrices, value):
    area, width = value.shape
    moved = matmul(matrices, value).astype(BF16)
    for tap in range(taps):
        target[index * area : (index + 1) * area, tap * width : (tap + 1) * width] = moved[
            tap * area : (tap + 1) * area
        ]


def split_latents(value, refs):
    area = refs[0].shape[0]
    for index, ref in enumerate(refs):
        ref[...] = value[index * area : (index + 1) * area].astype(ref.dtype)


def grad_kernel(taps, scatter, turned, c0, c1, c2, moved, g0, g1, g2):
    for index, ref in enumerate((c0, c1, c2)):
        move_into(moved, index, taps, scatter[...], ref[...])
    split_latents(matmul(moved[...], turned[...]), (g0, g1, g2))


def move_kernel(taps, scatter, top, bottom, moved):
    move_into(moved, 0, taps, scatter[...], jnp.concatenate([top[...], bottom[...]], axis=0))


def weight_kernel(taps, moved, a0, a1, a2, part, across):
    area, chans = a0.shape
    for index, ref in enumerate((a0, a1, a2)):
        across[:, index * area : (index + 1) * area] = ref[...].T
    for tap in range(taps):
        block = slice(tap * chans, (tap + 1) * chans)
        part[block, :] = matmul(across[...], moved[:, block])


def out_kernel(taps, gather, wide, a0, a1, a2, top, bottom, y0, y1, y2, y3, moved):
    last = jnp.concatenate([top[...], bottom[...]], axis=0)
    for index, value in enumerate((a0[...], a1[...], a2[...], last)):
        move_into(moved, index, taps, gather[...], value)
    split_latents(matmul(moved[...], wide[...]), (y0, y1, y2, y3))


def turn_twice(top, bottom, across):
    chans, half = top.shape[1], top.shape[0]
    for start in (0, chans):
        across[start : start + chans, :half] = top[...].T
        across[start : start + chans, half:] = bottom[...].T


def window_terms(start, rows, chans, across, moved, part):
    tap = lax.div(start, chans)
    offset = start - tap * chans
    picked = across[pl.ds(pl.multiple_of(offset, 16), rows), :]
    row = lax.broadcasted_iota(jnp.int32, picked.shape, 0)
    zero = jnp.zeros_like(picked)
    in_first = row < chans - offset
    left = jnp.concatenate(
        [jnp.where(in_first, picked, zero), jnp.where(in_first, zero, picked)], axis=1
    )
    right = jnp.concatenate(
        [moved[:, pl.ds(pl.multiple_of((tap + step) * chans, 128), chans)] for step in range(2)],
        axis=0,
    )
    return part[pl.ds(pl.multiple_of(start, 16), rows), :] + matmul(left, right)


def finish_kernel(factor, info, top, bottom, moved, part, send, across):
    turn_twice(top, bottom, across)
    terms = window_terms(info[2], send.shape[0], top.shape[1], across, moved, part)
    send[...] = (terms * factor).astype(BF16)


def keep_kernel(factor, info, turned, top, bottom, moved, part, keep, g3, across):
    turn_twice(top, bottom, across)
    keep[...] = window_terms(info[1], keep.shape[0], top.shape[1], across, moved, part) * factor
    g3[...] = matmul(moved[...], turned[...]).astype(BF16)


def join_kernel(keep, got, narrow):
    narrow[...] = (keep[...] + got[...].astype(F32)).astype(BF16)


def pair_kernel(chunks, bit, own, pair1, pair2, y0, y1, y2, y3, mean, out, made, done, leave):
    size = own.shape[0] // chunks
    done[...] = (y0[...] + sum(ref[...].astype(F32) for ref in (y1, y2, y3))).astype(BF16)
    stores = [pltpu.make_async_copy(done, out, leave.at[chunks])]
    stores[0].start()
    for index in range(chunks):
        rows = pl.ds(index * size, size)

        @pl.when(bit[0] == 0)
        def _():
            made[rows, :] = 0.5 * (own[rows, :].astype(F32) + pair1[rows, :].astype(F32))

        @pl.when(bit[0] != 0)
        def _():
            made[rows, :] = 0.5 * (own[rows, :].astype(F32) + pair2[rows, :].astype(F32))

        stores.append(pltpu.make_async_copy(made.at[rows], mean.at[rows], leave.at[index]))
        stores[-1].start()
    for store in stores:
        store.wait()


def back_kernel(groups, factor, latent, stats, params, g0, g1, g2, g3, grad, terms):
    gain, shift = params[0:1], params[1:2]
    values = latent[...].astype(F32)
    total = values.shape[0] * values.shape[1] // groups
    scale_inv = stats[1:2]
    normed = (values - stats[0:1]) * scale_inv
    pre = normed * gain + shift
    act_grad = g0[...] + sum(ref[...].astype(F32) for ref in (g1, g2, g3))
    sigma = 1.0 / (1.0 + jnp.exp(-pre))
    pre_grad = act_grad * sigma * (1.0 + pre * (1.0 - sigma))
    sums = col_sums(pre_grad * normed, pre_grad)
    terms[...] = sums[0:2] * factor
    means = group_mean(sums * gain, total, groups)
    grad[...] = (scale_inv * (pre_grad * gain - means[1:2] - normed * means[0:1])).astype(BF16)


def shards_plane(latents, cotangent, conv_weight, norm_gain, norm_shift, partner_bit):
    side, chans = latents.shape[1], latents.shape[3]
    area = side * side
    shard_total = lax.axis_size("fsdp")
    inv_batch = 1.0 / shard_total
    place = lax.axis_index("fsdp")
    weight = conv_weight[0]
    rows = weight.shape[0]
    starts = [2 * rows * chip for chip in range(shard_total // 2)]
    taps = max((start % chans + 2 * rows + chans - 1) // chans for start in starts)
    start = 2 * rows * (place // 2)
    first = jnp.minimum(start // chans, 9 - taps)
    offset = start - first * chans
    core = place % 2
    own_start, other_start = offset + rows * core, offset + rows * (1 - core)
    info = jnp.stack([first, own_start, other_start]).astype(jnp.int32)

    def columns(count, dtype=BF16):
        return shaped((count * area, taps * chans), dtype)

    plane, plane_b = shaped((area, chans), F32), shaped((area, chans), BF16)
    window = (taps * chans, chans)

    latent = latents.reshape(area, chans)
    cot0 = cotangent.reshape(area, chans)
    params = jnp.concatenate([norm_gain, norm_shift])
    other_weight = swap(weight, "fsdp", CORE)
    cot1 = swap(cot0, "fsdp", ACROSS)
    cot2 = swap(cot0, "fsdp", ALONG)
    act0, stats = call(
        functools.partial(norm_kernel, GROUPS),
        [plane_b, shaped((2, chans), F32)],
        [latent, params],
    )
    act2 = swap(act0, "fsdp", ALONG)
    act1 = swap(act0, "fsdp", ACROSS)
    wide, turned, gather, scatter = call(
        functools.partial(prepare_kernel, side, taps),
        [shaped(window, BF16)] * 2 + [shaped((taps * area, area), BF16)] * 2,
        [info, weight, other_weight],
        order=[stats],
    )
    cot1, cot2 = hold([cot1, cot2], [scatter])
    moved, grad0, grad1, grad2 = call(
        functools.partial(grad_kernel, taps),
        [columns(3), plane, plane_b, plane_b],
        [scatter, turned, cot0, cot1, cot2],
    )
    half = area // 2
    cot3 = [swap(cot2[:half], "fsdp", ACROSS), swap(cot1[half:], "fsdp", ALONG)]
    (moved3,) = call(functools.partial(move_kernel, taps), [columns(1)], [scatter, *cot3], order=[grad0])
    act2, act1 = hold([act2, act1], [moved3])
    act3 = [swap(act2[:half], "fsdp", ACROSS), swap(act1[half:], "fsdp", ALONG)]
    (part,) = call(
        functools.partial(weight_kernel, taps),
        [shaped(window, F32)],
        [moved, act0, act1, act2],
        [pltpu.VMEM((chans, 3 * area), BF16)],
    )
    (send,) = call(
        functools.partial(finish_kernel, inv_batch),
        [shaped((rows, chans), BF16)],
        [info, *act3, moved3, part],
        [pltpu.VMEM((2 * chans, area), BF16)],
    )
    got = swap(send, "fsdp", CORE)
    keep, grad3 = call(
        functools.partial(keep_kernel, inv_batch),
        [shaped((rows, chans), F32), plane_b],
        [info, turned, *act3, moved3, part],
        [pltpu.VMEM((2 * chans, area), BF16)],
    )
    (narrow,) = call(join_kernel, [shaped((rows, chans), BF16)], [keep, got])
    pair1 = swap(narrow, "rep", 1)
    pair2 = swap(narrow, "rep", 2)

    masks = (ACROSS, ALONG, ACROSS | ALONG)
    grads = hold([grad1, grad2, grad3], [narrow])
    grads = [swap(value, "fsdp", mask) for value, mask in zip(grads, masks)]
    out0, out1, out2, out3 = call(
        functools.partial(out_kernel, taps),
        [plane, plane_b, plane_b, plane_b],
        [gather, wide, act0, act1, act2, *act3],
        [pltpu.VMEM((4 * area, taps * chans), BF16)],
        order=[narrow],
    )
    out1, out2 = hold([out1, out2], [narrow])
    out1, out2 = swap(out1, "fsdp", ACROSS), swap(out2, "fsdp", ALONG)

    input_grad, terms = call(
        functools.partial(back_kernel, GROUPS, inv_batch),
        [plane_b, shaped((2, chans), F32)],
        [latent, stats, params, grad0, *grads],
        order=[out3],
    )
    (last,) = hold([out3], [terms])
    last = swap(last, "fsdp", ACROSS | ALONG)
    for mask in (ACROSS, ALONG):
        terms = terms + swap(terms, "fsdp", mask)
    (terms,) = hold([terms], [out1, out2])
    other = jnp.where(partner_bit[0] == 0, swap(terms, "rep", 1), swap(terms, "rep", 2))
    (terms,) = hold([0.5 * (terms + other)], [pair1, pair2, last])
    norm_avg = terms + swap(terms, "fsdp", CORE)
    shard_bit = lax.dynamic_slice_in_dim(partner_bit, place, 1)
    weight_avg, block_out = call(
        functools.partial(pair_kernel, 5),
        [shaped((rows, chans), F32), plane_b],
        [shard_bit, narrow, pair1, pair2, out0, out1, out2, last],
        [
            pltpu.VMEM((rows, chans), F32),
            pltpu.VMEM((area, chans), BF16),
            pltpu.SemaphoreType.DMA((6,)),
        ],
        copies_out=True,
    )
    shape = (1, side, side, chans)
    return (block_out.reshape(shape), input_grad.reshape(shape), weight_avg[None], norm_avg[None])


def solution(mesh):
    in_specs = (
        P(("rep", "fsdp"), None, None, None),
        P(("rep", "fsdp"), None, None, None),
        P("rep", "fsdp", None),
        P("rep", None),
        P("rep", None),
        P(),
    )
    out_specs = (
        P(("rep", "fsdp"), None, None, None),
        P(("rep", "fsdp"), None, None, None),
        P("rep", "fsdp", None),
        P("rep", None, None),
    )
    planes = mesh.shape["fsdp"] == 8 and mesh.shape["rep"] == 4
    shards = shards_plane if planes else shards_general
    return jax.shard_map(shards, mesh=mesh, in_specs=in_specs, out_specs=out_specs, check_vma=False)
```

```python
import functools

import jax
import jax.numpy as jnp
from jax import lax
from jax.experimental import pallas as pl
from jax.experimental.pallas import tpu as pltpu
from jax.sharding import PartitionSpec as P

GROUPS = 32


def partner(value, axis, stride):
    mask = 2**stride
    pairs = [(source, source ^ mask) for source in range(lax.axis_size(axis))]
    return lax.ppermute(value, axis, pairs)


def norm_forward(values_in, gain, shift, groups):
    count, side, chans = (values_in.shape[0], values_in.shape[1], values_in.shape[3])
    values = values_in.astype(jnp.float32).reshape(count, side * side, groups, chans // groups)
    center = jnp.mean(values, axis=(1, 3), keepdims=True)
    spread = jnp.mean(jnp.square(values - center), axis=(1, 3), keepdims=True)
    scale_inv = lax.rsqrt(spread + 1e-05)
    normed = (values - center) * scale_inv
    pre_act = normed * gain.reshape(groups, -1) + shift.reshape(groups, -1)
    return (normed, scale_inv, pre_act)


def make_patches(activation):
    count, side, chans = (activation.shape[0], activation.shape[1], activation.shape[3])
    padded = jnp.pad(activation, ((0, 0), (1, 1), (1, 1), (0, 0)))
    pieces = [
        padded[:, row_off : row_off + side, col_off : col_off + side, :]
        for row_off in range(3)
        for col_off in range(3)
    ]
    return jnp.concatenate(pieces, axis=-1).reshape(count * side * side, 9 * chans)


def fold_patches(patch_grad, count, side, chans):
    grads = patch_grad.reshape(count, side, side, 9, chans)
    total = jnp.zeros((count, side + 2, side + 2, chans), jnp.float32)
    for row_off in range(3):
        for col_off in range(3):
            tap = grads[:, :, :, row_off * 3 + col_off, :]
            total = total + jnp.pad(
                tap, ((0, 0), (row_off, 2 - row_off), (col_off, 2 - col_off), (0, 0))
            )
    return total[:, 1:-1, 1:-1, :]


def backward_rest(act_grad, normed, scale_inv, pre_act, gain, groups, inv_batch):
    count, side, chans = (act_grad.shape[0], act_grad.shape[1], act_grad.shape[3])
    act_grad = act_grad.reshape(count, side * side, groups, chans // groups)
    sigma = jax.nn.sigmoid(pre_act)
    pre_grad = act_grad * sigma * (1.0 + pre_act * (1.0 - sigma))
    gain_grad = jnp.sum(pre_grad * normed, axis=(0, 1)).reshape(-1) * inv_batch
    shift_grad = jnp.sum(pre_grad, axis=(0, 1)).reshape(-1) * inv_batch
    normed_grad = pre_grad * gain.reshape(groups, -1)
    first = jnp.mean(normed_grad, axis=(1, 3), keepdims=True)
    second = jnp.mean(normed_grad * normed, axis=(1, 3), keepdims=True)
    input_grad = scale_inv * (normed_grad - first - normed * second)
    return (
        input_grad.reshape(count, side, side, chans).astype(jnp.bfloat16),
        jnp.stack([gain_grad, shift_grad]),
    )


def shards_general(latents, cotangent, conv_weight, norm_gain, norm_shift, partner_bit):
    count, side, chans = (latents.shape[0], latents.shape[1], latents.shape[3])
    shard_total = lax.axis_size("fsdp")
    inv_batch = 1.0 / (count * shard_total)
    gain = norm_gain[0]
    normed, scale_inv, pre_act = norm_forward(latents, gain, norm_shift[0], GROUPS)
    activation = jax.nn.silu(pre_act).astype(jnp.bfloat16).reshape(count, side, side, chans)
    patches = make_patches(activation)
    cot_rows = cotangent.reshape(count * side * side, chans)
    weight_rows = conv_weight[0]
    output = jnp.dot(
        patches,
        lax.all_gather(weight_rows, "fsdp", axis=0, tiled=True),
        preferred_element_type=jnp.float32,
    )
    patch_grad = lax.dot_general(
        cot_rows,
        lax.all_gather(weight_rows, "fsdp", axis=0, tiled=True),
        (((1,), (1,)), ((), ())),
        preferred_element_type=jnp.float32,
    )
    block_out = output.astype(jnp.bfloat16).reshape(count, side, side, chans)
    act_grad = fold_patches(patch_grad, count, side, chans)
    input_grad, norm_term = backward_rest(
        act_grad, normed, scale_inv, pre_act, gain, GROUPS, inv_batch
    )
    weight_term = (
        lax.dot_general(
            patches, cot_rows, (((0,), (0,)), ((), ())), preferred_element_type=jnp.float32
        )
        * inv_batch
    )
    shard_rows = weight_rows.shape[0]
    term_pieces = weight_term.reshape(shard_total, shard_rows, chans)
    received = lax.all_to_all(
        term_pieces.astype(jnp.bfloat16), "fsdp", split_axis=0, concat_axis=0, tiled=True
    ).astype(term_pieces.dtype)
    weight_shard = jnp.sum(received, axis=0)
    bit_count = lax.axis_size("rep").bit_length() - 1
    shard_bit = lax.dynamic_index_in_dim(partner_bit, lax.axis_index("fsdp"), 0, keepdims=False)
    norm_bit = partner_bit[0]
    paired_norm = norm_term
    for bit_index in range(bit_count):
        other_norm = partner(norm_term, "rep", bit_index)
        paired_norm = jnp.where(norm_bit == bit_index, 0.5 * (norm_term + other_norm), paired_norm)
    norm_avg = lax.psum(paired_norm, "fsdp")
    weight_avg = weight_shard
    for bit_index in range(bit_count):
        other_weight = partner(weight_shard.astype(jnp.bfloat16), "rep", bit_index).astype(
            weight_shard.dtype
        )
        weight_avg = jnp.where(
            shard_bit == bit_index, 0.5 * (weight_shard + other_weight), weight_avg
        )
    return (block_out, input_grad, weight_avg[None], norm_avg[None])


CORE, ACROSS, ALONG = 1, 2, 4
VMEM_LIMIT = 12 * 1024 * 1024
F32, BF16 = jnp.float32, jnp.bfloat16


def swap(value, axis, mask):
    pairs = [(source, source ^ mask) for source in range(lax.axis_size(axis))]
    return lax.ppermute(value, axis, pairs)


def call(kernel, outs, args, scratch=(), order=(), copies_out=False):
    vmem = pl.BlockSpec(memory_space=pltpu.VMEM)
    smem = pl.BlockSpec(memory_space=pltpu.SMEM)
    untouched = pl.BlockSpec(memory_space=pl.ANY)

    def body(*refs):
        kernel(*refs[: len(args)], *refs[len(args) + len(order) :])

    return pl.pallas_call(
        body,
        out_shape=tuple(outs),
        in_specs=[
            smem if a.dtype == jnp.int32 else vmem
            for a in args
        ]
        + [untouched] * len(order),
        out_specs=tuple(untouched if copies_out else vmem for _ in outs),
        scratch_shapes=list(scratch),
        compiler_params=pltpu.CompilerParams(vmem_limit_bytes=VMEM_LIMIT),
    )(*args, *order)


def hold(values, order):
    untouched = pl.BlockSpec(memory_space=pl.ANY)
    return pl.pallas_call(
        lambda *refs: None,
        out_shape=tuple(shaped(value.shape, value.dtype) for value in values),
        in_specs=[untouched] * (len(values) + len(order)),
        out_specs=tuple(untouched for _ in values),
        input_output_aliases={index: index for index in range(len(values))},
        compiler_params=pltpu.CompilerParams(vmem_limit_bytes=1024 * 1024),
    )(*values, *order)


def shaped(shape, dtype):
    return jax.ShapeDtypeStruct(shape, dtype)


def matmul(left, right):
    return jnp.dot(left, right, preferred_element_type=F32)


def group_matrix(chans, groups, transpose):
    width = chans // groups
    shape = (128, chans) if transpose else (chans, 128)
    chan = lax.broadcasted_iota(jnp.int32, shape, 1 if transpose else 0)
    low = lax.broadcasted_iota(jnp.int32, shape, 0 if transpose else 1) * width
    return ((chan >= low) & (chan < low + width)).astype(F32)


def group_mean(columns, total, groups):
    chans = columns.shape[1]
    exact = dict(precision=lax.Precision.HIGHEST, preferred_element_type=F32)
    sums = jnp.dot(columns, group_matrix(chans, groups, False), **exact)
    return jnp.dot(sums, group_matrix(chans, groups, True), **exact) * (1.0 / total)


def col_sums(*values):
    rows = [jnp.sum(value, axis=0, keepdims=True) for value in values]
    fill = jnp.zeros((8 - len(rows), rows[0].shape[1]), F32)
    return jnp.concatenate(rows + [fill], axis=0)


def norm_kernel(groups, latent, params, act, stats):
    gain, shift = params[0:1], params[1:2]
    values = latent[...].astype(F32)
    total = values.shape[0] * values.shape[1] // groups
    center = group_mean(col_sums(values), total, groups)[0:1]
    moved = values - center
    spread = group_mean(col_sums(moved * moved), total, groups)[0:1]
    scale_inv = lax.rsqrt(spread + 1e-05)
    pre = moved * scale_inv * gain + shift
    act[...] = (pre / (1.0 + jnp.exp(-pre))).astype(BF16)
    stats[0:1] = center
    stats[1:2] = scale_inv


def tap_matrix(tap, side, transpose):
    shape = (side * side, side * side)
    here = lax.broadcasted_iota(jnp.int32, shape, 1 if transpose else 0)
    there = lax.broadcasted_iota(jnp.int32, shape, 0 if transpose else 1)
    row_off = lax.div(tap, 3)
    col_off = tap - 3 * row_off
    bits = side.bit_length() - 1
    rows = lax.shift_right_logical(there, bits) - lax.shift_right_logical(here, bits)
    cols = (there & (side - 1)) - (here & (side - 1))
    hit = (rows == row_off - 1) & (cols == col_off - 1)
    return hit.astype(F32).astype(BF16)


def prepare_kernel(side, taps, info, own, other, wide, turned, gather, scatter):
    rows, chans = own.shape
    area = side * side
    wide[...] = jnp.zeros_like(wide)
    wide[pl.ds(pl.multiple_of(info[1], 16), rows), :] = own[...]
    wide[pl.ds(pl.multiple_of(info[2], 16), rows), :] = other[...]
    for tap in range(taps):
        part = slice(tap * chans, (tap + 1) * chans)
        turned[part, :] = wide[part, :].T
        gather[tap * area : (tap + 1) * area, :] = tap_matrix(info[0] + tap, side, False)
        scatter[tap * area : (tap + 1) * area, :] = tap_matrix(info[0] + tap, side, True)


def move_into(target, index, taps, matrices, value):
    area, width = value.shape
    moved = matmul(matrices, value).astype(BF16)
    for tap in range(taps):
        target[index * area : (index + 1) * area, tap * width : (tap + 1) * width] = moved[
            tap * area : (tap + 1) * area
        ]


def split_latents(value, refs):
    area = refs[0].shape[0]
    for index, ref in enumerate(refs):
        ref[...] = value[index * area : (index + 1) * area].astype(ref.dtype)


def grad_kernel(taps, scatter, turned, c0, c1, c2, moved, g0, g1, g2):
    for index, ref in enumerate((c0, c1, c2)):
        move_into(moved, index, taps, scatter[...], ref[...])
    split_latents(matmul(moved[...], turned[...]), (g0, g1, g2))


def move_kernel(taps, scatter, top, bottom, moved):
    move_into(moved, 0, taps, scatter[...], jnp.concatenate([top[...], bottom[...]], axis=0))


def weight_kernel(taps, moved, a0, a1, a2, part, across):
    area, chans = a0.shape
    for index, ref in enumerate((a0, a1, a2)):
        across[:, index * area : (index + 1) * area] = ref[...].T
    for tap in range(taps):
        block = slice(tap * chans, (tap + 1) * chans)
        part[block, :] = matmul(across[...], moved[:, block])


def out_kernel(taps, gather, wide, a0, a1, a2, top, bottom, y0, y1, y2, y3, moved):
    last = jnp.concatenate([top[...], bottom[...]], axis=0)
    for index, value in enumerate((a0[...], a1[...], a2[...], last)):
        move_into(moved, index, taps, gather[...], value)
    split_latents(matmul(moved[...], wide[...]), (y0, y1, y2, y3))


def turn_twice(top, bottom, across):
    chans, half = top.shape[1], top.shape[0]
    for start in (0, chans):
        across[start : start + chans, :half] = top[...].T
        across[start : start + chans, half:] = bottom[...].T


def window_terms(start, rows, chans, across, moved, part):
    tap = lax.div(start, chans)
    offset = start - tap * chans
    picked = across[pl.ds(pl.multiple_of(offset, 16), rows), :]
    row = lax.broadcasted_iota(jnp.int32, picked.shape, 0)
    zero = jnp.zeros_like(picked)
    in_first = row < chans - offset
    left = jnp.concatenate(
        [jnp.where(in_first, picked, zero), jnp.where(in_first, zero, picked)], axis=1
    )
    right = jnp.concatenate(
        [moved[:, pl.ds(pl.multiple_of((tap + step) * chans, 128), chans)] for step in range(2)],
        axis=0,
    )
    return part[pl.ds(pl.multiple_of(start, 16), rows), :] + matmul(left, right)


def finish_kernel(factor, info, top, bottom, moved, part, send, across):
    turn_twice(top, bottom, across)
    terms = window_terms(info[2], send.shape[0], top.shape[1], across, moved, part)
    send[...] = (terms * factor).astype(BF16)


def keep_kernel(factor, info, turned, top, bottom, moved, part, keep, g3, across):
    turn_twice(top, bottom, across)
    keep[...] = window_terms(info[1], keep.shape[0], top.shape[1], across, moved, part) * factor
    g3[...] = matmul(moved[...], turned[...]).astype(BF16)


def join_kernel(keep, got, narrow):
    narrow[...] = (keep[...] + got[...].astype(F32)).astype(BF16)


def pair_kernel(chunks, bit, own, pair1, pair2, y0, y1, y2, y3, mean, out, made, done, leave):
    size = own.shape[0] // chunks
    done[...] = (y0[...] + sum(ref[...].astype(F32) for ref in (y1, y2, y3))).astype(BF16)
    stores = [pltpu.make_async_copy(done, out, leave.at[chunks])]
    stores[0].start()
    for index in range(chunks):
        rows = pl.ds(index * size, size)

        @pl.when(bit[0] == 0)
        def _():
            made[rows, :] = 0.5 * (own[rows, :].astype(F32) + pair1[rows, :].astype(F32))

        @pl.when(bit[0] != 0)
        def _():
            made[rows, :] = 0.5 * (own[rows, :].astype(F32) + pair2[rows, :].astype(F32))

        stores.append(pltpu.make_async_copy(made.at[rows], mean.at[rows], leave.at[index]))
        stores[-1].start()
    for store in stores:
        store.wait()


def back_kernel(groups, factor, latent, stats, params, g0, g1, g2, g3, grad, terms):
    gain, shift = params[0:1], params[1:2]
    values = latent[...].astype(F32)
    total = values.shape[0] * values.shape[1] // groups
    scale_inv = stats[1:2]
    normed = (values - stats[0:1]) * scale_inv
    pre = normed * gain + shift
    act_grad = g0[...] + sum(ref[...].astype(F32) for ref in (g1, g2, g3))
    sigma = 1.0 / (1.0 + jnp.exp(-pre))
    pre_grad = act_grad * sigma * (1.0 + pre * (1.0 - sigma))
    sums = col_sums(pre_grad * normed, pre_grad)
    terms[...] = sums[0:2] * factor
    means = group_mean(sums * gain, total, groups)
    grad[...] = (scale_inv * (pre_grad * gain - means[1:2] - normed * means[0:1])).astype(BF16)


def shards_plane(latents, cotangent, conv_weight, norm_gain, norm_shift, partner_bit):
    side, chans = latents.shape[1], latents.shape[3]
    area = side * side
    shard_total = lax.axis_size("fsdp")
    inv_batch = 1.0 / shard_total
    place = lax.axis_index("fsdp")
    weight = conv_weight[0]
    rows = weight.shape[0]
    starts = [2 * rows * chip for chip in range(shard_total // 2)]
    taps = max((start % chans + 2 * rows + chans - 1) // chans for start in starts)
    start = 2 * rows * (place // 2)
    first = jnp.minimum(start // chans, 9 - taps)
    offset = start - first * chans
    core = place % 2
    own_start, other_start = offset + rows * core, offset + rows * (1 - core)
    info = jnp.stack([first, own_start, other_start]).astype(jnp.int32)

    def columns(count, dtype=BF16):
        return shaped((count * area, taps * chans), dtype)

    plane, plane_b = shaped((area, chans), F32), shaped((area, chans), BF16)
    window = (taps * chans, chans)

    latent = latents.reshape(area, chans)
    cot0 = cotangent.reshape(area, chans)
    params = jnp.concatenate([norm_gain, norm_shift])
    other_weight = swap(weight, "fsdp", CORE)
    cot1 = swap(cot0, "fsdp", ACROSS)
    cot2 = swap(cot0, "fsdp", ALONG)
    act0, stats = call(
        functools.partial(norm_kernel, GROUPS),
        [plane_b, shaped((2, chans), F32)],
        [latent, params],
    )
    act2 = swap(act0, "fsdp", ALONG)
    act1 = swap(act0, "fsdp", ACROSS)
    wide, turned, gather, scatter = call(
        functools.partial(prepare_kernel, side, taps),
        [shaped(window, BF16)] * 2 + [shaped((taps * area, area), BF16)] * 2,
        [info, weight, other_weight],
        order=[stats],
    )
    cot1, cot2 = hold([cot1, cot2], [scatter])
    moved, grad0, grad1, grad2 = call(
        functools.partial(grad_kernel, taps),
        [columns(3), plane, plane_b, plane_b],
        [scatter, turned, cot0, cot1, cot2],
    )
    half = area // 2
    cot3 = [swap(cot2[:half], "fsdp", ACROSS), swap(cot1[half:], "fsdp", ALONG)]
    (moved3,) = call(functools.partial(move_kernel, taps), [columns(1)], [scatter, *cot3], order=[grad0])
    act2, act1 = hold([act2, act1], [moved3])
    act3 = [swap(act2[:half], "fsdp", ACROSS), swap(act1[half:], "fsdp", ALONG)]
    (part,) = call(
        functools.partial(weight_kernel, taps),
        [shaped(window, F32)],
        [moved, act0, act1, act2],
        [pltpu.VMEM((chans, 3 * area), BF16)],
    )
    (send,) = call(
        functools.partial(finish_kernel, inv_batch),
        [shaped((rows, chans), BF16)],
        [info, *act3, moved3, part],
        [pltpu.VMEM((2 * chans, area), BF16)],
    )
    got = swap(send, "fsdp", CORE)
    keep, grad3 = call(
        functools.partial(keep_kernel, inv_batch),
        [shaped((rows, chans), F32), plane_b],
        [info, turned, *act3, moved3, part],
        [pltpu.VMEM((2 * chans, area), BF16)],
    )
    (narrow,) = call(join_kernel, [shaped((rows, chans), BF16)], [keep, got])
    pair1 = swap(narrow, "rep", 1)
    pair2 = swap(narrow, "rep", 2)

    masks = (ACROSS, ALONG, ACROSS | ALONG)
    grads = hold([grad1, grad2, grad3], [narrow])
    grads = [swap(value, "fsdp", mask) for value, mask in zip(grads, masks)]
    out0, out1, out2, out3 = call(
        functools.partial(out_kernel, taps),
        [plane, plane_b, plane_b, plane_b],
        [gather, wide, act0, act1, act2, *act3],
        [pltpu.VMEM((4 * area, taps * chans), BF16)],
        order=[narrow],
    )
    out1, out2 = hold([out1, out2], [narrow])
    out1, out2 = swap(out1, "fsdp", ACROSS), swap(out2, "fsdp", ALONG)

    input_grad, terms = call(
        functools.partial(back_kernel, GROUPS, inv_batch),
        [plane_b, shaped((2, chans), F32)],
        [latent, stats, params, grad0, *grads],
        order=[out3],
    )
    (last,) = hold([out3], [terms])
    last = swap(last, "fsdp", ACROSS | ALONG)
    for mask in (ACROSS, ALONG):
        terms = terms + swap(terms, "fsdp", mask)
    (terms,) = hold([terms], [out1, out2])
    other = lax.cond(
        partner_bit[0] == 0, lambda x: swap(x, "rep", 1), lambda x: swap(x, "rep", 2), terms
    )
    (terms,) = hold([0.5 * (terms + other)], [pair1, pair2, last])
    norm_avg = terms + swap(terms, "fsdp", CORE)
    shard_bit = lax.dynamic_slice_in_dim(partner_bit, place, 1)
    weight_avg, block_out = call(
        functools.partial(pair_kernel, 5),
        [shaped((rows, chans), F32), plane_b],
        [shard_bit, narrow, pair1, pair2, out0, out1, out2, last],
        [
            pltpu.VMEM((rows, chans), F32),
            pltpu.VMEM((area, chans), BF16),
            pltpu.SemaphoreType.DMA((6,)),
        ],
        copies_out=True,
    )
    shape = (1, side, side, chans)
    return (block_out.reshape(shape), input_grad.reshape(shape), weight_avg[None], norm_avg[None])


def solution(mesh):
    in_specs = (
        P(("rep", "fsdp"), None, None, None),
        P(("rep", "fsdp"), None, None, None),
        P("rep", "fsdp", None),
        P("rep", None),
        P("rep", None),
        P(),
    )
    out_specs = (
        P(("rep", "fsdp"), None, None, None),
        P(("rep", "fsdp"), None, None, None),
        P("rep", "fsdp", None),
        P("rep", None, None),
    )
    planes = mesh.shape["fsdp"] == 8 and mesh.shape["rep"] == 4
    shards = shards_plane if planes else shards_general
    return jax.shard_map(shards, mesh=mesh, in_specs=in_specs, out_specs=out_specs, check_vma=False)
```

```python
import functools

import jax
import jax.numpy as jnp
from jax import lax
from jax.experimental import pallas as pl
from jax.experimental.pallas import tpu as pltpu
from jax.sharding import PartitionSpec as P

GROUPS = 32


def partner(value, axis, stride):
    mask = 2**stride
    pairs = [(source, source ^ mask) for source in range(lax.axis_size(axis))]
    return lax.ppermute(value, axis, pairs)


def norm_forward(values_in, gain, shift, groups):
    count, side, chans = (values_in.shape[0], values_in.shape[1], values_in.shape[3])
    values = values_in.astype(jnp.float32).reshape(count, side * side, groups, chans // groups)
    center = jnp.mean(values, axis=(1, 3), keepdims=True)
    spread = jnp.mean(jnp.square(values - center), axis=(1, 3), keepdims=True)
    scale_inv = lax.rsqrt(spread + 1e-05)
    normed = (values - center) * scale_inv
    pre_act = normed * gain.reshape(groups, -1) + shift.reshape(groups, -1)
    return (normed, scale_inv, pre_act)


def make_patches(activation):
    count, side, chans = (activation.shape[0], activation.shape[1], activation.shape[3])
    padded = jnp.pad(activation, ((0, 0), (1, 1), (1, 1), (0, 0)))
    pieces = [
        padded[:, row_off : row_off + side, col_off : col_off + side, :]
        for row_off in range(3)
        for col_off in range(3)
    ]
    return jnp.concatenate(pieces, axis=-1).reshape(count * side * side, 9 * chans)


def fold_patches(patch_grad, count, side, chans):
    grads = patch_grad.reshape(count, side, side, 9, chans)
    total = jnp.zeros((count, side + 2, side + 2, chans), jnp.float32)
    for row_off in range(3):
        for col_off in range(3):
            tap = grads[:, :, :, row_off * 3 + col_off, :]
            total = total + jnp.pad(
                tap, ((0, 0), (row_off, 2 - row_off), (col_off, 2 - col_off), (0, 0))
            )
    return total[:, 1:-1, 1:-1, :]


def backward_rest(act_grad, normed, scale_inv, pre_act, gain, groups, inv_batch):
    count, side, chans = (act_grad.shape[0], act_grad.shape[1], act_grad.shape[3])
    act_grad = act_grad.reshape(count, side * side, groups, chans // groups)
    sigma = jax.nn.sigmoid(pre_act)
    pre_grad = act_grad * sigma * (1.0 + pre_act * (1.0 - sigma))
    gain_grad = jnp.sum(pre_grad * normed, axis=(0, 1)).reshape(-1) * inv_batch
    shift_grad = jnp.sum(pre_grad, axis=(0, 1)).reshape(-1) * inv_batch
    normed_grad = pre_grad * gain.reshape(groups, -1)
    first = jnp.mean(normed_grad, axis=(1, 3), keepdims=True)
    second = jnp.mean(normed_grad * normed, axis=(1, 3), keepdims=True)
    input_grad = scale_inv * (normed_grad - first - normed * second)
    return (
        input_grad.reshape(count, side, side, chans).astype(jnp.bfloat16),
        jnp.stack([gain_grad, shift_grad]),
    )


def shards_general(latents, cotangent, conv_weight, norm_gain, norm_shift, partner_bit):
    count, side, chans = (latents.shape[0], latents.shape[1], latents.shape[3])
    shard_total = lax.axis_size("fsdp")
    inv_batch = 1.0 / (count * shard_total)
    gain = norm_gain[0]
    normed, scale_inv, pre_act = norm_forward(latents, gain, norm_shift[0], GROUPS)
    activation = jax.nn.silu(pre_act).astype(jnp.bfloat16).reshape(count, side, side, chans)
    patches = make_patches(activation)
    cot_rows = cotangent.reshape(count * side * side, chans)
    weight_rows = conv_weight[0]
    output = jnp.dot(
        patches,
        lax.all_gather(weight_rows, "fsdp", axis=0, tiled=True),
        preferred_element_type=jnp.float32,
    )
    patch_grad = lax.dot_general(
        cot_rows,
        lax.all_gather(weight_rows, "fsdp", axis=0, tiled=True),
        (((1,), (1,)), ((), ())),
        preferred_element_type=jnp.float32,
    )
    block_out = output.astype(jnp.bfloat16).reshape(count, side, side, chans)
    act_grad = fold_patches(patch_grad, count, side, chans)
    input_grad, norm_term = backward_rest(
        act_grad, normed, scale_inv, pre_act, gain, GROUPS, inv_batch
    )
    weight_term = (
        lax.dot_general(
            patches, cot_rows, (((0,), (0,)), ((), ())), preferred_element_type=jnp.float32
        )
        * inv_batch
    )
    shard_rows = weight_rows.shape[0]
    term_pieces = weight_term.reshape(shard_total, shard_rows, chans)
    received = lax.all_to_all(
        term_pieces.astype(jnp.bfloat16), "fsdp", split_axis=0, concat_axis=0, tiled=True
    ).astype(term_pieces.dtype)
    weight_shard = jnp.sum(received, axis=0)
    bit_count = lax.axis_size("rep").bit_length() - 1
    shard_bit = lax.dynamic_index_in_dim(partner_bit, lax.axis_index("fsdp"), 0, keepdims=False)
    norm_bit = partner_bit[0]
    paired_norm = norm_term
    for bit_index in range(bit_count):
        other_norm = partner(norm_term, "rep", bit_index)
        paired_norm = jnp.where(norm_bit == bit_index, 0.5 * (norm_term + other_norm), paired_norm)
    norm_avg = lax.psum(paired_norm, "fsdp")
    weight_avg = weight_shard
    for bit_index in range(bit_count):
        other_weight = partner(weight_shard.astype(jnp.bfloat16), "rep", bit_index).astype(
            weight_shard.dtype
        )
        weight_avg = jnp.where(
            shard_bit == bit_index, 0.5 * (weight_shard + other_weight), weight_avg
        )
    return (block_out, input_grad, weight_avg[None], norm_avg[None])


CORE, ACROSS, ALONG = 1, 2, 4
VMEM_LIMIT = 12 * 1024 * 1024
F32, BF16 = jnp.float32, jnp.bfloat16


def swap(value, axis, mask):
    pairs = [(source, source ^ mask) for source in range(lax.axis_size(axis))]
    return lax.ppermute(value, axis, pairs)


def call(kernel, outs, args, scratch=(), order=(), copies_out=False, outside=()):
    vmem = pl.BlockSpec(memory_space=pltpu.VMEM)
    smem = pl.BlockSpec(memory_space=pltpu.SMEM)
    untouched = pl.BlockSpec(memory_space=pl.ANY)

    def body(*refs):
        kernel(*refs[: len(args)], *refs[len(args) + len(order) :])

    return pl.pallas_call(
        body,
        out_shape=tuple(outs),
        in_specs=[
            untouched if index in outside else smem if a.dtype == jnp.int32 else vmem
            for index, a in enumerate(args)
        ]
        + [untouched] * len(order),
        out_specs=tuple(untouched if copies_out else vmem for _ in outs),
        scratch_shapes=list(scratch),
        compiler_params=pltpu.CompilerParams(vmem_limit_bytes=VMEM_LIMIT),
    )(*args, *order)


def hold(values, order):
    untouched = pl.BlockSpec(memory_space=pl.ANY)
    return pl.pallas_call(
        lambda *refs: None,
        out_shape=tuple(shaped(value.shape, value.dtype) for value in values),
        in_specs=[untouched] * (len(values) + len(order)),
        out_specs=tuple(untouched for _ in values),
        input_output_aliases={index: index for index in range(len(values))},
        compiler_params=pltpu.CompilerParams(vmem_limit_bytes=1024 * 1024),
    )(*values, *order)


def shaped(shape, dtype):
    return jax.ShapeDtypeStruct(shape, dtype)


def matmul(left, right):
    return jnp.dot(left, right, preferred_element_type=F32)


def group_matrix(chans, groups, transpose):
    width = chans // groups
    shape = (128, chans) if transpose else (chans, 128)
    chan = lax.broadcasted_iota(jnp.int32, shape, 1 if transpose else 0)
    low = lax.broadcasted_iota(jnp.int32, shape, 0 if transpose else 1) * width
    return ((chan >= low) & (chan < low + width)).astype(F32)


def group_mean(columns, total, groups):
    chans = columns.shape[1]
    exact = dict(precision=lax.Precision.HIGHEST, preferred_element_type=F32)
    sums = jnp.dot(columns, group_matrix(chans, groups, False), **exact)
    return jnp.dot(sums, group_matrix(chans, groups, True), **exact) * (1.0 / total)


def col_sums(*values):
    rows = [jnp.sum(value, axis=0, keepdims=True) for value in values]
    fill = jnp.zeros((8 - len(rows), rows[0].shape[1]), F32)
    return jnp.concatenate(rows + [fill], axis=0)


def norm_kernel(groups, latent, params, act, stats):
    gain, shift = params[0:1], params[1:2]
    values = latent[...].astype(F32)
    total = values.shape[0] * values.shape[1] // groups
    center = group_mean(col_sums(values), total, groups)[0:1]
    moved = values - center
    spread = group_mean(col_sums(moved * moved), total, groups)[0:1]
    scale_inv = lax.rsqrt(spread + 1e-05)
    pre = moved * scale_inv * gain + shift
    act[...] = (pre / (1.0 + jnp.exp(-pre))).astype(BF16)
    stats[0:1] = center
    stats[1:2] = scale_inv


def tap_matrix(tap, side, transpose):
    shape = (side * side, side * side)
    here = lax.broadcasted_iota(jnp.int32, shape, 1 if transpose else 0)
    there = lax.broadcasted_iota(jnp.int32, shape, 0 if transpose else 1)
    row_off = lax.div(tap, 3)
    col_off = tap - 3 * row_off
    bits = side.bit_length() - 1
    rows = lax.shift_right_logical(there, bits) - lax.shift_right_logical(here, bits)
    cols = (there & (side - 1)) - (here & (side - 1))
    hit = (rows == row_off - 1) & (cols == col_off - 1)
    return hit.astype(F32).astype(BF16)


def prepare_kernel(side, taps, info, own, other, wide, turned, gather, scatter):
    rows, chans = own.shape
    area = side * side
    wide[...] = jnp.zeros_like(wide)
    wide[pl.ds(pl.multiple_of(info[1], 16), rows), :] = own[...]
    wide[pl.ds(pl.multiple_of(info[2], 16), rows), :] = other[...]
    for tap in range(taps):
        part = slice(tap * chans, (tap + 1) * chans)
        turned[part, :] = wide[part, :].T
        gather[tap * area : (tap + 1) * area, :] = tap_matrix(info[0] + tap, side, False)
        scatter[tap * area : (tap + 1) * area, :] = tap_matrix(info[0] + tap, side, True)


def move_into(target, index, taps, matrices, value):
    area, width = value.shape
    moved = matmul(matrices, value).astype(BF16)
    for tap in range(taps):
        target[index * area : (index + 1) * area, tap * width : (tap + 1) * width] = moved[
            tap * area : (tap + 1) * area
        ]


def split_latents(value, refs):
    area = refs[0].shape[0]
    for index, ref in enumerate(refs):
        ref[...] = value[index * area : (index + 1) * area].astype(ref.dtype)


def grad_kernel(taps, scatter, turned, c0, c1, c2, moved, g0, g1, g2):
    for index, ref in enumerate((c0, c1, c2)):
        move_into(moved, index, taps, scatter[...], ref[...])
    split_latents(matmul(moved[...], turned[...]), (g0, g1, g2))


def move_kernel(taps, scatter, top, bottom, moved):
    move_into(moved, 0, taps, scatter[...], jnp.concatenate([top[...], bottom[...]], axis=0))


def weight_kernel(taps, moved, a0, a1, a2, part, across):
    area, chans = a0.shape
    for index, ref in enumerate((a0, a1, a2)):
        across[:, index * area : (index + 1) * area] = ref[...].T
    for tap in range(taps):
        block = slice(tap * chans, (tap + 1) * chans)
        part[block, :] = matmul(across[...], moved[:, block])


def out_kernel(taps, gather, wide, a0, a1, a2, top, bottom, y0, y1, y2, y3, moved):
    last = jnp.concatenate([top[...], bottom[...]], axis=0)
    for index, value in enumerate((a0[...], a1[...], a2[...], last)):
        move_into(moved, index, taps, gather[...], value)
    split_latents(matmul(moved[...], wide[...]), (y0, y1, y2, y3))


def turn_twice(top, bottom, across):
    chans, half = top.shape[1], top.shape[0]
    for start in (0, chans):
        across[start : start + chans, :half] = top[...].T
        across[start : start + chans, half:] = bottom[...].T


def window_terms(start, rows, chans, across, moved, part):
    tap = lax.div(start, chans)
    offset = start - tap * chans
    picked = across[pl.ds(pl.multiple_of(offset, 16), rows), :]
    row = lax.broadcasted_iota(jnp.int32, picked.shape, 0)
    zero = jnp.zeros_like(picked)
    in_first = row < chans - offset
    left = jnp.concatenate(
        [jnp.where(in_first, picked, zero), jnp.where(in_first, zero, picked)], axis=1
    )
    right = jnp.concatenate(
        [moved[:, pl.ds(pl.multiple_of((tap + step) * chans, 128), chans)] for step in range(2)],
        axis=0,
    )
    return part[pl.ds(pl.multiple_of(start, 16), rows), :] + matmul(left, right)


def finish_kernel(factor, info, top, bottom, moved, part, send, across):
    turn_twice(top, bottom, across)
    terms = window_terms(info[2], send.shape[0], top.shape[1], across, moved, part)
    send[...] = (terms * factor).astype(BF16)


def keep_kernel(factor, info, turned, top, bottom, moved, part, keep, g3, across):
    turn_twice(top, bottom, across)
    keep[...] = window_terms(info[1], keep.shape[0], top.shape[1], across, moved, part) * factor
    g3[...] = matmul(moved[...], turned[...]).astype(BF16)


def join_kernel(keep, got, narrow):
    narrow[...] = (keep[...] + got[...].astype(F32)).astype(BF16)


def pair_kernel(chunks, bit, own, pair1, pair2, terms, other, y0, y1, y2, y3, mean, out, norm, *rest):
    made, base, parts, done, both, arrive, leave = rest
    size = own.shape[0] // chunks
    fetches = [
        pltpu.make_async_copy(source, target, arrive.at[index])
        for index, (source, target) in enumerate(
            ((y0, base), (y1, parts.at[0]), (y2, parts.at[1]), (y3, parts.at[2]))
        )
    ]
    for fetch in fetches:
        fetch.start()
    stores = []
    for index in range(chunks):
        rows = pl.ds(index * size, size)

        @pl.when(bit[0] == 0)
        def _():
            made[rows, :] = 0.5 * (own[rows, :].astype(F32) + pair1[rows, :].astype(F32))

        @pl.when(bit[0] != 0)
        def _():
            made[rows, :] = 0.5 * (own[rows, :].astype(F32) + pair2[rows, :].astype(F32))

        stores.append(pltpu.make_async_copy(made.at[rows], mean.at[rows], leave.at[index]))
        stores[-1].start()
    both[...] = 0.5 * (terms[...] + other[...])
    stores.append(pltpu.make_async_copy(both, norm, leave.at[chunks]))
    stores[-1].start()
    for fetch in fetches:
        fetch.wait()
    total = base[...]
    for index in range(3):
        total = total + parts[index].astype(F32)
    done[...] = total.astype(BF16)
    stores.append(pltpu.make_async_copy(done, out, leave.at[chunks + 1]))
    stores[-1].start()
    for store in stores:
        store.wait()


def back_kernel(groups, factor, latent, stats, params, g0, g1, g2, g3, grad, terms):
    gain, shift = params[0:1], params[1:2]
    values = latent[...].astype(F32)
    total = values.shape[0] * values.shape[1] // groups
    scale_inv = stats[1:2]
    normed = (values - stats[0:1]) * scale_inv
    pre = normed * gain + shift
    act_grad = g0[...] + sum(ref[...].astype(F32) for ref in (g1, g2, g3))
    sigma = 1.0 / (1.0 + jnp.exp(-pre))
    pre_grad = act_grad * sigma * (1.0 + pre * (1.0 - sigma))
    sums = col_sums(pre_grad * normed, pre_grad)
    terms[...] = sums[0:2] * factor
    means = group_mean(sums * gain, total, groups)
    grad[...] = (scale_inv * (pre_grad * gain - means[1:2] - normed * means[0:1])).astype(BF16)


def shards_plane(latents, cotangent, conv_weight, norm_gain, norm_shift, partner_bit):
    side, chans = latents.shape[1], latents.shape[3]
    area = side * side
    shard_total = lax.axis_size("fsdp")
    inv_batch = 1.0 / shard_total
    place = lax.axis_index("fsdp")
    weight = conv_weight[0]
    rows = weight.shape[0]
    starts = [2 * rows * chip for chip in range(shard_total // 2)]
    taps = max((start % chans + 2 * rows + chans - 1) // chans for start in starts)
    start = 2 * rows * (place // 2)
    first = jnp.minimum(start // chans, 9 - taps)
    offset = start - first * chans
    core = place % 2
    own_start, other_start = offset + rows * core, offset + rows * (1 - core)
    info = jnp.stack([first, own_start, other_start]).astype(jnp.int32)

    def columns(count, dtype=BF16):
        return shaped((count * area, taps * chans), dtype)

    plane, plane_b = shaped((area, chans), F32), shaped((area, chans), BF16)
    window = (taps * chans, chans)

    latent = latents.reshape(area, chans)
    cot0 = cotangent.reshape(area, chans)
    params = jnp.concatenate([norm_gain, norm_shift])
    other_weight = swap(weight, "fsdp", CORE)
    cot1 = swap(cot0, "fsdp", ACROSS)
    cot2 = swap(cot0, "fsdp", ALONG)
    act0, stats = call(
        functools.partial(norm_kernel, GROUPS),
        [plane_b, shaped((2, chans), F32)],
        [latent, params],
    )
    act2 = swap(act0, "fsdp", ALONG)
    act1 = swap(act0, "fsdp", ACROSS)
    wide, turned, gather, scatter = call(
        functools.partial(prepare_kernel, side, taps),
        [shaped(window, BF16)] * 2 + [shaped((taps * area, area), BF16)] * 2,
        [info, weight, other_weight],
        order=[stats],
    )
    cot1, cot2 = hold([cot1, cot2], [scatter])
    moved, grad0, grad1, grad2 = call(
        functools.partial(grad_kernel, taps),
        [columns(3), plane, plane_b, plane_b],
        [scatter, turned, cot0, cot1, cot2],
    )
    half = area // 2
    cot3 = [swap(cot2[:half], "fsdp", ACROSS), swap(cot1[half:], "fsdp", ALONG)]
    (moved3,) = call(functools.partial(move_kernel, taps), [columns(1)], [scatter, *cot3], order=[grad0])
    act2, act1 = hold([act2, act1], [moved3])
    act3 = [swap(act2[:half], "fsdp", ACROSS), swap(act1[half:], "fsdp", ALONG)]
    (part,) = call(
        functools.partial(weight_kernel, taps),
        [shaped(window, F32)],
        [moved, act0, act1, act2],
        [pltpu.VMEM((chans, 3 * area), BF16)],
    )
    (send,) = call(
        functools.partial(finish_kernel, inv_batch),
        [shaped((rows, chans), BF16)],
        [info, *act3, moved3, part],
        [pltpu.VMEM((2 * chans, area), BF16)],
    )
    got = swap(send, "fsdp", CORE)
    keep, grad3 = call(
        functools.partial(keep_kernel, inv_batch),
        [shaped((rows, chans), F32), plane_b],
        [info, turned, *act3, moved3, part],
        [pltpu.VMEM((2 * chans, area), BF16)],
    )
    (narrow,) = call(join_kernel, [shaped((rows, chans), BF16)], [keep, got])
    pair1 = swap(narrow, "rep", 1)
    pair2 = swap(narrow, "rep", 2)

    masks = (ACROSS, ALONG, ACROSS | ALONG)
    grads = hold([grad1, grad2, grad3], [narrow])
    grads = [swap(value, "fsdp", mask) for value, mask in zip(grads, masks)]
    out0, out1, out2, out3 = call(
        functools.partial(out_kernel, taps),
        [plane, plane_b, plane_b, plane_b],
        [gather, wide, act0, act1, act2, *act3],
        [pltpu.VMEM((4 * area, taps * chans), BF16)],
        order=[narrow],
    )
    out1, out2 = hold([out1, out2], [narrow])
    out1, out2 = swap(out1, "fsdp", ACROSS), swap(out2, "fsdp", ALONG)

    input_grad, terms = call(
        functools.partial(back_kernel, GROUPS, inv_batch),
        [plane_b, shaped((2, chans), F32)],
        [latent, stats, params, grad0, *grads],
        order=[out3],
    )
    (last,) = hold([out3], [terms])
    last = swap(last, "fsdp", ACROSS | ALONG)
    for mask in (ACROSS, ALONG):
        terms = terms + swap(terms, "fsdp", mask)
    (terms,) = hold([terms], [out1, out2])
    terms = terms + swap(terms, "fsdp", CORE)
    other = lax.cond(
        partner_bit[0] == 0, lambda x: swap(x, "rep", 1), lambda x: swap(x, "rep", 2), terms
    )
    shard_bit = lax.dynamic_slice_in_dim(partner_bit, place, 1)
    weight_avg, block_out, norm_avg = call(
        functools.partial(pair_kernel, 5),
        [shaped((rows, chans), F32), plane_b, shaped((2, chans), F32)],
        [shard_bit, narrow, pair1, pair2, terms, other, out0, out1, out2, last],
        [
            pltpu.VMEM((rows, chans), F32),
            pltpu.VMEM((area, chans), F32),
            pltpu.VMEM((3, area, chans), BF16),
            pltpu.VMEM((area, chans), BF16),
            pltpu.VMEM((2, chans), F32),
            pltpu.SemaphoreType.DMA((4,)),
            pltpu.SemaphoreType.DMA((7,)),
        ],
        copies_out=True,
        outside=(6, 7, 8, 9),
    )
    shape = (1, side, side, chans)
    return (block_out.reshape(shape), input_grad.reshape(shape), weight_avg[None], norm_avg[None])


def solution(mesh):
    in_specs = (
        P(("rep", "fsdp"), None, None, None),
        P(("rep", "fsdp"), None, None, None),
        P("rep", "fsdp", None),
        P("rep", None),
        P("rep", None),
        P(),
    )
    out_specs = (
        P(("rep", "fsdp"), None, None, None),
        P(("rep", "fsdp"), None, None, None),
        P("rep", "fsdp", None),
        P("rep", None, None),
    )
    planes = mesh.shape["fsdp"] == 8 and mesh.shape["rep"] == 4
    shards = shards_plane if planes else shards_general
    return jax.shard_map(shards, mesh=mesh, in_specs=in_specs, out_specs=out_specs, check_vma=False)
```

```python
import functools

import jax
import jax.numpy as jnp
from jax import lax
from jax.experimental import pallas as pl
from jax.experimental.pallas import tpu as pltpu
from jax.sharding import PartitionSpec as P

GROUPS = 32


def partner(value, axis, stride):
    mask = 2**stride
    pairs = [(source, source ^ mask) for source in range(lax.axis_size(axis))]
    return lax.ppermute(value, axis, pairs)


def norm_forward(values_in, gain, shift, groups):
    count, side, chans = (values_in.shape[0], values_in.shape[1], values_in.shape[3])
    values = values_in.astype(jnp.float32).reshape(count, side * side, groups, chans // groups)
    center = jnp.mean(values, axis=(1, 3), keepdims=True)
    spread = jnp.mean(jnp.square(values - center), axis=(1, 3), keepdims=True)
    scale_inv = lax.rsqrt(spread + 1e-05)
    normed = (values - center) * scale_inv
    pre_act = normed * gain.reshape(groups, -1) + shift.reshape(groups, -1)
    return (normed, scale_inv, pre_act)


def make_patches(activation):
    count, side, chans = (activation.shape[0], activation.shape[1], activation.shape[3])
    padded = jnp.pad(activation, ((0, 0), (1, 1), (1, 1), (0, 0)))
    pieces = [
        padded[:, row_off : row_off + side, col_off : col_off + side, :]
        for row_off in range(3)
        for col_off in range(3)
    ]
    return jnp.concatenate(pieces, axis=-1).reshape(count * side * side, 9 * chans)


def fold_patches(patch_grad, count, side, chans):
    grads = patch_grad.reshape(count, side, side, 9, chans)
    total = jnp.zeros((count, side + 2, side + 2, chans), jnp.float32)
    for row_off in range(3):
        for col_off in range(3):
            tap = grads[:, :, :, row_off * 3 + col_off, :]
            total = total + jnp.pad(
                tap, ((0, 0), (row_off, 2 - row_off), (col_off, 2 - col_off), (0, 0))
            )
    return total[:, 1:-1, 1:-1, :]


def backward_rest(act_grad, normed, scale_inv, pre_act, gain, groups, inv_batch):
    count, side, chans = (act_grad.shape[0], act_grad.shape[1], act_grad.shape[3])
    act_grad = act_grad.reshape(count, side * side, groups, chans // groups)
    sigma = jax.nn.sigmoid(pre_act)
    pre_grad = act_grad * sigma * (1.0 + pre_act * (1.0 - sigma))
    gain_grad = jnp.sum(pre_grad * normed, axis=(0, 1)).reshape(-1) * inv_batch
    shift_grad = jnp.sum(pre_grad, axis=(0, 1)).reshape(-1) * inv_batch
    normed_grad = pre_grad * gain.reshape(groups, -1)
    first = jnp.mean(normed_grad, axis=(1, 3), keepdims=True)
    second = jnp.mean(normed_grad * normed, axis=(1, 3), keepdims=True)
    input_grad = scale_inv * (normed_grad - first - normed * second)
    return (
        input_grad.reshape(count, side, side, chans).astype(jnp.bfloat16),
        jnp.stack([gain_grad, shift_grad]),
    )


def shards_general(latents, cotangent, conv_weight, norm_gain, norm_shift, partner_bit):
    count, side, chans = (latents.shape[0], latents.shape[1], latents.shape[3])
    shard_total = lax.axis_size("fsdp")
    inv_batch = 1.0 / (count * shard_total)
    gain = norm_gain[0]
    normed, scale_inv, pre_act = norm_forward(latents, gain, norm_shift[0], GROUPS)
    activation = jax.nn.silu(pre_act).astype(jnp.bfloat16).reshape(count, side, side, chans)
    patches = make_patches(activation)
    cot_rows = cotangent.reshape(count * side * side, chans)
    weight_rows = conv_weight[0]
    output = jnp.dot(
        patches,
        lax.all_gather(weight_rows, "fsdp", axis=0, tiled=True),
        preferred_element_type=jnp.float32,
    )
    patch_grad = lax.dot_general(
        cot_rows,
        lax.all_gather(weight_rows, "fsdp", axis=0, tiled=True),
        (((1,), (1,)), ((), ())),
        preferred_element_type=jnp.float32,
    )
    block_out = output.astype(jnp.bfloat16).reshape(count, side, side, chans)
    act_grad = fold_patches(patch_grad, count, side, chans)
    input_grad, norm_term = backward_rest(
        act_grad, normed, scale_inv, pre_act, gain, GROUPS, inv_batch
    )
    weight_term = (
        lax.dot_general(
            patches, cot_rows, (((0,), (0,)), ((), ())), preferred_element_type=jnp.float32
        )
        * inv_batch
    )
    shard_rows = weight_rows.shape[0]
    term_pieces = weight_term.reshape(shard_total, shard_rows, chans)
    received = lax.all_to_all(
        term_pieces.astype(jnp.bfloat16), "fsdp", split_axis=0, concat_axis=0, tiled=True
    ).astype(term_pieces.dtype)
    weight_shard = jnp.sum(received, axis=0)
    bit_count = lax.axis_size("rep").bit_length() - 1
    shard_bit = lax.dynamic_index_in_dim(partner_bit, lax.axis_index("fsdp"), 0, keepdims=False)
    norm_bit = partner_bit[0]
    paired_norm = norm_term
    for bit_index in range(bit_count):
        other_norm = partner(norm_term, "rep", bit_index)
        paired_norm = jnp.where(norm_bit == bit_index, 0.5 * (norm_term + other_norm), paired_norm)
    norm_avg = lax.psum(paired_norm, "fsdp")
    weight_avg = weight_shard
    for bit_index in range(bit_count):
        other_weight = partner(weight_shard.astype(jnp.bfloat16), "rep", bit_index).astype(
            weight_shard.dtype
        )
        weight_avg = jnp.where(
            shard_bit == bit_index, 0.5 * (weight_shard + other_weight), weight_avg
        )
    return (block_out, input_grad, weight_avg[None], norm_avg[None])


CORE, ACROSS, ALONG = 1, 2, 4
VMEM_LIMIT = 12 * 1024 * 1024
F32, BF16 = jnp.float32, jnp.bfloat16


def swap(value, axis, mask):
    pairs = [(source, source ^ mask) for source in range(lax.axis_size(axis))]
    return lax.ppermute(value, axis, pairs)


def call(kernel, outs, args, scratch=(), order=(), copies_out=False, outside=()):
    vmem = pl.BlockSpec(memory_space=pltpu.VMEM)
    smem = pl.BlockSpec(memory_space=pltpu.SMEM)
    untouched = pl.BlockSpec(memory_space=pl.ANY)

    def body(*refs):
        kernel(*refs[: len(args)], *refs[len(args) + len(order) :])

    return pl.pallas_call(
        body,
        out_shape=tuple(outs),
        in_specs=[
            untouched if index in outside else smem if a.dtype == jnp.int32 else vmem
            for index, a in enumerate(args)
        ]
        + [untouched] * len(order),
        out_specs=tuple(untouched if copies_out else vmem for _ in outs),
        scratch_shapes=list(scratch),
        compiler_params=pltpu.CompilerParams(vmem_limit_bytes=VMEM_LIMIT),
    )(*args, *order)


def hold(values, order):
    untouched = pl.BlockSpec(memory_space=pl.ANY)
    return pl.pallas_call(
        lambda *refs: None,
        out_shape=tuple(shaped(value.shape, value.dtype) for value in values),
        in_specs=[untouched] * (len(values) + len(order)),
        out_specs=tuple(untouched for _ in values),
        input_output_aliases={index: index for index in range(len(values))},
        compiler_params=pltpu.CompilerParams(vmem_limit_bytes=1024 * 1024),
    )(*values, *order)


def shaped(shape, dtype):
    return jax.ShapeDtypeStruct(shape, dtype)


def matmul(left, right):
    return jnp.dot(left, right, preferred_element_type=F32)


def group_matrix(chans, groups, transpose):
    width = chans // groups
    shape = (128, chans) if transpose else (chans, 128)
    chan = lax.broadcasted_iota(jnp.int32, shape, 1 if transpose else 0)
    low = lax.broadcasted_iota(jnp.int32, shape, 0 if transpose else 1) * width
    return ((chan >= low) & (chan < low + width)).astype(F32)


def group_mean(columns, total, groups):
    chans = columns.shape[1]
    exact = dict(precision=lax.Precision.HIGHEST, preferred_element_type=F32)
    sums = jnp.dot(columns, group_matrix(chans, groups, False), **exact)
    return jnp.dot(sums, group_matrix(chans, groups, True), **exact) * (1.0 / total)


def col_sums(*values):
    rows = [jnp.sum(value, axis=0, keepdims=True) for value in values]
    fill = jnp.zeros((8 - len(rows), rows[0].shape[1]), F32)
    return jnp.concatenate(rows + [fill], axis=0)


def norm_kernel(groups, latent, params, act, stats):
    gain, shift = params[0:1], params[1:2]
    values = latent[...].astype(F32)
    total = values.shape[0] * values.shape[1] // groups
    center = group_mean(col_sums(values), total, groups)[0:1]
    moved = values - center
    spread = group_mean(col_sums(moved * moved), total, groups)[0:1]
    scale_inv = lax.rsqrt(spread + 1e-05)
    pre = moved * scale_inv * gain + shift
    act[...] = (pre / (1.0 + jnp.exp(-pre))).astype(BF16)
    stats[0:1] = center
    stats[1:2] = scale_inv


def tap_matrix(tap, side, transpose):
    shape = (side * side, side * side)
    here = lax.broadcasted_iota(jnp.int32, shape, 1 if transpose else 0)
    there = lax.broadcasted_iota(jnp.int32, shape, 0 if transpose else 1)
    row_off = lax.div(tap, 3)
    col_off = tap - 3 * row_off
    bits = side.bit_length() - 1
    rows = lax.shift_right_logical(there, bits) - lax.shift_right_logical(here, bits)
    cols = (there & (side - 1)) - (here & (side - 1))
    hit = (rows == row_off - 1) & (cols == col_off - 1)
    return hit.astype(F32).astype(BF16)


def prepare_kernel(side, taps, info, own, other, wide, turned, gather, scatter):
    rows, chans = own.shape
    area = side * side
    wide[...] = jnp.zeros_like(wide)
    wide[pl.ds(pl.multiple_of(info[1], 16), rows), :] = own[...]
    wide[pl.ds(pl.multiple_of(info[2], 16), rows), :] = other[...]
    for tap in range(taps):
        part = slice(tap * chans, (tap + 1) * chans)
        turned[part, :] = wide[part, :].T
        gather[tap * area : (tap + 1) * area, :] = tap_matrix(info[0] + tap, side, False)
        scatter[tap * area : (tap + 1) * area, :] = tap_matrix(info[0] + tap, side, True)


def move_into(target, index, taps, matrices, value):
    area, width = value.shape
    moved = matmul(matrices, value).astype(BF16)
    for tap in range(taps):
        target[index * area : (index + 1) * area, tap * width : (tap + 1) * width] = moved[
            tap * area : (tap + 1) * area
        ]


def split_latents(value, refs):
    area = refs[0].shape[0]
    for index, ref in enumerate(refs):
        ref[...] = value[index * area : (index + 1) * area].astype(ref.dtype)


def grad_kernel(taps, scatter, turned, c0, c1, c2, moved, g0, g1, g2):
    for index, ref in enumerate((c0, c1, c2)):
        move_into(moved, index, taps, scatter[...], ref[...])
    split_latents(matmul(moved[...], turned[...]), (g0, g1, g2))


def move_kernel(taps, scatter, top, bottom, moved):
    move_into(moved, 0, taps, scatter[...], jnp.concatenate([top[...], bottom[...]], axis=0))


def weight_kernel(taps, moved, a0, a1, a2, part, across):
    area, chans = a0.shape
    for index, ref in enumerate((a0, a1, a2)):
        across[:, index * area : (index + 1) * area] = ref[...].T
    for tap in range(taps):
        block = slice(tap * chans, (tap + 1) * chans)
        part[block, :] = matmul(across[...], moved[:, block])


def out_kernel(taps, gather, wide, a0, a1, a2, top, bottom, y0, y1, y2, y3, moved):
    last = jnp.concatenate([top[...], bottom[...]], axis=0)
    for index, value in enumerate((a0[...], a1[...], a2[...], last)):
        move_into(moved, index, taps, gather[...], value)
    split_latents(matmul(moved[...], wide[...]), (y0, y1, y2, y3))


def turn_twice(top, bottom, across):
    chans, half = top.shape[1], top.shape[0]
    for start in (0, chans):
        across[start : start + chans, :half] = top[...].T
        across[start : start + chans, half:] = bottom[...].T


def window_terms(start, rows, chans, across, moved, part):
    tap = lax.div(start, chans)
    offset = start - tap * chans
    picked = across[pl.ds(pl.multiple_of(offset, 16), rows), :]
    row = lax.broadcasted_iota(jnp.int32, picked.shape, 0)
    zero = jnp.zeros_like(picked)
    in_first = row < chans - offset
    left = jnp.concatenate(
        [jnp.where(in_first, picked, zero), jnp.where(in_first, zero, picked)], axis=1
    )
    right = jnp.concatenate(
        [moved[:, pl.ds(pl.multiple_of((tap + step) * chans, 128), chans)] for step in range(2)],
        axis=0,
    )
    return part[pl.ds(pl.multiple_of(start, 16), rows), :] + matmul(left, right)


def finish_kernel(factor, info, top, bottom, moved, part, send, across):
    turn_twice(top, bottom, across)
    terms = window_terms(info[2], send.shape[0], top.shape[1], across, moved, part)
    send[...] = (terms * factor).astype(BF16)


def keep_kernel(factor, info, turned, top, bottom, moved, part, keep, g3, across):
    turn_twice(top, bottom, across)
    keep[...] = window_terms(info[1], keep.shape[0], top.shape[1], across, moved, part) * factor
    g3[...] = matmul(moved[...], turned[...]).astype(BF16)


def sum_kernel(y0, y1, y2, y3, total):
    total[...] = (y0[...] + sum(ref[...].astype(F32) for ref in (y1, y2, y3))).astype(BF16)


def join_kernel(keep, got, narrow):
    narrow[...] = (keep[...] + got[...].astype(F32)).astype(BF16)


def pair_kernel(chunks, bit, own, pair1, pair2, terms, other, mean, norm, made, theirs, both, arrive, leave):
    size = own.shape[0] // chunks
    fetch = pltpu.make_async_copy(other, theirs, arrive.at[0])
    fetch.start()
    stores = []
    for index in range(chunks):
        rows = pl.ds(index * size, size)

        @pl.when(bit[0] == 0)
        def _():
            made[rows, :] = 0.5 * (own[rows, :].astype(F32) + pair1[rows, :].astype(F32))

        @pl.when(bit[0] != 0)
        def _():
            made[rows, :] = 0.5 * (own[rows, :].astype(F32) + pair2[rows, :].astype(F32))

        stores.append(pltpu.make_async_copy(made.at[rows], mean.at[rows], leave.at[index]))
        stores[-1].start()
    fetch.wait()
    both[...] = 0.5 * (terms[...] + theirs[...])
    stores.append(pltpu.make_async_copy(both, norm, leave.at[chunks]))
    stores[-1].start()
    for store in stores:
        store.wait()


def back_kernel(groups, factor, latent, stats, params, g0, g1, g2, g3, grad, terms):
    gain, shift = params[0:1], params[1:2]
    values = latent[...].astype(F32)
    total = values.shape[0] * values.shape[1] // groups
    scale_inv = stats[1:2]
    normed = (values - stats[0:1]) * scale_inv
    pre = normed * gain + shift
    act_grad = g0[...] + sum(ref[...].astype(F32) for ref in (g1, g2, g3))
    sigma = 1.0 / (1.0 + jnp.exp(-pre))
    pre_grad = act_grad * sigma * (1.0 + pre * (1.0 - sigma))
    sums = col_sums(pre_grad * normed, pre_grad)
    terms[...] = sums[0:2] * factor
    means = group_mean(sums * gain, total, groups)
    grad[...] = (scale_inv * (pre_grad * gain - means[1:2] - normed * means[0:1])).astype(BF16)


def shards_plane(latents, cotangent, conv_weight, norm_gain, norm_shift, partner_bit):
    side, chans = latents.shape[1], latents.shape[3]
    area = side * side
    shard_total = lax.axis_size("fsdp")
    inv_batch = 1.0 / shard_total
    place = lax.axis_index("fsdp")
    weight = conv_weight[0]
    rows = weight.shape[0]
    starts = [2 * rows * chip for chip in range(shard_total // 2)]
    taps = max((start % chans + 2 * rows + chans - 1) // chans for start in starts)
    start = 2 * rows * (place // 2)
    first = jnp.minimum(start // chans, 9 - taps)
    offset = start - first * chans
    core = place % 2
    own_start, other_start = offset + rows * core, offset + rows * (1 - core)
    info = jnp.stack([first, own_start, other_start]).astype(jnp.int32)

    def columns(count, dtype=BF16):
        return shaped((count * area, taps * chans), dtype)

    plane, plane_b = shaped((area, chans), F32), shaped((area, chans), BF16)
    window = (taps * chans, chans)

    latent = latents.reshape(area, chans)
    cot0 = cotangent.reshape(area, chans)
    params = jnp.concatenate([norm_gain, norm_shift])
    other_weight = swap(weight, "fsdp", CORE)
    cot1 = swap(cot0, "fsdp", ACROSS)
    cot2 = swap(cot0, "fsdp", ALONG)
    act0, stats = call(
        functools.partial(norm_kernel, GROUPS),
        [plane_b, shaped((2, chans), F32)],
        [latent, params],
    )
    act2 = swap(act0, "fsdp", ALONG)
    act1 = swap(act0, "fsdp", ACROSS)
    wide, turned, gather, scatter = call(
        functools.partial(prepare_kernel, side, taps),
        [shaped(window, BF16)] * 2 + [shaped((taps * area, area), BF16)] * 2,
        [info, weight, other_weight],
        order=[stats],
    )
    cot1, cot2 = hold([cot1, cot2], [scatter])
    moved, grad0, grad1, grad2 = call(
        functools.partial(grad_kernel, taps),
        [columns(3), plane, plane_b, plane_b],
        [scatter, turned, cot0, cot1, cot2],
    )
    half = area // 2
    cot3 = [swap(cot2[:half], "fsdp", ACROSS), swap(cot1[half:], "fsdp", ALONG)]
    (moved3,) = call(functools.partial(move_kernel, taps), [columns(1)], [scatter, *cot3], order=[grad0])
    act2, act1 = hold([act2, act1], [moved3])
    act3 = [swap(act2[:half], "fsdp", ACROSS), swap(act1[half:], "fsdp", ALONG)]
    (part,) = call(
        functools.partial(weight_kernel, taps),
        [shaped(window, F32)],
        [moved, act0, act1, act2],
        [pltpu.VMEM((chans, 3 * area), BF16)],
    )
    (send,) = call(
        functools.partial(finish_kernel, inv_batch),
        [shaped((rows, chans), BF16)],
        [info, *act3, moved3, part],
        [pltpu.VMEM((2 * chans, area), BF16)],
    )
    got = swap(send, "fsdp", CORE)
    keep, grad3 = call(
        functools.partial(keep_kernel, inv_batch),
        [shaped((rows, chans), F32), plane_b],
        [info, turned, *act3, moved3, part],
        [pltpu.VMEM((2 * chans, area), BF16)],
    )
    (narrow,) = call(join_kernel, [shaped((rows, chans), BF16)], [keep, got])
    pair1 = swap(narrow, "rep", 1)
    pair2 = swap(narrow, "rep", 2)

    masks = (ACROSS, ALONG, ACROSS | ALONG)
    grads = hold([grad1, grad2, grad3], [narrow])
    grads = [swap(value, "fsdp", mask) for value, mask in zip(grads, masks)]
    out0, out1, out2, out3 = call(
        functools.partial(out_kernel, taps),
        [plane, plane_b, plane_b, plane_b],
        [gather, wide, act0, act1, act2, *act3],
        [pltpu.VMEM((4 * area, taps * chans), BF16)],
        order=[narrow],
    )
    out1, out2 = hold([out1, out2], [narrow])
    out1, out2 = swap(out1, "fsdp", ACROSS), swap(out2, "fsdp", ALONG)

    input_grad, terms = call(
        functools.partial(back_kernel, GROUPS, inv_batch),
        [plane_b, shaped((2, chans), F32)],
        [latent, stats, params, grad0, *grads],
        order=[out3],
    )
    (last,) = hold([out3], [terms])
    last = swap(last, "fsdp", ACROSS | ALONG)
    terms = terms + swap(terms, "fsdp", ACROSS)
    (terms,) = hold([terms], [out1, out2])
    for mask in (ALONG, CORE):
        terms = terms + swap(terms, "fsdp", mask)
    (block_out,) = call(sum_kernel, [plane_b], [out0, out1, out2, last])
    (terms,) = hold([terms], [block_out])
    other = lax.cond(
        partner_bit[0] == 0, lambda x: swap(x, "rep", 1), lambda x: swap(x, "rep", 2), terms
    )
    shard_bit = lax.dynamic_slice_in_dim(partner_bit, place, 1)
    weight_avg, norm_avg = call(
        functools.partial(pair_kernel, 5),
        [shaped((rows, chans), F32), shaped((2, chans), F32)],
        [shard_bit, narrow, pair1, pair2, terms, other],
        [
            pltpu.VMEM((rows, chans), F32),
            pltpu.VMEM((2, chans), F32),
            pltpu.VMEM((2, chans), F32),
            pltpu.SemaphoreType.DMA((1,)),
            pltpu.SemaphoreType.DMA((6,)),
        ],
        copies_out=True,
        outside=(5,),
    )
    shape = (1, side, side, chans)
    return (block_out.reshape(shape), input_grad.reshape(shape), weight_avg[None], norm_avg[None])


def solution(mesh):
    in_specs = (
        P(("rep", "fsdp"), None, None, None),
        P(("rep", "fsdp"), None, None, None),
        P("rep", "fsdp", None),
        P("rep", None),
        P("rep", None),
        P(),
    )
    out_specs = (
        P(("rep", "fsdp"), None, None, None),
        P(("rep", "fsdp"), None, None, None),
        P("rep", "fsdp", None),
        P("rep", None, None),
    )
    planes = mesh.shape["fsdp"] == 8 and mesh.shape["rep"] == 4
    shards = shards_plane if planes else shards_general
    return jax.shard_map(shards, mesh=mesh, in_specs=in_specs, out_specs=out_specs, check_vma=False)
```

```python
import functools

import jax
import jax.numpy as jnp
from jax import lax
from jax.experimental import pallas as pl
from jax.experimental.pallas import tpu as pltpu
from jax.sharding import PartitionSpec as P

GROUPS = 32


def partner(value, axis, stride):
    mask = 2**stride
    pairs = [(source, source ^ mask) for source in range(lax.axis_size(axis))]
    return lax.ppermute(value, axis, pairs)


def norm_forward(values_in, gain, shift, groups):
    count, side, chans = (values_in.shape[0], values_in.shape[1], values_in.shape[3])
    values = values_in.astype(jnp.float32).reshape(count, side * side, groups, chans // groups)
    center = jnp.mean(values, axis=(1, 3), keepdims=True)
    spread = jnp.mean(jnp.square(values - center), axis=(1, 3), keepdims=True)
    scale_inv = lax.rsqrt(spread + 1e-05)
    normed = (values - center) * scale_inv
    pre_act = normed * gain.reshape(groups, -1) + shift.reshape(groups, -1)
    return (normed, scale_inv, pre_act)


def make_patches(activation):
    count, side, chans = (activation.shape[0], activation.shape[1], activation.shape[3])
    padded = jnp.pad(activation, ((0, 0), (1, 1), (1, 1), (0, 0)))
    pieces = [
        padded[:, row_off : row_off + side, col_off : col_off + side, :]
        for row_off in range(3)
        for col_off in range(3)
    ]
    return jnp.concatenate(pieces, axis=-1).reshape(count * side * side, 9 * chans)


def fold_patches(patch_grad, count, side, chans):
    grads = patch_grad.reshape(count, side, side, 9, chans)
    total = jnp.zeros((count, side + 2, side + 2, chans), jnp.float32)
    for row_off in range(3):
        for col_off in range(3):
            tap = grads[:, :, :, row_off * 3 + col_off, :]
            total = total + jnp.pad(
                tap, ((0, 0), (row_off, 2 - row_off), (col_off, 2 - col_off), (0, 0))
            )
    return total[:, 1:-1, 1:-1, :]


def backward_rest(act_grad, normed, scale_inv, pre_act, gain, groups, inv_batch):
    count, side, chans = (act_grad.shape[0], act_grad.shape[1], act_grad.shape[3])
    act_grad = act_grad.reshape(count, side * side, groups, chans // groups)
    sigma = jax.nn.sigmoid(pre_act)
    pre_grad = act_grad * sigma * (1.0 + pre_act * (1.0 - sigma))
    gain_grad = jnp.sum(pre_grad * normed, axis=(0, 1)).reshape(-1) * inv_batch
    shift_grad = jnp.sum(pre_grad, axis=(0, 1)).reshape(-1) * inv_batch
    normed_grad = pre_grad * gain.reshape(groups, -1)
    first = jnp.mean(normed_grad, axis=(1, 3), keepdims=True)
    second = jnp.mean(normed_grad * normed, axis=(1, 3), keepdims=True)
    input_grad = scale_inv * (normed_grad - first - normed * second)
    return (
        input_grad.reshape(count, side, side, chans).astype(jnp.bfloat16),
        jnp.stack([gain_grad, shift_grad]),
    )


def shards_general(latents, cotangent, conv_weight, norm_gain, norm_shift, partner_bit):
    count, side, chans = (latents.shape[0], latents.shape[1], latents.shape[3])
    shard_total = lax.axis_size("fsdp")
    inv_batch = 1.0 / (count * shard_total)
    gain = norm_gain[0]
    normed, scale_inv, pre_act = norm_forward(latents, gain, norm_shift[0], GROUPS)
    activation = jax.nn.silu(pre_act).astype(jnp.bfloat16).reshape(count, side, side, chans)
    patches = make_patches(activation)
    cot_rows = cotangent.reshape(count * side * side, chans)
    weight_rows = conv_weight[0]
    output = jnp.dot(
        patches,
        lax.all_gather(weight_rows, "fsdp", axis=0, tiled=True),
        preferred_element_type=jnp.float32,
    )
    patch_grad = lax.dot_general(
        cot_rows,
        lax.all_gather(weight_rows, "fsdp", axis=0, tiled=True),
        (((1,), (1,)), ((), ())),
        preferred_element_type=jnp.float32,
    )
    block_out = output.astype(jnp.bfloat16).reshape(count, side, side, chans)
    act_grad = fold_patches(patch_grad, count, side, chans)
    input_grad, norm_term = backward_rest(
        act_grad, normed, scale_inv, pre_act, gain, GROUPS, inv_batch
    )
    weight_term = (
        lax.dot_general(
            patches, cot_rows, (((0,), (0,)), ((), ())), preferred_element_type=jnp.float32
        )
        * inv_batch
    )
    shard_rows = weight_rows.shape[0]
    term_pieces = weight_term.reshape(shard_total, shard_rows, chans)
    received = lax.all_to_all(
        term_pieces.astype(jnp.bfloat16), "fsdp", split_axis=0, concat_axis=0, tiled=True
    ).astype(term_pieces.dtype)
    weight_shard = jnp.sum(received, axis=0)
    bit_count = lax.axis_size("rep").bit_length() - 1
    shard_bit = lax.dynamic_index_in_dim(partner_bit, lax.axis_index("fsdp"), 0, keepdims=False)
    norm_bit = partner_bit[0]
    paired_norm = norm_term
    for bit_index in range(bit_count):
        other_norm = partner(norm_term, "rep", bit_index)
        paired_norm = jnp.where(norm_bit == bit_index, 0.5 * (norm_term + other_norm), paired_norm)
    norm_avg = lax.psum(paired_norm, "fsdp")
    weight_avg = weight_shard
    for bit_index in range(bit_count):
        other_weight = partner(weight_shard.astype(jnp.bfloat16), "rep", bit_index).astype(
            weight_shard.dtype
        )
        weight_avg = jnp.where(
            shard_bit == bit_index, 0.5 * (weight_shard + other_weight), weight_avg
        )
    return (block_out, input_grad, weight_avg[None], norm_avg[None])


CORE, ACROSS, ALONG = 1, 2, 4
VMEM_LIMIT = 12 * 1024 * 1024
F32, BF16 = jnp.float32, jnp.bfloat16


def swap(value, axis, mask):
    pairs = [(source, source ^ mask) for source in range(lax.axis_size(axis))]
    return lax.ppermute(value, axis, pairs)


def call(kernel, outs, args, scratch=(), order=(), copies_out=False, outside=()):
    vmem = pl.BlockSpec(memory_space=pltpu.VMEM)
    smem = pl.BlockSpec(memory_space=pltpu.SMEM)
    untouched = pl.BlockSpec(memory_space=pl.ANY)

    def body(*refs):
        kernel(*refs[: len(args)], *refs[len(args) + len(order) :])

    return pl.pallas_call(
        body,
        out_shape=tuple(outs),
        in_specs=[
            untouched if index in outside else smem if a.dtype == jnp.int32 else vmem
            for index, a in enumerate(args)
        ]
        + [untouched] * len(order),
        out_specs=tuple(untouched if copies_out else vmem for _ in outs),
        scratch_shapes=list(scratch),
        compiler_params=pltpu.CompilerParams(vmem_limit_bytes=VMEM_LIMIT),
    )(*args, *order)


def hold(values, order):
    untouched = pl.BlockSpec(memory_space=pl.ANY)
    return pl.pallas_call(
        lambda *refs: None,
        out_shape=tuple(shaped(value.shape, value.dtype) for value in values),
        in_specs=[untouched] * (len(values) + len(order)),
        out_specs=tuple(untouched for _ in values),
        input_output_aliases={index: index for index in range(len(values))},
        compiler_params=pltpu.CompilerParams(vmem_limit_bytes=1024 * 1024),
    )(*values, *order)


def shaped(shape, dtype):
    return jax.ShapeDtypeStruct(shape, dtype)


def matmul(left, right):
    return jnp.dot(left, right, preferred_element_type=F32)


def group_matrix(chans, groups, transpose):
    width = chans // groups
    shape = (128, chans) if transpose else (chans, 128)
    chan = lax.broadcasted_iota(jnp.int32, shape, 1 if transpose else 0)
    low = lax.broadcasted_iota(jnp.int32, shape, 0 if transpose else 1) * width
    return ((chan >= low) & (chan < low + width)).astype(F32)


def group_mean(columns, total, groups):
    chans = columns.shape[1]
    exact = dict(precision=lax.Precision.HIGHEST, preferred_element_type=F32)
    sums = jnp.dot(columns, group_matrix(chans, groups, False), **exact)
    return jnp.dot(sums, group_matrix(chans, groups, True), **exact) * (1.0 / total)


def col_sums(*values):
    rows = [jnp.sum(value, axis=0, keepdims=True) for value in values]
    fill = jnp.zeros((8 - len(rows), rows[0].shape[1]), F32)
    return jnp.concatenate(rows + [fill], axis=0)


def norm_kernel(groups, latent, params, act, stats):
    gain, shift = params[0:1], params[1:2]
    values = latent[...].astype(F32)
    total = values.shape[0] * values.shape[1] // groups
    center = group_mean(col_sums(values), total, groups)[0:1]
    moved = values - center
    spread = group_mean(col_sums(moved * moved), total, groups)[0:1]
    scale_inv = lax.rsqrt(spread + 1e-05)
    pre = moved * scale_inv * gain + shift
    act[...] = (pre / (1.0 + jnp.exp(-pre))).astype(BF16)
    stats[0:1] = center
    stats[1:2] = scale_inv


def tap_matrix(tap, side, transpose):
    shape = (side * side, side * side)
    here = lax.broadcasted_iota(jnp.int32, shape, 1 if transpose else 0)
    there = lax.broadcasted_iota(jnp.int32, shape, 0 if transpose else 1)
    row_off = lax.div(tap, 3)
    col_off = tap - 3 * row_off
    bits = side.bit_length() - 1
    rows = lax.shift_right_logical(there, bits) - lax.shift_right_logical(here, bits)
    cols = (there & (side - 1)) - (here & (side - 1))
    hit = (rows == row_off - 1) & (cols == col_off - 1)
    return hit.astype(F32).astype(BF16)


def prepare_kernel(side, taps, info, own, other, wide, turned, gather, scatter):
    rows, chans = own.shape
    area = side * side
    wide[...] = jnp.zeros_like(wide)
    wide[pl.ds(pl.multiple_of(info[1], 16), rows), :] = own[...]
    wide[pl.ds(pl.multiple_of(info[2], 16), rows), :] = other[...]
    for tap in range(taps):
        part = slice(tap * chans, (tap + 1) * chans)
        turned[part, :] = wide[part, :].T
        gather[tap * area : (tap + 1) * area, :] = tap_matrix(info[0] + tap, side, False)
        scatter[tap * area : (tap + 1) * area, :] = tap_matrix(info[0] + tap, side, True)


def move_into(target, index, taps, matrices, value):
    area, width = value.shape
    moved = matmul(matrices, value).astype(BF16)
    for tap in range(taps):
        target[index * area : (index + 1) * area, tap * width : (tap + 1) * width] = moved[
            tap * area : (tap + 1) * area
        ]


def split_latents(value, refs):
    area = refs[0].shape[0]
    for index, ref in enumerate(refs):
        ref[...] = value[index * area : (index + 1) * area].astype(ref.dtype)


def spread_kernel(taps, scatter, c0, c1, c2, moved):
    for index, ref in enumerate((c0, c1, c2)):
        move_into(moved, index, taps, scatter[...], ref[...])


def grad_kernel(turned, moved, g0, g1, g2):
    split_latents(matmul(moved[...], turned[...]), (g0, g1, g2))


def move_kernel(taps, scatter, top, bottom, moved):
    move_into(moved, 0, taps, scatter[...], jnp.concatenate([top[...], bottom[...]], axis=0))


def weight_kernel(taps, moved, a0, a1, a2, part, across):
    area, chans = a0.shape
    for index, ref in enumerate((a0, a1, a2)):
        across[:, index * area : (index + 1) * area] = ref[...].T
    for tap in range(taps):
        block = slice(tap * chans, (tap + 1) * chans)
        part[block, :] = matmul(across[...], moved[:, block])


def out_kernel(taps, gather, wide, a0, a1, a2, top, bottom, y0, y1, y2, y3, moved):
    last = jnp.concatenate([top[...], bottom[...]], axis=0)
    for index, value in enumerate((a0[...], a1[...], a2[...], last)):
        move_into(moved, index, taps, gather[...], value)
    split_latents(matmul(moved[...], wide[...]), (y0, y1, y2, y3))


def turn_twice(top, bottom, across):
    chans, half = top.shape[1], top.shape[0]
    for start in (0, chans):
        across[start : start + chans, :half] = top[...].T
        across[start : start + chans, half:] = bottom[...].T


def window_terms(start, rows, chans, across, moved, part):
    tap = lax.div(start, chans)
    offset = start - tap * chans
    picked = across[pl.ds(pl.multiple_of(offset, 16), rows), :]
    row = lax.broadcasted_iota(jnp.int32, picked.shape, 0)
    zero = jnp.zeros_like(picked)
    in_first = row < chans - offset
    left = jnp.concatenate(
        [jnp.where(in_first, picked, zero), jnp.where(in_first, zero, picked)], axis=1
    )
    right = jnp.concatenate(
        [moved[:, pl.ds(pl.multiple_of((tap + step) * chans, 128), chans)] for step in range(2)],
        axis=0,
    )
    return part[pl.ds(pl.multiple_of(start, 16), rows), :] + matmul(left, right)


def finish_kernel(factor, info, top, bottom, moved, part, send, across):
    turn_twice(top, bottom, across)
    terms = window_terms(info[2], send.shape[0], top.shape[1], across, moved, part)
    send[...] = (terms * factor).astype(BF16)


def keep_kernel(factor, info, turned, top, bottom, moved, part, keep, g3, across):
    turn_twice(top, bottom, across)
    keep[...] = window_terms(info[1], keep.shape[0], top.shape[1], across, moved, part) * factor
    g3[...] = matmul(moved[...], turned[...]).astype(BF16)


def sum_kernel(y0, y1, y2, y3, total):
    total[...] = (y0[...] + sum(ref[...].astype(F32) for ref in (y1, y2, y3))).astype(BF16)


def join_kernel(keep, got, narrow):
    narrow[...] = (keep[...] + got[...].astype(F32)).astype(BF16)


def pair_kernel(chunks, bit, own, pair1, pair2, mean, made, leave):
    size = own.shape[0] // chunks
    stores = []
    for index in range(chunks):
        rows = pl.ds(index * size, size)

        @pl.when(bit[0] == 0)
        def _():
            made[rows, :] = 0.5 * (own[rows, :].astype(F32) + pair1[rows, :].astype(F32))

        @pl.when(bit[0] != 0)
        def _():
            made[rows, :] = 0.5 * (own[rows, :].astype(F32) + pair2[rows, :].astype(F32))

        stores.append(pltpu.make_async_copy(made.at[rows], mean.at[rows], leave.at[index]))
        stores[-1].start()
    for store in stores:
        store.wait()


def back_kernel(groups, factor, latent, stats, params, g0, g1, g2, g3, grad, terms):
    gain, shift = params[0:1], params[1:2]
    values = latent[...].astype(F32)
    total = values.shape[0] * values.shape[1] // groups
    scale_inv = stats[1:2]
    normed = (values - stats[0:1]) * scale_inv
    pre = normed * gain + shift
    act_grad = g0[...] + sum(ref[...].astype(F32) for ref in (g1, g2, g3))
    sigma = 1.0 / (1.0 + jnp.exp(-pre))
    pre_grad = act_grad * sigma * (1.0 + pre * (1.0 - sigma))
    sums = col_sums(pre_grad * normed, pre_grad)
    terms[...] = sums[0:2] * factor
    means = group_mean(sums * gain, total, groups)
    grad[...] = (scale_inv * (pre_grad * gain - means[1:2] - normed * means[0:1])).astype(BF16)


def shards_plane(latents, cotangent, conv_weight, norm_gain, norm_shift, partner_bit):
    side, chans = latents.shape[1], latents.shape[3]
    area = side * side
    shard_total = lax.axis_size("fsdp")
    inv_batch = 1.0 / shard_total
    place = lax.axis_index("fsdp")
    weight = conv_weight[0]
    rows = weight.shape[0]
    starts = [2 * rows * chip for chip in range(shard_total // 2)]
    taps = max((start % chans + 2 * rows + chans - 1) // chans for start in starts)
    start = 2 * rows * (place // 2)
    first = jnp.minimum(start // chans, 9 - taps)
    offset = start - first * chans
    core = place % 2
    own_start, other_start = offset + rows * core, offset + rows * (1 - core)
    info = jnp.stack([first, own_start, other_start]).astype(jnp.int32)

    def columns(count, dtype=BF16):
        return shaped((count * area, taps * chans), dtype)

    plane, plane_b = shaped((area, chans), F32), shaped((area, chans), BF16)
    window = (taps * chans, chans)

    latent = latents.reshape(area, chans)
    cot0 = cotangent.reshape(area, chans)
    params = jnp.concatenate([norm_gain, norm_shift])
    other_weight = swap(weight, "fsdp", CORE)
    cot1 = swap(cot0, "fsdp", ACROSS)
    cot2 = swap(cot0, "fsdp", ALONG)
    act0, stats = call(
        functools.partial(norm_kernel, GROUPS),
        [plane_b, shaped((2, chans), F32)],
        [latent, params],
    )
    act2 = swap(act0, "fsdp", ALONG)
    act1 = swap(act0, "fsdp", ACROSS)
    wide, turned, gather, scatter = call(
        functools.partial(prepare_kernel, side, taps),
        [shaped(window, BF16)] * 2 + [shaped((taps * area, area), BF16)] * 2,
        [info, weight, other_weight],
        order=[stats],
    )
    (moved,) = call(
        functools.partial(spread_kernel, taps), [columns(3)], [scatter, cot0, cot1, cot2]
    )
    cot1, cot2 = hold([cot1, cot2], [moved])
    grad0, grad1, grad2 = call(grad_kernel, [plane, plane_b, plane_b], [turned, moved])
    half = area // 2
    cot3 = [swap(cot2[:half], "fsdp", ACROSS), swap(cot1[half:], "fsdp", ALONG)]
    act2, act1 = hold([act2, act1], [grad0])
    act3 = [swap(act2[:half], "fsdp", ACROSS), swap(act1[half:], "fsdp", ALONG)]
    (part,) = call(
        functools.partial(weight_kernel, taps),
        [shaped(window, F32)],
        [moved, act0, act1, act2],
        [pltpu.VMEM((chans, 3 * area), BF16)],
    )
    (moved3,) = call(
        functools.partial(move_kernel, taps), [columns(1)], [scatter, *cot3], order=[part]
    )
    (send,) = call(
        functools.partial(finish_kernel, inv_batch),
        [shaped((rows, chans), BF16)],
        [info, *act3, moved3, part],
        [pltpu.VMEM((2 * chans, area), BF16)],
    )
    got = swap(send, "fsdp", CORE)
    keep, grad3 = call(
        functools.partial(keep_kernel, inv_batch),
        [shaped((rows, chans), F32), plane_b],
        [info, turned, *act3, moved3, part],
        [pltpu.VMEM((2 * chans, area), BF16)],
    )
    (narrow,) = call(join_kernel, [shaped((rows, chans), BF16)], [keep, got])
    pair1 = swap(narrow, "rep", 1)
    pair2 = swap(narrow, "rep", 2)

    masks = (ACROSS, ALONG, ACROSS | ALONG)
    grads = hold([grad1, grad2, grad3], [narrow])
    grads = [swap(value, "fsdp", mask) for value, mask in zip(grads, masks)]
    out0, out1, out2, out3 = call(
        functools.partial(out_kernel, taps),
        [plane, plane_b, plane_b, plane_b],
        [gather, wide, act0, act1, act2, *act3],
        [pltpu.VMEM((4 * area, taps * chans), BF16)],
        order=[narrow],
    )
    out1, out2 = hold([out1, out2], [narrow])
    out1, out2 = swap(out1, "fsdp", ACROSS), swap(out2, "fsdp", ALONG)

    input_grad, terms = call(
        functools.partial(back_kernel, GROUPS, inv_batch),
        [plane_b, shaped((2, chans), F32)],
        [latent, stats, params, grad0, *grads],
        order=[out3],
    )
    (last,) = hold([out3], [terms])
    last = swap(last, "fsdp", ACROSS | ALONG)
    terms = terms + swap(terms, "fsdp", ACROSS)
    (terms,) = hold([terms], [out1, out2])
    for mask in (ALONG, CORE):
        terms = terms + swap(terms, "fsdp", mask)
    (block_out,) = call(sum_kernel, [plane_b], [out0, out1, out2, last])
    (terms,) = hold([terms], [block_out])
    norm_avg = lax.cond(
        partner_bit[0] == 0,
        lambda own: 0.5 * (own + swap(own, "rep", 1)),
        lambda own: 0.5 * (own + swap(own, "rep", 2)),
        terms,
    )
    shard_bit = lax.dynamic_slice_in_dim(partner_bit, place, 1)
    (weight_avg,) = call(
        functools.partial(pair_kernel, 5),
        [shaped((rows, chans), F32)],
        [shard_bit, narrow, pair1, pair2],
        [pltpu.VMEM((rows, chans), F32), pltpu.SemaphoreType.DMA((5,))],
        copies_out=True,
    )
    shape = (1, side, side, chans)
    return (block_out.reshape(shape), input_grad.reshape(shape), weight_avg[None], norm_avg[None])


def solution(mesh):
    in_specs = (
        P(("rep", "fsdp"), None, None, None),
        P(("rep", "fsdp"), None, None, None),
        P("rep", "fsdp", None),
        P("rep", None),
        P("rep", None),
        P(),
    )
    out_specs = (
        P(("rep", "fsdp"), None, None, None),
        P(("rep", "fsdp"), None, None, None),
        P("rep", "fsdp", None),
        P("rep", None, None),
    )
    planes = mesh.shape["fsdp"] == 8 and mesh.shape["rep"] == 4
    shards = shards_plane if planes else shards_general
    return jax.shard_map(shards, mesh=mesh, in_specs=in_specs, out_specs=out_specs, check_vma=False)
```

```python
import functools

import jax
import jax.numpy as jnp
from jax import lax
from jax.experimental import pallas as pl
from jax.experimental.pallas import tpu as pltpu
from jax.sharding import PartitionSpec as P

GROUPS = 32


def partner(value, axis, stride):
    mask = 2**stride
    pairs = [(source, source ^ mask) for source in range(lax.axis_size(axis))]
    return lax.ppermute(value, axis, pairs)


def norm_forward(values_in, gain, shift, groups):
    count, side, chans = (values_in.shape[0], values_in.shape[1], values_in.shape[3])
    values = values_in.astype(jnp.float32).reshape(count, side * side, groups, chans // groups)
    center = jnp.mean(values, axis=(1, 3), keepdims=True)
    spread = jnp.mean(jnp.square(values - center), axis=(1, 3), keepdims=True)
    scale_inv = lax.rsqrt(spread + 1e-05)
    normed = (values - center) * scale_inv
    pre_act = normed * gain.reshape(groups, -1) + shift.reshape(groups, -1)
    return (normed, scale_inv, pre_act)


def make_patches(activation):
    count, side, chans = (activation.shape[0], activation.shape[1], activation.shape[3])
    padded = jnp.pad(activation, ((0, 0), (1, 1), (1, 1), (0, 0)))
    pieces = [
        padded[:, row_off : row_off + side, col_off : col_off + side, :]
        for row_off in range(3)
        for col_off in range(3)
    ]
    return jnp.concatenate(pieces, axis=-1).reshape(count * side * side, 9 * chans)


def fold_patches(patch_grad, count, side, chans):
    grads = patch_grad.reshape(count, side, side, 9, chans)
    total = jnp.zeros((count, side + 2, side + 2, chans), jnp.float32)
    for row_off in range(3):
        for col_off in range(3):
            tap = grads[:, :, :, row_off * 3 + col_off, :]
            total = total + jnp.pad(
                tap, ((0, 0), (row_off, 2 - row_off), (col_off, 2 - col_off), (0, 0))
            )
    return total[:, 1:-1, 1:-1, :]


def backward_rest(act_grad, normed, scale_inv, pre_act, gain, groups, inv_batch):
    count, side, chans = (act_grad.shape[0], act_grad.shape[1], act_grad.shape[3])
    act_grad = act_grad.reshape(count, side * side, groups, chans // groups)
    sigma = jax.nn.sigmoid(pre_act)
    pre_grad = act_grad * sigma * (1.0 + pre_act * (1.0 - sigma))
    gain_grad = jnp.sum(pre_grad * normed, axis=(0, 1)).reshape(-1) * inv_batch
    shift_grad = jnp.sum(pre_grad, axis=(0, 1)).reshape(-1) * inv_batch
    normed_grad = pre_grad * gain.reshape(groups, -1)
    first = jnp.mean(normed_grad, axis=(1, 3), keepdims=True)
    second = jnp.mean(normed_grad * normed, axis=(1, 3), keepdims=True)
    input_grad = scale_inv * (normed_grad - first - normed * second)
    return (
        input_grad.reshape(count, side, side, chans).astype(jnp.bfloat16),
        jnp.stack([gain_grad, shift_grad]),
    )


def shards_general(latents, cotangent, conv_weight, norm_gain, norm_shift, partner_bit):
    count, side, chans = (latents.shape[0], latents.shape[1], latents.shape[3])
    shard_total = lax.axis_size("fsdp")
    inv_batch = 1.0 / (count * shard_total)
    gain = norm_gain[0]
    normed, scale_inv, pre_act = norm_forward(latents, gain, norm_shift[0], GROUPS)
    activation = jax.nn.silu(pre_act).astype(jnp.bfloat16).reshape(count, side, side, chans)
    patches = make_patches(activation)
    cot_rows = cotangent.reshape(count * side * side, chans)
    weight_rows = conv_weight[0]
    output = jnp.dot(
        patches,
        lax.all_gather(weight_rows, "fsdp", axis=0, tiled=True),
        preferred_element_type=jnp.float32,
    )
    patch_grad = lax.dot_general(
        cot_rows,
        lax.all_gather(weight_rows, "fsdp", axis=0, tiled=True),
        (((1,), (1,)), ((), ())),
        preferred_element_type=jnp.float32,
    )
    block_out = output.astype(jnp.bfloat16).reshape(count, side, side, chans)
    act_grad = fold_patches(patch_grad, count, side, chans)
    input_grad, norm_term = backward_rest(
        act_grad, normed, scale_inv, pre_act, gain, GROUPS, inv_batch
    )
    weight_term = (
        lax.dot_general(
            patches, cot_rows, (((0,), (0,)), ((), ())), preferred_element_type=jnp.float32
        )
        * inv_batch
    )
    shard_rows = weight_rows.shape[0]
    term_pieces = weight_term.reshape(shard_total, shard_rows, chans)
    received = lax.all_to_all(
        term_pieces.astype(jnp.bfloat16), "fsdp", split_axis=0, concat_axis=0, tiled=True
    ).astype(term_pieces.dtype)
    weight_shard = jnp.sum(received, axis=0)
    bit_count = lax.axis_size("rep").bit_length() - 1
    shard_bit = lax.dynamic_index_in_dim(partner_bit, lax.axis_index("fsdp"), 0, keepdims=False)
    norm_bit = partner_bit[0]
    paired_norm = norm_term
    for bit_index in range(bit_count):
        other_norm = partner(norm_term, "rep", bit_index)
        paired_norm = jnp.where(norm_bit == bit_index, 0.5 * (norm_term + other_norm), paired_norm)
    norm_avg = lax.psum(paired_norm, "fsdp")
    weight_avg = weight_shard
    for bit_index in range(bit_count):
        other_weight = partner(weight_shard.astype(jnp.bfloat16), "rep", bit_index).astype(
            weight_shard.dtype
        )
        weight_avg = jnp.where(
            shard_bit == bit_index, 0.5 * (weight_shard + other_weight), weight_avg
        )
    return (block_out, input_grad, weight_avg[None], norm_avg[None])


CORE, ACROSS, ALONG = 1, 2, 4
VMEM_LIMIT = 8 * 1024 * 1024
F32, BF16 = jnp.float32, jnp.bfloat16


def swap(value, axis, mask):
    pairs = [(source, source ^ mask) for source in range(lax.axis_size(axis))]
    return lax.ppermute(value, axis, pairs)


def call(kernel, outs, args, scratch=(), order=(), copies_out=False, outside=()):
    vmem = pl.BlockSpec(memory_space=pltpu.VMEM)
    smem = pl.BlockSpec(memory_space=pltpu.SMEM)
    untouched = pl.BlockSpec(memory_space=pl.ANY)

    def body(*refs):
        kernel(*refs[: len(args)], *refs[len(args) + len(order) :])

    return pl.pallas_call(
        body,
        out_shape=tuple(outs),
        in_specs=[
            untouched if index in outside else smem if a.dtype == jnp.int32 else vmem
            for index, a in enumerate(args)
        ]
        + [untouched] * len(order),
        out_specs=tuple(untouched if copies_out else vmem for _ in outs),
        scratch_shapes=list(scratch),
        compiler_params=pltpu.CompilerParams(vmem_limit_bytes=VMEM_LIMIT),
    )(*args, *order)


def hold(values, order):
    untouched = pl.BlockSpec(memory_space=pl.ANY)
    return pl.pallas_call(
        lambda *refs: None,
        out_shape=tuple(shaped(value.shape, value.dtype) for value in values),
        in_specs=[untouched] * (len(values) + len(order)),
        out_specs=tuple(untouched for _ in values),
        input_output_aliases={index: index for index in range(len(values))},
        compiler_params=pltpu.CompilerParams(vmem_limit_bytes=1024 * 1024),
    )(*values, *order)


def shaped(shape, dtype):
    return jax.ShapeDtypeStruct(shape, dtype)


def matmul(left, right):
    return jnp.dot(left, right, preferred_element_type=F32)


def group_matrix(chans, groups, transpose):
    width = chans // groups
    shape = (128, chans) if transpose else (chans, 128)
    chan = lax.broadcasted_iota(jnp.int32, shape, 1 if transpose else 0)
    low = lax.broadcasted_iota(jnp.int32, shape, 0 if transpose else 1) * width
    return ((chan >= low) & (chan < low + width)).astype(F32)


def group_mean(columns, total, groups):
    chans = columns.shape[1]
    exact = dict(precision=lax.Precision.HIGHEST, preferred_element_type=F32)
    sums = jnp.dot(columns, group_matrix(chans, groups, False), **exact)
    return jnp.dot(sums, group_matrix(chans, groups, True), **exact) * (1.0 / total)


def col_sums(*values):
    rows = [jnp.sum(value, axis=0, keepdims=True) for value in values]
    fill = jnp.zeros((8 - len(rows), rows[0].shape[1]), F32)
    return jnp.concatenate(rows + [fill], axis=0)


def norm_kernel(groups, latent, params, act, stats):
    gain, shift = params[0:1], params[1:2]
    values = latent[...].astype(F32)
    total = values.shape[0] * values.shape[1] // groups
    center = group_mean(col_sums(values), total, groups)[0:1]
    moved = values - center
    spread = group_mean(col_sums(moved * moved), total, groups)[0:1]
    scale_inv = lax.rsqrt(spread + 1e-05)
    pre = moved * scale_inv * gain + shift
    act[...] = (pre / (1.0 + jnp.exp(-pre))).astype(BF16)
    stats[0:1] = center
    stats[1:2] = scale_inv


def tap_matrix(tap, side, transpose):
    shape = (side * side, side * side)
    here = lax.broadcasted_iota(jnp.int32, shape, 1 if transpose else 0)
    there = lax.broadcasted_iota(jnp.int32, shape, 0 if transpose else 1)
    row_off = lax.div(tap, 3)
    col_off = tap - 3 * row_off
    bits = side.bit_length() - 1
    rows = lax.shift_right_logical(there, bits) - lax.shift_right_logical(here, bits)
    cols = (there & (side - 1)) - (here & (side - 1))
    hit = (rows == row_off - 1) & (cols == col_off - 1)
    return hit.astype(F32).astype(BF16)


def prepare_kernel(side, taps, info, own, other, wide, turned, gather, scatter):
    rows, chans = own.shape
    area = side * side
    wide[...] = jnp.zeros_like(wide)
    wide[pl.ds(pl.multiple_of(info[1], 16), rows), :] = own[...]
    wide[pl.ds(pl.multiple_of(info[2], 16), rows), :] = other[...]
    for tap in range(taps):
        part = slice(tap * chans, (tap + 1) * chans)
        turned[part, :] = wide[part, :].T
        gather[tap * area : (tap + 1) * area, :] = tap_matrix(info[0] + tap, side, False)
        scatter[tap * area : (tap + 1) * area, :] = tap_matrix(info[0] + tap, side, True)


def move_into(target, index, taps, matrices, value):
    area, width = value.shape
    moved = matmul(matrices, value).astype(BF16)
    for tap in range(taps):
        target[index * area : (index + 1) * area, tap * width : (tap + 1) * width] = moved[
            tap * area : (tap + 1) * area
        ]


def split_latents(value, refs):
    area = refs[0].shape[0]
    for index, ref in enumerate(refs):
        ref[...] = value[index * area : (index + 1) * area].astype(ref.dtype)


def spread_kernel(taps, scatter, c0, c1, c2, moved):
    for index, ref in enumerate((c0, c1, c2)):
        move_into(moved, index, taps, scatter[...], ref[...])


def grad_kernel(turned, moved, g0, g1, g2):
    split_latents(matmul(moved[...], turned[...]), (g0, g1, g2))


def move_kernel(taps, scatter, top, bottom, moved):
    move_into(moved, 0, taps, scatter[...], jnp.concatenate([top[...], bottom[...]], axis=0))


def weight_kernel(taps, moved, a0, a1, a2, part, across):
    area, chans = a0.shape
    for index, ref in enumerate((a0, a1, a2)):
        across[:, index * area : (index + 1) * area] = ref[...].T
    for tap in range(taps):
        block = slice(tap * chans, (tap + 1) * chans)
        part[block, :] = matmul(across[...], moved[:, block])


def out_kernel(taps, gather, wide, a0, a1, a2, top, bottom, y0, y1, y2, y3, moved):
    last = jnp.concatenate([top[...], bottom[...]], axis=0)
    for index, value in enumerate((a0[...], a1[...], a2[...], last)):
        move_into(moved, index, taps, gather[...], value)
    split_latents(matmul(moved[...], wide[...]), (y0, y1, y2, y3))


def turn_twice(top, bottom, across):
    chans, half = top.shape[1], top.shape[0]
    for start in (0, chans):
        across[start : start + chans, :half] = top[...].T
        across[start : start + chans, half:] = bottom[...].T


def window_terms(start, rows, chans, across, moved, part):
    tap = lax.div(start, chans)
    offset = start - tap * chans
    picked = across[pl.ds(pl.multiple_of(offset, 16), rows), :]
    row = lax.broadcasted_iota(jnp.int32, picked.shape, 0)
    zero = jnp.zeros_like(picked)
    in_first = row < chans - offset
    left = jnp.concatenate(
        [jnp.where(in_first, picked, zero), jnp.where(in_first, zero, picked)], axis=1
    )
    right = jnp.concatenate(
        [moved[:, pl.ds(pl.multiple_of((tap + step) * chans, 128), chans)] for step in range(2)],
        axis=0,
    )
    return part[pl.ds(pl.multiple_of(start, 16), rows), :] + matmul(left, right)


def finish_kernel(factor, info, top, bottom, moved, part, send, across):
    turn_twice(top, bottom, across)
    terms = window_terms(info[2], send.shape[0], top.shape[1], across, moved, part)
    send[...] = (terms * factor).astype(BF16)


def keep_kernel(factor, info, turned, top, bottom, moved, part, keep, g3, across):
    turn_twice(top, bottom, across)
    keep[...] = window_terms(info[1], keep.shape[0], top.shape[1], across, moved, part) * factor
    g3[...] = matmul(moved[...], turned[...]).astype(BF16)


def sum_kernel(y0, y1, y2, y3, total):
    total[...] = (y0[...] + sum(ref[...].astype(F32) for ref in (y1, y2, y3))).astype(BF16)


def join_kernel(keep, got, narrow):
    narrow[...] = (keep[...] + got[...].astype(F32)).astype(BF16)


def pair_kernel(chunks, bit, own, pair1, pair2, mean, made, leave):
    size = own.shape[0] // chunks
    stores = []
    for index in range(chunks):
        rows = pl.ds(index * size, size)

        @pl.when(bit[0] == 0)
        def _():
            made[rows, :] = 0.5 * (own[rows, :].astype(F32) + pair1[rows, :].astype(F32))

        @pl.when(bit[0] != 0)
        def _():
            made[rows, :] = 0.5 * (own[rows, :].astype(F32) + pair2[rows, :].astype(F32))

        stores.append(pltpu.make_async_copy(made.at[rows], mean.at[rows], leave.at[index]))
        stores[-1].start()
    for store in stores:
        store.wait()


def back_kernel(groups, factor, latent, stats, params, g0, g1, g2, g3, grad, terms):
    gain, shift = params[0:1], params[1:2]
    values = latent[...].astype(F32)
    total = values.shape[0] * values.shape[1] // groups
    scale_inv = stats[1:2]
    normed = (values - stats[0:1]) * scale_inv
    pre = normed * gain + shift
    act_grad = g0[...] + sum(ref[...].astype(F32) for ref in (g1, g2, g3))
    sigma = 1.0 / (1.0 + jnp.exp(-pre))
    pre_grad = act_grad * sigma * (1.0 + pre * (1.0 - sigma))
    sums = col_sums(pre_grad * normed, pre_grad)
    terms[...] = sums[0:2] * factor
    means = group_mean(sums * gain, total, groups)
    grad[...] = (scale_inv * (pre_grad * gain - means[1:2] - normed * means[0:1])).astype(BF16)


def shards_plane(latents, cotangent, conv_weight, norm_gain, norm_shift, partner_bit):
    side, chans = latents.shape[1], latents.shape[3]
    area = side * side
    shard_total = lax.axis_size("fsdp")
    inv_batch = 1.0 / shard_total
    place = lax.axis_index("fsdp")
    weight = conv_weight[0]
    rows = weight.shape[0]
    starts = [2 * rows * chip for chip in range(shard_total // 2)]
    taps = max((start % chans + 2 * rows + chans - 1) // chans for start in starts)
    start = 2 * rows * (place // 2)
    first = jnp.minimum(start // chans, 9 - taps)
    offset = start - first * chans
    core = place % 2
    own_start, other_start = offset + rows * core, offset + rows * (1 - core)
    info = jnp.stack([first, own_start, other_start]).astype(jnp.int32)

    def columns(count, dtype=BF16):
        return shaped((count * area, taps * chans), dtype)

    plane, plane_b = shaped((area, chans), F32), shaped((area, chans), BF16)
    window = (taps * chans, chans)

    latent = latents.reshape(area, chans)
    cot0 = cotangent.reshape(area, chans)
    params = jnp.concatenate([norm_gain, norm_shift])
    other_weight = swap(weight, "fsdp", CORE)
    cot1 = swap(cot0, "fsdp", ACROSS)
    cot2 = swap(cot0, "fsdp", ALONG)
    act0, stats = call(
        functools.partial(norm_kernel, GROUPS),
        [plane_b, shaped((2, chans), F32)],
        [latent, params],
    )
    act2 = swap(act0, "fsdp", ALONG)
    act1 = swap(act0, "fsdp", ACROSS)
    wide, turned, gather, scatter = call(
        functools.partial(prepare_kernel, side, taps),
        [shaped(window, BF16)] * 2 + [shaped((taps * area, area), BF16)] * 2,
        [info, weight, other_weight],
        order=[stats],
    )
    (moved,) = call(
        functools.partial(spread_kernel, taps), [columns(3)], [scatter, cot0, cot1, cot2]
    )
    cot1, cot2 = hold([cot1, cot2], [moved])
    grad0, grad1, grad2 = call(grad_kernel, [plane, plane_b, plane_b], [turned, moved])
    half = area // 2
    cot3 = [swap(cot2[:half], "fsdp", ACROSS), swap(cot1[half:], "fsdp", ALONG)]
    act2, act1 = hold([act2, act1], [grad0])
    act3 = [swap(act2[:half], "fsdp", ACROSS), swap(act1[half:], "fsdp", ALONG)]
    (part,) = call(
        functools.partial(weight_kernel, taps),
        [shaped(window, F32)],
        [moved, act0, act1, act2],
        [pltpu.VMEM((chans, 3 * area), BF16)],
    )
    (moved3,) = call(
        functools.partial(move_kernel, taps), [columns(1)], [scatter, *cot3], order=[part]
    )
    (send,) = call(
        functools.partial(finish_kernel, inv_batch),
        [shaped((rows, chans), BF16)],
        [info, *act3, moved3, part],
        [pltpu.VMEM((2 * chans, area), BF16)],
    )
    got = swap(send, "fsdp", CORE)
    keep, grad3 = call(
        functools.partial(keep_kernel, inv_batch),
        [shaped((rows, chans), F32), plane_b],
        [info, turned, *act3, moved3, part],
        [pltpu.VMEM((2 * chans, area), BF16)],
    )
    (narrow,) = call(join_kernel, [shaped((rows, chans), BF16)], [keep, got])
    pair1 = swap(narrow, "rep", 1)
    pair2 = swap(narrow, "rep", 2)

    masks = (ACROSS, ALONG, ACROSS | ALONG)
    grads = hold([grad1, grad2, grad3], [narrow])
    grads = [swap(value, "fsdp", mask) for value, mask in zip(grads, masks)]
    out0, out1, out2, out3 = call(
        functools.partial(out_kernel, taps),
        [plane, plane_b, plane_b, plane_b],
        [gather, wide, act0, act1, act2, *act3],
        [pltpu.VMEM((4 * area, taps * chans), BF16)],
        order=[narrow],
    )
    out1, out2 = hold([out1, out2], [narrow])
    out1, out2 = swap(out1, "fsdp", ACROSS), swap(out2, "fsdp", ALONG)

    input_grad, terms = call(
        functools.partial(back_kernel, GROUPS, inv_batch),
        [plane_b, shaped((2, chans), F32)],
        [latent, stats, params, grad0, *grads],
        order=[out3],
    )
    (last,) = hold([out3], [terms])
    last = swap(last, "fsdp", ACROSS | ALONG)
    terms = terms + swap(terms, "fsdp", ACROSS)
    (terms,) = hold([terms], [out1, out2])
    for mask in (ALONG, CORE):
        terms = terms + swap(terms, "fsdp", mask)
    (block_out,) = call(sum_kernel, [plane_b], [out0, out1, out2, last])
    (terms,) = hold([terms], [block_out])
    norm_avg = lax.cond(
        partner_bit[0] == 0,
        lambda own: 0.5 * (own + swap(own, "rep", 1)),
        lambda own: 0.5 * (own + swap(own, "rep", 2)),
        terms,
    )
    shard_bit = lax.dynamic_slice_in_dim(partner_bit, place, 1)
    (weight_avg,) = call(
        functools.partial(pair_kernel, 5),
        [shaped((rows, chans), F32)],
        [shard_bit, narrow, pair1, pair2],
        [pltpu.VMEM((rows, chans), F32), pltpu.SemaphoreType.DMA((5,))],
        copies_out=True,
    )
    shape = (1, side, side, chans)
    return (block_out.reshape(shape), input_grad.reshape(shape), weight_avg[None], norm_avg[None])


def solution(mesh):
    in_specs = (
        P(("rep", "fsdp"), None, None, None),
        P(("rep", "fsdp"), None, None, None),
        P("rep", "fsdp", None),
        P("rep", None),
        P("rep", None),
        P(),
    )
    out_specs = (
        P(("rep", "fsdp"), None, None, None),
        P(("rep", "fsdp"), None, None, None),
        P("rep", "fsdp", None),
        P("rep", None, None),
    )
    planes = mesh.shape["fsdp"] == 8 and mesh.shape["rep"] == 4
    shards = shards_plane if planes else shards_general
    return jax.shard_map(shards, mesh=mesh, in_specs=in_specs, out_specs=out_specs, check_vma=False)
```

```python
import functools

import jax
import jax.numpy as jnp
from jax import lax
from jax.experimental import pallas as pl
from jax.experimental.pallas import tpu as pltpu
from jax.sharding import PartitionSpec as P

GROUPS = 32


def partner(value, axis, stride):
    mask = 2**stride
    pairs = [(source, source ^ mask) for source in range(lax.axis_size(axis))]
    return lax.ppermute(value, axis, pairs)


def norm_forward(values_in, gain, shift, groups):
    count, side, chans = (values_in.shape[0], values_in.shape[1], values_in.shape[3])
    values = values_in.astype(jnp.float32).reshape(count, side * side, groups, chans // groups)
    center = jnp.mean(values, axis=(1, 3), keepdims=True)
    spread = jnp.mean(jnp.square(values - center), axis=(1, 3), keepdims=True)
    scale_inv = lax.rsqrt(spread + 1e-05)
    normed = (values - center) * scale_inv
    pre_act = normed * gain.reshape(groups, -1) + shift.reshape(groups, -1)
    return (normed, scale_inv, pre_act)


def make_patches(activation):
    count, side, chans = (activation.shape[0], activation.shape[1], activation.shape[3])
    padded = jnp.pad(activation, ((0, 0), (1, 1), (1, 1), (0, 0)))
    pieces = [
        padded[:, row_off : row_off + side, col_off : col_off + side, :]
        for row_off in range(3)
        for col_off in range(3)
    ]
    return jnp.concatenate(pieces, axis=-1).reshape(count * side * side, 9 * chans)


def fold_patches(patch_grad, count, side, chans):
    grads = patch_grad.reshape(count, side, side, 9, chans)
    total = jnp.zeros((count, side + 2, side + 2, chans), jnp.float32)
    for row_off in range(3):
        for col_off in range(3):
            tap = grads[:, :, :, row_off * 3 + col_off, :]
            total = total + jnp.pad(
                tap, ((0, 0), (row_off, 2 - row_off), (col_off, 2 - col_off), (0, 0))
            )
    return total[:, 1:-1, 1:-1, :]


def backward_rest(act_grad, normed, scale_inv, pre_act, gain, groups, inv_batch):
    count, side, chans = (act_grad.shape[0], act_grad.shape[1], act_grad.shape[3])
    act_grad = act_grad.reshape(count, side * side, groups, chans // groups)
    sigma = jax.nn.sigmoid(pre_act)
    pre_grad = act_grad * sigma * (1.0 + pre_act * (1.0 - sigma))
    gain_grad = jnp.sum(pre_grad * normed, axis=(0, 1)).reshape(-1) * inv_batch
    shift_grad = jnp.sum(pre_grad, axis=(0, 1)).reshape(-1) * inv_batch
    normed_grad = pre_grad * gain.reshape(groups, -1)
    first = jnp.mean(normed_grad, axis=(1, 3), keepdims=True)
    second = jnp.mean(normed_grad * normed, axis=(1, 3), keepdims=True)
    input_grad = scale_inv * (normed_grad - first - normed * second)
    return (
        input_grad.reshape(count, side, side, chans).astype(jnp.bfloat16),
        jnp.stack([gain_grad, shift_grad]),
    )


def shards_general(latents, cotangent, conv_weight, norm_gain, norm_shift, partner_bit):
    count, side, chans = (latents.shape[0], latents.shape[1], latents.shape[3])
    shard_total = lax.axis_size("fsdp")
    inv_batch = 1.0 / (count * shard_total)
    gain = norm_gain[0]
    normed, scale_inv, pre_act = norm_forward(latents, gain, norm_shift[0], GROUPS)
    activation = jax.nn.silu(pre_act).astype(jnp.bfloat16).reshape(count, side, side, chans)
    patches = make_patches(activation)
    cot_rows = cotangent.reshape(count * side * side, chans)
    weight_rows = conv_weight[0]
    output = jnp.dot(
        patches,
        lax.all_gather(weight_rows, "fsdp", axis=0, tiled=True),
        preferred_element_type=jnp.float32,
    )
    patch_grad = lax.dot_general(
        cot_rows,
        lax.all_gather(weight_rows, "fsdp", axis=0, tiled=True),
        (((1,), (1,)), ((), ())),
        preferred_element_type=jnp.float32,
    )
    block_out = output.astype(jnp.bfloat16).reshape(count, side, side, chans)
    act_grad = fold_patches(patch_grad, count, side, chans)
    input_grad, norm_term = backward_rest(
        act_grad, normed, scale_inv, pre_act, gain, GROUPS, inv_batch
    )
    weight_term = (
        lax.dot_general(
            patches, cot_rows, (((0,), (0,)), ((), ())), preferred_element_type=jnp.float32
        )
        * inv_batch
    )
    shard_rows = weight_rows.shape[0]
    term_pieces = weight_term.reshape(shard_total, shard_rows, chans)
    received = lax.all_to_all(
        term_pieces.astype(jnp.bfloat16), "fsdp", split_axis=0, concat_axis=0, tiled=True
    ).astype(term_pieces.dtype)
    weight_shard = jnp.sum(received, axis=0)
    bit_count = lax.axis_size("rep").bit_length() - 1
    shard_bit = lax.dynamic_index_in_dim(partner_bit, lax.axis_index("fsdp"), 0, keepdims=False)
    norm_bit = partner_bit[0]
    paired_norm = norm_term
    for bit_index in range(bit_count):
        other_norm = partner(norm_term, "rep", bit_index)
        paired_norm = jnp.where(norm_bit == bit_index, 0.5 * (norm_term + other_norm), paired_norm)
    norm_avg = lax.psum(paired_norm, "fsdp")
    weight_avg = weight_shard
    for bit_index in range(bit_count):
        other_weight = partner(weight_shard.astype(jnp.bfloat16), "rep", bit_index).astype(
            weight_shard.dtype
        )
        weight_avg = jnp.where(
            shard_bit == bit_index, 0.5 * (weight_shard + other_weight), weight_avg
        )
    return (block_out, input_grad, weight_avg[None], norm_avg[None])


CORE, ACROSS, ALONG = 1, 2, 4
VMEM_LIMIT = 12 * 1024 * 1024
F32, BF16 = jnp.float32, jnp.bfloat16


def swap(value, axis, mask):
    pairs = [(source, source ^ mask) for source in range(lax.axis_size(axis))]
    return lax.ppermute(value, axis, pairs)


def call(kernel, outs, args, scratch=(), order=(), copies_out=False, outside=()):
    vmem = pl.BlockSpec(memory_space=pltpu.VMEM)
    smem = pl.BlockSpec(memory_space=pltpu.SMEM)
    untouched = pl.BlockSpec(memory_space=pl.ANY)

    def body(*refs):
        kernel(*refs[: len(args)], *refs[len(args) + len(order) :])

    return pl.pallas_call(
        body,
        out_shape=tuple(outs),
        in_specs=[
            untouched if index in outside else smem if a.dtype == jnp.int32 else vmem
            for index, a in enumerate(args)
        ]
        + [untouched] * len(order),
        out_specs=tuple(untouched if copies_out else vmem for _ in outs),
        scratch_shapes=list(scratch),
        compiler_params=pltpu.CompilerParams(vmem_limit_bytes=VMEM_LIMIT),
    )(*args, *order)


def hold(values, order):
    untouched = pl.BlockSpec(memory_space=pl.ANY)
    return pl.pallas_call(
        lambda *refs: None,
        out_shape=tuple(shaped(value.shape, value.dtype) for value in values),
        in_specs=[untouched] * (len(values) + len(order)),
        out_specs=tuple(untouched for _ in values),
        input_output_aliases={index: index for index in range(len(values))},
        compiler_params=pltpu.CompilerParams(vmem_limit_bytes=1024 * 1024),
    )(*values, *order)


def shaped(shape, dtype):
    return jax.ShapeDtypeStruct(shape, dtype)


def matmul(left, right):
    return jnp.dot(left, right, preferred_element_type=F32)


def group_matrix(chans, groups, transpose):
    width = chans // groups
    shape = (128, chans) if transpose else (chans, 128)
    chan = lax.broadcasted_iota(jnp.int32, shape, 1 if transpose else 0)
    low = lax.broadcasted_iota(jnp.int32, shape, 0 if transpose else 1) * width
    return ((chan >= low) & (chan < low + width)).astype(F32)


def group_mean(columns, total, groups):
    chans = columns.shape[1]
    exact = dict(precision=lax.Precision.HIGHEST, preferred_element_type=F32)
    sums = jnp.dot(columns, group_matrix(chans, groups, False), **exact)
    return jnp.dot(sums, group_matrix(chans, groups, True), **exact) * (1.0 / total)


def col_sums(*values):
    rows = [jnp.sum(value, axis=0, keepdims=True) for value in values]
    fill = jnp.zeros((8 - len(rows), rows[0].shape[1]), F32)
    return jnp.concatenate(rows + [fill], axis=0)


def norm_kernel(groups, latent, params, act, stats):
    gain, shift = params[0:1], params[1:2]
    values = latent[...].astype(F32)
    total = values.shape[0] * values.shape[1] // groups
    center = group_mean(col_sums(values), total, groups)[0:1]
    moved = values - center
    spread = group_mean(col_sums(moved * moved), total, groups)[0:1]
    scale_inv = lax.rsqrt(spread + 1e-05)
    pre = moved * scale_inv * gain + shift
    act[...] = (pre / (1.0 + jnp.exp(-pre))).astype(BF16)
    stats[0:1] = center
    stats[1:2] = scale_inv


def tap_matrix(tap, side, transpose):
    shape = (side * side, side * side)
    here = lax.broadcasted_iota(jnp.int32, shape, 1 if transpose else 0)
    there = lax.broadcasted_iota(jnp.int32, shape, 0 if transpose else 1)
    row_off = lax.div(tap, 3)
    col_off = tap - 3 * row_off
    bits = side.bit_length() - 1
    rows = lax.shift_right_logical(there, bits) - lax.shift_right_logical(here, bits)
    cols = (there & (side - 1)) - (here & (side - 1))
    hit = (rows == row_off - 1) & (cols == col_off - 1)
    return hit.astype(F32).astype(BF16)


def prepare_kernel(side, taps, info, own, other, wide, turned, gather, scatter):
    rows, chans = own.shape
    area = side * side
    wide[...] = jnp.zeros_like(wide)
    wide[pl.ds(pl.multiple_of(info[1], 16), rows), :] = own[...]
    wide[pl.ds(pl.multiple_of(info[2], 16), rows), :] = other[...]
    for tap in range(taps):
        part = slice(tap * chans, (tap + 1) * chans)
        turned[part, :] = wide[part, :].T
        gather[tap * area : (tap + 1) * area, :] = tap_matrix(info[0] + tap, side, False)
        scatter[tap * area : (tap + 1) * area, :] = tap_matrix(info[0] + tap, side, True)


def move_into(target, index, taps, matrices, value):
    area, width = value.shape
    moved = matmul(matrices, value).astype(BF16)
    for tap in range(taps):
        target[index * area : (index + 1) * area, tap * width : (tap + 1) * width] = moved[
            tap * area : (tap + 1) * area
        ]


def split_latents(value, refs):
    area = refs[0].shape[0]
    for index, ref in enumerate(refs):
        ref[...] = value[index * area : (index + 1) * area].astype(ref.dtype)


def spread_kernel(taps, scatter, c0, c1, c2, moved):
    for index, ref in enumerate((c0, c1, c2)):
        move_into(moved, index, taps, scatter[...], ref[...])


def grad_kernel(turned, moved, g0, g1, g2):
    split_latents(matmul(moved[...], turned[...]), (g0, g1, g2))


def move_kernel(taps, scatter, top, bottom, moved):
    move_into(moved, 0, taps, scatter[...], jnp.concatenate([top[...], bottom[...]], axis=0))


def weight_kernel(taps, moved, a0, a1, a2, part, across):
    area, chans = a0.shape
    for index, ref in enumerate((a0, a1, a2)):
        across[:, index * area : (index + 1) * area] = ref[...].T
    for tap in range(taps):
        block = slice(tap * chans, (tap + 1) * chans)
        part[block, :] = matmul(across[...], moved[:, block])


def out_kernel(taps, gather, wide, a0, a1, a2, top, bottom, y0, y1, y2, y3, moved):
    last = jnp.concatenate([top[...], bottom[...]], axis=0)
    for index, value in enumerate((a0[...], a1[...], a2[...], last)):
        move_into(moved, index, taps, gather[...], value)
    split_latents(matmul(moved[...], wide[...]), (y0, y1, y2, y3))


def turn_twice(top, bottom, across):
    chans, half = top.shape[1], top.shape[0]
    for start in (0, chans):
        across[start : start + chans, :half] = top[...].T
        across[start : start + chans, half:] = bottom[...].T


def window_terms(start, rows, chans, across, moved, part):
    tap = lax.div(start, chans)
    offset = start - tap * chans
    picked = across[pl.ds(pl.multiple_of(offset, 16), rows), :]
    row = lax.broadcasted_iota(jnp.int32, picked.shape, 0)
    zero = jnp.zeros_like(picked)
    in_first = row < chans - offset
    left = jnp.concatenate(
        [jnp.where(in_first, picked, zero), jnp.where(in_first, zero, picked)], axis=1
    )
    right = jnp.concatenate(
        [moved[:, pl.ds(pl.multiple_of((tap + step) * chans, 128), chans)] for step in range(2)],
        axis=0,
    )
    return part[pl.ds(pl.multiple_of(start, 16), rows), :] + matmul(left, right)


def finish_kernel(factor, info, top, bottom, moved, part, send, across):
    turn_twice(top, bottom, across)
    terms = window_terms(info[2], send.shape[0], top.shape[1], across, moved, part)
    send[...] = (terms * factor).astype(BF16)


def keep_kernel(factor, info, turned, top, bottom, moved, part, keep, g3, across):
    turn_twice(top, bottom, across)
    keep[...] = window_terms(info[1], keep.shape[0], top.shape[1], across, moved, part) * factor
    g3[...] = matmul(moved[...], turned[...]).astype(BF16)


def sum_kernel(y0, y1, y2, y3, total):
    total[...] = (y0[...] + sum(ref[...].astype(F32) for ref in (y1, y2, y3))).astype(BF16)


def join_kernel(keep, got, narrow):
    narrow[...] = (keep[...] + got[...].astype(F32)).astype(BF16)


def pair_kernel(chunks, bit, own, pair1, pair2, mean, made, got, arrive, leave):
    size = own.shape[0] // chunks
    parts = [pl.ds(index * size, size) for index in range(chunks)]

    def fetch(index):
        rows = parts[index]
        return pltpu.make_async_copy(pair1.at[rows], got.at[rows], arrive.at[index])

    @pl.when(bit[0] == 0)
    def _():
        for index in range(chunks):
            fetch(index).start()

    stores = []
    for index, rows in enumerate(parts):

        @pl.when(bit[0] == 0)
        def _():
            fetch(index).wait()
            made[rows, :] = 0.5 * (own[rows, :].astype(F32) + got[rows, :].astype(F32))

        @pl.when(bit[0] != 0)
        def _():
            made[rows, :] = 0.5 * (own[rows, :].astype(F32) + pair2[rows, :].astype(F32))

        stores.append(pltpu.make_async_copy(made.at[rows], mean.at[rows], leave.at[index]))
        stores[-1].start()
    for store in stores:
        store.wait()


def copy_kernel(source, target):
    target[...] = source[...]


def back_kernel(groups, factor, latent, stats, params, g0, g1, g2, g3, grad, terms):
    gain, shift = params[0:1], params[1:2]
    values = latent[...].astype(F32)
    total = values.shape[0] * values.shape[1] // groups
    scale_inv = stats[1:2]
    normed = (values - stats[0:1]) * scale_inv
    pre = normed * gain + shift
    act_grad = g0[...] + sum(ref[...].astype(F32) for ref in (g1, g2, g3))
    sigma = 1.0 / (1.0 + jnp.exp(-pre))
    pre_grad = act_grad * sigma * (1.0 + pre * (1.0 - sigma))
    sums = col_sums(pre_grad * normed, pre_grad)
    terms[...] = sums[0:2] * factor
    means = group_mean(sums * gain, total, groups)
    grad[...] = (scale_inv * (pre_grad * gain - means[1:2] - normed * means[0:1])).astype(BF16)


def shards_plane(latents, cotangent, conv_weight, norm_gain, norm_shift, partner_bit):
    side, chans = latents.shape[1], latents.shape[3]
    area = side * side
    shard_total = lax.axis_size("fsdp")
    inv_batch = 1.0 / shard_total
    place = lax.axis_index("fsdp")
    weight = conv_weight[0]
    rows = weight.shape[0]
    starts = [2 * rows * chip for chip in range(shard_total // 2)]
    taps = max((start % chans + 2 * rows + chans - 1) // chans for start in starts)
    start = 2 * rows * (place // 2)
    first = jnp.minimum(start // chans, 9 - taps)
    offset = start - first * chans
    core = place % 2
    own_start, other_start = offset + rows * core, offset + rows * (1 - core)
    info = jnp.stack([first, own_start, other_start]).astype(jnp.int32)

    def columns(count, dtype=BF16):
        return shaped((count * area, taps * chans), dtype)

    plane, plane_b = shaped((area, chans), F32), shaped((area, chans), BF16)
    window = (taps * chans, chans)

    latent = latents.reshape(area, chans)
    cot0 = cotangent.reshape(area, chans)
    params = jnp.concatenate([norm_gain, norm_shift])
    other_weight = swap(weight, "fsdp", CORE)
    cot1 = swap(cot0, "fsdp", ACROSS)
    cot2 = swap(cot0, "fsdp", ALONG)
    act0, stats = call(
        functools.partial(norm_kernel, GROUPS),
        [plane_b, shaped((2, chans), F32)],
        [latent, params],
    )
    act2 = swap(act0, "fsdp", ALONG)
    act1 = swap(act0, "fsdp", ACROSS)
    wide, turned, gather, scatter = call(
        functools.partial(prepare_kernel, side, taps),
        [shaped(window, BF16)] * 2 + [shaped((taps * area, area), BF16)] * 2,
        [info, weight, other_weight],
        order=[stats],
    )
    (moved,) = call(
        functools.partial(spread_kernel, taps), [columns(3)], [scatter, cot0, cot1, cot2]
    )
    cot1, cot2 = hold([cot1, cot2], [moved])
    grad0, grad1, grad2 = call(grad_kernel, [plane, plane_b, plane_b], [turned, moved])
    half = area // 2
    cot3 = [swap(cot2[:half], "fsdp", ACROSS), swap(cot1[half:], "fsdp", ALONG)]
    act2, act1 = hold([act2, act1], [grad0])
    act3 = [swap(act2[:half], "fsdp", ACROSS), swap(act1[half:], "fsdp", ALONG)]
    (part,) = call(
        functools.partial(weight_kernel, taps),
        [shaped(window, F32)],
        [moved, act0, act1, act2],
        [pltpu.VMEM((chans, 3 * area), BF16)],
    )
    (moved3,) = call(
        functools.partial(move_kernel, taps), [columns(1)], [scatter, *cot3], order=[part]
    )
    (send,) = call(
        functools.partial(finish_kernel, inv_batch),
        [shaped((rows, chans), BF16)],
        [info, *act3, moved3, part],
        [pltpu.VMEM((2 * chans, area), BF16)],
    )
    got = swap(send, "fsdp", CORE)
    keep, grad3 = call(
        functools.partial(keep_kernel, inv_batch),
        [shaped((rows, chans), F32), plane_b],
        [info, turned, *act3, moved3, part],
        [pltpu.VMEM((2 * chans, area), BF16)],
    )
    (narrow,) = call(join_kernel, [shaped((rows, chans), BF16)], [keep, got])
    pair1 = swap(narrow, "rep", 1)
    pair2 = swap(narrow, "rep", 2)

    masks = (ACROSS, ALONG, ACROSS | ALONG)
    grads = hold([grad1, grad2, grad3], [narrow])
    grads = [swap(value, "fsdp", mask) for value, mask in zip(grads, masks)]
    out0, out1, out2, out3 = call(
        functools.partial(out_kernel, taps),
        [plane, plane_b, plane_b, plane_b],
        [gather, wide, act0, act1, act2, *act3],
        [pltpu.VMEM((4 * area, taps * chans), BF16)],
        order=[narrow],
    )
    out1, out2 = hold([out1, out2], [narrow])
    out1, out2 = swap(out1, "fsdp", ACROSS), swap(out2, "fsdp", ALONG)

    input_grad, terms = call(
        functools.partial(back_kernel, GROUPS, inv_batch),
        [plane_b, shaped((2, chans), F32)],
        [latent, stats, params, grad0, *grads],
        order=[out3],
    )
    (last,) = hold([out3], [terms])
    last = swap(last, "fsdp", ACROSS | ALONG)
    terms = terms + swap(terms, "fsdp", ACROSS)
    (terms,) = hold([terms], [out1, out2])
    for mask in (ALONG, CORE):
        terms = terms + swap(terms, "fsdp", mask)
    (block_out,) = call(sum_kernel, [plane_b], [out0, out1, out2, last])
    (terms,) = hold([terms], [block_out])
    norm_avg = lax.cond(
        partner_bit[0] == 0,
        lambda own: 0.5 * (own + swap(own, "rep", 1)),
        lambda own: 0.5 * (own + swap(own, "rep", 2)),
        terms,
    )
    shard_bit = lax.dynamic_slice_in_dim(partner_bit, place, 1)
    (weight_avg,) = call(
        functools.partial(pair_kernel, 9),
        [shaped((rows, chans), F32)],
        [shard_bit, narrow, pair1, pair2],
        [
            pltpu.VMEM((rows, chans), F32),
            pltpu.VMEM((rows, chans), BF16),
            pltpu.SemaphoreType.DMA((9,)),
            pltpu.SemaphoreType.DMA((9,)),
        ],
        copies_out=True,
        outside=(2,),
    )
    shape = (1, side, side, chans)
    return (block_out.reshape(shape), input_grad.reshape(shape), weight_avg[None], norm_avg[None])


def solution(mesh):
    in_specs = (
        P(("rep", "fsdp"), None, None, None),
        P(("rep", "fsdp"), None, None, None),
        P("rep", "fsdp", None),
        P("rep", None),
        P("rep", None),
        P(),
    )
    out_specs = (
        P(("rep", "fsdp"), None, None, None),
        P(("rep", "fsdp"), None, None, None),
        P("rep", "fsdp", None),
        P("rep", None, None),
    )
    planes = mesh.shape["fsdp"] == 8 and mesh.shape["rep"] == 4
    shards = shards_plane if planes else shards_general
    return jax.shard_map(shards, mesh=mesh, in_specs=in_specs, out_specs=out_specs, check_vma=False)
```

```python
import functools

import jax
import jax.numpy as jnp
from jax import lax
from jax.experimental import pallas as pl
from jax.experimental.pallas import tpu as pltpu
from jax.sharding import PartitionSpec as P

GROUPS = 32


def partner(value, axis, stride):
    mask = 2**stride
    pairs = [(source, source ^ mask) for source in range(lax.axis_size(axis))]
    return lax.ppermute(value, axis, pairs)


def norm_forward(values_in, gain, shift, groups):
    count, side, chans = (values_in.shape[0], values_in.shape[1], values_in.shape[3])
    values = values_in.astype(jnp.float32).reshape(count, side * side, groups, chans // groups)
    center = jnp.mean(values, axis=(1, 3), keepdims=True)
    spread = jnp.mean(jnp.square(values - center), axis=(1, 3), keepdims=True)
    scale_inv = lax.rsqrt(spread + 1e-05)
    normed = (values - center) * scale_inv
    pre_act = normed * gain.reshape(groups, -1) + shift.reshape(groups, -1)
    return (normed, scale_inv, pre_act)


def make_patches(activation):
    count, side, chans = (activation.shape[0], activation.shape[1], activation.shape[3])
    padded = jnp.pad(activation, ((0, 0), (1, 1), (1, 1), (0, 0)))
    pieces = [
        padded[:, row_off : row_off + side, col_off : col_off + side, :]
        for row_off in range(3)
        for col_off in range(3)
    ]
    return jnp.concatenate(pieces, axis=-1).reshape(count * side * side, 9 * chans)


def fold_patches(patch_grad, count, side, chans):
    grads = patch_grad.reshape(count, side, side, 9, chans)
    total = jnp.zeros((count, side + 2, side + 2, chans), jnp.float32)
    for row_off in range(3):
        for col_off in range(3):
            tap = grads[:, :, :, row_off * 3 + col_off, :]
            total = total + jnp.pad(
                tap, ((0, 0), (row_off, 2 - row_off), (col_off, 2 - col_off), (0, 0))
            )
    return total[:, 1:-1, 1:-1, :]


def backward_rest(act_grad, normed, scale_inv, pre_act, gain, groups, inv_batch):
    count, side, chans = (act_grad.shape[0], act_grad.shape[1], act_grad.shape[3])
    act_grad = act_grad.reshape(count, side * side, groups, chans // groups)
    sigma = jax.nn.sigmoid(pre_act)
    pre_grad = act_grad * sigma * (1.0 + pre_act * (1.0 - sigma))
    gain_grad = jnp.sum(pre_grad * normed, axis=(0, 1)).reshape(-1) * inv_batch
    shift_grad = jnp.sum(pre_grad, axis=(0, 1)).reshape(-1) * inv_batch
    normed_grad = pre_grad * gain.reshape(groups, -1)
    first = jnp.mean(normed_grad, axis=(1, 3), keepdims=True)
    second = jnp.mean(normed_grad * normed, axis=(1, 3), keepdims=True)
    input_grad = scale_inv * (normed_grad - first - normed * second)
    return (
        input_grad.reshape(count, side, side, chans).astype(jnp.bfloat16),
        jnp.stack([gain_grad, shift_grad]),
    )


def shards_general(latents, cotangent, conv_weight, norm_gain, norm_shift, partner_bit):
    count, side, chans = (latents.shape[0], latents.shape[1], latents.shape[3])
    shard_total = lax.axis_size("fsdp")
    inv_batch = 1.0 / (count * shard_total)
    gain = norm_gain[0]
    normed, scale_inv, pre_act = norm_forward(latents, gain, norm_shift[0], GROUPS)
    activation = jax.nn.silu(pre_act).astype(jnp.bfloat16).reshape(count, side, side, chans)
    patches = make_patches(activation)
    cot_rows = cotangent.reshape(count * side * side, chans)
    weight_rows = conv_weight[0]
    output = jnp.dot(
        patches,
        lax.all_gather(weight_rows, "fsdp", axis=0, tiled=True),
        preferred_element_type=jnp.float32,
    )
    patch_grad = lax.dot_general(
        cot_rows,
        lax.all_gather(weight_rows, "fsdp", axis=0, tiled=True),
        (((1,), (1,)), ((), ())),
        preferred_element_type=jnp.float32,
    )
    block_out = output.astype(jnp.bfloat16).reshape(count, side, side, chans)
    act_grad = fold_patches(patch_grad, count, side, chans)
    input_grad, norm_term = backward_rest(
        act_grad, normed, scale_inv, pre_act, gain, GROUPS, inv_batch
    )
    weight_term = (
        lax.dot_general(
            patches, cot_rows, (((0,), (0,)), ((), ())), preferred_element_type=jnp.float32
        )
        * inv_batch
    )
    shard_rows = weight_rows.shape[0]
    term_pieces = weight_term.reshape(shard_total, shard_rows, chans)
    received = lax.all_to_all(
        term_pieces.astype(jnp.bfloat16), "fsdp", split_axis=0, concat_axis=0, tiled=True
    ).astype(term_pieces.dtype)
    weight_shard = jnp.sum(received, axis=0)
    bit_count = lax.axis_size("rep").bit_length() - 1
    shard_bit = lax.dynamic_index_in_dim(partner_bit, lax.axis_index("fsdp"), 0, keepdims=False)
    norm_bit = partner_bit[0]
    paired_norm = norm_term
    for bit_index in range(bit_count):
        other_norm = partner(norm_term, "rep", bit_index)
        paired_norm = jnp.where(norm_bit == bit_index, 0.5 * (norm_term + other_norm), paired_norm)
    norm_avg = lax.psum(paired_norm, "fsdp")
    weight_avg = weight_shard
    for bit_index in range(bit_count):
        other_weight = partner(weight_shard.astype(jnp.bfloat16), "rep", bit_index).astype(
            weight_shard.dtype
        )
        weight_avg = jnp.where(
            shard_bit == bit_index, 0.5 * (weight_shard + other_weight), weight_avg
        )
    return (block_out, input_grad, weight_avg[None], norm_avg[None])


CORE, ACROSS, ALONG = 1, 2, 4
VMEM_LIMIT = 12 * 1024 * 1024
F32, BF16 = jnp.float32, jnp.bfloat16


def swap(value, axis, mask):
    pairs = [(source, source ^ mask) for source in range(lax.axis_size(axis))]
    return lax.ppermute(value, axis, pairs)


def call(kernel, outs, args, scratch=(), order=(), copies_out=False, outside=()):
    vmem = pl.BlockSpec(memory_space=pltpu.VMEM)
    smem = pl.BlockSpec(memory_space=pltpu.SMEM)
    untouched = pl.BlockSpec(memory_space=pl.ANY)

    def body(*refs):
        kernel(*refs[: len(args)], *refs[len(args) + len(order) :])

    return pl.pallas_call(
        body,
        out_shape=tuple(outs),
        in_specs=[
            untouched if index in outside else smem if a.dtype == jnp.int32 else vmem
            for index, a in enumerate(args)
        ]
        + [untouched] * len(order),
        out_specs=tuple(untouched if copies_out else vmem for _ in outs),
        scratch_shapes=list(scratch),
        compiler_params=pltpu.CompilerParams(vmem_limit_bytes=VMEM_LIMIT),
    )(*args, *order)


def hold(values, order):
    untouched = pl.BlockSpec(memory_space=pl.ANY)
    return pl.pallas_call(
        lambda *refs: None,
        out_shape=tuple(shaped(value.shape, value.dtype) for value in values),
        in_specs=[untouched] * (len(values) + len(order)),
        out_specs=tuple(untouched for _ in values),
        input_output_aliases={index: index for index in range(len(values))},
        compiler_params=pltpu.CompilerParams(vmem_limit_bytes=1024 * 1024),
    )(*values, *order)


def shaped(shape, dtype):
    return jax.ShapeDtypeStruct(shape, dtype)


def matmul(left, right):
    return jnp.dot(left, right, preferred_element_type=F32)


def group_matrix(chans, groups, transpose):
    width = chans // groups
    shape = (128, chans) if transpose else (chans, 128)
    chan = lax.broadcasted_iota(jnp.int32, shape, 1 if transpose else 0)
    low = lax.broadcasted_iota(jnp.int32, shape, 0 if transpose else 1) * width
    return ((chan >= low) & (chan < low + width)).astype(F32)


def group_mean(columns, total, groups):
    chans = columns.shape[1]
    exact = dict(precision=lax.Precision.HIGHEST, preferred_element_type=F32)
    sums = jnp.dot(columns, group_matrix(chans, groups, False), **exact)
    return jnp.dot(sums, group_matrix(chans, groups, True), **exact) * (1.0 / total)


def col_sums(*values):
    rows = [jnp.sum(value, axis=0, keepdims=True) for value in values]
    fill = jnp.zeros((8 - len(rows), rows[0].shape[1]), F32)
    return jnp.concatenate(rows + [fill], axis=0)


def norm_kernel(groups, latent, params, act, stats):
    gain, shift = params[0:1], params[1:2]
    values = latent[...].astype(F32)
    total = values.shape[0] * values.shape[1] // groups
    center = group_mean(col_sums(values), total, groups)[0:1]
    moved = values - center
    spread = group_mean(col_sums(moved * moved), total, groups)[0:1]
    scale_inv = lax.rsqrt(spread + 1e-05)
    pre = moved * scale_inv * gain + shift
    act[...] = (pre / (1.0 + jnp.exp(-pre))).astype(BF16)
    stats[0:1] = center
    stats[1:2] = scale_inv


def tap_matrix(tap, side, transpose):
    shape = (side * side, side * side)
    here = lax.broadcasted_iota(jnp.int32, shape, 1 if transpose else 0)
    there = lax.broadcasted_iota(jnp.int32, shape, 0 if transpose else 1)
    row_off = lax.div(tap, 3)
    col_off = tap - 3 * row_off
    bits = side.bit_length() - 1
    rows = lax.shift_right_logical(there, bits) - lax.shift_right_logical(here, bits)
    cols = (there & (side - 1)) - (here & (side - 1))
    hit = (rows == row_off - 1) & (cols == col_off - 1)
    return hit.astype(F32).astype(BF16)


def prepare_kernel(side, taps, info, own, other, wide, turned, gather, scatter):
    rows, chans = own.shape
    area = side * side
    wide[...] = jnp.zeros_like(wide)
    wide[pl.ds(pl.multiple_of(info[1], 16), rows), :] = own[...]
    wide[pl.ds(pl.multiple_of(info[2], 16), rows), :] = other[...]
    for tap in range(taps):
        part = slice(tap * chans, (tap + 1) * chans)
        turned[part, :] = wide[part, :].T
        gather[tap * area : (tap + 1) * area, :] = tap_matrix(info[0] + tap, side, False)
        scatter[tap * area : (tap + 1) * area, :] = tap_matrix(info[0] + tap, side, True)


def move_into(target, index, taps, matrices, value):
    area, width = value.shape
    moved = matmul(matrices, value).astype(BF16)
    for tap in range(taps):
        target[index * area : (index + 1) * area, tap * width : (tap + 1) * width] = moved[
            tap * area : (tap + 1) * area
        ]


def split_latents(value, refs):
    area = refs[0].shape[0]
    for index, ref in enumerate(refs):
        ref[...] = value[index * area : (index + 1) * area].astype(ref.dtype)


def spread_kernel(taps, scatter, c0, c1, c2, moved):
    for index, ref in enumerate((c0, c1, c2)):
        move_into(moved, index, taps, scatter[...], ref[...])


def grad_kernel(turned, moved, g0, g1, g2):
    split_latents(matmul(moved[...], turned[...]), (g0, g1, g2))


def move_kernel(taps, scatter, top, bottom, moved):
    move_into(moved, 0, taps, scatter[...], jnp.concatenate([top[...], bottom[...]], axis=0))


def weight_kernel(taps, moved, a0, a1, a2, part, across):
    area, chans = a0.shape
    for index, ref in enumerate((a0, a1, a2)):
        across[:, index * area : (index + 1) * area] = ref[...].T
    for tap in range(taps):
        block = slice(tap * chans, (tap + 1) * chans)
        part[block, :] = matmul(across[...], moved[:, block])


def out_kernel(taps, gather, wide, a0, a1, a2, top, bottom, y0, y1, y2, y3, moved):
    last = jnp.concatenate([top[...], bottom[...]], axis=0)
    for index, value in enumerate((a0[...], a1[...], a2[...], last)):
        move_into(moved, index, taps, gather[...], value)
    split_latents(matmul(moved[...], wide[...]), (y0, y1, y2, y3))


def turn_twice(top, bottom, across):
    chans, half = top.shape[1], top.shape[0]
    for start in (0, chans):
        across[start : start + chans, :half] = top[...].T
        across[start : start + chans, half:] = bottom[...].T


def window_terms(start, rows, chans, across, moved, part):
    tap = lax.div(start, chans)
    offset = start - tap * chans
    picked = across[pl.ds(pl.multiple_of(offset, 16), rows), :]
    row = lax.broadcasted_iota(jnp.int32, picked.shape, 0)
    zero = jnp.zeros_like(picked)
    in_first = row < chans - offset
    left = jnp.concatenate(
        [jnp.where(in_first, picked, zero), jnp.where(in_first, zero, picked)], axis=1
    )
    right = jnp.concatenate(
        [moved[:, pl.ds(pl.multiple_of((tap + step) * chans, 128), chans)] for step in range(2)],
        axis=0,
    )
    return part[pl.ds(pl.multiple_of(start, 16), rows), :] + matmul(left, right)


def finish_kernel(factor, info, top, bottom, moved, part, send, across):
    turn_twice(top, bottom, across)
    terms = window_terms(info[2], send.shape[0], top.shape[1], across, moved, part)
    send[...] = (terms * factor).astype(BF16)


def keep_kernel(factor, info, turned, top, bottom, moved, part, keep, g3, across):
    turn_twice(top, bottom, across)
    keep[...] = window_terms(info[1], keep.shape[0], top.shape[1], across, moved, part) * factor
    g3[...] = matmul(moved[...], turned[...]).astype(BF16)


def sum_kernel(y0, y1, y2, y3, total):
    total[...] = (y0[...] + sum(ref[...].astype(F32) for ref in (y1, y2, y3))).astype(BF16)


def join_kernel(keep, got, narrow):
    narrow[...] = (keep[...] + got[...].astype(F32)).astype(BF16)


def pair_kernel(chunks, bit, own, pair1, pair2, mean, made, got, arrive, leave):
    size = own.shape[0] // chunks
    parts = [pl.ds(index * size, size) for index in range(chunks)]

    def fetch(index):
        rows = parts[index]
        return pltpu.make_async_copy(pair1.at[rows], got.at[rows], arrive.at[index])

    @pl.when(bit[0] == 0)
    def _():
        for index in range(chunks):
            fetch(index).start()

    stores = []
    for index, rows in enumerate(parts):

        @pl.when(bit[0] == 0)
        def _():
            fetch(index).wait()
            made[rows, :] = 0.5 * (own[rows, :].astype(F32) + got[rows, :].astype(F32))

        @pl.when(bit[0] != 0)
        def _():
            made[rows, :] = 0.5 * (own[rows, :].astype(F32) + pair2[rows, :].astype(F32))

        stores.append(pltpu.make_async_copy(made.at[rows], mean.at[rows], leave.at[index]))
        stores[-1].start()
    for store in stores:
        store.wait()


def copy_kernel(source, target):
    target[...] = source[...]


def back_kernel(groups, factor, latent, stats, params, g0, g1, g2, g3, grad, terms):
    gain, shift = params[0:1], params[1:2]
    values = latent[...].astype(F32)
    total = values.shape[0] * values.shape[1] // groups
    scale_inv = stats[1:2]
    normed = (values - stats[0:1]) * scale_inv
    pre = normed * gain + shift
    act_grad = g0[...] + sum(ref[...].astype(F32) for ref in (g1, g2, g3))
    sigma = 1.0 / (1.0 + jnp.exp(-pre))
    pre_grad = act_grad * sigma * (1.0 + pre * (1.0 - sigma))
    sums = col_sums(pre_grad * normed, pre_grad)
    terms[...] = sums[0:2] * factor
    means = group_mean(sums * gain, total, groups)
    grad[...] = (scale_inv * (pre_grad * gain - means[1:2] - normed * means[0:1])).astype(BF16)


def shards_plane(latents, cotangent, conv_weight, norm_gain, norm_shift, partner_bit):
    side, chans = latents.shape[1], latents.shape[3]
    area = side * side
    shard_total = lax.axis_size("fsdp")
    inv_batch = 1.0 / shard_total
    place = lax.axis_index("fsdp")
    weight = conv_weight[0]
    rows = weight.shape[0]
    starts = [2 * rows * chip for chip in range(shard_total // 2)]
    taps = max((start % chans + 2 * rows + chans - 1) // chans for start in starts)
    start = 2 * rows * (place // 2)
    first = jnp.minimum(start // chans, 9 - taps)
    offset = start - first * chans
    core = place % 2
    own_start, other_start = offset + rows * core, offset + rows * (1 - core)
    info = jnp.stack([first, own_start, other_start]).astype(jnp.int32)

    def columns(count, dtype=BF16):
        return shaped((count * area, taps * chans), dtype)

    plane, plane_b = shaped((area, chans), F32), shaped((area, chans), BF16)
    window = (taps * chans, chans)

    latent = latents.reshape(area, chans)
    cot0 = cotangent.reshape(area, chans)
    params = jnp.concatenate([norm_gain, norm_shift])
    other_weight = swap(weight, "fsdp", CORE)
    cot1 = swap(cot0, "fsdp", ACROSS)
    cot2 = swap(cot0, "fsdp", ALONG)
    act0, stats = call(
        functools.partial(norm_kernel, GROUPS),
        [plane_b, shaped((2, chans), F32)],
        [latent, params],
    )
    act2 = swap(act0, "fsdp", ALONG)
    act1 = swap(act0, "fsdp", ACROSS)
    wide, turned, gather, scatter = call(
        functools.partial(prepare_kernel, side, taps),
        [shaped(window, BF16)] * 2 + [shaped((taps * area, area), BF16)] * 2,
        [info, weight, other_weight],
        order=[stats],
    )
    (moved,) = call(
        functools.partial(spread_kernel, taps), [columns(3)], [scatter, cot0, cot1, cot2]
    )
    cot1, cot2 = hold([cot1, cot2], [moved])
    grad0, grad1, grad2 = call(grad_kernel, [plane, plane_b, plane_b], [turned, moved])
    half = area // 2
    cot3 = [swap(cot2[:half], "fsdp", ACROSS), swap(cot1[half:], "fsdp", ALONG)]
    act2, act1 = hold([act2, act1], [grad0])
    act3 = [swap(act2[:half], "fsdp", ACROSS), swap(act1[half:], "fsdp", ALONG)]
    (part,) = call(
        functools.partial(weight_kernel, taps),
        [shaped(window, F32)],
        [moved, act0, act1, act2],
        [pltpu.VMEM((chans, 3 * area), BF16)],
    )
    (moved3,) = call(
        functools.partial(move_kernel, taps), [columns(1)], [scatter, *cot3], order=[part]
    )
    (send,) = call(
        functools.partial(finish_kernel, inv_batch),
        [shaped((rows, chans), BF16)],
        [info, *act3, moved3, part],
        [pltpu.VMEM((2 * chans, area), BF16)],
    )
    got = swap(send, "fsdp", CORE)
    keep, grad3 = call(
        functools.partial(keep_kernel, inv_batch),
        [shaped((rows, chans), F32), plane_b],
        [info, turned, *act3, moved3, part],
        [pltpu.VMEM((2 * chans, area), BF16)],
    )
    (narrow,) = call(join_kernel, [shaped((rows, chans), BF16)], [keep, got])
    pair1 = swap(narrow, "rep", 1)
    pair2 = swap(narrow, "rep", 2)

    masks = (ACROSS, ALONG, ACROSS | ALONG)
    grads = hold([grad1, grad2, grad3], [narrow])
    grads = [swap(value, "fsdp", mask) for value, mask in zip(grads, masks)]
    out0, out1, out2, out3 = call(
        functools.partial(out_kernel, taps),
        [plane, plane_b, plane_b, plane_b],
        [gather, wide, act0, act1, act2, *act3],
        [pltpu.VMEM((4 * area, taps * chans), BF16)],
        order=[narrow],
    )
    out1, out2 = hold([out1, out2], [narrow])
    out1, out2 = swap(out1, "fsdp", ACROSS), swap(out2, "fsdp", ALONG)

    input_grad, terms = call(
        functools.partial(back_kernel, GROUPS, inv_batch),
        [plane_b, shaped((2, chans), F32)],
        [latent, stats, params, grad0, *grads],
        order=[out3],
    )
    (last,) = hold([out3], [terms])
    last = swap(last, "fsdp", ACROSS | ALONG)
    terms = terms + swap(terms, "fsdp", ACROSS)
    (terms,) = hold([terms], [out1, out2])
    for mask in (ALONG, CORE):
        terms = terms + swap(terms, "fsdp", mask)
    (block_out,) = call(sum_kernel, [plane_b], [out0, out1, out2, last])
    (terms,) = hold([terms], [block_out])
    norm_avg = lax.cond(
        partner_bit[0] == 0,
        lambda own: 0.5 * (own + swap(own, "rep", 1)),
        lambda own: 0.5 * (own + swap(own, "rep", 2)),
        terms,
    )
    shard_bit = lax.dynamic_slice_in_dim(partner_bit, place, 1)
    (weight_avg,) = call(
        functools.partial(pair_kernel, 3),
        [shaped((rows, chans), F32)],
        [shard_bit, narrow, pair1, pair2],
        [
            pltpu.VMEM((rows, chans), F32),
            pltpu.VMEM((rows, chans), BF16),
            pltpu.SemaphoreType.DMA((3,)),
            pltpu.SemaphoreType.DMA((3,)),
        ],
        copies_out=True,
        outside=(2,),
    )
    shape = (1, side, side, chans)
    return (block_out.reshape(shape), input_grad.reshape(shape), weight_avg[None], norm_avg[None])


def solution(mesh):
    in_specs = (
        P(("rep", "fsdp"), None, None, None),
        P(("rep", "fsdp"), None, None, None),
        P("rep", "fsdp", None),
        P("rep", None),
        P("rep", None),
        P(),
    )
    out_specs = (
        P(("rep", "fsdp"), None, None, None),
        P(("rep", "fsdp"), None, None, None),
        P("rep", "fsdp", None),
        P("rep", None, None),
    )
    planes = mesh.shape["fsdp"] == 8 and mesh.shape["rep"] == 4
    shards = shards_plane if planes else shards_general
    return jax.shard_map(shards, mesh=mesh, in_specs=in_specs, out_specs=out_specs, check_vma=False)
```

```python
import functools

import jax
import jax.numpy as jnp
from jax import lax
from jax.experimental import pallas as pl
from jax.experimental.pallas import tpu as pltpu
from jax.sharding import PartitionSpec as P

GROUPS = 32


def partner(value, axis, stride):
    mask = 2**stride
    pairs = [(source, source ^ mask) for source in range(lax.axis_size(axis))]
    return lax.ppermute(value, axis, pairs)


def norm_forward(values_in, gain, shift, groups):
    count, side, chans = (values_in.shape[0], values_in.shape[1], values_in.shape[3])
    values = values_in.astype(jnp.float32).reshape(count, side * side, groups, chans // groups)
    center = jnp.mean(values, axis=(1, 3), keepdims=True)
    spread = jnp.mean(jnp.square(values - center), axis=(1, 3), keepdims=True)
    scale_inv = lax.rsqrt(spread + 1e-05)
    normed = (values - center) * scale_inv
    pre_act = normed * gain.reshape(groups, -1) + shift.reshape(groups, -1)
    return (normed, scale_inv, pre_act)


def make_patches(activation):
    count, side, chans = (activation.shape[0], activation.shape[1], activation.shape[3])
    padded = jnp.pad(activation, ((0, 0), (1, 1), (1, 1), (0, 0)))
    pieces = [
        padded[:, row_off : row_off + side, col_off : col_off + side, :]
        for row_off in range(3)
        for col_off in range(3)
    ]
    return jnp.concatenate(pieces, axis=-1).reshape(count * side * side, 9 * chans)


def fold_patches(patch_grad, count, side, chans):
    grads = patch_grad.reshape(count, side, side, 9, chans)
    total = jnp.zeros((count, side + 2, side + 2, chans), jnp.float32)
    for row_off in range(3):
        for col_off in range(3):
            tap = grads[:, :, :, row_off * 3 + col_off, :]
            total = total + jnp.pad(
                tap, ((0, 0), (row_off, 2 - row_off), (col_off, 2 - col_off), (0, 0))
            )
    return total[:, 1:-1, 1:-1, :]


def backward_rest(act_grad, normed, scale_inv, pre_act, gain, groups, inv_batch):
    count, side, chans = (act_grad.shape[0], act_grad.shape[1], act_grad.shape[3])
    act_grad = act_grad.reshape(count, side * side, groups, chans // groups)
    sigma = jax.nn.sigmoid(pre_act)
    pre_grad = act_grad * sigma * (1.0 + pre_act * (1.0 - sigma))
    gain_grad = jnp.sum(pre_grad * normed, axis=(0, 1)).reshape(-1) * inv_batch
    shift_grad = jnp.sum(pre_grad, axis=(0, 1)).reshape(-1) * inv_batch
    normed_grad = pre_grad * gain.reshape(groups, -1)
    first = jnp.mean(normed_grad, axis=(1, 3), keepdims=True)
    second = jnp.mean(normed_grad * normed, axis=(1, 3), keepdims=True)
    input_grad = scale_inv * (normed_grad - first - normed * second)
    return (
        input_grad.reshape(count, side, side, chans).astype(jnp.bfloat16),
        jnp.stack([gain_grad, shift_grad]),
    )


def shards_general(latents, cotangent, conv_weight, norm_gain, norm_shift, partner_bit):
    count, side, chans = (latents.shape[0], latents.shape[1], latents.shape[3])
    shard_total = lax.axis_size("fsdp")
    inv_batch = 1.0 / (count * shard_total)
    gain = norm_gain[0]
    normed, scale_inv, pre_act = norm_forward(latents, gain, norm_shift[0], GROUPS)
    activation = jax.nn.silu(pre_act).astype(jnp.bfloat16).reshape(count, side, side, chans)
    patches = make_patches(activation)
    cot_rows = cotangent.reshape(count * side * side, chans)
    weight_rows = conv_weight[0]
    output = jnp.dot(
        patches,
        lax.all_gather(weight_rows, "fsdp", axis=0, tiled=True),
        preferred_element_type=jnp.float32,
    )
    patch_grad = lax.dot_general(
        cot_rows,
        lax.all_gather(weight_rows, "fsdp", axis=0, tiled=True),
        (((1,), (1,)), ((), ())),
        preferred_element_type=jnp.float32,
    )
    block_out = output.astype(jnp.bfloat16).reshape(count, side, side, chans)
    act_grad = fold_patches(patch_grad, count, side, chans)
    input_grad, norm_term = backward_rest(
        act_grad, normed, scale_inv, pre_act, gain, GROUPS, inv_batch
    )
    weight_term = (
        lax.dot_general(
            patches, cot_rows, (((0,), (0,)), ((), ())), preferred_element_type=jnp.float32
        )
        * inv_batch
    )
    shard_rows = weight_rows.shape[0]
    term_pieces = weight_term.reshape(shard_total, shard_rows, chans)
    received = lax.all_to_all(
        term_pieces.astype(jnp.bfloat16), "fsdp", split_axis=0, concat_axis=0, tiled=True
    ).astype(term_pieces.dtype)
    weight_shard = jnp.sum(received, axis=0)
    bit_count = lax.axis_size("rep").bit_length() - 1
    shard_bit = lax.dynamic_index_in_dim(partner_bit, lax.axis_index("fsdp"), 0, keepdims=False)
    norm_bit = partner_bit[0]
    paired_norm = norm_term
    for bit_index in range(bit_count):
        other_norm = partner(norm_term, "rep", bit_index)
        paired_norm = jnp.where(norm_bit == bit_index, 0.5 * (norm_term + other_norm), paired_norm)
    norm_avg = lax.psum(paired_norm, "fsdp")
    weight_avg = weight_shard
    for bit_index in range(bit_count):
        other_weight = partner(weight_shard.astype(jnp.bfloat16), "rep", bit_index).astype(
            weight_shard.dtype
        )
        weight_avg = jnp.where(
            shard_bit == bit_index, 0.5 * (weight_shard + other_weight), weight_avg
        )
    return (block_out, input_grad, weight_avg[None], norm_avg[None])


CORE, ACROSS, ALONG = 1, 2, 4
VMEM_LIMIT = 12 * 1024 * 1024
F32, BF16 = jnp.float32, jnp.bfloat16


def swap(value, axis, mask):
    pairs = [(source, source ^ mask) for source in range(lax.axis_size(axis))]
    return lax.ppermute(value, axis, pairs)


def call(kernel, outs, args, scratch=(), order=(), copies_out=False, outside=()):
    vmem = pl.BlockSpec(memory_space=pltpu.VMEM)
    smem = pl.BlockSpec(memory_space=pltpu.SMEM)
    untouched = pl.BlockSpec(memory_space=pl.ANY)

    def body(*refs):
        kernel(*refs[: len(args)], *refs[len(args) + len(order) :])

    return pl.pallas_call(
        body,
        out_shape=tuple(outs),
        in_specs=[
            untouched if index in outside else smem if a.dtype == jnp.int32 else vmem
            for index, a in enumerate(args)
        ]
        + [untouched] * len(order),
        out_specs=tuple(untouched if copies_out else vmem for _ in outs),
        scratch_shapes=list(scratch),
        compiler_params=pltpu.CompilerParams(vmem_limit_bytes=VMEM_LIMIT),
    )(*args, *order)


def hold(values, order):
    untouched = pl.BlockSpec(memory_space=pl.ANY)
    return pl.pallas_call(
        lambda *refs: None,
        out_shape=tuple(shaped(value.shape, value.dtype) for value in values),
        in_specs=[untouched] * (len(values) + len(order)),
        out_specs=tuple(untouched for _ in values),
        input_output_aliases={index: index for index in range(len(values))},
        compiler_params=pltpu.CompilerParams(vmem_limit_bytes=1024 * 1024),
    )(*values, *order)


def shaped(shape, dtype):
    return jax.ShapeDtypeStruct(shape, dtype)


def matmul(left, right):
    return jnp.dot(left, right, preferred_element_type=F32)


def group_matrix(chans, groups, transpose):
    width = chans // groups
    shape = (128, chans) if transpose else (chans, 128)
    chan = lax.broadcasted_iota(jnp.int32, shape, 1 if transpose else 0)
    low = lax.broadcasted_iota(jnp.int32, shape, 0 if transpose else 1) * width
    return ((chan >= low) & (chan < low + width)).astype(F32)


def group_mean(columns, total, groups):
    chans = columns.shape[1]
    exact = dict(precision=lax.Precision.HIGHEST, preferred_element_type=F32)
    sums = jnp.dot(columns, group_matrix(chans, groups, False), **exact)
    return jnp.dot(sums, group_matrix(chans, groups, True), **exact) * (1.0 / total)


def col_sums(*values):
    rows = [jnp.sum(value, axis=0, keepdims=True) for value in values]
    fill = jnp.zeros((8 - len(rows), rows[0].shape[1]), F32)
    return jnp.concatenate(rows + [fill], axis=0)


def norm_kernel(groups, latent, params, act, stats):
    gain, shift = params[0:1], params[1:2]
    values = latent[...].astype(F32)
    total = values.shape[0] * values.shape[1] // groups
    center = group_mean(col_sums(values), total, groups)[0:1]
    moved = values - center
    spread = group_mean(col_sums(moved * moved), total, groups)[0:1]
    scale_inv = lax.rsqrt(spread + 1e-05)
    pre = moved * scale_inv * gain + shift
    act[...] = (pre / (1.0 + jnp.exp(-pre))).astype(BF16)
    stats[0:1] = center
    stats[1:2] = scale_inv


def tap_matrix(tap, side, transpose):
    shape = (side * side, side * side)
    here = lax.broadcasted_iota(jnp.int32, shape, 1 if transpose else 0)
    there = lax.broadcasted_iota(jnp.int32, shape, 0 if transpose else 1)
    row_off = lax.div(tap, 3)
    col_off = tap - 3 * row_off
    bits = side.bit_length() - 1
    rows = lax.shift_right_logical(there, bits) - lax.shift_right_logical(here, bits)
    cols = (there & (side - 1)) - (here & (side - 1))
    hit = (rows == row_off - 1) & (cols == col_off - 1)
    return hit.astype(F32).astype(BF16)


def prepare_kernel(side, taps, info, own, other, wide, turned, gather, scatter):
    rows, chans = own.shape
    area = side * side
    wide[...] = jnp.zeros_like(wide)
    wide[pl.ds(pl.multiple_of(info[1], 16), rows), :] = own[...]
    wide[pl.ds(pl.multiple_of(info[2], 16), rows), :] = other[...]
    for tap in range(taps):
        part = slice(tap * chans, (tap + 1) * chans)
        turned[part, :] = wide[part, :].T
        gather[tap * area : (tap + 1) * area, :] = tap_matrix(info[0] + tap, side, False)
        scatter[tap * area : (tap + 1) * area, :] = tap_matrix(info[0] + tap, side, True)


def move_into(target, index, taps, matrices, value):
    area, width = value.shape
    moved = matmul(matrices, value).astype(BF16)
    for tap in range(taps):
        target[index * area : (index + 1) * area, tap * width : (tap + 1) * width] = moved[
            tap * area : (tap + 1) * area
        ]


def split_latents(value, refs):
    area = refs[0].shape[0]
    for index, ref in enumerate(refs):
        ref[...] = value[index * area : (index + 1) * area].astype(ref.dtype)


def spread_kernel(taps, scatter, c0, c1, c2, moved):
    for index, ref in enumerate((c0, c1, c2)):
        move_into(moved, index, taps, scatter[...], ref[...])


def grad_kernel(turned, moved, g0, g1, g2):
    split_latents(matmul(moved[...], turned[...]), (g0, g1, g2))


def move_kernel(taps, scatter, top, bottom, moved):
    move_into(moved, 0, taps, scatter[...], jnp.concatenate([top[...], bottom[...]], axis=0))


def weight_kernel(taps, moved, a0, a1, a2, part, across):
    area, chans = a0.shape
    for index, ref in enumerate((a0, a1, a2)):
        across[:, index * area : (index + 1) * area] = ref[...].T
    for tap in range(taps):
        block = slice(tap * chans, (tap + 1) * chans)
        part[block, :] = matmul(across[...], moved[:, block])


def out_kernel(taps, gather, wide, a0, a1, a2, top, bottom, y0, y1, y2, y3, moved):
    last = jnp.concatenate([top[...], bottom[...]], axis=0)
    for index, value in enumerate((a0[...], a1[...], a2[...], last)):
        move_into(moved, index, taps, gather[...], value)
    split_latents(matmul(moved[...], wide[...]), (y0, y1, y2, y3))


def turn_twice(top, bottom, across):
    chans, half = top.shape[1], top.shape[0]
    left, right = top[...].T, bottom[...].T
    for start in (0, chans):
        across[start : start + chans, :half] = left
        across[start : start + chans, half:] = right


def window_terms(start, rows, chans, across, moved, part):
    tap = lax.div(start, chans)
    offset = start - tap * chans
    picked = across[pl.ds(pl.multiple_of(offset, 16), rows), :]
    row = lax.broadcasted_iota(jnp.int32, picked.shape, 0)
    zero = jnp.zeros_like(picked)
    in_first = row < chans - offset
    left = jnp.concatenate(
        [jnp.where(in_first, picked, zero), jnp.where(in_first, zero, picked)], axis=1
    )
    right = jnp.concatenate(
        [moved[:, pl.ds(pl.multiple_of((tap + step) * chans, 128), chans)] for step in range(2)],
        axis=0,
    )
    return part[pl.ds(pl.multiple_of(start, 16), rows), :] + matmul(left, right)


def finish_kernel(factor, info, top, bottom, moved, part, send, across):
    turn_twice(top, bottom, across)
    terms = window_terms(info[2], send.shape[0], top.shape[1], across, moved, part)
    send[...] = (terms * factor).astype(BF16)


def keep_kernel(factor, info, turned, top, bottom, moved, part, keep, g3, across):
    turn_twice(top, bottom, across)
    keep[...] = window_terms(info[1], keep.shape[0], top.shape[1], across, moved, part) * factor
    g3[...] = matmul(moved[...], turned[...]).astype(BF16)


def sum_kernel(y0, y1, y2, y3, total):
    total[...] = (y0[...] + sum(ref[...].astype(F32) for ref in (y1, y2, y3))).astype(BF16)


def join_kernel(keep, got, narrow):
    narrow[...] = (keep[...] + got[...].astype(F32)).astype(BF16)


def pair_kernel(chunks, bit, own, pair1, pair2, mean, made, got, arrive, leave):
    size = own.shape[0] // chunks
    parts = [pl.ds(index * size, size) for index in range(chunks)]

    def fetch(index):
        rows = parts[index]
        return pltpu.make_async_copy(pair1.at[rows], got.at[rows], arrive.at[index])

    @pl.when(bit[0] == 0)
    def _():
        for index in range(chunks):
            fetch(index).start()

    stores = []
    for index, rows in enumerate(parts):

        @pl.when(bit[0] == 0)
        def _():
            fetch(index).wait()
            made[rows, :] = 0.5 * (own[rows, :].astype(F32) + got[rows, :].astype(F32))

        @pl.when(bit[0] != 0)
        def _():
            made[rows, :] = 0.5 * (own[rows, :].astype(F32) + pair2[rows, :].astype(F32))

        stores.append(pltpu.make_async_copy(made.at[rows], mean.at[rows], leave.at[index]))
        stores[-1].start()
    for store in stores:
        store.wait()


def copy_kernel(source, target):
    target[...] = source[...]


def back_kernel(groups, factor, latent, stats, params, g0, g1, g2, g3, grad, terms):
    gain, shift = params[0:1], params[1:2]
    values = latent[...].astype(F32)
    total = values.shape[0] * values.shape[1] // groups
    scale_inv = stats[1:2]
    normed = (values - stats[0:1]) * scale_inv
    pre = normed * gain + shift
    act_grad = g0[...] + sum(ref[...].astype(F32) for ref in (g1, g2, g3))
    sigma = 1.0 / (1.0 + jnp.exp(-pre))
    pre_grad = act_grad * sigma * (1.0 + pre * (1.0 - sigma))
    sums = col_sums(pre_grad * normed, pre_grad)
    terms[...] = sums[0:2] * factor
    means = group_mean(sums * gain, total, groups)
    grad[...] = (scale_inv * (pre_grad * gain - means[1:2] - normed * means[0:1])).astype(BF16)


def shards_plane(latents, cotangent, conv_weight, norm_gain, norm_shift, partner_bit):
    side, chans = latents.shape[1], latents.shape[3]
    area = side * side
    shard_total = lax.axis_size("fsdp")
    inv_batch = 1.0 / shard_total
    place = lax.axis_index("fsdp")
    weight = conv_weight[0]
    rows = weight.shape[0]
    starts = [2 * rows * chip for chip in range(shard_total // 2)]
    taps = max((start % chans + 2 * rows + chans - 1) // chans for start in starts)
    start = 2 * rows * (place // 2)
    first = jnp.minimum(start // chans, 9 - taps)
    offset = start - first * chans
    core = place % 2
    own_start, other_start = offset + rows * core, offset + rows * (1 - core)
    info = jnp.stack([first, own_start, other_start]).astype(jnp.int32)

    def columns(count, dtype=BF16):
        return shaped((count * area, taps * chans), dtype)

    plane, plane_b = shaped((area, chans), F32), shaped((area, chans), BF16)
    window = (taps * chans, chans)

    latent = latents.reshape(area, chans)
    cot0 = cotangent.reshape(area, chans)
    params = jnp.concatenate([norm_gain, norm_shift])
    other_weight = swap(weight, "fsdp", CORE)
    cot1 = swap(cot0, "fsdp", ACROSS)
    cot2 = swap(cot0, "fsdp", ALONG)
    act0, stats = call(
        functools.partial(norm_kernel, GROUPS),
        [plane_b, shaped((2, chans), F32)],
        [latent, params],
    )
    act2 = swap(act0, "fsdp", ALONG)
    act1 = swap(act0, "fsdp", ACROSS)
    wide, turned, gather, scatter = call(
        functools.partial(prepare_kernel, side, taps),
        [shaped(window, BF16)] * 2 + [shaped((taps * area, area), BF16)] * 2,
        [info, weight, other_weight],
        order=[stats],
    )
    (moved,) = call(
        functools.partial(spread_kernel, taps), [columns(3)], [scatter, cot0, cot1, cot2]
    )
    cot1, cot2 = hold([cot1, cot2], [moved])
    grad0, grad1, grad2 = call(grad_kernel, [plane, plane_b, plane_b], [turned, moved])
    half = area // 2
    cot3 = [swap(cot2[:half], "fsdp", ACROSS), swap(cot1[half:], "fsdp", ALONG)]
    act2, act1 = hold([act2, act1], [grad0])
    act3 = [swap(act2[:half], "fsdp", ACROSS), swap(act1[half:], "fsdp", ALONG)]
    (part,) = call(
        functools.partial(weight_kernel, taps),
        [shaped(window, F32)],
        [moved, act0, act1, act2],
        [pltpu.VMEM((chans, 3 * area), BF16)],
    )
    (moved3,) = call(
        functools.partial(move_kernel, taps), [columns(1)], [scatter, *cot3], order=[part]
    )
    (send,) = call(
        functools.partial(finish_kernel, inv_batch),
        [shaped((rows, chans), BF16)],
        [info, *act3, moved3, part],
        [pltpu.VMEM((2 * chans, area), BF16)],
    )
    got = swap(send, "fsdp", CORE)
    keep, grad3 = call(
        functools.partial(keep_kernel, inv_batch),
        [shaped((rows, chans), F32), plane_b],
        [info, turned, *act3, moved3, part],
        [pltpu.VMEM((2 * chans, area), BF16)],
    )
    (narrow,) = call(join_kernel, [shaped((rows, chans), BF16)], [keep, got])
    pair1 = swap(narrow, "rep", 1)
    pair2 = swap(narrow, "rep", 2)

    masks = (ACROSS, ALONG, ACROSS | ALONG)
    grads = hold([grad1, grad2, grad3], [narrow])
    grads = [swap(value, "fsdp", mask) for value, mask in zip(grads, masks)]
    out0, out1, out2, out3 = call(
        functools.partial(out_kernel, taps),
        [plane, plane_b, plane_b, plane_b],
        [gather, wide, act0, act1, act2, *act3],
        [pltpu.VMEM((4 * area, taps * chans), BF16)],
        order=[narrow],
    )
    out1, out2 = hold([out1, out2], [narrow])
    out1, out2 = swap(out1, "fsdp", ACROSS), swap(out2, "fsdp", ALONG)

    input_grad, terms = call(
        functools.partial(back_kernel, GROUPS, inv_batch),
        [plane_b, shaped((2, chans), F32)],
        [latent, stats, params, grad0, *grads],
        order=[out3],
    )
    (last,) = hold([out3], [terms])
    last = swap(last, "fsdp", ACROSS | ALONG)
    terms = terms + swap(terms, "fsdp", ACROSS)
    (terms,) = hold([terms], [out1, out2])
    for mask in (ALONG, CORE):
        terms = terms + swap(terms, "fsdp", mask)
    (block_out,) = call(sum_kernel, [plane_b], [out0, out1, out2, last])
    (terms,) = hold([terms], [block_out])
    norm_avg = lax.cond(
        partner_bit[0] == 0,
        lambda own: 0.5 * (own + swap(own, "rep", 1)),
        lambda own: 0.5 * (own + swap(own, "rep", 2)),
        terms,
    )
    shard_bit = lax.dynamic_slice_in_dim(partner_bit, place, 1)
    (weight_avg,) = call(
        functools.partial(pair_kernel, 9),
        [shaped((rows, chans), F32)],
        [shard_bit, narrow, pair1, pair2],
        [
            pltpu.VMEM((rows, chans), F32),
            pltpu.VMEM((rows, chans), BF16),
            pltpu.SemaphoreType.DMA((9,)),
            pltpu.SemaphoreType.DMA((9,)),
        ],
        copies_out=True,
        outside=(2,),
    )
    shape = (1, side, side, chans)
    return (block_out.reshape(shape), input_grad.reshape(shape), weight_avg[None], norm_avg[None])


def solution(mesh):
    in_specs = (
        P(("rep", "fsdp"), None, None, None),
        P(("rep", "fsdp"), None, None, None),
        P("rep", "fsdp", None),
        P("rep", None),
        P("rep", None),
        P(),
    )
    out_specs = (
        P(("rep", "fsdp"), None, None, None),
        P(("rep", "fsdp"), None, None, None),
        P("rep", "fsdp", None),
        P("rep", None, None),
    )
    planes = mesh.shape["fsdp"] == 8 and mesh.shape["rep"] == 4
    shards = shards_plane if planes else shards_general
    return jax.shard_map(shards, mesh=mesh, in_specs=in_specs, out_specs=out_specs, check_vma=False)
```

```python
import functools

import jax
import jax.numpy as jnp
from jax import lax
from jax.experimental import pallas as pl
from jax.experimental.pallas import tpu as pltpu
from jax.sharding import PartitionSpec as P

GROUPS = 32


def partner(value, axis, stride):
    mask = 2**stride
    pairs = [(source, source ^ mask) for source in range(lax.axis_size(axis))]
    return lax.ppermute(value, axis, pairs)


def norm_forward(values_in, gain, shift, groups):
    count, side, chans = (values_in.shape[0], values_in.shape[1], values_in.shape[3])
    values = values_in.astype(jnp.float32).reshape(count, side * side, groups, chans // groups)
    center = jnp.mean(values, axis=(1, 3), keepdims=True)
    spread = jnp.mean(jnp.square(values - center), axis=(1, 3), keepdims=True)
    scale_inv = lax.rsqrt(spread + 1e-05)
    normed = (values - center) * scale_inv
    pre_act = normed * gain.reshape(groups, -1) + shift.reshape(groups, -1)
    return (normed, scale_inv, pre_act)


def make_patches(activation):
    count, side, chans = (activation.shape[0], activation.shape[1], activation.shape[3])
    padded = jnp.pad(activation, ((0, 0), (1, 1), (1, 1), (0, 0)))
    pieces = [
        padded[:, row_off : row_off + side, col_off : col_off + side, :]
        for row_off in range(3)
        for col_off in range(3)
    ]
    return jnp.concatenate(pieces, axis=-1).reshape(count * side * side, 9 * chans)


def fold_patches(patch_grad, count, side, chans):
    grads = patch_grad.reshape(count, side, side, 9, chans)
    total = jnp.zeros((count, side + 2, side + 2, chans), jnp.float32)
    for row_off in range(3):
        for col_off in range(3):
            tap = grads[:, :, :, row_off * 3 + col_off, :]
            total = total + jnp.pad(
                tap, ((0, 0), (row_off, 2 - row_off), (col_off, 2 - col_off), (0, 0))
            )
    return total[:, 1:-1, 1:-1, :]


def backward_rest(act_grad, normed, scale_inv, pre_act, gain, groups, inv_batch):
    count, side, chans = (act_grad.shape[0], act_grad.shape[1], act_grad.shape[3])
    act_grad = act_grad.reshape(count, side * side, groups, chans // groups)
    sigma = jax.nn.sigmoid(pre_act)
    pre_grad = act_grad * sigma * (1.0 + pre_act * (1.0 - sigma))
    gain_grad = jnp.sum(pre_grad * normed, axis=(0, 1)).reshape(-1) * inv_batch
    shift_grad = jnp.sum(pre_grad, axis=(0, 1)).reshape(-1) * inv_batch
    normed_grad = pre_grad * gain.reshape(groups, -1)
    first = jnp.mean(normed_grad, axis=(1, 3), keepdims=True)
    second = jnp.mean(normed_grad * normed, axis=(1, 3), keepdims=True)
    input_grad = scale_inv * (normed_grad - first - normed * second)
    return (
        input_grad.reshape(count, side, side, chans).astype(jnp.bfloat16),
        jnp.stack([gain_grad, shift_grad]),
    )


def shards_general(latents, cotangent, conv_weight, norm_gain, norm_shift, partner_bit):
    count, side, chans = (latents.shape[0], latents.shape[1], latents.shape[3])
    shard_total = lax.axis_size("fsdp")
    inv_batch = 1.0 / (count * shard_total)
    gain = norm_gain[0]
    normed, scale_inv, pre_act = norm_forward(latents, gain, norm_shift[0], GROUPS)
    activation = jax.nn.silu(pre_act).astype(jnp.bfloat16).reshape(count, side, side, chans)
    patches = make_patches(activation)
    cot_rows = cotangent.reshape(count * side * side, chans)
    weight_rows = conv_weight[0]
    output = jnp.dot(
        patches,
        lax.all_gather(weight_rows, "fsdp", axis=0, tiled=True),
        preferred_element_type=jnp.float32,
    )
    patch_grad = lax.dot_general(
        cot_rows,
        lax.all_gather(weight_rows, "fsdp", axis=0, tiled=True),
        (((1,), (1,)), ((), ())),
        preferred_element_type=jnp.float32,
    )
    block_out = output.astype(jnp.bfloat16).reshape(count, side, side, chans)
    act_grad = fold_patches(patch_grad, count, side, chans)
    input_grad, norm_term = backward_rest(
        act_grad, normed, scale_inv, pre_act, gain, GROUPS, inv_batch
    )
    weight_term = (
        lax.dot_general(
            patches, cot_rows, (((0,), (0,)), ((), ())), preferred_element_type=jnp.float32
        )
        * inv_batch
    )
    shard_rows = weight_rows.shape[0]
    term_pieces = weight_term.reshape(shard_total, shard_rows, chans)
    received = lax.all_to_all(
        term_pieces.astype(jnp.bfloat16), "fsdp", split_axis=0, concat_axis=0, tiled=True
    ).astype(term_pieces.dtype)
    weight_shard = jnp.sum(received, axis=0)
    bit_count = lax.axis_size("rep").bit_length() - 1
    shard_bit = lax.dynamic_index_in_dim(partner_bit, lax.axis_index("fsdp"), 0, keepdims=False)
    norm_bit = partner_bit[0]
    paired_norm = norm_term
    for bit_index in range(bit_count):
        other_norm = partner(norm_term, "rep", bit_index)
        paired_norm = jnp.where(norm_bit == bit_index, 0.5 * (norm_term + other_norm), paired_norm)
    norm_avg = lax.psum(paired_norm, "fsdp")
    weight_avg = weight_shard
    for bit_index in range(bit_count):
        other_weight = partner(weight_shard.astype(jnp.bfloat16), "rep", bit_index).astype(
            weight_shard.dtype
        )
        weight_avg = jnp.where(
            shard_bit == bit_index, 0.5 * (weight_shard + other_weight), weight_avg
        )
    return (block_out, input_grad, weight_avg[None], norm_avg[None])


CORE, ACROSS, ALONG = 1, 2, 4
VMEM_LIMIT = 12 * 1024 * 1024
F32, BF16 = jnp.float32, jnp.bfloat16


def swap(value, axis, mask):
    pairs = [(source, source ^ mask) for source in range(lax.axis_size(axis))]
    return lax.ppermute(value, axis, pairs)


def call(kernel, outs, args, scratch=(), order=(), copies_out=False, outside=()):
    vmem = pl.BlockSpec(memory_space=pltpu.VMEM)
    smem = pl.BlockSpec(memory_space=pltpu.SMEM)
    untouched = pl.BlockSpec(memory_space=pl.ANY)

    def body(*refs):
        kernel(*refs[: len(args)], *refs[len(args) + len(order) :])

    return pl.pallas_call(
        body,
        out_shape=tuple(outs),
        in_specs=[
            untouched if index in outside else smem if a.dtype == jnp.int32 else vmem
            for index, a in enumerate(args)
        ]
        + [untouched] * len(order),
        out_specs=tuple(untouched if copies_out else vmem for _ in outs),
        scratch_shapes=list(scratch),
        compiler_params=pltpu.CompilerParams(vmem_limit_bytes=VMEM_LIMIT),
    )(*args, *order)


def hold(values, order):
    untouched = pl.BlockSpec(memory_space=pl.ANY)
    return pl.pallas_call(
        lambda *refs: None,
        out_shape=tuple(shaped(value.shape, value.dtype) for value in values),
        in_specs=[untouched] * (len(values) + len(order)),
        out_specs=tuple(untouched for _ in values),
        input_output_aliases={index: index for index in range(len(values))},
        compiler_params=pltpu.CompilerParams(vmem_limit_bytes=1024 * 1024),
    )(*values, *order)


def shaped(shape, dtype):
    return jax.ShapeDtypeStruct(shape, dtype)


def matmul(left, right):
    return jnp.dot(left, right, preferred_element_type=F32)


def group_matrix(chans, groups, transpose):
    width = chans // groups
    shape = (128, chans) if transpose else (chans, 128)
    chan = lax.broadcasted_iota(jnp.int32, shape, 1 if transpose else 0)
    low = lax.broadcasted_iota(jnp.int32, shape, 0 if transpose else 1) * width
    return ((chan >= low) & (chan < low + width)).astype(F32)


def group_mean(columns, total, groups):
    chans = columns.shape[1]
    exact = dict(precision=lax.Precision.HIGHEST, preferred_element_type=F32)
    sums = jnp.dot(columns, group_matrix(chans, groups, False), **exact)
    return jnp.dot(sums, group_matrix(chans, groups, True), **exact) * (1.0 / total)


def col_sums(*values):
    rows = [jnp.sum(value, axis=0, keepdims=True) for value in values]
    fill = jnp.zeros((8 - len(rows), rows[0].shape[1]), F32)
    return jnp.concatenate(rows + [fill], axis=0)


def norm_kernel(groups, latent, params, act, stats):
    gain, shift = params[0:1], params[1:2]
    values = latent[...].astype(F32)
    total = values.shape[0] * values.shape[1] // groups
    center = group_mean(col_sums(values), total, groups)[0:1]
    moved = values - center
    spread = group_mean(col_sums(moved * moved), total, groups)[0:1]
    scale_inv = lax.rsqrt(spread + 1e-05)
    pre = moved * scale_inv * gain + shift
    act[...] = (pre / (1.0 + jnp.exp(-pre))).astype(BF16)
    stats[0:1] = center
    stats[1:2] = scale_inv


def tap_matrix(tap, side, transpose):
    shape = (side * side, side * side)
    here = lax.broadcasted_iota(jnp.int32, shape, 1 if transpose else 0)
    there = lax.broadcasted_iota(jnp.int32, shape, 0 if transpose else 1)
    row_off = lax.div(tap, 3)
    col_off = tap - 3 * row_off
    bits = side.bit_length() - 1
    rows = lax.shift_right_logical(there, bits) - lax.shift_right_logical(here, bits)
    cols = (there & (side - 1)) - (here & (side - 1))
    hit = (rows == row_off - 1) & (cols == col_off - 1)
    return hit.astype(F32).astype(BF16)


def prepare_kernel(side, taps, info, own, other, wide, turned, gather, scatter):
    rows, chans = own.shape
    area = side * side
    wide[...] = jnp.zeros_like(wide)
    wide[pl.ds(pl.multiple_of(info[1], 16), rows), :] = own[...]
    wide[pl.ds(pl.multiple_of(info[2], 16), rows), :] = other[...]
    for tap in range(taps):
        part = slice(tap * chans, (tap + 1) * chans)
        turned[part, :] = wide[part, :].T
        gather[tap * area : (tap + 1) * area, :] = tap_matrix(info[0] + tap, side, False)
        scatter[tap * area : (tap + 1) * area, :] = tap_matrix(info[0] + tap, side, True)


def move_into(target, index, taps, matrices, value):
    area, width = value.shape
    moved = matmul(matrices, value).astype(BF16)
    for tap in range(taps):
        target[index * area : (index + 1) * area, tap * width : (tap + 1) * width] = moved[
            tap * area : (tap + 1) * area
        ]


def split_latents(value, refs):
    area = refs[0].shape[0]
    for index, ref in enumerate(refs):
        ref[...] = value[index * area : (index + 1) * area].astype(ref.dtype)


def spread_kernel(taps, scatter, c0, c1, c2, moved):
    for index, ref in enumerate((c0, c1, c2)):
        move_into(moved, index, taps, scatter[...], ref[...])


def grad_kernel(turned, moved, g0, g1, g2):
    split_latents(matmul(moved[...], turned[...]), (g0, g1, g2))


def move_kernel(taps, scatter, top, bottom, moved):
    move_into(moved, 0, taps, scatter[...], jnp.concatenate([top[...], bottom[...]], axis=0))


def weight_kernel(taps, moved, a0, a1, a2, part, across):
    area, chans = a0.shape
    for index, ref in enumerate((a0, a1, a2)):
        across[:, index * area : (index + 1) * area] = ref[...].T
    for tap in range(taps):
        block = slice(tap * chans, (tap + 1) * chans)
        part[block, :] = matmul(across[...], moved[:, block])


def out_kernel(taps, gather, wide, a0, a1, a2, top, bottom, y0, y1, y2, y3, moved):
    last = jnp.concatenate([top[...], bottom[...]], axis=0)
    for index, value in enumerate((a0[...], a1[...], a2[...], last)):
        move_into(moved, index, taps, gather[...], value)
    split_latents(matmul(moved[...], wide[...]), (y0, y1, y2, y3))


def turn_twice(top, bottom, across):
    chans, half = top.shape[1], top.shape[0]
    for start in (0, chans):
        across[start : start + chans, :half] = top[...].T
        across[start : start + chans, half:] = bottom[...].T


def window_terms(start, rows, chans, across, moved, part):
    tap = lax.div(start, chans)
    offset = start - tap * chans
    picked = across[pl.ds(pl.multiple_of(offset, 16), rows), :]
    row = lax.broadcasted_iota(jnp.int32, picked.shape, 0)
    zero = jnp.zeros_like(picked)
    in_first = row < chans - offset
    left = jnp.concatenate(
        [jnp.where(in_first, picked, zero), jnp.where(in_first, zero, picked)], axis=1
    )
    right = jnp.concatenate(
        [moved[:, pl.ds(pl.multiple_of((tap + step) * chans, 128), chans)] for step in range(2)],
        axis=0,
    )
    return part[pl.ds(pl.multiple_of(start, 16), rows), :] + matmul(left, right)


def finish_kernel(factor, info, top, bottom, moved, part, upper, lower, across):
    turn_twice(top, bottom, across)
    split, rows = upper.shape[0], upper.shape[0] + lower.shape[0]
    terms = window_terms(info[2], rows, top.shape[1], across, moved, part) * factor
    upper[...] = terms[:split].astype(BF16)
    lower[...] = terms[split:].astype(BF16)


def keep_kernel(factor, info, top, bottom, moved, part, keep, across):
    turn_twice(top, bottom, across)
    keep[...] = window_terms(info[1], keep.shape[0], top.shape[1], across, moved, part) * factor


def diagonal_kernel(turned, moved, g3):
    g3[...] = matmul(moved[...], turned[...]).astype(BF16)


def sum_kernel(y0, y1, y2, y3, total):
    total[...] = (y0[...] + sum(ref[...].astype(F32) for ref in (y1, y2, y3))).astype(BF16)


def join_kernel(keep, upper, lower, narrow):
    split = upper.shape[0]
    narrow[:split] = (keep[:split] + upper[...].astype(F32)).astype(BF16)
    narrow[split:] = (keep[split:] + lower[...].astype(F32)).astype(BF16)


def pair_kernel(chunks, bit, own, pair1, pair2, mean, made, got, arrive, leave):
    size = own.shape[0] // chunks
    parts = [pl.ds(index * size, size) for index in range(chunks)]

    def fetch(index):
        rows = parts[index]
        return pltpu.make_async_copy(pair1.at[rows], got.at[rows], arrive.at[index])

    @pl.when(bit[0] == 0)
    def _():
        for index in range(chunks):
            fetch(index).start()

    stores = []
    for index, rows in enumerate(parts):

        @pl.when(bit[0] == 0)
        def _():
            fetch(index).wait()
            made[rows, :] = 0.5 * (own[rows, :].astype(F32) + got[rows, :].astype(F32))

        @pl.when(bit[0] != 0)
        def _():
            made[rows, :] = 0.5 * (own[rows, :].astype(F32) + pair2[rows, :].astype(F32))

        stores.append(pltpu.make_async_copy(made.at[rows], mean.at[rows], leave.at[index]))
        stores[-1].start()
    for store in stores:
        store.wait()


def copy_kernel(source, target):
    target[...] = source[...]


def back_kernel(groups, factor, latent, stats, params, g0, g1, g2, g3, grad, terms):
    gain, shift = params[0:1], params[1:2]
    values = latent[...].astype(F32)
    total = values.shape[0] * values.shape[1] // groups
    scale_inv = stats[1:2]
    normed = (values - stats[0:1]) * scale_inv
    pre = normed * gain + shift
    act_grad = g0[...] + sum(ref[...].astype(F32) for ref in (g1, g2, g3))
    sigma = 1.0 / (1.0 + jnp.exp(-pre))
    pre_grad = act_grad * sigma * (1.0 + pre * (1.0 - sigma))
    sums = col_sums(pre_grad * normed, pre_grad)
    terms[...] = sums[0:2] * factor
    means = group_mean(sums * gain, total, groups)
    grad[...] = (scale_inv * (pre_grad * gain - means[1:2] - normed * means[0:1])).astype(BF16)


def shards_plane(latents, cotangent, conv_weight, norm_gain, norm_shift, partner_bit):
    side, chans = latents.shape[1], latents.shape[3]
    area = side * side
    shard_total = lax.axis_size("fsdp")
    inv_batch = 1.0 / shard_total
    place = lax.axis_index("fsdp")
    weight = conv_weight[0]
    rows = weight.shape[0]
    starts = [2 * rows * chip for chip in range(shard_total // 2)]
    taps = max((start % chans + 2 * rows + chans - 1) // chans for start in starts)
    start = 2 * rows * (place // 2)
    first = jnp.minimum(start // chans, 9 - taps)
    offset = start - first * chans
    core = place % 2
    own_start, other_start = offset + rows * core, offset + rows * (1 - core)
    info = jnp.stack([first, own_start, other_start]).astype(jnp.int32)

    def columns(count, dtype=BF16):
        return shaped((count * area, taps * chans), dtype)

    plane, plane_b = shaped((area, chans), F32), shaped((area, chans), BF16)
    window = (taps * chans, chans)

    latent = latents.reshape(area, chans)
    cot0 = cotangent.reshape(area, chans)
    params = jnp.concatenate([norm_gain, norm_shift])
    other_weight = swap(weight, "fsdp", CORE)
    cot1 = swap(cot0, "fsdp", ACROSS)
    cot2 = swap(cot0, "fsdp", ALONG)
    act0, stats = call(
        functools.partial(norm_kernel, GROUPS),
        [plane_b, shaped((2, chans), F32)],
        [latent, params],
    )
    act2 = swap(act0, "fsdp", ALONG)
    act1 = swap(act0, "fsdp", ACROSS)
    wide, turned, gather, scatter = call(
        functools.partial(prepare_kernel, side, taps),
        [shaped(window, BF16)] * 2 + [shaped((taps * area, area), BF16)] * 2,
        [info, weight, other_weight],
        order=[stats],
    )
    (moved,) = call(
        functools.partial(spread_kernel, taps), [columns(3)], [scatter, cot0, cot1, cot2]
    )
    cot1, cot2 = hold([cot1, cot2], [moved])
    grad0, grad1, grad2 = call(grad_kernel, [plane, plane_b, plane_b], [turned, moved])
    half = area // 2
    cot3 = [swap(cot2[:half], "fsdp", ACROSS), swap(cot1[half:], "fsdp", ALONG)]
    act2, act1 = hold([act2, act1], [grad0])
    act3 = [swap(act2[:half], "fsdp", ACROSS), swap(act1[half:], "fsdp", ALONG)]
    (part,) = call(
        functools.partial(weight_kernel, taps),
        [shaped(window, F32)],
        [moved, act0, act1, act2],
        [pltpu.VMEM((chans, 3 * area), BF16)],
    )
    (moved3,) = call(
        functools.partial(move_kernel, taps), [columns(1)], [scatter, *cot3], order=[part]
    )
    upper = rows // 32 * 16
    sends = call(
        functools.partial(finish_kernel, inv_batch),
        [shaped((upper, chans), BF16), shaped((rows - upper, chans), BF16)],
        [info, *act3, moved3, part],
        [pltpu.VMEM((2 * chans, area), BF16)],
    )
    got = [swap(send, "fsdp", CORE) for send in sends]
    (keep,) = call(
        functools.partial(keep_kernel, inv_batch),
        [shaped((rows, chans), F32)],
        [info, *act3, moved3, part],
        [pltpu.VMEM((2 * chans, area), BF16)],
        order=[sends[0]],
    )
    (narrow,) = call(join_kernel, [shaped((rows, chans), BF16)], [keep, *got])
    (grad3,) = call(diagonal_kernel, [plane_b], [turned, moved3], order=[narrow])
    pair1 = swap(narrow, "rep", 1)
    pair2 = swap(narrow, "rep", 2)

    masks = (ACROSS, ALONG, ACROSS | ALONG)
    grads = hold([grad1, grad2, grad3], [narrow])
    grads = [swap(value, "fsdp", mask) for value, mask in zip(grads, masks)]
    out0, out1, out2, out3 = call(
        functools.partial(out_kernel, taps),
        [plane, plane_b, plane_b, plane_b],
        [gather, wide, act0, act1, act2, *act3],
        [pltpu.VMEM((4 * area, taps * chans), BF16)],
        order=[narrow],
    )
    out1, out2 = hold([out1, out2], [narrow])
    out1, out2 = swap(out1, "fsdp", ACROSS), swap(out2, "fsdp", ALONG)

    input_grad, terms = call(
        functools.partial(back_kernel, GROUPS, inv_batch),
        [plane_b, shaped((2, chans), F32)],
        [latent, stats, params, grad0, *grads],
        order=[out3],
    )
    (last,) = hold([out3], [terms])
    last = swap(last, "fsdp", ACROSS | ALONG)
    terms = terms + swap(terms, "fsdp", ACROSS)
    (terms,) = hold([terms], [out1, out2])
    for mask in (ALONG, CORE):
        terms = terms + swap(terms, "fsdp", mask)
    (block_out,) = call(sum_kernel, [plane_b], [out0, out1, out2, last])
    (terms,) = hold([terms], [block_out])
    norm_avg = lax.cond(
        partner_bit[0] == 0,
        lambda own: 0.5 * (own + swap(own, "rep", 1)),
        lambda own: 0.5 * (own + swap(own, "rep", 2)),
        terms,
    )
    shard_bit = lax.dynamic_slice_in_dim(partner_bit, place, 1)
    (weight_avg,) = call(
        functools.partial(pair_kernel, 9),
        [shaped((rows, chans), F32)],
        [shard_bit, narrow, pair1, pair2],
        [
            pltpu.VMEM((rows, chans), F32),
            pltpu.VMEM((rows, chans), BF16),
            pltpu.SemaphoreType.DMA((9,)),
            pltpu.SemaphoreType.DMA((9,)),
        ],
        copies_out=True,
        outside=(2,),
    )
    shape = (1, side, side, chans)
    return (block_out.reshape(shape), input_grad.reshape(shape), weight_avg[None], norm_avg[None])


def solution(mesh):
    in_specs = (
        P(("rep", "fsdp"), None, None, None),
        P(("rep", "fsdp"), None, None, None),
        P("rep", "fsdp", None),
        P("rep", None),
        P("rep", None),
        P(),
    )
    out_specs = (
        P(("rep", "fsdp"), None, None, None),
        P(("rep", "fsdp"), None, None, None),
        P("rep", "fsdp", None),
        P("rep", None, None),
    )
    planes = mesh.shape["fsdp"] == 8 and mesh.shape["rep"] == 4
    shards = shards_plane if planes else shards_general
    return jax.shard_map(shards, mesh=mesh, in_specs=in_specs, out_specs=out_specs, check_vma=False)
```
